32 devices in a mesh: sect: 2 (over y), seq: 16 (over z, x, core).
Axes of the slice: x: 2, y: 2, z: 4, core: 2. Of those that a mesh axis runs over, the one named last changes fastest.
Arguments:
- queries: bfloat16 [1024, 2048], P('seq'), may hold values from -160 to 160
- key_tokens: bfloat16 [1024, 2048], P('seq'), may hold values from -6 to 6
- value_tokens: bfloat16 [1024, 2048], P('seq'), may hold values from -17 to 17
- latent: bfloat16 [64, 2560], P('seq'), may hold values from -6 to 6
- tile_rows: int32 [16], replicated, may hold values from 1 to 4, 32 in all
- conv_in_weight: bfloat16 [3, 3, 3, 16, 384], replicated, may hold values from -0.3125 to 0.3125
- conv_in_bias: float32 [384], replicated, may hold values from -3 to 3
- norm_gain: float32 [384], replicated, may hold values from 0.5 to 2
- conv_mid_weight: bfloat16 [3, 3, 3, 384, 384], replicated, may hold values from -0.0625 to 0.0625
- conv_mid_bias: float32 [384], replicated, may hold values from -3 to 3
Outputs:
- attended: bfloat16 [1024, 2048], P('seq', 'sect')
- frames: bfloat16 [2, 128, 80, 384], P(None, 'seq', 'sect')
The draws below stay inside these ranges and needn't reach their ends.
Inputs may be any that keep to these rules, and one draw needn't show every extreme that they name: `tile_rows`: the tiles cover the 32 token rows in order; some tile has exactly 4 rows.
All inputs are finite; a program needn't handle non-finite values.
Results may differ from the reference program's by a relative error of at most 0.012.
Values may be sent and summed in bfloat16 or wider, within the bound.
No kernel may reach another device: no remote copies, remote signals or barrier semaphores. Data moves between devices by JAX's collectives and lax.ppermute only.
A program may use at most 128 MiB of HBM per device.

```python
import math
import jax
import jax.numpy as jnp
import numpy as np
from jax import lax

DH = 128
CL = 16
CH = 384
LF = 2
MAXT = 4
D = 2048
TOKENS = 1024
GH = 32
GW = 40
N_SEQ = 16


def paired_draw(key):
    first_key, second_key = jax.random.split(jax.random.fold_in(key, 17), 2)
    shape = (TOKENS, D)
    query_part = jnp.clip(jax.random.normal(first_key, shape, jnp.float32), -6.0, 6.0)
    key_part = jnp.clip(jax.random.normal(second_key, shape, jnp.float32), -6.0, 6.0)
    return (query_part, key_part)


def draw_queries(key, part):
    return paired_draw(key)[0].astype(jnp.bfloat16)


def draw_key_tokens(key, part):
    return paired_draw(key)[1].astype(jnp.bfloat16)


def draw_value_tokens(key, part):
    value_key = jax.random.fold_in(jax.random.fold_in(key, 29), 0)
    shape = (TOKENS, D)
    values_drawn = jnp.clip(jax.random.normal(value_key, shape, jnp.float32), -6.0, 6.0)
    return values_drawn.astype(jnp.bfloat16)


def steps_of(rng, shape, cuts, low, largest):
    def one(dim, parts):
        draws = jax.random.uniform(jax.random.fold_in(jax.random.fold_in(rng, 6), dim), (parts,), jnp.float32, low / len(cuts), largest / len(cuts))
        return jnp.repeat(jnp.exp(draws), shape[dim] // parts).reshape((-1,) + (1,) * (len(shape) - dim - 1))

    level = one(*cuts[0])
    for cut in cuts[1:]:
        level = level * one(*cut)
    return level


def split_up(number_of, total, reach, lean):
    weights = [(1 << 20) // math.isqrt(standing ** lean) + 1 for standing in range(2, number_of + 1)]
    spare, counts = total - reach - (number_of - 1), [1] * (number_of - 1)
    while spare > 0:
        candidates = [i for i in range(number_of - 1) if counts[i] < reach]
        mass, left = sum([weights[i] for i in candidates]), spare
        for i in candidates:
            addition = min(reach - counts[i], max(1, left * weights[i] // mass), spare)
            counts[i] = counts[i] + addition
            spare = spare - addition
    return np.array([reach] + counts)


def uneven_parts(stream_key, number_of, total, bound, skew):
    if number_of == 2:
        one = jax.random.randint(stream_key, (), max(1, total - bound), min(bound, total - 1) + 1)
        return jnp.stack([one, total - one])
    lengths = jnp.asarray(split_up(number_of, total, bound, skew), jnp.int32)
    pairs = (number_of - 1) // 2
    source_of, sink = lengths[1:1 + 2 * pairs:2], lengths[2:2 + 2 * pairs:2]
    margin = jnp.minimum(source_of - 1, bound - sink)
    shifted = jax.random.randint(jax.random.fold_in(stream_key, 1), (pairs,), 0, 1 << 20) % (margin + 1)
    lengths = lengths.at[1:1 + 2 * pairs:2].set(source_of - shifted).at[2:2 + 2 * pairs:2].set(sink + shifted)
    return lengths[jax.random.permutation(jax.random.fold_in(stream_key, 2), number_of)]


def noise(rng, extent, deviation, limit, cuts=(), kind=jnp.bfloat16):
    entries = deviation * jax.random.normal(rng, extent, jnp.float32)
    if cuts:
        entries = entries * steps_of(rng, extent, cuts, -0.22, 0.18)
    return jnp.clip(entries, -limit, limit).astype(kind)


def setup_inputs(seed: int = 0) -> dict:
    seeds = jax.random.split(jax.random.key(seed), 11)
    queries = draw_queries(jax.random.fold_in(seeds[10], 71), 0)
    key_tokens = draw_key_tokens(jax.random.fold_in(seeds[10], 71), 0)
    value_tokens = draw_value_tokens(jax.random.fold_in(seeds[10], 71), 0)
    latent = noise(seeds[3], (LF * GH, GW * 4 * CL), 1.0, 6.0, ((0, 16),))
    tile_rows = uneven_parts(seeds[4], N_SEQ, GH, MAXT, 2).astype(jnp.int32)
    conv_in_weight = noise(seeds[5], (3, 3, 3, CL, CH), (27 * CL) ** -0.5, 0.3125)
    conv_in_bias = noise(seeds[6], (CH,), 0.5, 3.0, (), jnp.float32)
    norm_gain = jnp.clip(jnp.exp(jax.random.uniform(seeds[7], (CH,), jnp.float32, math.log(0.5), math.log(2.0))), 0.5, 2.0)
    conv_mid_weight = noise(seeds[8], (3, 3, 3, CH, CH), (27 * CH) ** -0.5, 0.0625)
    conv_mid_bias = noise(seeds[9], (CH,), 0.5, 3.0, (), jnp.float32)
    return dict(queries=queries, key_tokens=key_tokens, value_tokens=value_tokens, latent=latent, tile_rows=tile_rows, conv_in_weight=conv_in_weight, conv_in_bias=conv_in_bias, norm_gain=norm_gain, conv_mid_weight=conv_mid_weight, conv_mid_bias=conv_mid_bias)


def head_attention(query_head, key_head, value_head):
    block_rows = min(512, TOKENS)
    scale_factor = 1.0 / math.sqrt(DH)

    def one_block(query_block):
        scores = jnp.dot(query_block, key_head.T, preferred_element_type=jnp.float32) * scale_factor
        exponents = jnp.exp(scores - lax.optimization_barrier(jnp.max(scores, axis=1, keepdims=True)))
        totals = lax.optimization_barrier(jnp.sum(exponents, axis=1, keepdims=True))
        probabilities = exponents.astype(jnp.bfloat16)
        mixed = jnp.dot(probabilities, value_head, preferred_element_type=jnp.float32) / totals
        return mixed.astype(jnp.bfloat16)
    return lax.map(one_block, query_head.reshape(-1, block_rows, DH)).reshape(TOKENS, DH)

def split_heads(matrix, heads_total):
    return jnp.transpose(matrix.reshape(TOKENS, heads_total, DH), (1, 0, 2))

def causal_conv(field, kernel):
    result = lax.conv_general_dilated(field[None], kernel, (1, 1, 1), [(2, 0), (1, 1), (1, 1)], dimension_numbers=('NDHWC', 'DHWIO', 'NDHWC'), preferred_element_type=jnp.float32)
    return result[0]

def activate(hidden, norm_gain):
    values_wide = hidden.astype(jnp.float32)
    scaled = values_wide * lax.rsqrt(lax.optimization_barrier(jnp.mean(values_wide * values_wide, axis=-1, keepdims=True)) + 1e-06) * norm_gain
    return jax.nn.silu(scaled).astype(jnp.bfloat16)

def reference(queries, key_tokens, value_tokens, latent, tile_rows, conv_in_weight, conv_in_bias, norm_gain, conv_mid_weight, conv_mid_bias):
    heads_total = queries.shape[1] // DH

    def one_head(triple):
        return head_attention(triple[0], triple[1], triple[2])
    per_head = lax.map(one_head, (split_heads(queries, heads_total), split_heads(key_tokens, heads_total), split_heads(value_tokens, heads_total)))
    attended = jnp.transpose(per_head, (1, 0, 2)).reshape(TOKENS, heads_total * DH)
    grid = latent.reshape(LF, GH, GW, 2, 2, CL).transpose(0, 1, 3, 2, 4, 5).reshape(LF, 2 * GH, 2 * GW, CL)
    hidden_first = (causal_conv(grid, conv_in_weight) + conv_in_bias).astype(jnp.bfloat16)
    activated = activate(hidden_first, norm_gain)
    decoded = causal_conv(activated, conv_mid_weight) + conv_mid_bias + hidden_first.astype(jnp.float32)
    tile_starts = (jnp.cumsum(tile_rows) - tile_rows).astype(jnp.int32)
    offsets = jnp.arange(2 * MAXT, dtype=jnp.int32)
    row_index = 2 * tile_starts[:, None] + offsets[None, :]
    inside = offsets[None, :] < 2 * tile_rows[:, None]
    safe_index = jnp.where(inside, row_index, 0).reshape(-1).astype(jnp.int32)
    picked = jnp.take(decoded, safe_index, axis=1)
    frames = jnp.where(inside.reshape(-1)[None, :, None, None], picked, 0.0).astype(jnp.bfloat16)
    return (attended, frames)
```

```python
import functools
import math

import jax
import jax.numpy as jnp
from jax import lax
from jax.experimental import pallas as pl
from jax.experimental.pallas import tpu as pltpu
from jax.sharding import PartitionSpec as P

DH = 128
LF = 2
MAXT = 4
TAPS = (1, 2)
ROWS = 2 * MAXT
UNITS = 3 * LF * ROWS
VMEM_LIMIT = 56 * 1024 * 1024


def parity_groups(devices):
    return [list(range(parity, devices, 2)) for parity in range(2)]


def pack_body(section_ref, query_ref, key_ref, value_ref, out_ref):
    for head in range(out_ref.shape[0]):
        columns = slice(head * DH, (head + 1) * DH)
        for place, ref in enumerate((query_ref, key_ref, value_ref)):
            out_ref[head, place] = ref[:, columns]


def pack_heads(section, queries, key_tokens, value_tokens):
    token_rows, width = queries.shape
    heads = width // DH // lax.axis_size("sect")
    steps = 2
    block = pl.BlockSpec((token_rows, heads // steps * DH), lambda i, sec: (0, sec[0] * steps + i))
    return pl.pallas_call(
        pack_body,
        grid_spec=pltpu.PrefetchScalarGridSpec(
            num_scalar_prefetch=1,
            grid=(steps,),
            in_specs=[block] * 3,
            out_specs=pl.BlockSpec(
                (heads // steps, 3, token_rows, DH), lambda i, sec: (i, 0, 0, 0)
            ),
        ),
        out_shape=jax.ShapeDtypeStruct((heads, 3, token_rows, DH), queries.dtype),
        name="pack_heads",
    )(section, queries, key_tokens, value_tokens)


def softmax_part(query, key, value):
    scores = lax.dot_general(
        query, key, (((1,), (1,)), ((), ())), preferred_element_type=jnp.float32
    ) * (1.0 / math.sqrt(DH))
    largest = jnp.max(scores, axis=1, keepdims=True)
    exponents = jnp.exp(scores - largest)
    totals = jnp.sum(exponents, axis=1, keepdims=True)
    mixed = jnp.dot(exponents.astype(jnp.bfloat16), value, preferred_element_type=jnp.float32)
    return largest, totals, mixed


def flat(array):
    return array.reshape(-1, array.shape[-1])


def own_body(query_ref, kv_ref, mixed_ref, largest_ref, totals_ref):
    largest, totals, mixed = softmax_part(
        flat(query_ref[:, 0]), flat(kv_ref[:, 1]), flat(kv_ref[:, 2])
    )
    mixed_ref[...] = mixed
    largest_ref[...] = largest
    totals_ref[...] = totals


def merge_body(query_ref, kv_ref, mixed_ref, largest_ref, totals_ref, out_ref):
    largest, totals, mixed = softmax_part(
        flat(query_ref[:, 0]), flat(kv_ref[:, 1]), flat(kv_ref[:, 2])
    )
    top = jnp.maximum(largest, largest_ref[...])
    here = jnp.exp(largest - top)
    there = jnp.exp(largest_ref[...] - top)
    totals = totals * here + totals_ref[...] * there
    mixed = mixed * here + mixed_ref[...] * there
    out_ref[...] = (mixed / totals).astype(out_ref.dtype).reshape(out_ref.shape)


def attend(own, other_of):
    members, _, token_rows, _ = own.shape
    block = min(8, members)
    rows = block * token_rows
    total = members * token_rows
    query_spec = pl.BlockSpec((block, 1, token_rows, DH), lambda i: (i, 0, 0, 0))
    kv_spec = pl.BlockSpec(own.shape, lambda i: (0, 0, 0, 0))
    mixed_spec = pl.BlockSpec((rows, DH), lambda i: (i, 0))
    stat_spec = pl.BlockSpec((rows, 1), lambda i: (i, 0))
    flops = 4 * total * total * DH
    cost = pl.CostEstimate(flops=flops, bytes_accessed=4 * total * DH, transcendentals=total**2)
    params = pltpu.CompilerParams(vmem_limit_bytes=VMEM_LIMIT)
    stats = jax.ShapeDtypeStruct((total, 1), jnp.float32)
    mixed, largest, totals = pl.pallas_call(
        own_body,
        grid=(members // block,),
        in_specs=[query_spec, kv_spec],
        out_specs=[mixed_spec, stat_spec, stat_spec],
        out_shape=[jax.ShapeDtypeStruct((total, DH), jnp.float32), stats, stats],
        compiler_params=params,
        cost_estimate=cost,
        name="attend_own",
    )(own, own)
    other = other_of()
    return pl.pallas_call(
        merge_body,
        grid=(members // block,),
        in_specs=[query_spec, kv_spec, mixed_spec, stat_spec, stat_spec],
        out_specs=pl.BlockSpec((block, token_rows, DH), lambda i: (i, 0, 0)),
        out_shape=jax.ShapeDtypeStruct((members, token_rows, DH), own.dtype),
        compiler_params=params,
        cost_estimate=cost,
        name="attend_merge",
    )(own, other, mixed, largest, totals)


def unpack_body(in_ref, out_ref):
    for head in range(in_ref.shape[0]):
        out_ref[:, head * DH : (head + 1) * DH] = in_ref[head]


def unpack_heads(array):
    heads, token_rows, _ = array.shape
    return pl.pallas_call(
        unpack_body,
        out_shape=jax.ShapeDtypeStruct((token_rows, heads * DH), array.dtype),
        name="unpack_heads",
    )(array)


def decode_body(
    grid_rows,
    width,
    place_ref,
    latent_ref,
    in_weight_ref,
    in_bias_ref,
    gain_ref,
    mid_weight_ref,
    mid_bias_ref,
    out_ref,
    mid_weight,
    taps,
    patches,
    active,
    hidden_mid,
    summed,
    weight_sems,
):
    corners = active.shape[2] // 16
    channels = in_weight_ref.shape[3]
    features = in_weight_ref.shape[4]
    columns = out_ref.shape[2]
    first_row, filled, section = place_ref[0], place_ref[1], place_ref[2]

    def load(row_tap):
        return [
            pltpu.make_async_copy(
                mid_weight_ref.at[tap, row_tap, col_tap],
                mid_weight.at[row_tap, col_tap, pl.ds(slot * features, features)],
                weight_sems.at[row_tap, col_tap, slot],
            )
            for col_tap in range(3)
            for slot, tap in enumerate(TAPS)
        ]

    for row_tap in range(3):
        for copy in load(row_tap):
            copy.start()

    nothing = jnp.zeros((channels, features), jnp.bfloat16)
    base = 0
    for tap in TAPS:
        for row_parity in range(2):
            for i, j, p, q in [
                (i, j, p, q) for i in range(2) for j in range(2) for p in range(2) for q in range(2)
            ]:
                for col_parity in range(2):
                    row_tap, col_tap = 2 * i + p - row_parity, 2 * j + q - col_parity
                    inside = 0 <= row_tap < 3 and 0 <= col_tap < 3
                    taps[base : base + channels, col_parity * features : (col_parity + 1) * features] = (
                        in_weight_ref[tap, row_tap, col_tap] if inside else nothing
                    )
                base += channels

    held_rows = latent_ref.shape[0]
    unit = lax.broadcasted_iota(jnp.int32, (UNITS, held_rows), 0)
    held = lax.broadcasted_iota(jnp.int32, (UNITS, held_rows), 1)
    reach = (unit >> 4) + (unit & 7)
    frame = (unit >> 3) & 1
    group = 0
    for tap in TAPS:
        for row_parity in range(2):
            for i in range(2):
                token_row = first_row + (reach >> 1) - 1 + i
                source = frame + tap - 2
                wanted = (
                    ((reach & 1) == row_parity)
                    & (token_row >= 0)
                    & (token_row < grid_rows)
                    & (source >= 0)
                )
                target = jnp.where(wanted, source * grid_rows + token_row, -1)
                selector = jnp.where(held == target, 1.0, 0.0).astype(jnp.bfloat16)
                picked = jnp.dot(selector, latent_ref[...], preferred_element_type=jnp.float32)
                aside = picked[:, 64 : 64 + corners // 2 * 128]
                lanes = slice(group * 128, (group + 1) * 128)
                for corner in range(corners):
                    chunk = slice(corner // 2 * 128, corner // 2 * 128 + 128)
                    piece = (aside if corner % 2 else picked)[:, chunk]
                    patches[corner * UNITS : (corner + 1) * UNITS, lanes] = piece.astype(jnp.bfloat16)
                group += 1

    unit_row = lax.broadcasted_iota(jnp.int32, (UNITS, 1), 0)
    pixel_row = 2 * first_row + (unit_row >> 4) + (unit_row & 7) - 1
    row_inside = (pixel_row >= 0) & (pixel_row < 2 * grid_rows)
    step_corners = 3

    def first_layer(step, carried):
        start = pl.multiple_of(step * step_corners * UNITS, 16)
        block = jnp.dot(
            patches[pl.ds(start, step_corners * UNITS)],
            taps[...],
            preferred_element_type=jnp.float32,
        )
        hiddens, actives = [carried[0]], [carried[1]]
        for corner in range(step_corners):
            for col_parity in range(2):
                hidden = (
                    block[
                        corner * UNITS : (corner + 1) * UNITS,
                        col_parity * features : (col_parity + 1) * features,
                    ]
                    + in_bias_ref[...]
                )
                hidden = hidden.astype(jnp.bfloat16).astype(jnp.float32)
                scale = lax.rsqrt(jnp.mean(hidden * hidden, axis=1, keepdims=True) + 1e-06)
                scaled = hidden * scale * gain_ref[...]
                activated = scaled / (1.0 + jnp.exp(-scaled))
                pixel = section * columns + 2 * (step * step_corners + corner) + col_parity - 1
                keep = row_inside & (pixel >= 0) & (pixel < width)
                actives.append(jnp.where(keep, activated, 0.0))
                hiddens.append(hidden[16:32])
        for pair in range(step_corners):
            at = pl.ds(pl.multiple_of((step * step_corners + pair) * 16, 16), 16)
            for phase in range(2):
                left, right = actives[2 * pair + 1 - phase], actives[2 * pair + 2 - phase]
                for row_tap in range(3):
                    for field in range(LF):
                        low = row_tap * 16 + field * 8
                        joined = jnp.concatenate([left[low : low + 8], right[low : low + 8]], axis=0)
                        active[row_tap, phase, at, field * features : (field + 1) * features] = (
                            joined.astype(jnp.bfloat16)
                        )
            left, right = hiddens[2 * pair], hiddens[2 * pair + 1]
            for field in range(LF):
                low = field * 8
                joined = jnp.concatenate([left[low : low + 8], right[low : low + 8]], axis=0)
                hidden_mid[at, field * features : (field + 1) * features] = joined.astype(jnp.bfloat16)
        return hiddens[-1], actives[-1]

    lax.fori_loop(
        0,
        corners // step_corners,
        first_layer,
        (jnp.zeros((16, features), jnp.float32), jnp.zeros((UNITS, features), jnp.float32)),
    )

    rows = columns * ROWS
    for row_tap in range(3):
        for copy in load(row_tap):
            copy.wait()
        early, late = None, None
        for col_tap in range(3):
            low = 0 if col_tap == 0 else 16
            window = active[row_tap, col_tap % 2, low : low + rows]
            first = jnp.dot(
                window[:, :features],
                mid_weight[row_tap, col_tap, features:],
                preferred_element_type=jnp.float32,
            )
            second = jnp.dot(
                window, mid_weight[row_tap, col_tap], preferred_element_type=jnp.float32
            )
            early = first if early is None else early + first
            late = second if late is None else late + second
        for field, part in enumerate((early, late)):
            for lane in range(features // 128):
                lanes = slice(lane * 128, (lane + 1) * 128)
                value = part[:, lanes]
                if row_tap:
                    value = value + summed[field, lane]
                if row_tap == 2:
                    from_lane = field * features + lane * 128
                    value = (
                        value
                        + mid_bias_ref[:, lanes]
                        + hidden_mid[16 : 16 + rows, from_lane : from_lane + 128].astype(jnp.float32)
                    )
                summed[field, lane] = value

    for field in range(LF):
        for row in range(ROWS):
            for lane in range(features // 128):
                value = summed[field, lane, pl.ds(row, columns, stride=ROWS), :]
                value = jnp.where(row < 2 * filled, value, 0.0)
                out_ref[field, row, :, lane * 128 : (lane + 1) * 128] = value.astype(jnp.bfloat16)


def decode_tile(
    section,
    latent,
    tile_rows,
    conv_in_weight,
    conv_in_bias,
    norm_gain,
    conv_mid_weight,
    conv_mid_bias,
):
    devices = lax.axis_size("seq")
    sections = lax.axis_size("sect")
    position = lax.axis_index("seq")
    channels, features = conv_in_weight.shape[3:]
    token_width = 4 * channels
    tokens = latent.shape[1] // token_width
    grid_rows = latent.shape[0] * devices // LF
    width = 2 * tokens
    columns = width // sections
    span = tokens // sections
    tile_starts = jnp.cumsum(tile_rows) - tile_rows
    place = jnp.stack([tile_starts[position], tile_rows[position], section]).astype(jnp.int32)
    padded = jnp.pad(latent, ((0, 0), (token_width, token_width)))
    share = lax.dynamic_slice_in_dim(
        padded, section * span * token_width, (span + 2) * token_width, 1
    )
    gathered = lax.all_gather(share, "seq", axis=0, tiled=True)
    corners = span + 1
    vmem = pl.BlockSpec(memory_space=pltpu.VMEM)
    slots = len(TAPS)
    return pl.pallas_call(
        functools.partial(decode_body, grid_rows, width),
        in_specs=[
            pl.BlockSpec(memory_space=pltpu.SMEM),
            vmem,
            vmem,
            vmem,
            vmem,
            pl.BlockSpec(memory_space=pl.ANY),
            vmem,
        ],
        out_specs=vmem,
        out_shape=jax.ShapeDtypeStruct((LF, ROWS, columns, features), jnp.bfloat16),
        scratch_shapes=[
            pltpu.VMEM((3, 3, slots * features, features), jnp.bfloat16),
            pltpu.VMEM((slots * 2 * 4 * token_width, 2 * features), jnp.bfloat16),
            pltpu.VMEM((corners * UNITS, slots * 2 * 4 * token_width), jnp.bfloat16),
            pltpu.VMEM((3, 2, corners * 16, LF * features), jnp.bfloat16),
            pltpu.VMEM((corners * 16, LF * features), jnp.bfloat16),
            pltpu.VMEM((LF, features // 128, columns * ROWS, 128), jnp.float32),
            pltpu.SemaphoreType.DMA((3, 3, slots)),
        ],
        compiler_params=pltpu.CompilerParams(vmem_limit_bytes=VMEM_LIMIT),
        cost_estimate=pl.CostEstimate(
            flops=2 * 3 * 9 * columns * ROWS * features * features,
            bytes_accessed=slots * 9 * features * features * 2,
            transcendentals=corners * UNITS * 2 * features,
        ),
        name="decode_tile",
    )(
        place,
        gathered,
        conv_in_weight,
        conv_in_bias.reshape(1, -1),
        norm_gain.reshape(1, -1),
        conv_mid_weight,
        conv_mid_bias.reshape(1, -1),
    )


def attend_tokens(section, queries, key_tokens, value_tokens):
    devices = lax.axis_size("seq")
    groups = parity_groups(devices)
    packed = pack_heads(section.reshape(1), queries, key_tokens, value_tokens)
    own = lax.all_to_all(packed, "seq", 0, 0, axis_index_groups=groups, tiled=True)
    pairs = [(i, i ^ 1) for i in range(devices)]
    mixed = attend(own, lambda: lax.ppermute(own, "seq", pairs))
    returned = lax.all_to_all(mixed, "seq", 0, 0, axis_index_groups=groups, tiled=True)
    return unpack_heads(returned)


def on_device(
    queries,
    key_tokens,
    value_tokens,
    latent,
    tile_rows,
    conv_in_weight,
    conv_in_bias,
    norm_gain,
    conv_mid_weight,
    conv_mid_bias,
):
    section = lax.axis_index("sect").astype(jnp.int32)
    attended = attend_tokens(section, queries, key_tokens, value_tokens)
    frames = decode_tile(
        section,
        latent,
        tile_rows,
        conv_in_weight,
        conv_in_bias,
        norm_gain,
        conv_mid_weight,
        conv_mid_bias,
    )
    return (attended, frames)


def solution(mesh):
    in_specs = (
        P("seq", None),
        P("seq", None),
        P("seq", None),
        P("seq", None),
        P(),
        P(),
        P(),
        P(),
        P(),
        P(),
    )
    out_specs = (P("seq", "sect"), P(None, "seq", "sect", None))
    return jax.shard_map(
        on_device, mesh=mesh, in_specs=in_specs, out_specs=out_specs, check_vma=False
    )
```

```python
import functools
import math

import jax
import jax.numpy as jnp
from jax import lax
from jax.experimental import pallas as pl
from jax.experimental.pallas import tpu as pltpu
from jax.sharding import PartitionSpec as P

DH = 128
LF = 2
MAXT = 4
TAPS = (1, 2)
ROWS = 2 * MAXT
UNITS = 3 * LF * ROWS
ATTEND_VMEM = 32 * 1024 * 1024
DECODE_VMEM = 48 * 1024 * 1024


def parity_groups(devices):
    return [list(range(parity, devices, 2)) for parity in range(2)]


def pack_body(query_ref, key_ref, value_ref, latent_ref, packed_ref, share_ref, sems):
    heads = packed_ref.shape[0]
    section = lax.axis_index("sect")
    copies = []
    for head in range(heads):
        columns = pl.ds(pl.multiple_of((section * heads + head) * DH, DH), DH)
        for place, ref in enumerate((query_ref, key_ref, value_ref)):
            copy = pltpu.make_async_copy(
                ref.at[:, columns], packed_ref.at[head, place], sems.at[head, place]
            )
            copy.start()
            copies.append(copy)
    rows, width = latent_ref.shape
    span = share_ref.shape[2]
    rim = (2 * span - width) // 4
    wide = latent_ref[...].astype(jnp.float32)
    rim_zeros = jnp.zeros((rows, rim), jnp.float32)
    lower = jnp.concatenate([rim_zeros, wide[:, : span - rim]], axis=1)
    upper = jnp.concatenate([wide[:, width - span + rim :], rim_zeros], axis=1)
    share = jnp.where(section == 0, lower, upper).astype(share_ref.dtype)
    for member in range(share_ref.shape[0]):
        share_ref[member] = share
    for copy in copies:
        copy.wait()


def pack_heads(queries, key_tokens, value_tokens, latent, token_width):
    token_rows, width = queries.shape
    sections = lax.axis_size("sect")
    heads = width // DH // sections
    span = latent.shape[1] // sections + 2 * token_width
    hbm = pl.BlockSpec(memory_space=pl.ANY)
    vmem = pl.BlockSpec(memory_space=pltpu.VMEM)
    return pl.pallas_call(
        pack_body,
        in_specs=[hbm, hbm, hbm, vmem],
        out_specs=[vmem, vmem],
        out_shape=[
            jax.ShapeDtypeStruct((heads, 3, token_rows, DH), queries.dtype),
            jax.ShapeDtypeStruct((lax.axis_size("seq"), latent.shape[0], span), latent.dtype),
        ],
        scratch_shapes=[pltpu.SemaphoreType.DMA((heads, 3))],
        name="pack_heads",
    )(queries, key_tokens, value_tokens, latent)


def flat(array):
    return array.reshape(-1, array.shape[-1])


def attend_body(block, own_ref, other_ref, out_ref):
    members, _, token_rows, _ = own_ref.shape
    keys = jnp.concatenate([flat(own_ref[:, 1]), flat(other_ref[:, 1])], axis=0)
    values = jnp.concatenate([flat(own_ref[:, 2]), flat(other_ref[:, 2])], axis=0)

    def one_block(step):
        at = pl.ds(step * block, block)
        scores = lax.dot_general(
            flat(own_ref[at, 0]),
            keys,
            (((1,), (1,)), ((), ())),
            preferred_element_type=jnp.float32,
        ) * (1.0 / math.sqrt(DH))
        exponents = jnp.exp(scores - jnp.max(scores, axis=1, keepdims=True))
        totals = jnp.sum(exponents, axis=1, keepdims=True)
        mixed = jnp.dot(
            exponents.astype(jnp.bfloat16), values, preferred_element_type=jnp.float32
        )
        out_ref[at] = (mixed / totals).astype(out_ref.dtype).reshape(block, token_rows, DH)

    if members <= 8:
        for step in range(members // block):
            one_block(step)
    else:
        pl.loop(0, members // block)(one_block)


def attend(own, other):
    members, _, token_rows, _ = own.shape
    total = members * token_rows
    vmem = pl.BlockSpec(memory_space=pltpu.VMEM)
    return pl.pallas_call(
        functools.partial(attend_body, min(4, members)),
        in_specs=[vmem, vmem],
        out_specs=vmem,
        out_shape=jax.ShapeDtypeStruct((members, token_rows, DH), own.dtype),
        compiler_params=pltpu.CompilerParams(vmem_limit_bytes=ATTEND_VMEM),
        cost_estimate=pl.CostEstimate(
            flops=8 * total * total * DH,
            bytes_accessed=7 * total * DH * 2,
            transcendentals=2 * total * total,
        ),
        name="attend",
    )(own, other)


def unpack_body(in_ref, out_ref):
    for head in range(in_ref.shape[0]):
        out_ref[:, head * DH : (head + 1) * DH] = in_ref[head]


def unpack_heads(array):
    heads, token_rows, _ = array.shape
    return pl.pallas_call(
        unpack_body,
        in_specs=[pl.BlockSpec(memory_space=pltpu.VMEM)],
        out_shape=jax.ShapeDtypeStruct((token_rows, heads * DH), array.dtype),
        name="unpack_heads",
    )(array)


def decode_body(
    grid_rows,
    width,
    tile_ref,
    latent_ref,
    in_weight_ref,
    in_bias_ref,
    gain_ref,
    mid_weight_ref,
    mid_bias_ref,
    out_ref,
    mid_weight,
    taps,
    rows_held,
    patches,
    active,
    hidden_mid,
    summed,
    weight_sems,
):
    corners = active.shape[1] // 16
    channels = in_weight_ref.shape[3]
    features = in_weight_ref.shape[4]
    columns = out_ref.shape[2]
    position = lax.axis_index("seq")
    section = lax.axis_index("sect")
    filled = tile_ref[position]
    first_row = lax.fori_loop(0, position, lambda d, total: total + tile_ref[d], jnp.int32(0))

    def load(col_tap):
        return [
            pltpu.make_async_copy(
                mid_weight_ref.at[tap, row_tap, col_tap],
                mid_weight.at[col_tap, pl.ds((slot * 3 + row_tap) * features, features)],
                weight_sems.at[col_tap, row_tap, slot],
            )
            for row_tap in range(3)
            for slot, tap in enumerate(TAPS)
        ]

    for col_tap in range(3):
        for copy in load(col_tap):
            copy.start()

    nothing = jnp.zeros((channels, features), jnp.bfloat16)
    base = 0
    for tap in TAPS:
        for row_parity in range(2):
            for i, j, p, q in [
                (i, j, p, q) for i in range(2) for j in range(2) for p in range(2) for q in range(2)
            ]:
                for col_parity in range(2):
                    row_tap, col_tap = 2 * i + p - row_parity, 2 * j + q - col_parity
                    inside = 0 <= row_tap < 3 and 0 <= col_tap < 3
                    taps[base : base + channels, col_parity * features : (col_parity + 1) * features] = (
                        in_weight_ref[tap, row_tap, col_tap] if inside else nothing
                    )
                base += channels

    members, share_rows, _ = latent_ref.shape
    for member in range(members):
        rows_held[member * share_rows : (member + 1) * share_rows] = latent_ref[member].astype(
            jnp.float32
        )
    latent = rows_held[...]
    held_rows = latent.shape[0]
    aside = pltpu.roll(latent, latent.shape[1] - 64, 1).astype(jnp.bfloat16)
    latent = latent.astype(jnp.bfloat16)
    unit = lax.broadcasted_iota(jnp.int32, (UNITS, held_rows), 0)
    held = lax.broadcasted_iota(jnp.int32, (UNITS, held_rows), 1)
    reach = (unit >> 4) + (unit & 7)
    frame = (unit >> 3) & 1
    selectors = []
    for tap in TAPS:
        for row_parity in range(2):
            for i in range(2):
                token_row = first_row + (reach >> 1) - 1 + i
                source = frame + tap - 2
                wanted = (
                    ((reach & 1) == row_parity)
                    & (token_row >= 0)
                    & (token_row < grid_rows)
                    & (source >= 0)
                )
                target = jnp.where(wanted, source * grid_rows + token_row, -1)
                selectors.append(jnp.where(held == target, 1.0, 0.0).astype(jnp.bfloat16))
    selector = jnp.concatenate(selectors, axis=0)
    even = jnp.dot(selector, latent, preferred_element_type=jnp.float32).astype(jnp.bfloat16)
    odd = jnp.dot(
        selector, aside[:, : corners // 2 * 128], preferred_element_type=jnp.float32
    ).astype(jnp.bfloat16)
    for corner in range(corners):
        chunk = slice(corner // 2 * 128, corner // 2 * 128 + 128)
        for group in range(len(selectors)):
            patches[corner * UNITS : (corner + 1) * UNITS, group * 128 : (group + 1) * 128] = (
                odd if corner % 2 else even
            )[group * UNITS : (group + 1) * UNITS, chunk]

    unit_row = lax.broadcasted_iota(jnp.int32, (UNITS, 1), 0)
    pixel_row = 2 * first_row + (unit_row >> 4) + (unit_row & 7) - 1
    row_inside = (pixel_row >= 0) & (pixel_row < 2 * grid_rows)
    step_corners = 3
    in_bias = in_bias_ref[...].reshape(1, features)
    half_gain = gain_ref[...].reshape(1, features) * 0.5

    def first_layer(step, carried):
        start = pl.multiple_of(step * step_corners * UNITS, 16)
        block = jnp.dot(
            patches[pl.ds(start, step_corners * UNITS)],
            taps[...],
            preferred_element_type=jnp.float32,
        )
        hiddens, actives = [carried[0]], [carried[1]]
        for corner in range(step_corners):
            for col_parity in range(2):
                hidden = (
                    block[
                        corner * UNITS : (corner + 1) * UNITS,
                        col_parity * features : (col_parity + 1) * features,
                    ]
                    + in_bias
                )
                hidden = hidden.astype(jnp.bfloat16).astype(jnp.float32)
                scale = lax.rsqrt(jnp.mean(hidden * hidden, axis=1, keepdims=True) + 1e-06)
                pixel = section * columns + 2 * (step * step_corners + corner) + col_parity - 1
                keep = row_inside & (pixel >= 0) & (pixel < width)
                half = hidden * jnp.where(keep, scale, 0.0) * half_gain
                actives.append(half + half * jnp.tanh(half))
                hiddens.append(hidden[16:32])
        for pair in range(step_corners):
            at = pl.ds(pl.multiple_of((step * step_corners + pair) * 16, 16), 16)
            for phase in range(2):
                left, right = actives[2 * pair + 1 - phase], actives[2 * pair + 2 - phase]
                for field in range(LF):
                    for row_tap in range(3):
                        low = row_tap * 16 + field * 8
                        lane = (field * 3 + row_tap) * features
                        joined = jnp.concatenate([left[low : low + 8], right[low : low + 8]], axis=0)
                        active[phase, at, lane : lane + features] = joined.astype(jnp.bfloat16)
            left, right = hiddens[2 * pair], hiddens[2 * pair + 1]
            for field in range(LF):
                low = field * 8
                joined = jnp.concatenate([left[low : low + 8], right[low : low + 8]], axis=0)
                hidden_mid[at, field * features : (field + 1) * features] = joined.astype(jnp.bfloat16)
        return hiddens[-1], actives[-1]

    lax.fori_loop(
        0,
        corners // step_corners,
        first_layer,
        (jnp.zeros((16, features), jnp.float32), jnp.zeros((UNITS, features), jnp.float32)),
    )

    rows = columns * ROWS
    depth = 3 * features
    mid_bias = mid_bias_ref[...].reshape(1, features)
    for col_tap in range(3):
        for copy in load(col_tap):
            copy.wait()
        low = 0 if col_tap == 0 else 16
        window = active[col_tap % 2, low : low + rows]
        early = jnp.dot(
            window[:, :depth], mid_weight[col_tap, depth:], preferred_element_type=jnp.float32
        )
        late = jnp.dot(window, mid_weight[col_tap], preferred_element_type=jnp.float32)
        for field, part in enumerate((early, late)):
            for lane in range(features // 128):
                lanes = slice(lane * 128, (lane + 1) * 128)
                value = part[:, lanes]
                if col_tap:
                    value = value + summed[field, lane]
                if col_tap == 2:
                    from_lane = field * features + lane * 128
                    value = (
                        value
                        + mid_bias[:, lanes]
                        + hidden_mid[16 : 16 + rows, from_lane : from_lane + 128].astype(jnp.float32)
                    )
                summed[field, lane] = value

    for field in range(LF):
        for row in range(ROWS):
            for lane in range(features // 128):
                value = summed[field, lane, pl.ds(row, columns, stride=ROWS), :]
                value = jnp.where(row < 2 * filled, value, 0.0)
                out_ref[field, row, :, lane * 128 : (lane + 1) * 128] = value.astype(jnp.bfloat16)


def decode_tile(
    latent,
    grid_rows,
    tile_rows,
    conv_in_weight,
    conv_in_bias,
    norm_gain,
    conv_mid_weight,
    conv_mid_bias,
):
    sections = lax.axis_size("sect")
    channels, features = conv_in_weight.shape[3:]
    token_width = 4 * channels
    span = latent.shape[2] // token_width - 2
    columns = 2 * span
    corners = span + 1
    vmem = pl.BlockSpec(memory_space=pltpu.VMEM)
    slots = len(TAPS)
    depth = slots * 2 * 4 * token_width
    return pl.pallas_call(
        functools.partial(decode_body, grid_rows, columns * sections),
        in_specs=[
            pl.BlockSpec(memory_space=pltpu.SMEM),
            vmem,
            vmem,
            vmem,
            vmem,
            pl.BlockSpec(memory_space=pl.ANY),
            vmem,
        ],
        out_specs=vmem,
        out_shape=jax.ShapeDtypeStruct((LF, ROWS, columns, features), jnp.bfloat16),
        scratch_shapes=[
            pltpu.VMEM((3, slots * 3 * features, features), jnp.bfloat16),
            pltpu.VMEM((depth, 2 * features), jnp.bfloat16),
            pltpu.VMEM((latent.shape[0] * latent.shape[1], latent.shape[2]), jnp.float32),
            pltpu.VMEM((corners * UNITS, depth), jnp.bfloat16),
            pltpu.VMEM((2, corners * 16, LF * 3 * features), jnp.bfloat16),
            pltpu.VMEM((corners * 16, LF * features), jnp.bfloat16),
            pltpu.VMEM((LF, features // 128, columns * ROWS, 128), jnp.float32),
            pltpu.SemaphoreType.DMA((3, 3, slots)),
        ],
        compiler_params=pltpu.CompilerParams(vmem_limit_bytes=DECODE_VMEM),
        cost_estimate=pl.CostEstimate(
            flops=2 * 3 * 9 * columns * ROWS * features * features,
            bytes_accessed=slots * 9 * features * features * 2,
            transcendentals=corners * UNITS * 2 * features,
        ),
        name="decode_tile",
    )(
        tile_rows,
        latent,
        conv_in_weight,
        conv_in_bias,
        norm_gain,
        conv_mid_weight,
        conv_mid_bias,
    )


def on_device(
    queries,
    key_tokens,
    value_tokens,
    latent,
    tile_rows,
    conv_in_weight,
    conv_in_bias,
    norm_gain,
    conv_mid_weight,
    conv_mid_bias,
):
    devices = lax.axis_size("seq")
    groups = parity_groups(devices)
    grid_rows = latent.shape[0] * devices // LF
    packed, share = pack_heads(
        queries, key_tokens, value_tokens, latent, 4 * conv_in_weight.shape[3]
    )
    own = lax.all_to_all(packed, "seq", 0, 0, axis_index_groups=groups, tiled=True)
    gathered = lax.all_to_all(share, "seq", 0, 0, tiled=True)
    frames = decode_tile(
        gathered,
        grid_rows,
        tile_rows,
        conv_in_weight,
        conv_in_bias,
        norm_gain,
        conv_mid_weight,
        conv_mid_bias,
    )
    own, frames = lax.optimization_barrier((own, frames))
    other = lax.ppermute(own, "seq", [(i, i ^ 1) for i in range(devices)])
    mixed = attend(own, other)
    returned = lax.all_to_all(mixed, "seq", 0, 0, axis_index_groups=groups, tiled=True)
    return (unpack_heads(returned), frames)


def solution(mesh):
    in_specs = (
        P("seq", None),
        P("seq", None),
        P("seq", None),
        P("seq", None),
        P(),
        P(),
        P(),
        P(),
        P(),
        P(),
    )
    out_specs = (P("seq", "sect"), P(None, "seq", "sect", None))
    return jax.shard_map(
        on_device, mesh=mesh, in_specs=in_specs, out_specs=out_specs, check_vma=False
    )
```

```python
import functools
import math

import jax
import jax.numpy as jnp
from jax import lax
from jax.experimental import pallas as pl
from jax.experimental.pallas import tpu as pltpu
from jax.sharding import PartitionSpec as P

DH = 128
LF = 2
MAXT = 4
TAPS = (1, 2)
ROWS = 2 * MAXT
UNITS = 3 * LF * ROWS
DECODE_VMEM = 44 * 1024 * 1024
ATTEND_VMEM = 32 * 1024 * 1024
COPY_VMEM = 16 * 1024 * 1024


def parity_groups(devices):
    return [list(range(parity, devices, 2)) for parity in range(2)]


def pack_body(query_ref, key_ref, value_ref, latent_ref, packed_ref, share_ref, sems):
    heads = packed_ref.shape[0]
    section = lax.axis_index("sect")
    copies = []
    for head in range(heads):
        columns = pl.ds(pl.multiple_of((section * heads + head) * DH, DH), DH)
        for place, ref in enumerate((query_ref, key_ref, value_ref)):
            copy = pltpu.make_async_copy(
                ref.at[:, columns], packed_ref.at[head, place], sems.at[head, place]
            )
            copy.start()
            copies.append(copy)
    rows, width = latent_ref.shape
    span = share_ref.shape[1]
    rim = (2 * span - width) // 4
    wide = latent_ref[...].astype(jnp.float32)
    rim_zeros = jnp.zeros((rows, rim), jnp.float32)
    lower = jnp.concatenate([rim_zeros, wide[:, : span - rim]], axis=1)
    upper = jnp.concatenate([wide[:, width - span + rim :], rim_zeros], axis=1)
    share_ref[...] = jnp.where(section == 0, lower, upper).astype(share_ref.dtype)
    for copy in copies:
        copy.wait()


def pack_heads(queries, key_tokens, value_tokens, latent, token_width):
    token_rows, width = queries.shape
    sections = lax.axis_size("sect")
    heads = width // DH // sections
    span = latent.shape[1] // sections + 2 * token_width
    hbm = pl.BlockSpec(memory_space=pltpu.HBM)
    vmem = pl.BlockSpec(memory_space=pltpu.VMEM)
    return pl.pallas_call(
        pack_body,
        in_specs=[hbm, hbm, hbm, vmem],
        out_specs=[hbm, vmem],
        out_shape=[
            jax.ShapeDtypeStruct((heads, 3, token_rows, DH), queries.dtype),
            jax.ShapeDtypeStruct((latent.shape[0], span), latent.dtype),
        ],
        scratch_shapes=[pltpu.SemaphoreType.DMA((heads, 3))],
        compiler_params=pltpu.CompilerParams(vmem_limit_bytes=COPY_VMEM),
        name="pack_heads",
    )(*in_hbm(queries, key_tokens, value_tokens, latent))


def in_hbm(*arrays):
    return [pltpu.with_memory_space_constraint(array, pltpu.HBM) for array in arrays]


def gather_rows(array):
    devices = lax.axis_size("seq")
    reach = 1
    parts = [array]
    while reach < devices:
        block = parts[0] if len(parts) == 1 else jnp.concatenate(parts, axis=0)
        parts = [block]
        for step in range(1, min(4, devices // reach)):
            parts.append(lax.ppermute(block, "seq", xor_pairs(step * reach)))
        reach *= 4
    return parts


def xor_pairs(distance):
    return [(i, i ^ distance) for i in range(lax.axis_size("seq"))]


def flat(array):
    return array.reshape(-1, array.shape[-1])


def attend_body(block, own_ref, other_ref, *out_refs):
    members, _, token_rows, _ = own_ref.shape
    chip = lax.axis_index("seq") // 2
    keys = jnp.concatenate([flat(own_ref[:, 1]), flat(other_ref[:, 1])], axis=0)
    values = jnp.concatenate([flat(own_ref[:, 2]), flat(other_ref[:, 2])], axis=0)
    for step in range(0, members, block):
        query = jnp.concatenate([own_ref[chip ^ m, 0] for m in range(step, step + block)], axis=0)
        scores = lax.dot_general(
            query, keys, (((1,), (1,)), ((), ())), preferred_element_type=jnp.float32
        ) * (1.0 / math.sqrt(DH))
        exponents = jnp.exp(scores - jnp.max(scores, axis=1, keepdims=True))
        totals = jnp.sum(exponents, axis=1, keepdims=True)
        mixed = jnp.dot(
            exponents.astype(jnp.bfloat16), values, preferred_element_type=jnp.float32
        )
        mixed = (mixed / totals).astype(jnp.bfloat16)
        for m in range(block):
            out_refs[step + m][...] = mixed[m * token_rows : (m + 1) * token_rows]


def attend(own, other):
    members, _, token_rows, _ = own.shape
    total = members * token_rows
    vmem = pl.BlockSpec(memory_space=pltpu.VMEM)
    return pl.pallas_call(
        functools.partial(attend_body, min(4, members)),
        in_specs=[vmem, vmem],
        out_specs=[vmem] * members,
        out_shape=[jax.ShapeDtypeStruct((token_rows, DH), own.dtype)] * members,
        compiler_params=pltpu.CompilerParams(vmem_limit_bytes=ATTEND_VMEM),
        cost_estimate=pl.CostEstimate(
            flops=8 * total * total * DH,
            bytes_accessed=7 * total * DH * 2,
            transcendentals=2 * total * total,
        ),
        name="attend",
    )(own, other)


def unpack_body(*refs):
    in_refs, out_ref, sems = refs[:-2], refs[-2], refs[-1]
    chip = lax.axis_index("seq") // 2
    copies = []
    for m, ref in enumerate(in_refs):
        columns = pl.ds(pl.multiple_of((chip ^ m) * DH, DH), DH)
        copy = pltpu.make_async_copy(ref, out_ref.at[:, columns], sems.at[m])
        copy.start()
        copies.append(copy)
    for copy in copies:
        copy.wait()


def unpack_heads(pieces):
    heads = len(pieces)
    token_rows = pieces[0].shape[0]
    hbm = pl.BlockSpec(memory_space=pltpu.HBM)
    vmem = pl.BlockSpec(memory_space=pltpu.VMEM)
    return pl.pallas_call(
        unpack_body,
        in_specs=[vmem] * heads,
        out_specs=hbm,
        out_shape=jax.ShapeDtypeStruct((token_rows, heads * DH), pieces[0].dtype),
        scratch_shapes=[pltpu.SemaphoreType.DMA((heads,))],
        compiler_params=pltpu.CompilerParams(vmem_limit_bytes=COPY_VMEM),
        name="unpack_heads",
    )(*pieces)


def decode_body(
    grid_rows,
    width,
    blocks,
    *refs,
):
    latent_refs, refs = refs[:blocks], refs[blocks:]
    (
        tile_ref,
        in_weight_hbm,
        in_bias_hbm,
        gain_hbm,
        mid_weight_ref,
        mid_bias_hbm,
        out_ref,
        mid_weight,
        in_weight_ref,
        in_bias_ref,
        gain_ref,
        mid_bias_ref,
        taps,
        patches,
        active,
        hidden_mid,
        summed,
        weight_sems,
        small_sems,
    ) = refs
    small = [
        pltpu.make_async_copy(source, target, small_sems.at[place])
        for place, (source, target) in enumerate(
            (
                (in_weight_hbm, in_weight_ref),
                (in_bias_hbm, in_bias_ref),
                (gain_hbm, gain_ref),
                (mid_bias_hbm, mid_bias_ref),
            )
        )
    ]
    for copy in small:
        copy.start()
    corners = active.shape[1] // 16
    channels = in_weight_ref.shape[3]
    features = in_weight_ref.shape[4]
    columns = out_ref.shape[2]
    position = lax.axis_index("seq")
    section = lax.axis_index("sect")
    filled = tile_ref[position]
    first_row = lax.fori_loop(0, position, lambda d, total: total + tile_ref[d], jnp.int32(0))

    def load(col_tap):
        return [
            pltpu.make_async_copy(
                mid_weight_ref.at[tap, row_tap, col_tap],
                mid_weight.at[col_tap, pl.ds((slot * 3 + row_tap) * features, features)],
                weight_sems.at[col_tap, row_tap, slot],
            )
            for row_tap in range(3)
            for slot, tap in enumerate(TAPS)
        ]

    for col_tap in range(3):
        for copy in load(col_tap):
            copy.start()

    for copy in small:
        copy.wait()
    nothing = jnp.zeros((channels, features), jnp.bfloat16)
    base = 0
    for tap in TAPS:
        for row_parity in range(2):
            for i, j, p, q in [
                (i, j, p, q) for i in range(2) for j in range(2) for p in range(2) for q in range(2)
            ]:
                for col_parity in range(2):
                    row_tap, col_tap = 2 * i + p - row_parity, 2 * j + q - col_parity
                    inside = 0 <= row_tap < 3 and 0 <= col_tap < 3
                    taps[base : base + channels, col_parity * features : (col_parity + 1) * features] = (
                        in_weight_ref[tap, row_tap, col_tap] if inside else nothing
                    )
                base += channels

    latent = jnp.concatenate([ref[...] for ref in latent_refs], axis=0).astype(jnp.float32)
    held_rows = latent.shape[0]
    share_rows = held_rows // lax.axis_size("seq")
    aside = pltpu.roll(latent, latent.shape[1] - 64, 1).astype(jnp.bfloat16)
    latent = latent.astype(jnp.bfloat16)
    unit = lax.broadcasted_iota(jnp.int32, (UNITS, held_rows), 0)
    held = lax.broadcasted_iota(jnp.int32, (UNITS, held_rows), 1)
    held = ((held // share_rows) ^ position) * share_rows + held % share_rows
    reach = (unit >> 4) + (unit & 7)
    frame = (unit >> 3) & 1
    selectors = []
    for tap in TAPS:
        for row_parity in range(2):
            for i in range(2):
                token_row = first_row + (reach >> 1) - 1 + i
                source = frame + tap - 2
                wanted = (
                    ((reach & 1) == row_parity)
                    & (token_row >= 0)
                    & (token_row < grid_rows)
                    & (source >= 0)
                )
                target = jnp.where(wanted, source * grid_rows + token_row, -1)
                selectors.append(jnp.where(held == target, 1.0, 0.0).astype(jnp.bfloat16))
    selector = jnp.concatenate(selectors, axis=0)
    even = jnp.dot(selector, latent, preferred_element_type=jnp.float32).astype(jnp.bfloat16)
    odd = jnp.dot(
        selector, aside[:, : corners // 2 * 128], preferred_element_type=jnp.float32
    ).astype(jnp.bfloat16)
    for corner in range(corners):
        chunk = slice(corner // 2 * 128, corner // 2 * 128 + 128)
        for group in range(len(selectors)):
            patches[corner * UNITS : (corner + 1) * UNITS, group * 128 : (group + 1) * 128] = (
                odd if corner % 2 else even
            )[group * UNITS : (group + 1) * UNITS, chunk]

    unit_row = lax.broadcasted_iota(jnp.int32, (UNITS, 1), 0)
    pixel_row = 2 * first_row + (unit_row >> 4) + (unit_row & 7) - 1
    row_inside = (pixel_row >= 0) & (pixel_row < 2 * grid_rows)
    step_corners = 3
    in_bias = in_bias_ref[...].reshape(1, features)
    half_gain = gain_ref[...].reshape(1, features) * 0.5

    def first_layer(step, carried):
        start = pl.multiple_of(step * step_corners * UNITS, 16)
        block = jnp.dot(
            patches[pl.ds(start, step_corners * UNITS)],
            taps[...],
            preferred_element_type=jnp.float32,
        )
        hiddens, actives = [carried[0]], [carried[1]]
        for corner in range(step_corners):
            for col_parity in range(2):
                hidden = (
                    block[
                        corner * UNITS : (corner + 1) * UNITS,
                        col_parity * features : (col_parity + 1) * features,
                    ]
                    + in_bias
                )
                hidden = hidden.astype(jnp.bfloat16).astype(jnp.float32)
                scale = lax.rsqrt(jnp.mean(hidden * hidden, axis=1, keepdims=True) + 1e-06)
                pixel = section * columns + 2 * (step * step_corners + corner) + col_parity - 1
                keep = row_inside & (pixel >= 0) & (pixel < width)
                half = hidden * jnp.where(keep, scale, 0.0) * half_gain
                actives.append(half + half * jnp.tanh(half))
                hiddens.append(hidden[16:32])
        for pair in range(step_corners):
            at = pl.ds(pl.multiple_of((step * step_corners + pair) * 16, 16), 16)
            for phase in range(2):
                left, right = actives[2 * pair + 1 - phase], actives[2 * pair + 2 - phase]
                for field in range(LF):
                    for row_tap in range(3):
                        low = row_tap * 16 + field * 8
                        lane = (field * 3 + row_tap) * features
                        joined = jnp.concatenate([left[low : low + 8], right[low : low + 8]], axis=0)
                        active[phase, at, lane : lane + features] = joined.astype(jnp.bfloat16)
            left, right = hiddens[2 * pair], hiddens[2 * pair + 1]
            for field in range(LF):
                low = field * 8
                joined = jnp.concatenate([left[low : low + 8], right[low : low + 8]], axis=0)
                hidden_mid[at, field * features : (field + 1) * features] = joined.astype(jnp.bfloat16)
        return hiddens[-1], actives[-1]

    lax.fori_loop(
        0,
        corners // step_corners,
        first_layer,
        (jnp.zeros((16, features), jnp.float32), jnp.zeros((UNITS, features), jnp.float32)),
    )

    rows = columns * ROWS
    depth = 3 * features
    mid_bias = mid_bias_ref[...].reshape(1, features)
    for col_tap in range(3):
        for copy in load(col_tap):
            copy.wait()
        low = 0 if col_tap == 0 else 16
        window = active[col_tap % 2, low : low + rows]
        early = jnp.dot(
            window[:, :depth], mid_weight[col_tap, depth:], preferred_element_type=jnp.float32
        )
        late = jnp.dot(window, mid_weight[col_tap], preferred_element_type=jnp.float32)
        for field, part in enumerate((early, late)):
            for lane in range(features // 128):
                lanes = slice(lane * 128, (lane + 1) * 128)
                value = part[:, lanes]
                if col_tap:
                    value = value + summed[field, lane]
                if col_tap == 2:
                    from_lane = field * features + lane * 128
                    value = (
                        value
                        + mid_bias[:, lanes]
                        + hidden_mid[16 : 16 + rows, from_lane : from_lane + 128].astype(jnp.float32)
                    )
                summed[field, lane] = value

    for field in range(LF):
        for row in range(ROWS):
            for lane in range(features // 128):
                value = summed[field, lane, pl.ds(row, columns, stride=ROWS), :]
                value = jnp.where(row < 2 * filled, value, 0.0)
                out_ref[field, row, :, lane * 128 : (lane + 1) * 128] = value.astype(jnp.bfloat16)


def decode_tile(
    latents,
    grid_rows,
    tile_rows,
    conv_in_weight,
    conv_in_bias,
    norm_gain,
    conv_mid_weight,
    conv_mid_bias,
):
    sections = lax.axis_size("sect")
    channels, features = conv_in_weight.shape[3:]
    token_width = 4 * channels
    span = latents[0].shape[1] // token_width - 2
    columns = 2 * span
    corners = span + 1
    vmem = pl.BlockSpec(memory_space=pltpu.VMEM)
    hbm = pl.BlockSpec(memory_space=pltpu.HBM)
    slots = len(TAPS)
    depth = slots * 2 * 4 * token_width
    return pl.pallas_call(
        functools.partial(decode_body, grid_rows, columns * sections, len(latents)),
        in_specs=[vmem] * len(latents) + [pl.BlockSpec(memory_space=pltpu.SMEM)] + [hbm] * 5,
        out_specs=vmem,
        out_shape=jax.ShapeDtypeStruct((LF, ROWS, columns, features), jnp.bfloat16),
        scratch_shapes=[
            pltpu.VMEM((3, slots * 3 * features, features), jnp.bfloat16),
            pltpu.VMEM(conv_in_weight.shape, jnp.bfloat16),
            pltpu.VMEM(conv_in_bias.shape, jnp.float32),
            pltpu.VMEM(norm_gain.shape, jnp.float32),
            pltpu.VMEM(conv_mid_bias.shape, jnp.float32),
            pltpu.VMEM((depth, 2 * features), jnp.bfloat16),
            pltpu.VMEM((corners * UNITS, depth), jnp.bfloat16),
            pltpu.VMEM((2, corners * 16, LF * 3 * features), jnp.bfloat16),
            pltpu.VMEM((corners * 16, LF * features), jnp.bfloat16),
            pltpu.VMEM((LF, features // 128, columns * ROWS, 128), jnp.float32),
            pltpu.SemaphoreType.DMA((3, 3, slots)),
            pltpu.SemaphoreType.DMA((4,)),
        ],
        compiler_params=pltpu.CompilerParams(vmem_limit_bytes=DECODE_VMEM),
        cost_estimate=pl.CostEstimate(
            flops=2 * 3 * 9 * columns * ROWS * features * features,
            bytes_accessed=slots * 9 * features * features * 2,
            transcendentals=corners * UNITS * 2 * features,
        ),
        name="decode_tile",
    )(
        *latents,
        *in_hbm(
            tile_rows, conv_in_weight, conv_in_bias, norm_gain, conv_mid_weight, conv_mid_bias
        ),
    )


def on_device(
    queries,
    key_tokens,
    value_tokens,
    latent,
    tile_rows,
    conv_in_weight,
    conv_in_bias,
    norm_gain,
    conv_mid_weight,
    conv_mid_bias,
):
    devices = lax.axis_size("seq")
    groups = parity_groups(devices)
    grid_rows = latent.shape[0] * devices // LF
    packed, share = pack_heads(
        queries, key_tokens, value_tokens, latent, 4 * conv_in_weight.shape[3]
    )
    latents = gather_rows(share)
    own = lax.all_to_all(packed, "seq", 0, 0, axis_index_groups=groups, tiled=True)
    frames = decode_tile(
        latents,
        grid_rows,
        tile_rows,
        conv_in_weight,
        conv_in_bias,
        norm_gain,
        conv_mid_weight,
        conv_mid_bias,
    )
    own, frames = lax.optimization_barrier((own, frames))
    other = lax.ppermute(own, "seq", xor_pairs(1))
    pieces = attend(own, other)
    returned = [pieces[0]] + [
        lax.ppermute(pieces[m], "seq", xor_pairs(2 * m)) for m in range(1, len(pieces))
    ]
    return (unpack_heads(returned), frames)


def solution(mesh):
    in_specs = (
        P("seq", None),
        P("seq", None),
        P("seq", None),
        P("seq", None),
        P(),
        P(),
        P(),
        P(),
        P(),
        P(),
    )
    out_specs = (P("seq", "sect"), P(None, "seq", "sect", None))
    return jax.shard_map(
        on_device, mesh=mesh, in_specs=in_specs, out_specs=out_specs, check_vma=False
    )
```

```python
import functools
import math

import jax
import jax.numpy as jnp
from jax import lax
from jax.experimental import pallas as pl
from jax.experimental.pallas import tpu as pltpu
from jax.sharding import PartitionSpec as P

DH = 128
LF = 2
MAXT = 4
TAPS = (1, 2)
ROWS = 2 * MAXT
REACH = ROWS + 2
UNITS = -(-LF * REACH // 8) * 8
DECODE_VMEM = 32 * 1024 * 1024
ATTEND_VMEM = 32 * 1024 * 1024
COPY_VMEM = 16 * 1024 * 1024


def parity_groups(devices):
    return [list(range(parity, devices, 2)) for parity in range(2)]


def in_hbm(*arrays):
    return [pltpu.with_memory_space_constraint(array, pltpu.HBM) for array in arrays]


def pack_body(query_ref, key_ref, value_ref, latent_ref, packed_ref, spread_ref, held, sems):
    heads = packed_ref.shape[0]
    section = lax.axis_index("sect")
    position = lax.axis_index("seq")
    wide_columns = pl.ds(pl.multiple_of(section * heads * DH, DH), heads * DH)
    copies = [
        pltpu.make_async_copy(ref.at[:, wide_columns], held.at[place], sems.at[place])
        for place, ref in enumerate((query_ref, key_ref, value_ref))
    ]
    for copy in copies:
        copy.start()
    rows, width = latent_ref.shape
    held_rows, span = spread_ref.shape
    rim = (2 * span - width) // 4
    wide = latent_ref[...].astype(jnp.float32)
    rim_zeros = jnp.zeros((rows, rim), jnp.float32)
    lower = jnp.concatenate([rim_zeros, wide[:, : span - rim]], axis=1)
    upper = jnp.concatenate([wide[:, width - span + rim :], rim_zeros], axis=1)
    share = jnp.where(section == 0, lower, upper).astype(jnp.bfloat16)
    place = lax.broadcasted_iota(jnp.int32, (held_rows, rows), 0)
    own = lax.broadcasted_iota(jnp.int32, (held_rows, rows), 1) + position * rows
    selector = jnp.where(place == own, 1.0, 0.0).astype(jnp.bfloat16)
    spread = jnp.dot(selector, share, preferred_element_type=jnp.float32)
    spread_ref[...] = spread.astype(spread_ref.dtype)
    for place, copy in enumerate(copies):
        copy.wait()
        for head in range(heads):
            packed_ref[head, place] = held[place, :, head * DH : (head + 1) * DH]


def pack_heads(queries, key_tokens, value_tokens, latent, token_width):
    token_rows, width = queries.shape
    sections = lax.axis_size("sect")
    heads = width // DH // sections
    span = latent.shape[1] // sections + 2 * token_width
    held_rows = latent.shape[0] * lax.axis_size("seq")
    hbm = pl.BlockSpec(memory_space=pltpu.HBM)
    vmem = pl.BlockSpec(memory_space=pltpu.VMEM)
    return pl.pallas_call(
        pack_body,
        in_specs=[hbm, hbm, hbm, vmem],
        out_specs=[vmem, vmem],
        out_shape=[
            jax.ShapeDtypeStruct((heads, 3, token_rows, DH), queries.dtype),
            jax.ShapeDtypeStruct((held_rows, span), latent.dtype),
        ],
        scratch_shapes=[
            pltpu.VMEM((3, token_rows, heads * DH), queries.dtype),
            pltpu.SemaphoreType.DMA((3,)),
        ],
        compiler_params=pltpu.CompilerParams(vmem_limit_bytes=COPY_VMEM),
        name="pack_heads",
    )(*in_hbm(queries, key_tokens, value_tokens, latent))


def xor_pairs(distance):
    return [(i, i ^ distance) for i in range(lax.axis_size("seq"))]


def flat(array):
    return array.reshape(-1, array.shape[-1])


def attend_body(block, own_ref, other_ref, out_ref):
    members, _, token_rows, _ = own_ref.shape
    keys = jnp.concatenate([flat(own_ref[:, 1]), flat(other_ref[:, 1])], axis=0)
    values = jnp.concatenate([flat(own_ref[:, 2]), flat(other_ref[:, 2])], axis=0)

    def one_block(step):
        at = pl.ds(step * block, block)
        scores = lax.dot_general(
            flat(own_ref[at, 0]),
            keys,
            (((1,), (1,)), ((), ())),
            preferred_element_type=jnp.float32,
        ) * (1.0 / math.sqrt(DH))
        exponents = jnp.exp(scores - jnp.max(scores, axis=1, keepdims=True))
        totals = jnp.sum(exponents, axis=1, keepdims=True)
        mixed = jnp.dot(
            exponents.astype(jnp.bfloat16), values, preferred_element_type=jnp.float32
        )
        out_ref[at] = (mixed / totals).astype(out_ref.dtype).reshape(block, token_rows, DH)

    if members <= 8:
        for step in range(members // block):
            one_block(step)
    else:
        pl.loop(0, members // block)(one_block)


def attend(own, other):
    members, _, token_rows, _ = own.shape
    total = members * token_rows
    vmem = pl.BlockSpec(memory_space=pltpu.VMEM)
    return pl.pallas_call(
        functools.partial(attend_body, min(4, members)),
        in_specs=[vmem, vmem],
        out_specs=vmem,
        out_shape=jax.ShapeDtypeStruct((members, token_rows, DH), own.dtype),
        compiler_params=pltpu.CompilerParams(vmem_limit_bytes=ATTEND_VMEM),
        cost_estimate=pl.CostEstimate(
            flops=8 * total * total * DH,
            bytes_accessed=7 * total * DH * 2,
            transcendentals=2 * total * total,
        ),
        name="attend",
    )(own, other)


def unpack_body(in_ref, out_ref, sems):
    copies = [
        pltpu.make_async_copy(
            in_ref.at[head], out_ref.at[:, pl.ds(head * DH, DH)], sems.at[head]
        )
        for head in range(in_ref.shape[0])
    ]
    for copy in copies:
        copy.start()
    for copy in copies:
        copy.wait()


def unpack_heads(array):
    heads, token_rows, _ = array.shape
    return pl.pallas_call(
        unpack_body,
        in_specs=[pl.BlockSpec(memory_space=pltpu.VMEM)],
        out_specs=pl.BlockSpec(memory_space=pltpu.HBM),
        out_shape=jax.ShapeDtypeStruct((token_rows, heads * DH), array.dtype),
        scratch_shapes=[pltpu.SemaphoreType.DMA((heads,))],
        compiler_params=pltpu.CompilerParams(vmem_limit_bytes=COPY_VMEM),
        name="unpack_heads",
    )(array)


def decode_body(
    grid_rows,
    width,
    latent_ref,
    tile_ref,
    in_weight_hbm,
    in_bias_hbm,
    gain_hbm,
    mid_weight_hbm,
    mid_bias_hbm,
    out_ref,
    mid_weight,
    in_weight_ref,
    in_bias_ref,
    gain_ref,
    mid_bias_ref,
    taps,
    patches,
    raw,
    hidden,
    activated,
    active,
    summed,
    weight_sems,
    small_sems,
):
    pairs = active.shape[1] // 16
    channels, features = in_weight_ref.shape[3:]
    columns = out_ref.shape[2]
    lane_tiles = features // 128
    position = lax.axis_index("seq")
    section = lax.axis_index("sect")
    small = [
        pltpu.make_async_copy(source, target, small_sems.at[place])
        for place, (source, target) in enumerate(
            (
                (in_weight_hbm, in_weight_ref),
                (in_bias_hbm, in_bias_ref),
                (gain_hbm, gain_ref),
                (mid_bias_hbm, mid_bias_ref),
            )
        )
    ]
    for copy in small:
        copy.start()

    def load(col_tap):
        return [
            pltpu.make_async_copy(
                mid_weight_hbm.at[tap, row_tap, col_tap],
                mid_weight.at[
                    col_tap,
                    pl.ds(row_tap * features, features),
                    pl.ds((2 - tap) * features, features),
                ],
                weight_sems.at[col_tap, row_tap, slot],
            )
            for row_tap in range(3)
            for slot, tap in enumerate(TAPS)
        ]

    for col_tap in range(3):
        for copy in load(col_tap):
            copy.start()

    filled = tile_ref[position]
    first_row = lax.fori_loop(0, position, lambda d, total: total + tile_ref[d], jnp.int32(0))

    latent = latent_ref[...].astype(jnp.float32)
    aside = pltpu.roll(latent, latent.shape[1] - 64, 1).astype(jnp.bfloat16)
    latent = latent_ref[...]
    held_rows = latent.shape[0]
    unit = lax.broadcasted_iota(jnp.int32, (UNITS, held_rows), 0)
    held = lax.broadcasted_iota(jnp.int32, (UNITS, held_rows), 1)
    frame = sum((unit >= (k + 1) * REACH).astype(jnp.int32) for k in range(LF))
    reach = unit - frame * REACH
    selectors = []
    for tap in TAPS:
        for row_parity in range(2):
            for i in range(2):
                token_row = first_row + (reach >> 1) - 1 + i
                source = frame + tap - 2
                wanted = (
                    ((reach & 1) == row_parity)
                    & (token_row >= 0)
                    & (token_row < grid_rows)
                    & (source >= 0)
                    & (source < LF)
                )
                target = jnp.where(wanted, source * grid_rows + token_row, -1)
                selectors.append(jnp.where(held == target, 1.0, 0.0).astype(jnp.bfloat16))
    selector = jnp.concatenate(selectors, axis=0)
    even = jnp.dot(selector, latent, preferred_element_type=jnp.float32)
    odd = jnp.dot(selector, aside, preferred_element_type=jnp.float32)
    chunks = latent.shape[1] // 128
    for chunk in range(chunks):
        lanes = slice(chunk * 128, (chunk + 1) * 128)
        for group in range(len(selectors)):
            rows = slice(group * UNITS, (group + 1) * UNITS)
            piece = jnp.concatenate([even[rows, lanes], odd[rows, lanes]], axis=0)
            patches[
                chunk * 2 * UNITS : (chunk + 1) * 2 * UNITS, group * 128 : (group + 1) * 128
            ] = piece.astype(jnp.bfloat16)

    for copy in small:
        copy.wait()
    nothing = jnp.zeros((channels, features), jnp.bfloat16)
    base = 0
    for tap in TAPS:
        for row_parity in range(2):
            for i, j, p, q in [
                (i, j, p, q) for i in range(2) for j in range(2) for p in range(2) for q in range(2)
            ]:
                for col_parity in range(2):
                    row_tap, col_tap = 2 * i + p - row_parity, 2 * j + q - col_parity
                    inside = 0 <= row_tap < 3 and 0 <= col_tap < 3
                    taps[base : base + channels, col_parity * features : (col_parity + 1) * features] = (
                        in_weight_ref[tap, row_tap, col_tap] if inside else nothing
                    )
                base += channels

    raw[...] = jnp.dot(patches[...], taps[...], preferred_element_type=jnp.float32)

    unit_row = lax.broadcasted_iota(jnp.int32, (UNITS, 1), 0)
    row_frame = sum((unit_row >= (k + 1) * REACH).astype(jnp.int32) for k in range(LF))
    pixel_row = 2 * first_row + unit_row - row_frame * REACH - 1
    row_inside = (pixel_row >= 0) & (pixel_row < 2 * grid_rows)
    in_bias = in_bias_ref[...].reshape(1, features)
    half_gain = gain_ref[...].reshape(1, features) * 0.5

    @pl.loop(0, chunks)
    def _(chunk):
        for corner in range(2):
            start = pl.multiple_of((chunk * 2 + corner) * UNITS, 8)
            for col_parity in range(2):
                value = (
                    raw[pl.ds(start, UNITS), col_parity * features : (col_parity + 1) * features]
                    + in_bias
                )
                value = value.astype(jnp.bfloat16).astype(jnp.float32)
                scale = lax.rsqrt(jnp.mean(value * value, axis=1, keepdims=True) + 1e-06)
                column = chunk * 4 + corner * 2 + col_parity
                pixel = section * columns + column - 1
                keep = row_inside & (pixel >= 0) & (pixel < width)
                half = value * jnp.where(keep, scale, 0.0) * half_gain
                result = half + half * jnp.tanh(half)
                at = pl.ds(pl.multiple_of(column * UNITS, 8), UNITS)
                for lane in range(lane_tiles):
                    lanes = slice(lane * 128, (lane + 1) * 128)
                    hidden[lane, at] = value[:, lanes]
                    activated[lane, at] = result[:, lanes]

    @pl.loop(0, pairs)
    def _(pair):
        at = pl.ds(pl.multiple_of(pair * 16, 16), 16)
        for lane in range(lane_tiles):
            for field in range(LF):
                for row_tap in range(3):
                    units = [
                        activated[
                            lane, pl.ds((2 * pair + k) * UNITS + field * REACH + row_tap, ROWS)
                        ]
                        for k in range(3)
                    ]
                    to_lane = (field * 3 + row_tap) * features + lane * 128
                    for phase in range(2):
                        joined = jnp.concatenate(units[phase : phase + 2], axis=0)
                        active[phase, at, to_lane : to_lane + 128] = joined.astype(jnp.bfloat16)

    rows = columns * ROWS
    depth = 3 * features
    for col_tap in range(3):
        for copy in load(col_tap):
            copy.wait()
        low = 16 * (col_tap // 2)
        window = active[col_tap % 2, low : low + rows]
        both = jnp.dot(window[:, :depth], mid_weight[col_tap], preferred_element_type=jnp.float32)
        late = jnp.dot(
            window[:, depth:], mid_weight[col_tap, :, :features], preferred_element_type=jnp.float32
        )
        for lane in range(lane_tiles):
            lanes = slice(lane * 128, (lane + 1) * 128)
            further = slice(features + lane * 128, features + (lane + 1) * 128)
            for field, value in enumerate((both[:, lanes], both[:, further] + late[:, lanes])):
                summed[field, lane] = value + summed[field, lane] if col_tap else value

    mid_bias = mid_bias_ref[...].reshape(1, features)
    for field in range(LF):
        for row in range(ROWS):
            for lane in range(lane_tiles):
                lanes = slice(lane * 128, (lane + 1) * 128)
                skip = hidden[lane, pl.ds(UNITS + field * REACH + 1 + row, columns, stride=UNITS), :]
                value = summed[field, lane, pl.ds(row, columns, stride=ROWS), :]
                value = value + skip + mid_bias[:, lanes]
                value = jnp.where(row < 2 * filled, value, 0.0)
                out_ref[field, row, :, lanes] = value.astype(jnp.bfloat16)


def decode_tile(
    latent,
    grid_rows,
    tile_rows,
    conv_in_weight,
    conv_in_bias,
    norm_gain,
    conv_mid_weight,
    conv_mid_bias,
):
    sections = lax.axis_size("sect")
    channels, features = conv_in_weight.shape[3:]
    token_width = 4 * channels
    span = latent.shape[1] // token_width - 2
    columns = 2 * span
    pairs = span + 1
    chunks = latent.shape[1] // 128
    lane_tiles = features // 128
    vmem = pl.BlockSpec(memory_space=pltpu.VMEM)
    hbm = pl.BlockSpec(memory_space=pltpu.HBM)
    slots = len(TAPS)
    depth = slots * 2 * 4 * token_width
    held = chunks * 4 * UNITS
    return pl.pallas_call(
        functools.partial(decode_body, grid_rows, columns * sections),
        in_specs=[vmem, pl.BlockSpec(memory_space=pltpu.SMEM)] + [hbm] * 5,
        out_specs=vmem,
        out_shape=jax.ShapeDtypeStruct((LF, ROWS, columns, features), jnp.bfloat16),
        scratch_shapes=[
            pltpu.VMEM((3, 3 * features, slots * features), jnp.bfloat16),
            pltpu.VMEM(conv_in_weight.shape, jnp.bfloat16),
            pltpu.VMEM(conv_in_bias.shape, jnp.float32),
            pltpu.VMEM(norm_gain.shape, jnp.float32),
            pltpu.VMEM(conv_mid_bias.shape, jnp.float32),
            pltpu.VMEM((depth, 2 * features), jnp.bfloat16),
            pltpu.VMEM((chunks * 2 * UNITS, depth), jnp.bfloat16),
            pltpu.VMEM((chunks * 2 * UNITS, 2 * features), jnp.float32),
            pltpu.VMEM((lane_tiles, held, 128), jnp.float32),
            pltpu.VMEM((lane_tiles, held, 128), jnp.float32),
            pltpu.VMEM((2, pairs * 16, LF * 3 * features), jnp.bfloat16),
            pltpu.VMEM((LF, lane_tiles, columns * ROWS, 128), jnp.float32),
            pltpu.SemaphoreType.DMA((3, 3, slots)),
            pltpu.SemaphoreType.DMA((4,)),
        ],
        compiler_params=pltpu.CompilerParams(vmem_limit_bytes=DECODE_VMEM),
        cost_estimate=pl.CostEstimate(
            flops=2 * 3 * 9 * columns * ROWS * features * features,
            bytes_accessed=slots * 9 * features * features * 2,
            transcendentals=held * features,
        ),
        name="decode_tile",
    )(
        latent,
        *in_hbm(
            tile_rows, conv_in_weight, conv_in_bias, norm_gain, conv_mid_weight, conv_mid_bias
        ),
    )


def on_device(
    queries,
    key_tokens,
    value_tokens,
    latent,
    tile_rows,
    conv_in_weight,
    conv_in_bias,
    norm_gain,
    conv_mid_weight,
    conv_mid_bias,
):
    devices = lax.axis_size("seq")
    groups = parity_groups(devices)
    grid_rows = latent.shape[0] * devices // LF
    packed, spread = pack_heads(
        queries, key_tokens, value_tokens, latent, 4 * conv_in_weight.shape[3]
    )
    own = lax.all_to_all(packed, "seq", 0, 0, axis_index_groups=groups, tiled=True)
    gathered = lax.psum(spread, "seq")
    other = lax.ppermute(own, "seq", xor_pairs(1))
    mixed = attend(own, other)
    returned = lax.all_to_all(mixed, "seq", 0, 0, axis_index_groups=groups, tiled=True)
    frames = decode_tile(
        gathered,
        grid_rows,
        tile_rows,
        conv_in_weight,
        conv_in_bias,
        norm_gain,
        conv_mid_weight,
        conv_mid_bias,
    )
    return (unpack_heads(returned), frames)


def solution(mesh):
    in_specs = (
        P("seq", None),
        P("seq", None),
        P("seq", None),
        P("seq", None),
        P(),
        P(),
        P(),
        P(),
        P(),
        P(),
    )
    out_specs = (P("seq", "sect"), P(None, "seq", "sect", None))
    return jax.shard_map(
        on_device, mesh=mesh, in_specs=in_specs, out_specs=out_specs, check_vma=False
    )
```

```python
import functools
import math

import jax
import jax.numpy as jnp
from jax import lax
from jax.experimental import pallas as pl
from jax.experimental.pallas import tpu as pltpu
from jax.sharding import PartitionSpec as P

DH = 128
LF = 2
MAXT = 4
RIM = 64
TAPS = (1, 2)
ROWS = 2 * MAXT
REACH = ROWS + 2
UNITS = -(-LF * REACH // 8) * 8
DECODE_VMEM = 32 * 1024 * 1024
ATTEND_VMEM = 32 * 1024 * 1024
COPY_VMEM = 16 * 1024 * 1024


def parity_groups(devices):
    return [list(range(parity, devices, 2)) for parity in range(2)]


def in_hbm(*arrays):
    return [pltpu.with_memory_space_constraint(array, pltpu.HBM) for array in arrays]


def pack_body(query_ref, key_ref, value_ref, latent_ref, packed_ref, held, sems):
    heads = packed_ref.shape[0]
    token_rows = query_ref.shape[0]
    section = lax.axis_index("sect")
    wide_columns = pl.ds(pl.multiple_of(section * heads * DH, DH), heads * DH)
    copies = [
        pltpu.make_async_copy(ref.at[:, wide_columns], held.at[place], sems.at[place])
        for place, ref in enumerate((query_ref, key_ref, value_ref))
    ]
    for copy in copies:
        copy.start()
    rows, width = latent_ref.shape
    half, rim = width // 2, RIM
    wide = latent_ref[...].astype(jnp.float32)
    rim_zeros = jnp.zeros((rows, rim), jnp.float32)
    lower = jnp.concatenate([rim_zeros, wide[:, : half + rim]], axis=1)
    upper = jnp.concatenate([wide[:, half - rim :], rim_zeros], axis=1)
    share = jnp.where(section == 0, lower, upper)
    chunks = share.shape[1] // DH
    lines = [share[:, chunk * DH : (chunk + 1) * DH] for chunk in range(chunks)]
    spare = packed_ref.shape[1] - 3 * token_rows - chunks * rows
    lines.append(jnp.zeros((spare, DH), jnp.float32))
    share = jnp.concatenate(lines, axis=0).astype(packed_ref.dtype)
    for head in range(heads):
        packed_ref[head, 3 * token_rows :] = share
    for place, copy in enumerate(copies):
        copy.wait()
        for head in range(heads):
            packed_ref[head, place * token_rows : (place + 1) * token_rows] = held[
                place, :, head * DH : (head + 1) * DH
            ]


def pack_heads(queries, key_tokens, value_tokens, latent, token_width):
    token_rows, width = queries.shape
    sections = lax.axis_size("sect")
    heads = width // DH // sections
    span = latent.shape[1] // sections + 2 * token_width
    extra = -(-latent.shape[0] * (span // DH) // 16) * 16
    hbm = pl.BlockSpec(memory_space=pltpu.HBM)
    vmem = pl.BlockSpec(memory_space=pltpu.VMEM)
    return pl.pallas_call(
        pack_body,
        in_specs=[hbm, hbm, hbm, vmem],
        out_specs=vmem,
        out_shape=jax.ShapeDtypeStruct((heads, 3 * token_rows + extra, DH), queries.dtype),
        scratch_shapes=[
            pltpu.VMEM((3, token_rows, heads * DH), queries.dtype),
            pltpu.SemaphoreType.DMA((3,)),
        ],
        compiler_params=pltpu.CompilerParams(vmem_limit_bytes=COPY_VMEM),
        name="pack_heads",
    )(*in_hbm(queries, key_tokens, value_tokens, latent))


def xor_pairs(distance):
    return [(i, i ^ distance) for i in range(lax.axis_size("seq"))]


def flat(array):
    return array.reshape(-1, array.shape[-1])


def attend_body(block, own_ref, other_ref, out_ref):
    members, token_rows, _ = out_ref.shape
    at_keys = slice(token_rows, 2 * token_rows)
    at_values = slice(2 * token_rows, 3 * token_rows)
    keys = jnp.concatenate([flat(own_ref[:, at_keys]), flat(other_ref[:, at_keys])], axis=0)
    values = jnp.concatenate([flat(own_ref[:, at_values]), flat(other_ref[:, at_values])], axis=0)

    def one_block(step):
        at = pl.ds(step * block, block)
        scores = lax.dot_general(
            flat(own_ref[at, :token_rows]),
            keys,
            (((1,), (1,)), ((), ())),
            preferred_element_type=jnp.float32,
        ) * (1.0 / math.sqrt(DH))
        exponents = jnp.exp(scores - jnp.max(scores, axis=1, keepdims=True))
        totals = jnp.sum(exponents, axis=1, keepdims=True)
        mixed = jnp.dot(
            exponents.astype(jnp.bfloat16), values, preferred_element_type=jnp.float32
        )
        out_ref[at] = (mixed / totals).astype(out_ref.dtype).reshape(block, token_rows, DH)

    if members <= 8:
        for step in range(members // block):
            one_block(step)
    else:
        pl.loop(0, members // block)(one_block)


def attend(own, other, token_rows):
    members = own.shape[0]
    total = members * token_rows
    vmem = pl.BlockSpec(memory_space=pltpu.VMEM)
    return pl.pallas_call(
        functools.partial(attend_body, min(4, members)),
        in_specs=[vmem, vmem],
        out_specs=vmem,
        out_shape=jax.ShapeDtypeStruct((members, token_rows, DH), own.dtype),
        compiler_params=pltpu.CompilerParams(vmem_limit_bytes=ATTEND_VMEM),
        cost_estimate=pl.CostEstimate(
            flops=8 * total * total * DH,
            bytes_accessed=7 * total * DH * 2,
            transcendentals=2 * total * total,
        ),
        name="attend",
    )(own, other)


def unpack_body(in_ref, out_ref, sems):
    copies = [
        pltpu.make_async_copy(
            in_ref.at[head], out_ref.at[:, pl.ds(head * DH, DH)], sems.at[head]
        )
        for head in range(in_ref.shape[0])
    ]
    for copy in copies:
        copy.start()
    for copy in copies:
        copy.wait()


def unpack_heads(array):
    heads, token_rows, _ = array.shape
    return pl.pallas_call(
        unpack_body,
        in_specs=[pl.BlockSpec(memory_space=pltpu.VMEM)],
        out_specs=pl.BlockSpec(memory_space=pltpu.HBM),
        out_shape=jax.ShapeDtypeStruct((token_rows, heads * DH), array.dtype),
        scratch_shapes=[pltpu.SemaphoreType.DMA((heads,))],
        compiler_params=pltpu.CompilerParams(vmem_limit_bytes=COPY_VMEM),
        name="unpack_heads",
    )(array)


def decode_body(
    grid_rows,
    width,
    share_rows,
    own_ref,
    other_ref,
    tile_ref,
    in_weight_hbm,
    in_bias_hbm,
    gain_hbm,
    mid_weight_hbm,
    mid_bias_hbm,
    out_ref,
    mid_weight,
    in_weight_ref,
    in_bias_ref,
    gain_ref,
    mid_bias_ref,
    taps,
    rows_held,
    patches,
    raw,
    hidden,
    activated,
    active,
    summed,
    weight_sems,
    small_sems,
):
    pairs = active.shape[1] // 16
    channels, features = in_weight_ref.shape[3:]
    columns = out_ref.shape[2]
    lane_tiles = features // 128
    position = lax.axis_index("seq")
    section = lax.axis_index("sect")
    small = [
        pltpu.make_async_copy(source, target, small_sems.at[place])
        for place, (source, target) in enumerate(
            (
                (in_weight_hbm, in_weight_ref),
                (in_bias_hbm, in_bias_ref),
                (gain_hbm, gain_ref),
                (mid_bias_hbm, mid_bias_ref),
            )
        )
    ]
    for copy in small:
        copy.start()

    def load(col_tap):
        return [
            pltpu.make_async_copy(
                mid_weight_hbm.at[tap, row_tap, col_tap],
                mid_weight.at[
                    col_tap,
                    pl.ds(row_tap * features, features),
                    pl.ds((2 - tap) * features, features),
                ],
                weight_sems.at[col_tap, row_tap, slot],
            )
            for row_tap in range(3)
            for slot, tap in enumerate(TAPS)
        ]

    for col_tap in range(3):
        for copy in load(col_tap):
            copy.start()

    filled = tile_ref[position]
    first_row = lax.fori_loop(0, position, lambda d, total: total + tile_ref[d], jnp.int32(0))

    members, message, _ = own_ref.shape
    chunks = rows_held.shape[1] // 128
    extra = -(-share_rows * chunks // 16) * 16
    for side, ref in enumerate((own_ref, other_ref)):
        for member in range(members):
            lines = ref[member, message - extra :].astype(jnp.float32)
            low = (side * members + member) * share_rows
            for chunk in range(chunks):
                rows_held[low : low + share_rows, chunk * 128 : (chunk + 1) * 128] = lines[
                    chunk * share_rows : (chunk + 1) * share_rows
                ]
    latent = rows_held[...]
    aside = pltpu.roll(latent, latent.shape[1] - RIM, 1).astype(jnp.bfloat16)
    latent = latent.astype(jnp.bfloat16)
    held_rows = latent.shape[0]
    unit = lax.broadcasted_iota(jnp.int32, (UNITS, held_rows), 0)
    held = lax.broadcasted_iota(jnp.int32, (UNITS, held_rows), 1)
    side = (held >= members * share_rows).astype(jnp.int32)
    member = held // share_rows - side * members
    held = (2 * member + ((position & 1) ^ side)) * share_rows + held % share_rows
    frame = sum((unit >= (k + 1) * REACH).astype(jnp.int32) for k in range(LF))
    reach = unit - frame * REACH
    selectors = []
    for tap in TAPS:
        for row_parity in range(2):
            for i in range(2):
                token_row = first_row + (reach >> 1) - 1 + i
                source = frame + tap - 2
                wanted = (
                    ((reach & 1) == row_parity)
                    & (token_row >= 0)
                    & (token_row < grid_rows)
                    & (source >= 0)
                    & (source < LF)
                )
                target = jnp.where(wanted, source * grid_rows + token_row, -1)
                selectors.append(jnp.where(held == target, 1.0, 0.0).astype(jnp.bfloat16))
    selector = jnp.concatenate(selectors, axis=0)
    even = jnp.dot(selector, latent, preferred_element_type=jnp.float32)
    odd = jnp.dot(selector, aside, preferred_element_type=jnp.float32)
    for chunk in range(chunks):
        lanes = slice(chunk * 128, (chunk + 1) * 128)
        for group in range(len(selectors)):
            rows = slice(group * UNITS, (group + 1) * UNITS)
            piece = jnp.concatenate([even[rows, lanes], odd[rows, lanes]], axis=0)
            patches[
                chunk * 2 * UNITS : (chunk + 1) * 2 * UNITS, group * 128 : (group + 1) * 128
            ] = piece.astype(jnp.bfloat16)

    for copy in small:
        copy.wait()
    nothing = jnp.zeros((channels, features), jnp.bfloat16)
    base = 0
    for tap in TAPS:
        for row_parity in range(2):
            for i, j, p, q in [
                (i, j, p, q) for i in range(2) for j in range(2) for p in range(2) for q in range(2)
            ]:
                for col_parity in range(2):
                    row_tap, col_tap = 2 * i + p - row_parity, 2 * j + q - col_parity
                    inside = 0 <= row_tap < 3 and 0 <= col_tap < 3
                    taps[base : base + channels, col_parity * features : (col_parity + 1) * features] = (
                        in_weight_ref[tap, row_tap, col_tap] if inside else nothing
                    )
                base += channels

    raw[...] = jnp.dot(patches[...], taps[...], preferred_element_type=jnp.float32)

    unit_row = lax.broadcasted_iota(jnp.int32, (UNITS, 1), 0)
    row_frame = sum((unit_row >= (k + 1) * REACH).astype(jnp.int32) for k in range(LF))
    pixel_row = 2 * first_row + unit_row - row_frame * REACH - 1
    row_inside = (pixel_row >= 0) & (pixel_row < 2 * grid_rows)
    in_bias = in_bias_ref[...].reshape(1, features)
    half_gain = gain_ref[...].reshape(1, features) * 0.5

    for chunk in range(chunks):
        for corner in range(2):
            start = (chunk * 2 + corner) * UNITS
            for col_parity in range(2):
                value = (
                    raw[pl.ds(start, UNITS), col_parity * features : (col_parity + 1) * features]
                    + in_bias
                )
                value = value.astype(jnp.bfloat16).astype(jnp.float32)
                scale = lax.rsqrt(jnp.mean(value * value, axis=1, keepdims=True) + 1e-06)
                column = chunk * 4 + corner * 2 + col_parity
                pixel = section * columns + column - 1
                keep = row_inside & (pixel >= 0) & (pixel < width)
                half = value * jnp.where(keep, scale, 0.0) * half_gain
                result = half + half * jnp.tanh(half)
                at = pl.ds(column * UNITS, UNITS)
                for lane in range(lane_tiles):
                    lanes = slice(lane * 128, (lane + 1) * 128)
                    hidden[lane, at] = value[:, lanes]
                    activated[lane, at] = result[:, lanes]

    def pair_up(phase, pair):
        at = slice(pair * 16, pair * 16 + 16)
        for lane in range(lane_tiles):
            for field in range(LF):
                for row_tap in range(3):
                    start = (2 * pair + phase) * UNITS + field * REACH + row_tap
                    joined = jnp.concatenate(
                        [activated[lane, pl.ds(start + k * UNITS, ROWS)] for k in range(2)], axis=0
                    )
                    to_lane = (field * 3 + row_tap) * features + lane * 128
                    active[phase, at, to_lane : to_lane + 128] = joined.astype(jnp.bfloat16)

    for phase in range(2):
        for pair in range(pairs - phase):
            pair_up(phase, pair)

    rows = columns * ROWS
    depth = 3 * features
    windows = [active[col_tap % 2, 16 * (col_tap // 2) : 16 * (col_tap // 2) + rows] for col_tap in range(3)]
    for col_tap in range(3):
        for copy in load(col_tap):
            copy.wait()
    early = jnp.concatenate([window[:, :depth] for window in windows], axis=1)
    both = jnp.dot(early, flat(mid_weight[...]), preferred_element_type=jnp.float32)
    late = jnp.concatenate([window[:, depth:] for window in windows], axis=1)
    late = jnp.dot(late, flat(mid_weight[:, :, :features]), preferred_element_type=jnp.float32)
    for lane in range(lane_tiles):
        lanes = slice(lane * 128, (lane + 1) * 128)
        further = slice(features + lane * 128, features + (lane + 1) * 128)
        summed[0, lane] = both[:, lanes]
        summed[1, lane] = both[:, further] + late[:, lanes]

    mid_bias = mid_bias_ref[...].reshape(1, features)
    for field in range(LF):
        for row in range(ROWS):
            for lane in range(lane_tiles):
                lanes = slice(lane * 128, (lane + 1) * 128)
                skip = hidden[lane, pl.ds(UNITS + field * REACH + 1 + row, columns, stride=UNITS), :]
                value = summed[field, lane, pl.ds(row, columns, stride=ROWS), :]
                value = value + skip + mid_bias[:, lanes]
                value = jnp.where(row < 2 * filled, value, 0.0)
                out_ref[field, row, :, lanes] = value.astype(jnp.bfloat16)


def decode_tile(
    own,
    other,
    share_rows,
    grid_rows,
    width,
    tile_rows,
    conv_in_weight,
    conv_in_bias,
    norm_gain,
    conv_mid_weight,
    conv_mid_bias,
):
    sections = lax.axis_size("sect")
    channels, features = conv_in_weight.shape[3:]
    token_width = 4 * channels
    columns = width // sections
    span = columns // 2
    pairs = span + 1
    chunks = (span + 2) * token_width // 128
    lane_tiles = features // 128
    vmem = pl.BlockSpec(memory_space=pltpu.VMEM)
    hbm = pl.BlockSpec(memory_space=pltpu.HBM)
    slots = len(TAPS)
    depth = slots * 2 * 4 * token_width
    held = chunks * 4 * UNITS
    return pl.pallas_call(
        functools.partial(decode_body, grid_rows, width, share_rows),
        in_specs=[vmem, vmem, pl.BlockSpec(memory_space=pltpu.SMEM)] + [hbm] * 5,
        out_specs=vmem,
        out_shape=jax.ShapeDtypeStruct((LF, ROWS, columns, features), jnp.bfloat16),
        scratch_shapes=[
            pltpu.VMEM((3, 3 * features, slots * features), jnp.bfloat16),
            pltpu.VMEM(conv_in_weight.shape, jnp.bfloat16),
            pltpu.VMEM(conv_in_bias.shape, jnp.float32),
            pltpu.VMEM(norm_gain.shape, jnp.float32),
            pltpu.VMEM(conv_mid_bias.shape, jnp.float32),
            pltpu.VMEM((depth, 2 * features), jnp.bfloat16),
            pltpu.VMEM((2 * own.shape[0] * share_rows, chunks * 128), jnp.float32),
            pltpu.VMEM((chunks * 2 * UNITS, depth), jnp.bfloat16),
            pltpu.VMEM((chunks * 2 * UNITS, 2 * features), jnp.float32),
            pltpu.VMEM((lane_tiles, held, 128), jnp.float32),
            pltpu.VMEM((lane_tiles, held, 128), jnp.float32),
            pltpu.VMEM((2, pairs * 16, LF * 3 * features), jnp.bfloat16),
            pltpu.VMEM((LF, lane_tiles, columns * ROWS, 128), jnp.float32),
            pltpu.SemaphoreType.DMA((3, 3, slots)),
            pltpu.SemaphoreType.DMA((4,)),
        ],
        compiler_params=pltpu.CompilerParams(vmem_limit_bytes=DECODE_VMEM),
        cost_estimate=pl.CostEstimate(
            flops=2 * 3 * 9 * columns * ROWS * features * features,
            bytes_accessed=slots * 9 * features * features * 2,
            transcendentals=held * features,
        ),
        name="decode_tile",
    )(
        own,
        other,
        *in_hbm(
            tile_rows, conv_in_weight, conv_in_bias, norm_gain, conv_mid_weight, conv_mid_bias
        ),
    )


def on_device(
    queries,
    key_tokens,
    value_tokens,
    latent,
    tile_rows,
    conv_in_weight,
    conv_in_bias,
    norm_gain,
    conv_mid_weight,
    conv_mid_bias,
):
    devices = lax.axis_size("seq")
    groups = parity_groups(devices)
    grid_rows = latent.shape[0] * devices // LF
    token_width = 4 * conv_in_weight.shape[3]
    packed = pack_heads(queries, key_tokens, value_tokens, latent, token_width)
    own = lax.all_to_all(packed, "seq", 0, 0, axis_index_groups=groups, tiled=True)
    other = lax.ppermute(own, "seq", xor_pairs(1))
    mixed = attend(own, other, queries.shape[0])
    returned = lax.all_to_all(mixed, "seq", 0, 0, axis_index_groups=groups, tiled=True)
    frames = decode_tile(
        own,
        other,
        latent.shape[0],
        grid_rows,
        2 * latent.shape[1] // token_width,
        tile_rows,
        conv_in_weight,
        conv_in_bias,
        norm_gain,
        conv_mid_weight,
        conv_mid_bias,
    )
    return (unpack_heads(returned), frames)


def solution(mesh):
    in_specs = (
        P("seq", None),
        P("seq", None),
        P("seq", None),
        P("seq", None),
        P(),
        P(),
        P(),
        P(),
        P(),
        P(),
    )
    out_specs = (P("seq", "sect"), P(None, "seq", "sect", None))
    return jax.shard_map(
        on_device, mesh=mesh, in_specs=in_specs, out_specs=out_specs, check_vma=False
    )
```

```python
import functools
import math

import jax
import jax.numpy as jnp
from jax import lax
from jax.experimental import pallas as pl
from jax.experimental.pallas import tpu as pltpu
from jax.sharding import PartitionSpec as P

DH = 128
LF = 2
MAXT = 4
RIM = 64
TAPS = (1, 2)
ROWS = 2 * MAXT
REACH = ROWS + 2
UNITS = -(-LF * REACH // 8) * 8
DECODE_VMEM = 32 * 1024 * 1024
ATTEND_VMEM = 32 * 1024 * 1024
COPY_VMEM = 16 * 1024 * 1024


def parity_groups(devices):
    return [list(range(parity, devices, 2)) for parity in range(2)]


def in_hbm(*arrays):
    return [pltpu.with_memory_space_constraint(array, pltpu.HBM) for array in arrays]


def pack_body(query_ref, key_ref, value_ref, latent_ref, packed_ref, held, sems):
    heads = packed_ref.shape[0]
    token_rows = query_ref.shape[0]
    section = lax.axis_index("sect")
    wide_columns = pl.ds(pl.multiple_of(section * heads * DH, DH), heads * DH)
    copies = [
        pltpu.make_async_copy(ref.at[:, wide_columns], held.at[place], sems.at[place])
        for place, ref in enumerate((query_ref, key_ref, value_ref))
    ]
    for copy in copies:
        copy.start()
    rows, width = latent_ref.shape
    half, rim = width // 2, RIM
    wide = latent_ref[...].astype(jnp.float32)
    rim_zeros = jnp.zeros((rows, rim), jnp.float32)
    lower = jnp.concatenate([rim_zeros, wide[:, : half + rim]], axis=1)
    upper = jnp.concatenate([wide[:, half - rim :], rim_zeros], axis=1)
    share = jnp.where(section == 0, lower, upper)
    chunks = share.shape[1] // DH
    lines = [share[:, chunk * DH : (chunk + 1) * DH] for chunk in range(chunks)]
    spare = packed_ref.shape[1] - 3 * token_rows - chunks * rows
    lines.append(jnp.zeros((spare, DH), jnp.float32))
    share = jnp.concatenate(lines, axis=0).astype(packed_ref.dtype)
    for head in range(heads):
        packed_ref[head, 3 * token_rows :] = share
    for place, copy in enumerate(copies):
        copy.wait()
        for head in range(heads):
            packed_ref[head, place * token_rows : (place + 1) * token_rows] = held[
                place, :, head * DH : (head + 1) * DH
            ]


def pack_heads(queries, key_tokens, value_tokens, latent, token_width):
    token_rows, width = queries.shape
    sections = lax.axis_size("sect")
    heads = width // DH // sections
    span = latent.shape[1] // sections + 2 * token_width
    extra = -(-latent.shape[0] * (span // DH) // 16) * 16
    hbm = pl.BlockSpec(memory_space=pltpu.HBM)
    vmem = pl.BlockSpec(memory_space=pltpu.VMEM)
    return pl.pallas_call(
        pack_body,
        in_specs=[hbm, hbm, hbm, vmem],
        out_specs=vmem,
        out_shape=jax.ShapeDtypeStruct((heads, 3 * token_rows + extra, DH), queries.dtype),
        scratch_shapes=[
            pltpu.VMEM((3, token_rows, heads * DH), queries.dtype),
            pltpu.SemaphoreType.DMA((3,)),
        ],
        compiler_params=pltpu.CompilerParams(vmem_limit_bytes=COPY_VMEM),
        name="pack_heads",
    )(*in_hbm(queries, key_tokens, value_tokens, latent))


def xor_pairs(distance):
    return [(i, i ^ distance) for i in range(lax.axis_size("seq"))]


def flat(array):
    return array.reshape(-1, array.shape[-1])


def attend_body(block, own_ref, other_ref, out_ref):
    members, token_rows, _ = out_ref.shape
    at_keys = slice(token_rows, 2 * token_rows)
    at_values = slice(2 * token_rows, 3 * token_rows)
    keys = jnp.concatenate([flat(own_ref[:, at_keys]), flat(other_ref[:, at_keys])], axis=0)
    values = jnp.concatenate([flat(own_ref[:, at_values]), flat(other_ref[:, at_values])], axis=0)

    def one_block(step):
        at = pl.ds(step * block, block)
        scores = lax.dot_general(
            flat(own_ref[at, :token_rows]),
            keys,
            (((1,), (1,)), ((), ())),
            preferred_element_type=jnp.float32,
        ) * (1.0 / math.sqrt(DH))
        exponents = jnp.exp(scores - jnp.max(scores, axis=1, keepdims=True))
        totals = jnp.sum(exponents, axis=1, keepdims=True)
        mixed = jnp.dot(
            exponents.astype(jnp.bfloat16), values, preferred_element_type=jnp.float32
        )
        out_ref[at] = (mixed / totals).astype(out_ref.dtype).reshape(block, token_rows, DH)

    if members <= 8:
        for step in range(members // block):
            one_block(step)
    else:
        pl.loop(0, members // block)(one_block)


def attend(own, other, token_rows):
    members = own.shape[0]
    total = members * token_rows
    vmem = pl.BlockSpec(memory_space=pltpu.VMEM)
    return pl.pallas_call(
        functools.partial(attend_body, min(4, members)),
        in_specs=[vmem, vmem],
        out_specs=vmem,
        out_shape=jax.ShapeDtypeStruct((members, token_rows, DH), own.dtype),
        compiler_params=pltpu.CompilerParams(vmem_limit_bytes=ATTEND_VMEM),
        cost_estimate=pl.CostEstimate(
            flops=8 * total * total * DH,
            bytes_accessed=7 * total * DH * 2,
            transcendentals=2 * total * total,
        ),
        name="attend",
    )(own, other)


def unpack_body(in_ref, out_ref, sems):
    copies = [
        pltpu.make_async_copy(
            in_ref.at[head], out_ref.at[:, pl.ds(head * DH, DH)], sems.at[head]
        )
        for head in range(in_ref.shape[0])
    ]
    for copy in copies:
        copy.start()
    for copy in copies:
        copy.wait()


def unpack_heads(array):
    heads, token_rows, _ = array.shape
    return pl.pallas_call(
        unpack_body,
        in_specs=[pl.BlockSpec(memory_space=pltpu.VMEM)],
        out_specs=pl.BlockSpec(memory_space=pltpu.HBM),
        out_shape=jax.ShapeDtypeStruct((token_rows, heads * DH), array.dtype),
        scratch_shapes=[pltpu.SemaphoreType.DMA((heads,))],
        compiler_params=pltpu.CompilerParams(vmem_limit_bytes=COPY_VMEM),
        name="unpack_heads",
    )(array)


def decode_body(
    grid_rows,
    width,
    share_rows,
    own_ref,
    other_ref,
    tile_ref,
    in_weight_hbm,
    in_bias_hbm,
    gain_hbm,
    mid_weight_hbm,
    mid_bias_hbm,
    out_ref,
    mid_weight,
    in_weight_ref,
    in_bias_ref,
    gain_ref,
    mid_bias_ref,
    taps,
    rows_held,
    patches,
    raw,
    hidden,
    activated,
    active,
    summed,
    weight_sems,
    small_sems,
):
    pairs = active.shape[1] // 16
    channels, features = in_weight_ref.shape[3:]
    columns = out_ref.shape[2]
    lane_tiles = features // 128
    position = lax.axis_index("seq")
    section = lax.axis_index("sect")
    small = [
        pltpu.make_async_copy(source, target, small_sems.at[place])
        for place, (source, target) in enumerate(
            (
                (in_weight_hbm, in_weight_ref),
                (in_bias_hbm, in_bias_ref),
                (gain_hbm, gain_ref),
                (mid_bias_hbm, mid_bias_ref),
            )
        )
    ]
    for copy in small:
        copy.start()

    def load(col_tap):
        return [
            pltpu.make_async_copy(
                mid_weight_hbm.at[tap, row_tap, col_tap],
                mid_weight.at[
                    col_tap,
                    pl.ds(row_tap * features, features),
                    pl.ds((2 - tap) * features, features),
                ],
                weight_sems.at[col_tap, row_tap, slot],
            )
            for row_tap in range(3)
            for slot, tap in enumerate(TAPS)
        ]

    for col_tap in range(3):
        for copy in load(col_tap):
            copy.start()

    filled = tile_ref[position]
    first_row = lax.fori_loop(0, position, lambda d, total: total + tile_ref[d], jnp.int32(0))

    members, message, _ = own_ref.shape
    chunks = rows_held.shape[1] // 128
    extra = -(-share_rows * chunks // 16) * 16
    for side, ref in enumerate((own_ref, other_ref)):
        for member in range(members):
            lines = ref[member, message - extra :].astype(jnp.float32)
            low = (side * members + member) * share_rows
            for chunk in range(chunks):
                rows_held[low : low + share_rows, chunk * 128 : (chunk + 1) * 128] = lines[
                    chunk * share_rows : (chunk + 1) * share_rows
                ]
    latent = rows_held[...]
    aside = pltpu.roll(latent, latent.shape[1] - RIM, 1).astype(jnp.bfloat16)
    latent = latent.astype(jnp.bfloat16)
    held_rows = latent.shape[0]
    unit = lax.broadcasted_iota(jnp.int32, (UNITS, held_rows), 0)
    held = lax.broadcasted_iota(jnp.int32, (UNITS, held_rows), 1)
    side = (held >= members * share_rows).astype(jnp.int32)
    member = held // share_rows - side * members
    held = (2 * member + ((position & 1) ^ side)) * share_rows + held % share_rows
    frame = sum((unit >= (k + 1) * REACH).astype(jnp.int32) for k in range(LF))
    reach = unit - frame * REACH
    selectors = []
    for tap in TAPS:
        for row_parity in range(2):
            for i in range(2):
                token_row = first_row + (reach >> 1) - 1 + i
                source = frame + tap - 2
                wanted = (
                    ((reach & 1) == row_parity)
                    & (token_row >= 0)
                    & (token_row < grid_rows)
                    & (source >= 0)
                    & (source < LF)
                )
                target = jnp.where(wanted, source * grid_rows + token_row, -1)
                selectors.append(jnp.where(held == target, 1.0, 0.0).astype(jnp.bfloat16))
    selector = jnp.concatenate(selectors, axis=0)
    even = jnp.dot(selector, latent, preferred_element_type=jnp.float32)
    odd = jnp.dot(selector, aside, preferred_element_type=jnp.float32)
    for chunk in range(chunks):
        lanes = slice(chunk * 128, (chunk + 1) * 128)
        for group in range(len(selectors)):
            rows = slice(group * UNITS, (group + 1) * UNITS)
            piece = jnp.concatenate([even[rows, lanes], odd[rows, lanes]], axis=0)
            patches[
                chunk * 2 * UNITS : (chunk + 1) * 2 * UNITS, group * 128 : (group + 1) * 128
            ] = piece.astype(jnp.bfloat16)

    for copy in small:
        copy.wait()
    nothing = jnp.zeros((channels, features), jnp.bfloat16)
    base = 0
    for tap in TAPS:
        for row_parity in range(2):
            for i, j, p, q in [
                (i, j, p, q) for i in range(2) for j in range(2) for p in range(2) for q in range(2)
            ]:
                for col_parity in range(2):
                    row_tap, col_tap = 2 * i + p - row_parity, 2 * j + q - col_parity
                    inside = 0 <= row_tap < 3 and 0 <= col_tap < 3
                    taps[base : base + channels, col_parity * features : (col_parity + 1) * features] = (
                        in_weight_ref[tap, row_tap, col_tap] if inside else nothing
                    )
                base += channels

    unit_row = lax.broadcasted_iota(jnp.int32, (UNITS, 1), 0)
    row_frame = sum((unit_row >= (k + 1) * REACH).astype(jnp.int32) for k in range(LF))
    pixel_row = 2 * first_row + unit_row - row_frame * REACH - 1
    row_inside = (pixel_row >= 0) & (pixel_row < 2 * grid_rows)
    in_bias = in_bias_ref[...].reshape(1, features)
    half_gain = gain_ref[...].reshape(1, features) * 0.5

    def first_layer(chunk):
        for corner in range(2):
            start = (chunk * 2 + corner) * UNITS
            for col_parity in range(2):
                value = (
                    raw[pl.ds(start, UNITS), col_parity * features : (col_parity + 1) * features]
                    + in_bias
                )
                value = value.astype(jnp.bfloat16).astype(jnp.float32)
                scale = lax.rsqrt(jnp.mean(value * value, axis=1, keepdims=True) + 1e-06)
                column = chunk * 4 + corner * 2 + col_parity
                pixel = section * columns + column - 1
                keep = row_inside & (pixel >= 0) & (pixel < width)
                half = value * jnp.where(keep, scale, 0.0) * half_gain
                result = half + half * jnp.tanh(half)
                at = pl.ds(column * UNITS, UNITS)
                for lane in range(lane_tiles):
                    lanes = slice(lane * 128, (lane + 1) * 128)
                    hidden[lane, at] = value[:, lanes]
                    activated[lane, at] = result[:, lanes]

    middle = (chunks + 1) // 2
    groups = ((0, middle), (middle, chunks))
    for low, high in groups:
        rows = slice(low * 2 * UNITS, high * 2 * UNITS)
        raw[rows] = jnp.dot(patches[rows], taps[...], preferred_element_type=jnp.float32)
    for low, high in groups:
        for chunk in range(low, high):
            first_layer(chunk)

    def pair_up(phase, pair):
        at = slice(pair * 16, pair * 16 + 16)
        for lane in range(lane_tiles):
            for field in range(LF):
                for row_tap in range(3):
                    start = (2 * pair + phase) * UNITS + field * REACH + row_tap
                    joined = jnp.concatenate(
                        [activated[lane, pl.ds(start + k * UNITS, ROWS)] for k in range(2)], axis=0
                    )
                    to_lane = (field * 3 + row_tap) * features + lane * 128
                    active[phase, at, to_lane : to_lane + 128] = joined.astype(jnp.bfloat16)

    rows = columns * ROWS
    depth = 3 * features

    def second_layer(col_taps):
        windows = []
        for col_tap in col_taps:
            for copy in load(col_tap):
                copy.wait()
            low = 16 * (col_tap // 2)
            windows.append(active[col_tap % 2, low : low + rows])
        weights = jnp.concatenate([mid_weight[col_tap] for col_tap in col_taps], axis=0)
        early = jnp.concatenate([window[:, :depth] for window in windows], axis=1)
        late = jnp.concatenate([window[:, depth:] for window in windows], axis=1)
        return (
            jnp.dot(early, weights, preferred_element_type=jnp.float32),
            jnp.dot(late, weights[:, :features], preferred_element_type=jnp.float32),
        )

    mid_bias = mid_bias_ref[...].reshape(1, features)

    def finish(field):
        for row in range(ROWS):
            for lane in range(lane_tiles):
                lanes = slice(lane * 128, (lane + 1) * 128)
                skip = hidden[lane, pl.ds(UNITS + field * REACH + 1 + row, columns, stride=UNITS), :]
                value = summed[field, lane, pl.ds(row, columns, stride=ROWS), :]
                value = value + skip + mid_bias[:, lanes]
                value = jnp.where(row < 2 * filled, value, 0.0)
                out_ref[field, row, :, lanes] = value.astype(jnp.bfloat16)

    for pair in range(pairs):
        pair_up(0, pair)
    both, late = second_layer((0, 2))
    for lane in range(lane_tiles):
        lanes = slice(lane * 128, (lane + 1) * 128)
        further = slice(features + lane * 128, features + (lane + 1) * 128)
        summed[0, lane] = both[:, lanes]
        summed[1, lane] = both[:, further] + late[:, lanes]
    for pair in range(pairs - 1):
        pair_up(1, pair)
    both, late = second_layer((1,))
    for lane in range(lane_tiles):
        lanes = slice(lane * 128, (lane + 1) * 128)
        further = slice(features + lane * 128, features + (lane + 1) * 128)
        summed[0, lane] = summed[0, lane] + both[:, lanes]
        summed[1, lane] = summed[1, lane] + (both[:, further] + late[:, lanes])
    for field in range(LF):
        finish(field)


def decode_tile(
    own,
    other,
    share_rows,
    grid_rows,
    width,
    tile_rows,
    conv_in_weight,
    conv_in_bias,
    norm_gain,
    conv_mid_weight,
    conv_mid_bias,
):
    sections = lax.axis_size("sect")
    channels, features = conv_in_weight.shape[3:]
    token_width = 4 * channels
    columns = width // sections
    span = columns // 2
    pairs = span + 1
    chunks = (span + 2) * token_width // 128
    lane_tiles = features // 128
    vmem = pl.BlockSpec(memory_space=pltpu.VMEM)
    hbm = pl.BlockSpec(memory_space=pltpu.HBM)
    slots = len(TAPS)
    depth = slots * 2 * 4 * token_width
    held = chunks * 4 * UNITS
    return pl.pallas_call(
        functools.partial(decode_body, grid_rows, width, share_rows),
        in_specs=[vmem, vmem, pl.BlockSpec(memory_space=pltpu.SMEM)] + [hbm] * 5,
        out_specs=vmem,
        out_shape=jax.ShapeDtypeStruct((LF, ROWS, columns, features), jnp.bfloat16),
        scratch_shapes=[
            pltpu.VMEM((3, 3 * features, slots * features), jnp.bfloat16),
            pltpu.VMEM(conv_in_weight.shape, jnp.bfloat16),
            pltpu.VMEM(conv_in_bias.shape, jnp.float32),
            pltpu.VMEM(norm_gain.shape, jnp.float32),
            pltpu.VMEM(conv_mid_bias.shape, jnp.float32),
            pltpu.VMEM((depth, 2 * features), jnp.bfloat16),
            pltpu.VMEM((2 * own.shape[0] * share_rows, chunks * 128), jnp.float32),
            pltpu.VMEM((chunks * 2 * UNITS, depth), jnp.bfloat16),
            pltpu.VMEM((chunks * 2 * UNITS, 2 * features), jnp.float32),
            pltpu.VMEM((lane_tiles, held, 128), jnp.float32),
            pltpu.VMEM((lane_tiles, held, 128), jnp.float32),
            pltpu.VMEM((2, pairs * 16, LF * 3 * features), jnp.bfloat16),
            pltpu.VMEM((LF, lane_tiles, columns * ROWS, 128), jnp.float32),
            pltpu.SemaphoreType.DMA((3, 3, slots)),
            pltpu.SemaphoreType.DMA((4,)),
        ],
        compiler_params=pltpu.CompilerParams(vmem_limit_bytes=DECODE_VMEM),
        cost_estimate=pl.CostEstimate(
            flops=2 * 3 * 9 * columns * ROWS * features * features,
            bytes_accessed=slots * 9 * features * features * 2,
            transcendentals=held * features,
        ),
        name="decode_tile",
    )(
        own,
        other,
        *in_hbm(
            tile_rows, conv_in_weight, conv_in_bias, norm_gain, conv_mid_weight, conv_mid_bias
        ),
    )


def on_device(
    queries,
    key_tokens,
    value_tokens,
    latent,
    tile_rows,
    conv_in_weight,
    conv_in_bias,
    norm_gain,
    conv_mid_weight,
    conv_mid_bias,
):
    devices = lax.axis_size("seq")
    groups = parity_groups(devices)
    grid_rows = latent.shape[0] * devices // LF
    token_width = 4 * conv_in_weight.shape[3]
    packed = pack_heads(queries, key_tokens, value_tokens, latent, token_width)
    own = lax.all_to_all(packed, "seq", 0, 0, axis_index_groups=groups, tiled=True)
    other = lax.ppermute(own, "seq", xor_pairs(1))
    mixed = attend(own, other, queries.shape[0])
    returned = lax.all_to_all(mixed, "seq", 0, 0, axis_index_groups=groups, tiled=True)
    frames = decode_tile(
        own,
        other,
        latent.shape[0],
        grid_rows,
        2 * latent.shape[1] // token_width,
        tile_rows,
        conv_in_weight,
        conv_in_bias,
        norm_gain,
        conv_mid_weight,
        conv_mid_bias,
    )
    return (unpack_heads(returned), frames)


def solution(mesh):
    in_specs = (
        P("seq", None),
        P("seq", None),
        P("seq", None),
        P("seq", None),
        P(),
        P(),
        P(),
        P(),
        P(),
        P(),
    )
    out_specs = (P("seq", "sect"), P(None, "seq", "sect", None))
    return jax.shard_map(
        on_device, mesh=mesh, in_specs=in_specs, out_specs=out_specs, check_vma=False
    )
```

```python
import functools
import math

import jax
import jax.numpy as jnp
from jax import lax
from jax.experimental import pallas as pl
from jax.experimental.pallas import tpu as pltpu
from jax.sharding import PartitionSpec as P

DH = 128
LF = 2
MAXT = 4
RIM = 64
TAPS = (1, 2)
ROWS = 2 * MAXT
REACH = ROWS + 2
UNITS = -(-LF * REACH // 8) * 8
DECODE_VMEM = 32 * 1024 * 1024
ATTEND_VMEM = 32 * 1024 * 1024
COPY_VMEM = 16 * 1024 * 1024


def parity_groups(devices):
    return [list(range(parity, devices, 2)) for parity in range(2)]


def in_hbm(*arrays):
    return [pltpu.with_memory_space_constraint(array, pltpu.HBM) for array in arrays]


def pack_body(query_ref, key_ref, value_ref, latent_ref, packed_ref, held, sems):
    heads = packed_ref.shape[0]
    token_rows = query_ref.shape[0]
    section = lax.axis_index("sect")
    wide_columns = pl.ds(pl.multiple_of(section * heads * DH, DH), heads * DH)
    copies = [
        pltpu.make_async_copy(ref.at[:, wide_columns], held.at[place], sems.at[place])
        for place, ref in enumerate((query_ref, key_ref, value_ref))
    ]
    for copy in copies:
        copy.start()
    rows, width = latent_ref.shape
    half, rim = width // 2, RIM
    wide = latent_ref[...].astype(jnp.float32)
    rim_zeros = jnp.zeros((rows, rim), jnp.float32)
    lower = jnp.concatenate([rim_zeros, wide[:, : half + rim]], axis=1)
    upper = jnp.concatenate([wide[:, half - rim :], rim_zeros], axis=1)
    share = jnp.where(section == 0, lower, upper)
    chunks = share.shape[1] // DH
    lines = [share[:, chunk * DH : (chunk + 1) * DH] for chunk in range(chunks)]
    spare = packed_ref.shape[1] - 3 * token_rows - chunks * rows
    lines.append(jnp.zeros((spare, DH), jnp.float32))
    share = jnp.concatenate(lines, axis=0).astype(packed_ref.dtype)
    for head in range(heads):
        packed_ref[head, 3 * token_rows :] = share
    for place, copy in enumerate(copies):
        copy.wait()
        for head in range(heads):
            packed_ref[head, place * token_rows : (place + 1) * token_rows] = held[
                place, :, head * DH : (head + 1) * DH
            ]


def pack_heads(queries, key_tokens, value_tokens, latent, token_width):
    token_rows, width = queries.shape
    sections = lax.axis_size("sect")
    heads = width // DH // sections
    span = latent.shape[1] // sections + 2 * token_width
    extra = -(-latent.shape[0] * (span // DH) // 16) * 16
    hbm = pl.BlockSpec(memory_space=pltpu.HBM)
    vmem = pl.BlockSpec(memory_space=pltpu.VMEM)
    return pl.pallas_call(
        pack_body,
        in_specs=[hbm, hbm, hbm, vmem],
        out_specs=vmem,
        out_shape=jax.ShapeDtypeStruct((heads, 3 * token_rows + extra, DH), queries.dtype),
        scratch_shapes=[
            pltpu.VMEM((3, token_rows, heads * DH), queries.dtype),
            pltpu.SemaphoreType.DMA((3,)),
        ],
        compiler_params=pltpu.CompilerParams(vmem_limit_bytes=COPY_VMEM),
        name="pack_heads",
    )(*in_hbm(queries, key_tokens, value_tokens, latent))


def xor_pairs(distance):
    return [(i, i ^ distance) for i in range(lax.axis_size("seq"))]


def flat(array):
    return array.reshape(-1, array.shape[-1])


def attend_body(block, own_ref, other_ref, out_ref):
    members, token_rows, _ = out_ref.shape
    at_keys = slice(token_rows, 2 * token_rows)
    at_values = slice(2 * token_rows, 3 * token_rows)
    keys = jnp.concatenate([flat(own_ref[:, at_keys]), flat(other_ref[:, at_keys])], axis=0)
    values = jnp.concatenate([flat(own_ref[:, at_values]), flat(other_ref[:, at_values])], axis=0)

    def one_block(step):
        at = pl.ds(step * block, block)
        scores = lax.dot_general(
            flat(own_ref[at, :token_rows]),
            keys,
            (((1,), (1,)), ((), ())),
            preferred_element_type=jnp.float32,
        ) * (1.0 / math.sqrt(DH))
        exponents = jnp.exp(scores - jnp.max(scores, axis=1, keepdims=True))
        totals = jnp.sum(exponents, axis=1, keepdims=True)
        mixed = jnp.dot(
            exponents.astype(jnp.bfloat16), values, preferred_element_type=jnp.float32
        )
        out_ref[at] = (mixed / totals).astype(out_ref.dtype).reshape(block, token_rows, DH)

    if members <= 8:
        for step in range(members // block):
            one_block(step)
    else:
        pl.loop(0, members // block)(one_block)


def attend(own, other, token_rows):
    members = own.shape[0]
    total = members * token_rows
    vmem = pl.BlockSpec(memory_space=pltpu.VMEM)
    return pl.pallas_call(
        functools.partial(attend_body, min(4, members)),
        in_specs=[vmem, vmem],
        out_specs=vmem,
        out_shape=jax.ShapeDtypeStruct((members, token_rows, DH), own.dtype),
        compiler_params=pltpu.CompilerParams(vmem_limit_bytes=ATTEND_VMEM),
        cost_estimate=pl.CostEstimate(
            flops=8 * total * total * DH,
            bytes_accessed=7 * total * DH * 2,
            transcendentals=2 * total * total,
        ),
        name="attend",
    )(own, other)


def unpack_body(in_ref, out_ref, sems):
    copies = [
        pltpu.make_async_copy(
            in_ref.at[head], out_ref.at[:, pl.ds(head * DH, DH)], sems.at[head]
        )
        for head in range(in_ref.shape[0])
    ]
    for copy in copies:
        copy.start()
    for copy in copies:
        copy.wait()


def unpack_heads(array):
    heads, token_rows, _ = array.shape
    return pl.pallas_call(
        unpack_body,
        in_specs=[pl.BlockSpec(memory_space=pltpu.VMEM)],
        out_specs=pl.BlockSpec(memory_space=pltpu.HBM),
        out_shape=jax.ShapeDtypeStruct((token_rows, heads * DH), array.dtype),
        scratch_shapes=[pltpu.SemaphoreType.DMA((heads,))],
        compiler_params=pltpu.CompilerParams(vmem_limit_bytes=COPY_VMEM),
        name="unpack_heads",
    )(array)


def decode_body(
    grid_rows,
    width,
    share_rows,
    own_ref,
    other_ref,
    tile_ref,
    in_weight_hbm,
    in_bias_hbm,
    gain_hbm,
    mid_weight_hbm,
    mid_bias_hbm,
    out_ref,
    mid_weight,
    in_weight_ref,
    in_bias_ref,
    gain_ref,
    mid_bias_ref,
    taps,
    rows_held,
    patches,
    raw,
    hidden,
    activated,
    active,
    summed,
    weight_sems,
    small_sems,
):
    pairs = active.shape[1] // 16
    channels, features = in_weight_ref.shape[3:]
    columns = out_ref.shape[2]
    lane_tiles = features // 128
    position = lax.axis_index("seq")
    section = lax.axis_index("sect")
    small = [
        pltpu.make_async_copy(source, target, small_sems.at[place])
        for place, (source, target) in enumerate(
            (
                (in_weight_hbm, in_weight_ref),
                (in_bias_hbm, in_bias_ref),
                (gain_hbm, gain_ref),
                (mid_bias_hbm, mid_bias_ref),
            )
        )
    ]
    for copy in small:
        copy.start()

    def load(col_tap):
        return [
            pltpu.make_async_copy(
                mid_weight_hbm.at[tap, row_tap, col_tap],
                mid_weight.at[
                    col_tap,
                    pl.ds(row_tap * features, features),
                    pl.ds((2 - tap) * features, features),
                ],
                weight_sems.at[col_tap, row_tap, slot],
            )
            for row_tap in range(3)
            for slot, tap in enumerate(TAPS)
        ]

    for col_tap in range(3):
        for copy in load(col_tap):
            copy.start()

    filled = tile_ref[position]
    first_row = lax.fori_loop(0, position, lambda d, total: total + tile_ref[d], jnp.int32(0))

    members, message, _ = own_ref.shape
    chunks = rows_held.shape[1] // 128
    extra = -(-share_rows * chunks // 16) * 16
    for side, ref in enumerate((own_ref, other_ref)):
        for member in range(members):
            lines = ref[member, message - extra :].astype(jnp.float32)
            low = (side * members + member) * share_rows
            for chunk in range(chunks):
                rows_held[low : low + share_rows, chunk * 128 : (chunk + 1) * 128] = lines[
                    chunk * share_rows : (chunk + 1) * share_rows
                ]
    latent = rows_held[...]
    aside = pltpu.roll(latent, latent.shape[1] - RIM, 1).astype(jnp.bfloat16)
    latent = latent.astype(jnp.bfloat16)
    held_rows = latent.shape[0]
    unit = lax.broadcasted_iota(jnp.int32, (UNITS, held_rows), 0)
    held = lax.broadcasted_iota(jnp.int32, (UNITS, held_rows), 1)
    side = (held >= members * share_rows).astype(jnp.int32)
    member = held // share_rows - side * members
    held = (2 * member + ((position & 1) ^ side)) * share_rows + held % share_rows
    frame = sum((unit >= (k + 1) * REACH).astype(jnp.int32) for k in range(LF))
    reach = unit - frame * REACH
    selectors = []
    for tap in TAPS:
        for row_parity in range(2):
            for i in range(2):
                token_row = first_row + (reach >> 1) - 1 + i
                source = frame + tap - 2
                wanted = (
                    ((reach & 1) == row_parity)
                    & (token_row >= 0)
                    & (token_row < grid_rows)
                    & (source >= 0)
                    & (source < LF)
                )
                target = jnp.where(wanted, source * grid_rows + token_row, -1)
                selectors.append(jnp.where(held == target, 1.0, 0.0).astype(jnp.bfloat16))
    selector = jnp.concatenate(selectors, axis=0)
    even = jnp.dot(selector, latent, preferred_element_type=jnp.float32)
    odd = jnp.dot(selector, aside, preferred_element_type=jnp.float32)
    for chunk in range(chunks):
        lanes = slice(chunk * 128, (chunk + 1) * 128)
        for group in range(len(selectors)):
            rows = slice(group * UNITS, (group + 1) * UNITS)
            piece = jnp.concatenate([even[rows, lanes], odd[rows, lanes]], axis=0)
            patches[
                chunk * 2 * UNITS : (chunk + 1) * 2 * UNITS, group * 128 : (group + 1) * 128
            ] = piece.astype(jnp.bfloat16)

    for copy in small:
        copy.wait()
    nothing = jnp.zeros((channels, features), jnp.bfloat16)
    base = 0
    for tap in TAPS:
        for row_parity in range(2):
            for i, j, p, q in [
                (i, j, p, q) for i in range(2) for j in range(2) for p in range(2) for q in range(2)
            ]:
                for col_parity in range(2):
                    row_tap, col_tap = 2 * i + p - row_parity, 2 * j + q - col_parity
                    inside = 0 <= row_tap < 3 and 0 <= col_tap < 3
                    taps[base : base + channels, col_parity * features : (col_parity + 1) * features] = (
                        in_weight_ref[tap, row_tap, col_tap] if inside else nothing
                    )
                base += channels

    unit_row = lax.broadcasted_iota(jnp.int32, (UNITS, 1), 0)
    row_frame = sum((unit_row >= (k + 1) * REACH).astype(jnp.int32) for k in range(LF))
    pixel_row = 2 * first_row + unit_row - row_frame * REACH - 1
    row_inside = (pixel_row >= 0) & (pixel_row < 2 * grid_rows)
    in_bias = in_bias_ref[...].reshape(1, features)
    half_gain = gain_ref[...].reshape(1, features) * 0.5

    def first_layer(chunk):
        for corner in range(2):
            start = (chunk * 2 + corner) * UNITS
            for col_parity in range(2):
                value = (
                    raw[pl.ds(start, UNITS), col_parity * features : (col_parity + 1) * features]
                    + in_bias
                )
                value = value.astype(jnp.bfloat16).astype(jnp.float32)
                scale = lax.rsqrt(jnp.mean(value * value, axis=1, keepdims=True) + 1e-06)
                column = chunk * 4 + corner * 2 + col_parity
                pixel = section * columns + column - 1
                keep = row_inside & (pixel >= 0) & (pixel < width)
                half = value * jnp.where(keep, scale, 0.0) * half_gain
                result = half + half * jnp.tanh(half)
                at = pl.ds(column * UNITS, UNITS)
                for lane in range(lane_tiles):
                    lanes = slice(lane * 128, (lane + 1) * 128)
                    hidden[lane, at] = value[:, lanes]
                    activated[lane, at] = result[:, lanes]

    middle = (chunks + 1) // 2
    groups = ((0, middle), (middle, chunks))
    for low, high in groups:
        rows = slice(low * 2 * UNITS, high * 2 * UNITS)
        raw[rows] = jnp.dot(patches[rows], taps[...], preferred_element_type=jnp.float32)
    for low, high in groups:
        for chunk in range(low, high):
            first_layer(chunk)

    def pair_up(phase, pair):
        at = slice(pair * 16, pair * 16 + 16)
        for lane in range(lane_tiles):
            for field in range(LF):
                for row_tap in range(3):
                    start = (2 * pair + phase) * UNITS + field * REACH + row_tap
                    joined = jnp.concatenate(
                        [activated[lane, pl.ds(start + k * UNITS, ROWS)] for k in range(2)], axis=0
                    )
                    to_lane = (field * 3 + row_tap) * features + lane * 128
                    active[phase, at, to_lane : to_lane + 128] = joined.astype(jnp.bfloat16)

    rows = columns * ROWS
    depth = 3 * features

    def windows(low, high, lanes):
        return jnp.concatenate(
            [
                active[tap % 2, 16 * (tap // 2) + low : 16 * (tap // 2) + high, lanes]
                for tap in range(3)
            ],
            axis=1,
        )

    def weights(lanes):
        return jnp.concatenate([mid_weight[tap, :, lanes] for tap in range(3)], axis=0)

    mid_bias = mid_bias_ref[...].reshape(1, features)

    def finish(field):
        for row in range(ROWS):
            for lane in range(lane_tiles):
                lanes = slice(lane * 128, (lane + 1) * 128)
                skip = hidden[lane, pl.ds(UNITS + field * REACH + 1 + row, columns, stride=UNITS), :]
                value = summed[field, lane, pl.ds(row, columns, stride=ROWS), :]
                value = value + skip + mid_bias[:, lanes]
                value = jnp.where(row < 2 * filled, value, 0.0)
                out_ref[field, row, :, lanes] = value.astype(jnp.bfloat16)

    for phase in range(2):
        for pair in range(pairs - phase):
            pair_up(phase, pair)
    for tap in range(3):
        for copy in load(tap):
            copy.wait()
    step = rows // 2
    for low in (0, step):
        at = slice(low, low + step)
        early = windows(low, low + step, slice(0, depth))
        late = windows(low, low + step, slice(depth, 2 * depth))
        for left in range(0, 2 * features, 256):
            block = jnp.dot(
                early, weights(slice(left, left + 256)), preferred_element_type=jnp.float32
            )
            for lane in range(2):
                field, tile = divmod(left // 128 + lane, lane_tiles)
                summed[field, tile, at] = block[:, lane * 128 : (lane + 1) * 128]
        for left in range(0, features, 256):
            right = min(left + 256, features)
            block = jnp.dot(
                late, weights(slice(left, right)), preferred_element_type=jnp.float32
            )
            for lane in range((right - left) // 128):
                tile = left // 128 + lane
                summed[1, tile, at] = (
                    summed[1, tile, at] + block[:, lane * 128 : (lane + 1) * 128]
                )
    for field in range(LF):
        finish(field)


def decode_tile(
    own,
    other,
    share_rows,
    grid_rows,
    width,
    tile_rows,
    conv_in_weight,
    conv_in_bias,
    norm_gain,
    conv_mid_weight,
    conv_mid_bias,
):
    sections = lax.axis_size("sect")
    channels, features = conv_in_weight.shape[3:]
    token_width = 4 * channels
    columns = width // sections
    span = columns // 2
    pairs = span + 1
    chunks = (span + 2) * token_width // 128
    lane_tiles = features // 128
    vmem = pl.BlockSpec(memory_space=pltpu.VMEM)
    hbm = pl.BlockSpec(memory_space=pltpu.HBM)
    slots = len(TAPS)
    depth = slots * 2 * 4 * token_width
    held = chunks * 4 * UNITS
    return pl.pallas_call(
        functools.partial(decode_body, grid_rows, width, share_rows),
        in_specs=[vmem, vmem, pl.BlockSpec(memory_space=pltpu.SMEM)] + [hbm] * 5,
        out_specs=vmem,
        out_shape=jax.ShapeDtypeStruct((LF, ROWS, columns, features), jnp.bfloat16),
        scratch_shapes=[
            pltpu.VMEM((3, 3 * features, slots * features), jnp.bfloat16),
            pltpu.VMEM(conv_in_weight.shape, jnp.bfloat16),
            pltpu.VMEM(conv_in_bias.shape, jnp.float32),
            pltpu.VMEM(norm_gain.shape, jnp.float32),
            pltpu.VMEM(conv_mid_bias.shape, jnp.float32),
            pltpu.VMEM((depth, 2 * features), jnp.bfloat16),
            pltpu.VMEM((2 * own.shape[0] * share_rows, chunks * 128), jnp.float32),
            pltpu.VMEM((chunks * 2 * UNITS, depth), jnp.bfloat16),
            pltpu.VMEM((chunks * 2 * UNITS, 2 * features), jnp.float32),
            pltpu.VMEM((lane_tiles, held, 128), jnp.float32),
            pltpu.VMEM((lane_tiles, held, 128), jnp.float32),
            pltpu.VMEM((2, pairs * 16, LF * 3 * features), jnp.bfloat16),
            pltpu.VMEM((LF, lane_tiles, columns * ROWS, 128), jnp.float32),
            pltpu.SemaphoreType.DMA((3, 3, slots)),
            pltpu.SemaphoreType.DMA((4,)),
        ],
        compiler_params=pltpu.CompilerParams(vmem_limit_bytes=DECODE_VMEM),
        cost_estimate=pl.CostEstimate(
            flops=2 * 3 * 9 * columns * ROWS * features * features,
            bytes_accessed=slots * 9 * features * features * 2,
            transcendentals=held * features,
        ),
        name="decode_tile",
    )(
        own,
        other,
        *in_hbm(
            tile_rows, conv_in_weight, conv_in_bias, norm_gain, conv_mid_weight, conv_mid_bias
        ),
    )


def on_device(
    queries,
    key_tokens,
    value_tokens,
    latent,
    tile_rows,
    conv_in_weight,
    conv_in_bias,
    norm_gain,
    conv_mid_weight,
    conv_mid_bias,
):
    devices = lax.axis_size("seq")
    groups = parity_groups(devices)
    grid_rows = latent.shape[0] * devices // LF
    token_width = 4 * conv_in_weight.shape[3]
    packed = pack_heads(queries, key_tokens, value_tokens, latent, token_width)
    own = lax.all_to_all(packed, "seq", 0, 0, axis_index_groups=groups, tiled=True)
    other = lax.ppermute(own, "seq", xor_pairs(1))
    mixed = attend(own, other, queries.shape[0])
    returned = lax.all_to_all(mixed, "seq", 0, 0, axis_index_groups=groups, tiled=True)
    frames = decode_tile(
        own,
        other,
        latent.shape[0],
        grid_rows,
        2 * latent.shape[1] // token_width,
        tile_rows,
        conv_in_weight,
        conv_in_bias,
        norm_gain,
        conv_mid_weight,
        conv_mid_bias,
    )
    return (unpack_heads(returned), frames)


def solution(mesh):
    in_specs = (
        P("seq", None),
        P("seq", None),
        P("seq", None),
        P("seq", None),
        P(),
        P(),
        P(),
        P(),
        P(),
        P(),
    )
    out_specs = (P("seq", "sect"), P(None, "seq", "sect", None))
    return jax.shard_map(
        on_device, mesh=mesh, in_specs=in_specs, out_specs=out_specs, check_vma=False
    )
```

```python
import functools
import math

import jax
import jax.numpy as jnp
from jax import lax
from jax.experimental import pallas as pl
from jax.experimental.pallas import tpu as pltpu
from jax.sharding import PartitionSpec as P

DH = 128
LF = 2
MAXT = 4
RIM = 64
TAPS = (1, 2)
ROWS = 2 * MAXT
REACH = ROWS + 2
UNITS = -(-LF * REACH // 8) * 8
DECODE_VMEM = 32 * 1024 * 1024
ATTEND_VMEM = 32 * 1024 * 1024
COPY_VMEM = 16 * 1024 * 1024


def parity_groups(devices):
    return [list(range(parity, devices, 2)) for parity in range(2)]


def in_hbm(*arrays):
    return [pltpu.with_memory_space_constraint(array, pltpu.HBM) for array in arrays]


def pack_body(query_ref, key_ref, value_ref, latent_ref, packed_ref, held, sems):
    heads = packed_ref.shape[0]
    token_rows = query_ref.shape[0]
    section = lax.axis_index("sect")
    wide_columns = pl.ds(pl.multiple_of(section * heads * DH, DH), heads * DH)
    copies = [
        pltpu.make_async_copy(ref.at[:, wide_columns], held.at[place], sems.at[place])
        for place, ref in enumerate((query_ref, key_ref, value_ref))
    ]
    for copy in copies:
        copy.start()
    rows, width = latent_ref.shape
    half, rim = width // 2, RIM
    wide = latent_ref[...].astype(jnp.float32)
    rim_zeros = jnp.zeros((rows, rim), jnp.float32)
    lower = jnp.concatenate([rim_zeros, wide[:, : half + rim]], axis=1)
    upper = jnp.concatenate([wide[:, half - rim :], rim_zeros], axis=1)
    share = jnp.where(section == 0, lower, upper)
    chunks = share.shape[1] // DH
    lines = [share[:, chunk * DH : (chunk + 1) * DH] for chunk in range(chunks)]
    spare = packed_ref.shape[1] - 3 * token_rows - chunks * rows
    lines.append(jnp.zeros((spare, DH), jnp.float32))
    share = jnp.concatenate(lines, axis=0).astype(packed_ref.dtype)
    for head in range(heads):
        packed_ref[head, 3 * token_rows :] = share
    for place, copy in enumerate(copies):
        copy.wait()
        for head in range(heads):
            packed_ref[head, place * token_rows : (place + 1) * token_rows] = held[
                place, :, head * DH : (head + 1) * DH
            ]


def pack_heads(queries, key_tokens, value_tokens, latent, token_width):
    token_rows, width = queries.shape
    sections = lax.axis_size("sect")
    heads = width // DH // sections
    span = latent.shape[1] // sections + 2 * token_width
    extra = -(-latent.shape[0] * (span // DH) // 16) * 16
    hbm = pl.BlockSpec(memory_space=pltpu.HBM)
    vmem = pl.BlockSpec(memory_space=pltpu.VMEM)
    return pl.pallas_call(
        pack_body,
        in_specs=[hbm, hbm, hbm, vmem],
        out_specs=vmem,
        out_shape=jax.ShapeDtypeStruct((heads, 3 * token_rows + extra, DH), queries.dtype),
        scratch_shapes=[
            pltpu.VMEM((3, token_rows, heads * DH), queries.dtype),
            pltpu.SemaphoreType.DMA((3,)),
        ],
        compiler_params=pltpu.CompilerParams(vmem_limit_bytes=COPY_VMEM),
        name="pack_heads",
    )(*in_hbm(queries, key_tokens, value_tokens, latent))


def xor_pairs(distance):
    return [(i, i ^ distance) for i in range(lax.axis_size("seq"))]


def flat(array):
    return array.reshape(-1, array.shape[-1])


def attend_body(block, own_ref, other_ref, out_ref, mixed_ref, sems):
    members, token_rows, _ = out_ref.shape
    at_keys = slice(token_rows, 2 * token_rows)
    at_values = slice(2 * token_rows, 3 * token_rows)
    keys = jnp.concatenate([flat(own_ref[:, at_keys]), flat(other_ref[:, at_keys])], axis=0)
    values = jnp.concatenate([flat(own_ref[:, at_values]), flat(other_ref[:, at_values])], axis=0)

    def one_block(step):
        at = pl.ds(step * block, block)
        scores = lax.dot_general(
            flat(own_ref[at, :token_rows]),
            keys,
            (((1,), (1,)), ((), ())),
            preferred_element_type=jnp.float32,
        ) * (1.0 / math.sqrt(DH))
        exponents = jnp.exp(scores - jnp.max(scores, axis=1, keepdims=True))
        totals = jnp.sum(exponents, axis=1, keepdims=True)
        mixed = jnp.dot(
            exponents.astype(jnp.bfloat16), values, preferred_element_type=jnp.float32
        )
        mixed = (mixed / totals).astype(out_ref.dtype)
        mixed_ref[at] = mixed.reshape(block, token_rows, DH)
        move(step).start()

    def move(step):
        at = pl.ds(step * block, block)
        return pltpu.make_async_copy(mixed_ref.at[at], out_ref.at[at], sems.at[step])

    steps = members // block
    if members <= 8:
        for step in range(steps):
            one_block(step)
    else:
        pl.loop(0, steps)(one_block)
    for step in range(steps):
        move(step).wait()


def attend(own, other, token_rows):
    members = own.shape[0]
    total = members * token_rows
    block = 2 if members <= 8 else 4
    vmem = pl.BlockSpec(memory_space=pltpu.VMEM)
    return pl.pallas_call(
        functools.partial(attend_body, block),
        in_specs=[vmem, vmem],
        out_specs=pl.BlockSpec(memory_space=pltpu.HBM),
        out_shape=jax.ShapeDtypeStruct((members, token_rows, DH), own.dtype),
        scratch_shapes=[
            pltpu.VMEM((members, token_rows, DH), own.dtype),
            pltpu.SemaphoreType.DMA((members // block,)),
        ],
        compiler_params=pltpu.CompilerParams(vmem_limit_bytes=ATTEND_VMEM),
        cost_estimate=pl.CostEstimate(
            flops=8 * total * total * DH,
            bytes_accessed=7 * total * DH * 2,
            transcendentals=2 * total * total,
        ),
        name="attend",
    )(own, other)


def unpack_body(in_ref, out_ref, sems):
    copies = [
        pltpu.make_async_copy(
            in_ref.at[head], out_ref.at[:, pl.ds(head * DH, DH)], sems.at[head]
        )
        for head in range(in_ref.shape[0])
    ]
    for copy in copies:
        copy.start()
    for copy in copies:
        copy.wait()


def unpack_heads(array):
    heads, token_rows, _ = array.shape
    return pl.pallas_call(
        unpack_body,
        in_specs=[pl.BlockSpec(memory_space=pltpu.VMEM)],
        out_specs=pl.BlockSpec(memory_space=pltpu.HBM),
        out_shape=jax.ShapeDtypeStruct((token_rows, heads * DH), array.dtype),
        scratch_shapes=[pltpu.SemaphoreType.DMA((heads,))],
        compiler_params=pltpu.CompilerParams(vmem_limit_bytes=COPY_VMEM),
        name="unpack_heads",
    )(array)


def decode_body(
    grid_rows,
    width,
    share_rows,
    own_ref,
    other_ref,
    tile_ref,
    in_weight_hbm,
    in_bias_hbm,
    gain_hbm,
    mid_weight_hbm,
    mid_bias_hbm,
    out_ref,
    mid_weight,
    in_weight_ref,
    in_bias_ref,
    gain_ref,
    mid_bias_ref,
    taps,
    rows_held,
    patches,
    raw,
    hidden,
    activated,
    active,
    summed,
    weight_sems,
    small_sems,
):
    pairs = active.shape[1] // 16
    channels, features = in_weight_ref.shape[3:]
    columns = out_ref.shape[2]
    lane_tiles = features // 128
    position = lax.axis_index("seq")
    section = lax.axis_index("sect")
    small = [
        pltpu.make_async_copy(source, target, small_sems.at[place])
        for place, (source, target) in enumerate(
            (
                (in_weight_hbm, in_weight_ref),
                (in_bias_hbm, in_bias_ref),
                (gain_hbm, gain_ref),
                (mid_bias_hbm, mid_bias_ref),
            )
        )
    ]
    for copy in small:
        copy.start()

    def load(col_tap):
        return [
            pltpu.make_async_copy(
                mid_weight_hbm.at[tap, row_tap, col_tap],
                mid_weight.at[
                    col_tap,
                    pl.ds(row_tap * features, features),
                    pl.ds((2 - tap) * features, features),
                ],
                weight_sems.at[col_tap, row_tap, slot],
            )
            for row_tap in range(3)
            for slot, tap in enumerate(TAPS)
        ]

    for col_tap in range(3):
        for copy in load(col_tap):
            copy.start()

    filled = tile_ref[position]
    first_row = lax.fori_loop(0, position, lambda d, total: total + tile_ref[d], jnp.int32(0))

    members, message, _ = own_ref.shape
    chunks = rows_held.shape[1] // 128
    extra = -(-share_rows * chunks // 16) * 16
    for side, ref in enumerate((own_ref, other_ref)):
        for member in range(members):
            lines = ref[member, message - extra :].astype(jnp.float32)
            low = (side * members + member) * share_rows
            for chunk in range(chunks):
                rows_held[low : low + share_rows, chunk * 128 : (chunk + 1) * 128] = lines[
                    chunk * share_rows : (chunk + 1) * share_rows
                ]
    latent = rows_held[...]
    aside = pltpu.roll(latent, latent.shape[1] - RIM, 1).astype(jnp.bfloat16)
    latent = latent.astype(jnp.bfloat16)
    held_rows = latent.shape[0]
    unit = lax.broadcasted_iota(jnp.int32, (UNITS, held_rows), 0)
    held = lax.broadcasted_iota(jnp.int32, (UNITS, held_rows), 1)
    side = (held >= members * share_rows).astype(jnp.int32)
    member = held // share_rows - side * members
    held = (2 * member + ((position & 1) ^ side)) * share_rows + held % share_rows
    frame = sum((unit >= (k + 1) * REACH).astype(jnp.int32) for k in range(LF))
    reach = unit - frame * REACH
    selectors = []
    for tap in TAPS:
        for row_parity in range(2):
            for i in range(2):
                token_row = first_row + (reach >> 1) - 1 + i
                source = frame + tap - 2
                wanted = (
                    ((reach & 1) == row_parity)
                    & (token_row >= 0)
                    & (token_row < grid_rows)
                    & (source >= 0)
                    & (source < LF)
                )
                target = jnp.where(wanted, source * grid_rows + token_row, -1)
                selectors.append(jnp.where(held == target, 1.0, 0.0).astype(jnp.bfloat16))
    selector = jnp.concatenate(selectors, axis=0)
    even = jnp.dot(selector, latent, preferred_element_type=jnp.float32)
    odd = jnp.dot(selector, aside, preferred_element_type=jnp.float32)
    for chunk in range(chunks):
        lanes = slice(chunk * 128, (chunk + 1) * 128)
        for group in range(len(selectors)):
            rows = slice(group * UNITS, (group + 1) * UNITS)
            piece = jnp.concatenate([even[rows, lanes], odd[rows, lanes]], axis=0)
            patches[
                chunk * 2 * UNITS : (chunk + 1) * 2 * UNITS, group * 128 : (group + 1) * 128
            ] = piece.astype(jnp.bfloat16)

    for copy in small:
        copy.wait()
    nothing = jnp.zeros((channels, features), jnp.bfloat16)
    base = 0
    for tap in TAPS:
        for row_parity in range(2):
            for i, j, p, q in [
                (i, j, p, q) for i in range(2) for j in range(2) for p in range(2) for q in range(2)
            ]:
                for col_parity in range(2):
                    row_tap, col_tap = 2 * i + p - row_parity, 2 * j + q - col_parity
                    inside = 0 <= row_tap < 3 and 0 <= col_tap < 3
                    taps[base : base + channels, col_parity * features : (col_parity + 1) * features] = (
                        in_weight_ref[tap, row_tap, col_tap] if inside else nothing
                    )
                base += channels

    unit_row = lax.broadcasted_iota(jnp.int32, (UNITS, 1), 0)
    row_frame = sum((unit_row >= (k + 1) * REACH).astype(jnp.int32) for k in range(LF))
    pixel_row = 2 * first_row + unit_row - row_frame * REACH - 1
    row_inside = (pixel_row >= 0) & (pixel_row < 2 * grid_rows)
    in_bias = in_bias_ref[...].reshape(1, features)
    half_gain = gain_ref[...].reshape(1, features) * 0.5

    def first_layer(chunk):
        for corner in range(2):
            start = (chunk * 2 + corner) * UNITS
            for col_parity in range(2):
                value = (
                    raw[pl.ds(start, UNITS), col_parity * features : (col_parity + 1) * features]
                    + in_bias
                )
                value = value.astype(jnp.bfloat16).astype(jnp.float32)
                scale = lax.rsqrt(jnp.mean(value * value, axis=1, keepdims=True) + 1e-06)
                column = chunk * 4 + corner * 2 + col_parity
                pixel = section * columns + column - 1
                keep = row_inside & (pixel >= 0) & (pixel < width)
                half = value * jnp.where(keep, scale, 0.0) * half_gain
                result = half + half * jnp.tanh(half)
                at = pl.ds(column * UNITS, UNITS)
                for lane in range(lane_tiles):
                    lanes = slice(lane * 128, (lane + 1) * 128)
                    hidden[lane, at] = value[:, lanes]
                    activated[lane, at] = result[:, lanes]

    groups = [(low, min(low + 4, chunks)) for low in range(0, chunks, 4)]
    for low, high in groups:
        rows = slice(low * 2 * UNITS, high * 2 * UNITS)
        for left in range(0, 2 * features, 256):
            lanes = slice(left, left + 256)
            raw[rows, lanes] = jnp.dot(
                patches[rows], taps[:, lanes], preferred_element_type=jnp.float32
            )
        for chunk in range(low, high):
            first_layer(chunk)

    def pair_up(phase, pair):
        at = slice(pair * 16, pair * 16 + 16)
        for lane in range(lane_tiles):
            for field in range(LF):
                for row_tap in range(3):
                    start = (2 * pair + phase) * UNITS + field * REACH + row_tap
                    joined = jnp.concatenate(
                        [activated[lane, pl.ds(start + k * UNITS, ROWS)] for k in range(2)], axis=0
                    )
                    to_lane = (field * 3 + row_tap) * features + lane * 128
                    active[phase, at, to_lane : to_lane + 128] = joined.astype(jnp.bfloat16)

    rows = columns * ROWS
    depth = 3 * features

    def windows(low, high, lanes):
        return jnp.concatenate(
            [
                active[tap % 2, 16 * (tap // 2) + low : 16 * (tap // 2) + high, lanes]
                for tap in range(3)
            ],
            axis=1,
        )

    def weights(lanes):
        return jnp.concatenate([mid_weight[tap, :, lanes] for tap in range(3)], axis=0)

    mid_bias = mid_bias_ref[...].reshape(1, features)

    def finish(field):
        for row in range(ROWS):
            for lane in range(lane_tiles):
                lanes = slice(lane * 128, (lane + 1) * 128)
                skip = hidden[lane, pl.ds(UNITS + field * REACH + 1 + row, columns, stride=UNITS), :]
                value = summed[field, lane, pl.ds(row, columns, stride=ROWS), :]
                value = value + skip + mid_bias[:, lanes]
                value = jnp.where(row < 2 * filled, value, 0.0)
                out_ref[field, row, :, lanes] = value.astype(jnp.bfloat16)

    for phase in range(2):
        for pair in range(pairs - phase):
            pair_up(phase, pair)
    for tap in range(3):
        for copy in load(tap):
            copy.wait()
    step = rows // 2
    for low in (0, step):
        at = slice(low, low + step)
        early = windows(low, low + step, slice(0, depth))
        late = windows(low, low + step, slice(depth, 2 * depth))
        for left in range(0, 2 * features, 256):
            block = jnp.dot(
                early, weights(slice(left, left + 256)), preferred_element_type=jnp.float32
            )
            for lane in range(2):
                field, tile = divmod(left // 128 + lane, lane_tiles)
                summed[field, tile, at] = block[:, lane * 128 : (lane + 1) * 128]
        for left in range(0, features, 256):
            right = min(left + 256, features)
            block = jnp.dot(
                late, weights(slice(left, right)), preferred_element_type=jnp.float32
            )
            for lane in range((right - left) // 128):
                tile = left // 128 + lane
                summed[1, tile, at] = (
                    summed[1, tile, at] + block[:, lane * 128 : (lane + 1) * 128]
                )
    for field in range(LF):
        finish(field)


def decode_tile(
    own,
    other,
    share_rows,
    grid_rows,
    width,
    tile_rows,
    conv_in_weight,
    conv_in_bias,
    norm_gain,
    conv_mid_weight,
    conv_mid_bias,
):
    sections = lax.axis_size("sect")
    channels, features = conv_in_weight.shape[3:]
    token_width = 4 * channels
    columns = width // sections
    span = columns // 2
    pairs = span + 1
    chunks = (span + 2) * token_width // 128
    lane_tiles = features // 128
    vmem = pl.BlockSpec(memory_space=pltpu.VMEM)
    hbm = pl.BlockSpec(memory_space=pltpu.HBM)
    slots = len(TAPS)
    depth = slots * 2 * 4 * token_width
    held = chunks * 4 * UNITS
    return pl.pallas_call(
        functools.partial(decode_body, grid_rows, width, share_rows),
        in_specs=[vmem, vmem, pl.BlockSpec(memory_space=pltpu.SMEM)] + [hbm] * 5,
        out_specs=vmem,
        out_shape=jax.ShapeDtypeStruct((LF, ROWS, columns, features), jnp.bfloat16),
        scratch_shapes=[
            pltpu.VMEM((3, 3 * features, slots * features), jnp.bfloat16),
            pltpu.VMEM(conv_in_weight.shape, jnp.bfloat16),
            pltpu.VMEM(conv_in_bias.shape, jnp.float32),
            pltpu.VMEM(norm_gain.shape, jnp.float32),
            pltpu.VMEM(conv_mid_bias.shape, jnp.float32),
            pltpu.VMEM((depth, 2 * features), jnp.bfloat16),
            pltpu.VMEM((2 * own.shape[0] * share_rows, chunks * 128), jnp.float32),
            pltpu.VMEM((chunks * 2 * UNITS, depth), jnp.bfloat16),
            pltpu.VMEM((chunks * 2 * UNITS, 2 * features), jnp.float32),
            pltpu.VMEM((lane_tiles, held, 128), jnp.float32),
            pltpu.VMEM((lane_tiles, held, 128), jnp.float32),
            pltpu.VMEM((2, pairs * 16, LF * 3 * features), jnp.bfloat16),
            pltpu.VMEM((LF, lane_tiles, columns * ROWS, 128), jnp.float32),
            pltpu.SemaphoreType.DMA((3, 3, slots)),
            pltpu.SemaphoreType.DMA((4,)),
        ],
        compiler_params=pltpu.CompilerParams(vmem_limit_bytes=DECODE_VMEM),
        cost_estimate=pl.CostEstimate(
            flops=2 * 3 * 9 * columns * ROWS * features * features,
            bytes_accessed=slots * 9 * features * features * 2,
            transcendentals=held * features,
        ),
        name="decode_tile",
    )(
        own,
        other,
        *in_hbm(
            tile_rows, conv_in_weight, conv_in_bias, norm_gain, conv_mid_weight, conv_mid_bias
        ),
    )


def on_device(
    queries,
    key_tokens,
    value_tokens,
    latent,
    tile_rows,
    conv_in_weight,
    conv_in_bias,
    norm_gain,
    conv_mid_weight,
    conv_mid_bias,
):
    devices = lax.axis_size("seq")
    groups = parity_groups(devices)
    grid_rows = latent.shape[0] * devices // LF
    token_width = 4 * conv_in_weight.shape[3]
    packed = pack_heads(queries, key_tokens, value_tokens, latent, token_width)
    own = lax.all_to_all(packed, "seq", 0, 0, axis_index_groups=groups, tiled=True)
    other = lax.ppermute(own, "seq", xor_pairs(1))
    mixed = attend(own, other, queries.shape[0])
    returned = lax.all_to_all(mixed, "seq", 0, 0, axis_index_groups=groups, tiled=True)
    frames = decode_tile(
        own,
        other,
        latent.shape[0],
        grid_rows,
        2 * latent.shape[1] // token_width,
        tile_rows,
        conv_in_weight,
        conv_in_bias,
        norm_gain,
        conv_mid_weight,
        conv_mid_bias,
    )
    return (unpack_heads(returned), frames)


def solution(mesh):
    in_specs = (
        P("seq", None),
        P("seq", None),
        P("seq", None),
        P("seq", None),
        P(),
        P(),
        P(),
        P(),
        P(),
        P(),
    )
    out_specs = (P("seq", "sect"), P(None, "seq", "sect", None))
    return jax.shard_map(
        on_device, mesh=mesh, in_specs=in_specs, out_specs=out_specs, check_vma=False
    )
```

```python
import functools
import math

import jax
import jax.numpy as jnp
from jax import lax
from jax.experimental import pallas as pl
from jax.experimental.pallas import tpu as pltpu
from jax.sharding import PartitionSpec as P

DH = 128
LF = 2
MAXT = 4
RIM = 64
TAPS = (1, 2)
ROWS = 2 * MAXT
REACH = ROWS + 2
UNITS = -(-LF * REACH // 8) * 8
DECODE_VMEM = 32 * 1024 * 1024
ATTEND_VMEM = 32 * 1024 * 1024
COPY_VMEM = 16 * 1024 * 1024


def parity_groups(devices):
    return [list(range(parity, devices, 2)) for parity in range(2)]


def in_hbm(*arrays):
    return [pltpu.with_memory_space_constraint(array, pltpu.HBM) for array in arrays]


def pack_body(query_ref, key_ref, value_ref, latent_ref, packed_ref, held, sems):
    heads = packed_ref.shape[0]
    token_rows = query_ref.shape[0]
    section = lax.axis_index("sect")
    wide_columns = pl.ds(pl.multiple_of(section * heads * DH, DH), heads * DH)
    copies = [
        pltpu.make_async_copy(ref.at[:, wide_columns], held.at[place], sems.at[place])
        for place, ref in enumerate((query_ref, key_ref, value_ref))
    ]
    for copy in copies:
        copy.start()
    rows, width = latent_ref.shape
    half, rim = width // 2, RIM
    wide = latent_ref[...].astype(jnp.float32)
    rim_zeros = jnp.zeros((rows, rim), jnp.float32)
    lower = jnp.concatenate([rim_zeros, wide[:, : half + rim]], axis=1)
    upper = jnp.concatenate([wide[:, half - rim :], rim_zeros], axis=1)
    share = jnp.where(section == 0, lower, upper)
    chunks = share.shape[1] // DH
    lines = [share[:, chunk * DH : (chunk + 1) * DH] for chunk in range(chunks)]
    spare = packed_ref.shape[1] - 3 * token_rows - chunks * rows
    lines.append(jnp.zeros((spare, DH), jnp.float32))
    share = jnp.concatenate(lines, axis=0).astype(packed_ref.dtype)
    for head in range(heads):
        packed_ref[head, 3 * token_rows :] = share
    for place, copy in enumerate(copies):
        copy.wait()
        for head in range(heads):
            packed_ref[head, place * token_rows : (place + 1) * token_rows] = held[
                place, :, head * DH : (head + 1) * DH
            ]


def pack_heads(queries, key_tokens, value_tokens, latent, token_width):
    token_rows, width = queries.shape
    sections = lax.axis_size("sect")
    heads = width // DH // sections
    span = latent.shape[1] // sections + 2 * token_width
    extra = -(-latent.shape[0] * (span // DH) // 16) * 16
    hbm = pl.BlockSpec(memory_space=pltpu.HBM)
    vmem = pl.BlockSpec(memory_space=pltpu.VMEM)
    return pl.pallas_call(
        pack_body,
        in_specs=[hbm, hbm, hbm, vmem],
        out_specs=vmem,
        out_shape=jax.ShapeDtypeStruct((heads, 3 * token_rows + extra, DH), queries.dtype),
        scratch_shapes=[
            pltpu.VMEM((3, token_rows, heads * DH), queries.dtype),
            pltpu.SemaphoreType.DMA((3,)),
        ],
        compiler_params=pltpu.CompilerParams(vmem_limit_bytes=COPY_VMEM),
        name="pack_heads",
    )(*in_hbm(queries, key_tokens, value_tokens, latent))


def xor_pairs(distance):
    return [(i, i ^ distance) for i in range(lax.axis_size("seq"))]


def flat(array):
    return array.reshape(-1, array.shape[-1])


def attend_body(block, own_ref, other_ref, out_ref):
    members, token_rows, _ = out_ref.shape
    at_keys = slice(token_rows, 2 * token_rows)
    at_values = slice(2 * token_rows, 3 * token_rows)
    keys = jnp.concatenate([flat(own_ref[:, at_keys]), flat(other_ref[:, at_keys])], axis=0)
    values = jnp.concatenate([flat(own_ref[:, at_values]), flat(other_ref[:, at_values])], axis=0)

    def one_block(step):
        at = pl.ds(step * block, block)
        scores = lax.dot_general(
            flat(own_ref[at, :token_rows]),
            keys,
            (((1,), (1,)), ((), ())),
            preferred_element_type=jnp.float32,
        ) * (1.0 / math.sqrt(DH))
        exponents = jnp.exp(scores - jnp.max(scores, axis=1, keepdims=True))
        totals = jnp.sum(exponents, axis=1, keepdims=True)
        mixed = jnp.dot(
            exponents.astype(jnp.bfloat16), values, preferred_element_type=jnp.float32
        )
        out_ref[at] = (mixed / totals).astype(out_ref.dtype).reshape(block, token_rows, DH)

    if members <= 8:
        for step in range(members // block):
            one_block(step)
    else:
        pl.loop(0, members // block)(one_block)


def attend(own, other, token_rows):
    members = own.shape[0]
    total = members * token_rows
    vmem = pl.BlockSpec(memory_space=pltpu.VMEM)
    return pl.pallas_call(
        functools.partial(attend_body, min(4, members)),
        in_specs=[vmem, vmem],
        out_specs=vmem,
        out_shape=jax.ShapeDtypeStruct((members, token_rows, DH), own.dtype),
        compiler_params=pltpu.CompilerParams(vmem_limit_bytes=ATTEND_VMEM),
        cost_estimate=pl.CostEstimate(
            flops=8 * total * total * DH,
            bytes_accessed=7 * total * DH * 2,
            transcendentals=2 * total * total,
        ),
        name="attend",
    )(own, other)


def unpack_body(in_ref, out_ref, sems):
    copies = [
        pltpu.make_async_copy(
            in_ref.at[head], out_ref.at[:, pl.ds(head * DH, DH)], sems.at[head]
        )
        for head in range(in_ref.shape[0])
    ]
    for copy in copies:
        copy.start()
    for copy in copies:
        copy.wait()


def unpack_heads(array):
    heads, token_rows, _ = array.shape
    return pl.pallas_call(
        unpack_body,
        in_specs=[pl.BlockSpec(memory_space=pltpu.VMEM)],
        out_specs=pl.BlockSpec(memory_space=pltpu.HBM),
        out_shape=jax.ShapeDtypeStruct((token_rows, heads * DH), array.dtype),
        scratch_shapes=[pltpu.SemaphoreType.DMA((heads,))],
        compiler_params=pltpu.CompilerParams(vmem_limit_bytes=COPY_VMEM),
        name="unpack_heads",
    )(array)


def decode_body(
    grid_rows,
    width,
    share_rows,
    own_ref,
    other_ref,
    tile_ref,
    in_weight_hbm,
    in_bias_hbm,
    gain_hbm,
    mid_weight_hbm,
    mid_bias_hbm,
    out_ref,
    mid_weight,
    in_weight_ref,
    in_bias_ref,
    gain_ref,
    mid_bias_ref,
    taps,
    rows_held,
    patches,
    raw,
    hidden,
    activated,
    active,
    summed,
    weight_sems,
    small_sems,
):
    pairs = active.shape[1] // 16
    channels, features = in_weight_ref.shape[3:]
    columns = out_ref.shape[2]
    lane_tiles = features // 128
    position = lax.axis_index("seq")
    section = lax.axis_index("sect")
    small = [
        pltpu.make_async_copy(source, target, small_sems.at[place])
        for place, (source, target) in enumerate(
            (
                (in_weight_hbm, in_weight_ref),
                (in_bias_hbm, in_bias_ref),
                (gain_hbm, gain_ref),
                (mid_bias_hbm, mid_bias_ref),
            )
        )
    ]
    for copy in small:
        copy.start()

    def load(col_tap):
        return [
            pltpu.make_async_copy(
                mid_weight_hbm.at[tap, row_tap, col_tap],
                mid_weight.at[
                    col_tap,
                    pl.ds(row_tap * features, features),
                    pl.ds((2 - tap) * features, features),
                ],
                weight_sems.at[col_tap, row_tap, slot],
            )
            for row_tap in range(3)
            for slot, tap in enumerate(TAPS)
        ]

    for col_tap in range(3):
        for copy in load(col_tap):
            copy.start()

    filled = tile_ref[position]
    first_row = lax.fori_loop(0, position, lambda d, total: total + tile_ref[d], jnp.int32(0))

    members, message, _ = own_ref.shape
    chunks = rows_held.shape[1] // 128
    extra = -(-share_rows * chunks // 16) * 16
    for side, ref in enumerate((own_ref, other_ref)):
        for member in range(members):
            lines = ref[member, message - extra :].astype(jnp.float32)
            low = (side * members + member) * share_rows
            for chunk in range(chunks):
                rows_held[low : low + share_rows, chunk * 128 : (chunk + 1) * 128] = lines[
                    chunk * share_rows : (chunk + 1) * share_rows
                ]
    latent = rows_held[...]
    aside = pltpu.roll(latent, latent.shape[1] - RIM, 1).astype(jnp.bfloat16)
    latent = latent.astype(jnp.bfloat16)
    held_rows = latent.shape[0]
    unit = lax.broadcasted_iota(jnp.int32, (UNITS, held_rows), 0)
    held = lax.broadcasted_iota(jnp.int32, (UNITS, held_rows), 1)
    side = (held >= members * share_rows).astype(jnp.int32)
    member = held // share_rows - side * members
    held = (2 * member + ((position & 1) ^ side)) * share_rows + held % share_rows
    frame = sum((unit >= (k + 1) * REACH).astype(jnp.int32) for k in range(LF))
    reach = unit - frame * REACH
    selectors = []
    for tap in TAPS:
        for row_parity in range(2):
            for i in range(2):
                token_row = first_row + (reach >> 1) - 1 + i
                source = frame + tap - 2
                wanted = (
                    ((reach & 1) == row_parity)
                    & (token_row >= 0)
                    & (token_row < grid_rows)
                    & (source >= 0)
                    & (source < LF)
                )
                target = jnp.where(wanted, source * grid_rows + token_row, -1)
                selectors.append(jnp.where(held == target, 1.0, 0.0).astype(jnp.bfloat16))
    selector = jnp.concatenate(selectors, axis=0)
    even = jnp.dot(selector, latent, preferred_element_type=jnp.float32)
    odd = jnp.dot(selector, aside, preferred_element_type=jnp.float32)
    for chunk in range(chunks):
        lanes = slice(chunk * 128, (chunk + 1) * 128)
        for group in range(len(selectors)):
            rows = slice(group * UNITS, (group + 1) * UNITS)
            piece = jnp.concatenate([even[rows, lanes], odd[rows, lanes]], axis=0)
            patches[
                chunk * 2 * UNITS : (chunk + 1) * 2 * UNITS, group * 128 : (group + 1) * 128
            ] = piece.astype(jnp.bfloat16)

    for copy in small:
        copy.wait()
    nothing = jnp.zeros((channels, features), jnp.bfloat16)
    base = 0
    for tap in TAPS:
        for row_parity in range(2):
            for i, j, p, q in [
                (i, j, p, q) for i in range(2) for j in range(2) for p in range(2) for q in range(2)
            ]:
                for col_parity in range(2):
                    row_tap, col_tap = 2 * i + p - row_parity, 2 * j + q - col_parity
                    inside = 0 <= row_tap < 3 and 0 <= col_tap < 3
                    taps[base : base + channels, col_parity * features : (col_parity + 1) * features] = (
                        in_weight_ref[tap, row_tap, col_tap] if inside else nothing
                    )
                base += channels

    unit_row = lax.broadcasted_iota(jnp.int32, (UNITS, 1), 0)
    row_frame = sum((unit_row >= (k + 1) * REACH).astype(jnp.int32) for k in range(LF))
    pixel_row = 2 * first_row + unit_row - row_frame * REACH - 1
    row_inside = (pixel_row >= 0) & (pixel_row < 2 * grid_rows)
    in_bias = in_bias_ref[...].reshape(1, features)
    half_gain = gain_ref[...].reshape(1, features) * 0.5

    def first_layer(chunk):
        for corner in range(2):
            start = (chunk * 2 + corner) * UNITS
            for col_parity in range(2):
                value = (
                    raw[pl.ds(start, UNITS), col_parity * features : (col_parity + 1) * features]
                    + in_bias
                )
                value = value.astype(jnp.bfloat16).astype(jnp.float32)
                scale = lax.rsqrt(jnp.mean(value * value, axis=1, keepdims=True) + 1e-06)
                column = chunk * 4 + corner * 2 + col_parity
                pixel = section * columns + column - 1
                keep = row_inside & (pixel >= 0) & (pixel < width)
                half = value * jnp.where(keep, scale, 0.0) * half_gain
                result = half + half * jnp.tanh(half)
                at = pl.ds(column * UNITS, UNITS)
                for lane in range(lane_tiles):
                    lanes = slice(lane * 128, (lane + 1) * 128)
                    hidden[lane, at] = value[:, lanes]
                    activated[lane, at] = result[:, lanes]

    middle = (chunks + 1) // 2
    groups = ((0, middle), (middle, chunks))
    for low, high in groups:
        rows = slice(low * 2 * UNITS, high * 2 * UNITS)
        raw[rows] = jnp.dot(patches[rows], taps[...], preferred_element_type=jnp.float32)
    for low, high in groups:
        for chunk in range(low, high):
            first_layer(chunk)

    def pair_up(phase, pair):
        at = slice(pair * 16, pair * 16 + 16)
        for lane in range(lane_tiles):
            for field in range(LF):
                for row_tap in range(3):
                    start = (2 * pair + phase) * UNITS + field * REACH + row_tap
                    joined = jnp.concatenate(
                        [activated[lane, pl.ds(start + k * UNITS, ROWS)] for k in range(2)], axis=0
                    )
                    to_lane = (field * 3 + row_tap) * features + lane * 128
                    active[phase, at, to_lane : to_lane + 128] = joined.astype(jnp.bfloat16)

    rows = columns * ROWS
    depth = 3 * features

    def windows(low, high, lanes):
        return jnp.concatenate(
            [
                active[tap % 2, 16 * (tap // 2) + low : 16 * (tap // 2) + high, lanes]
                for tap in range(3)
            ],
            axis=1,
        )

    def weights(lanes):
        return jnp.concatenate([mid_weight[tap, :, lanes] for tap in range(3)], axis=0)

    mid_bias = mid_bias_ref[...].reshape(1, features)

    def finish(field):
        for row in range(ROWS):
            for lane in range(lane_tiles):
                lanes = slice(lane * 128, (lane + 1) * 128)
                skip = hidden[lane, pl.ds(UNITS + field * REACH + 1 + row, columns, stride=UNITS), :]
                value = summed[field, lane, pl.ds(row, columns, stride=ROWS), :]
                value = value + skip + mid_bias[:, lanes]
                value = jnp.where(row < 2 * filled, value, 0.0)
                out_ref[field, row, :, lanes] = value.astype(jnp.bfloat16)

    for phase in range(2):
        for pair in range(pairs - phase):
            pair_up(phase, pair)
    for tap in range(3):
        for copy in load(tap):
            copy.wait()
    early = windows(0, rows, slice(0, depth))
    late = windows(0, rows, slice(depth, 2 * depth))
    for left in range(0, 2 * features, 256):
        block = jnp.dot(
            early, weights(slice(left, left + 256)), preferred_element_type=jnp.float32
        )
        for lane in range(2):
            field, tile = divmod(left // 128 + lane, lane_tiles)
            summed[field, tile] = block[:, lane * 128 : (lane + 1) * 128]
    for left in range(0, features, 256):
        right = min(left + 256, features)
        block = jnp.dot(late, weights(slice(left, right)), preferred_element_type=jnp.float32)
        for lane in range((right - left) // 128):
            tile = left // 128 + lane
            summed[1, tile] = summed[1, tile] + block[:, lane * 128 : (lane + 1) * 128]
    for field in range(LF):
        finish(field)


def decode_tile(
    own,
    other,
    share_rows,
    grid_rows,
    width,
    tile_rows,
    conv_in_weight,
    conv_in_bias,
    norm_gain,
    conv_mid_weight,
    conv_mid_bias,
):
    sections = lax.axis_size("sect")
    channels, features = conv_in_weight.shape[3:]
    token_width = 4 * channels
    columns = width // sections
    span = columns // 2
    pairs = span + 1
    chunks = (span + 2) * token_width // 128
    lane_tiles = features // 128
    vmem = pl.BlockSpec(memory_space=pltpu.VMEM)
    hbm = pl.BlockSpec(memory_space=pltpu.HBM)
    slots = len(TAPS)
    depth = slots * 2 * 4 * token_width
    held = chunks * 4 * UNITS
    return pl.pallas_call(
        functools.partial(decode_body, grid_rows, width, share_rows),
        in_specs=[vmem, vmem, pl.BlockSpec(memory_space=pltpu.SMEM)] + [hbm] * 5,
        out_specs=vmem,
        out_shape=jax.ShapeDtypeStruct((LF, ROWS, columns, features), jnp.bfloat16),
        scratch_shapes=[
            pltpu.VMEM((3, 3 * features, slots * features), jnp.bfloat16),
            pltpu.VMEM(conv_in_weight.shape, jnp.bfloat16),
            pltpu.VMEM(conv_in_bias.shape, jnp.float32),
            pltpu.VMEM(norm_gain.shape, jnp.float32),
            pltpu.VMEM(conv_mid_bias.shape, jnp.float32),
            pltpu.VMEM((depth, 2 * features), jnp.bfloat16),
            pltpu.VMEM((2 * own.shape[0] * share_rows, chunks * 128), jnp.float32),
            pltpu.VMEM((chunks * 2 * UNITS, depth), jnp.bfloat16),
            pltpu.VMEM((chunks * 2 * UNITS, 2 * features), jnp.float32),
            pltpu.VMEM((lane_tiles, held, 128), jnp.float32),
            pltpu.VMEM((lane_tiles, held, 128), jnp.float32),
            pltpu.VMEM((2, pairs * 16, LF * 3 * features), jnp.bfloat16),
            pltpu.VMEM((LF, lane_tiles, columns * ROWS, 128), jnp.float32),
            pltpu.SemaphoreType.DMA((3, 3, slots)),
            pltpu.SemaphoreType.DMA((4,)),
        ],
        compiler_params=pltpu.CompilerParams(vmem_limit_bytes=DECODE_VMEM),
        cost_estimate=pl.CostEstimate(
            flops=2 * 3 * 9 * columns * ROWS * features * features,
            bytes_accessed=slots * 9 * features * features * 2,
            transcendentals=held * features,
        ),
        name="decode_tile",
    )(
        own,
        other,
        *in_hbm(
            tile_rows, conv_in_weight, conv_in_bias, norm_gain, conv_mid_weight, conv_mid_bias
        ),
    )


def on_device(
    queries,
    key_tokens,
    value_tokens,
    latent,
    tile_rows,
    conv_in_weight,
    conv_in_bias,
    norm_gain,
    conv_mid_weight,
    conv_mid_bias,
):
    devices = lax.axis_size("seq")
    groups = parity_groups(devices)
    grid_rows = latent.shape[0] * devices // LF
    token_width = 4 * conv_in_weight.shape[3]
    packed = pack_heads(queries, key_tokens, value_tokens, latent, token_width)
    own = lax.all_to_all(packed, "seq", 0, 0, axis_index_groups=groups, tiled=True)
    other = lax.ppermute(own, "seq", xor_pairs(1))
    mixed = attend(own, other, queries.shape[0])
    returned = lax.all_to_all(mixed, "seq", 0, 0, axis_index_groups=groups, tiled=True)
    frames = decode_tile(
        own,
        other,
        latent.shape[0],
        grid_rows,
        2 * latent.shape[1] // token_width,
        tile_rows,
        conv_in_weight,
        conv_in_bias,
        norm_gain,
        conv_mid_weight,
        conv_mid_bias,
    )
    return (unpack_heads(returned), frames)


def solution(mesh):
    in_specs = (
        P("seq", None),
        P("seq", None),
        P("seq", None),
        P("seq", None),
        P(),
        P(),
        P(),
        P(),
        P(),
        P(),
    )
    out_specs = (P("seq", "sect"), P(None, "seq", "sect", None))
    return jax.shard_map(
        on_device, mesh=mesh, in_specs=in_specs, out_specs=out_specs, check_vma=False
    )
```

```python
import functools
import math

import jax
import jax.numpy as jnp
from jax import lax
from jax.experimental import pallas as pl
from jax.experimental.pallas import tpu as pltpu
from jax.sharding import PartitionSpec as P

DH = 128
LF = 2
MAXT = 4
RIM = 64
TAPS = (1, 2)
ROWS = 2 * MAXT
REACH = ROWS + 2
UNITS = -(-LF * REACH // 8) * 8
DECODE_VMEM = 32 * 1024 * 1024
ATTEND_VMEM = 32 * 1024 * 1024
COPY_VMEM = 16 * 1024 * 1024


def parity_groups(devices):
    return [list(range(parity, devices, 2)) for parity in range(2)]


def in_hbm(*arrays):
    return [pltpu.with_memory_space_constraint(array, pltpu.HBM) for array in arrays]


def pack_body(query_ref, key_ref, value_ref, latent_ref, packed_ref, held, sems):
    heads = packed_ref.shape[0]
    token_rows = query_ref.shape[0]
    section = lax.axis_index("sect")
    wide_columns = pl.ds(pl.multiple_of(section * heads * DH, DH), heads * DH)
    copies = [
        pltpu.make_async_copy(ref.at[:, wide_columns], held.at[place], sems.at[place])
        for place, ref in enumerate((query_ref, key_ref, value_ref))
    ]
    for copy in copies:
        copy.start()
    rows, width = latent_ref.shape
    half, rim = width // 2, RIM
    wide = latent_ref[...].astype(jnp.float32)
    rim_zeros = jnp.zeros((rows, rim), jnp.float32)
    lower = jnp.concatenate([rim_zeros, wide[:, : half + rim]], axis=1)
    upper = jnp.concatenate([wide[:, half - rim :], rim_zeros], axis=1)
    share = jnp.where(section == 0, lower, upper)
    chunks = share.shape[1] // DH
    lines = [share[:, chunk * DH : (chunk + 1) * DH] for chunk in range(chunks)]
    spare = packed_ref.shape[1] - 3 * token_rows - chunks * rows
    lines.append(jnp.zeros((spare, DH), jnp.float32))
    share = jnp.concatenate(lines, axis=0).astype(packed_ref.dtype)
    for head in range(heads):
        packed_ref[head, 3 * token_rows :] = share
    for place, copy in enumerate(copies):
        copy.wait()
        for head in range(heads):
            packed_ref[head, place * token_rows : (place + 1) * token_rows] = held[
                place, :, head * DH : (head + 1) * DH
            ]


def pack_heads(queries, key_tokens, value_tokens, latent, token_width):
    token_rows, width = queries.shape
    sections = lax.axis_size("sect")
    heads = width // DH // sections
    span = latent.shape[1] // sections + 2 * token_width
    extra = -(-latent.shape[0] * (span // DH) // 16) * 16
    hbm = pl.BlockSpec(memory_space=pltpu.HBM)
    vmem = pl.BlockSpec(memory_space=pltpu.VMEM)
    return pl.pallas_call(
        pack_body,
        in_specs=[hbm, hbm, hbm, vmem],
        out_specs=vmem,
        out_shape=jax.ShapeDtypeStruct((heads, 3 * token_rows + extra, DH), queries.dtype),
        scratch_shapes=[
            pltpu.VMEM((3, token_rows, heads * DH), queries.dtype),
            pltpu.SemaphoreType.DMA((3,)),
        ],
        compiler_params=pltpu.CompilerParams(vmem_limit_bytes=COPY_VMEM),
        name="pack_heads",
    )(*in_hbm(queries, key_tokens, value_tokens, latent))


def xor_pairs(distance):
    return [(i, i ^ distance) for i in range(lax.axis_size("seq"))]


def flat(array):
    return array.reshape(-1, array.shape[-1])


def attend_body(block, own_ref, other_ref, out_ref):
    members, token_rows, _ = out_ref.shape
    at_keys = slice(token_rows, 2 * token_rows)
    at_values = slice(2 * token_rows, 3 * token_rows)
    keys = jnp.concatenate([flat(own_ref[:, at_keys]), flat(other_ref[:, at_keys])], axis=0)
    values = jnp.concatenate([flat(own_ref[:, at_values]), flat(other_ref[:, at_values])], axis=0)

    def one_block(step):
        at = pl.ds(step * block, block)
        scores = lax.dot_general(
            flat(own_ref[at, :token_rows]),
            keys,
            (((1,), (1,)), ((), ())),
            preferred_element_type=jnp.float32,
        ) * (1.0 / math.sqrt(DH))
        exponents = jnp.exp(scores - jnp.max(scores, axis=1, keepdims=True))
        totals = jnp.sum(exponents, axis=1, keepdims=True)
        mixed = jnp.dot(
            exponents.astype(jnp.bfloat16), values, preferred_element_type=jnp.float32
        )
        out_ref[at] = (mixed / totals).astype(out_ref.dtype).reshape(block, token_rows, DH)

    if members <= 8:
        for step in range(members // block):
            one_block(step)
    else:
        pl.loop(0, members // block)(one_block)


def attend(own, other, token_rows):
    members = own.shape[0]
    total = members * token_rows
    vmem = pl.BlockSpec(memory_space=pltpu.VMEM)
    return pl.pallas_call(
        functools.partial(attend_body, min(4, members)),
        in_specs=[vmem, vmem],
        out_specs=vmem,
        out_shape=jax.ShapeDtypeStruct((members, token_rows, DH), own.dtype),
        compiler_params=pltpu.CompilerParams(vmem_limit_bytes=ATTEND_VMEM),
        cost_estimate=pl.CostEstimate(
            flops=8 * total * total * DH,
            bytes_accessed=7 * total * DH * 2,
            transcendentals=2 * total * total,
        ),
        name="attend",
    )(own, other)


def unpack_body(in_ref, out_ref, sems):
    copies = [
        pltpu.make_async_copy(
            in_ref.at[head], out_ref.at[:, pl.ds(head * DH, DH)], sems.at[head]
        )
        for head in range(in_ref.shape[0])
    ]
    for copy in copies:
        copy.start()
    for copy in copies:
        copy.wait()


def unpack_heads(array):
    heads, token_rows, _ = array.shape
    return pl.pallas_call(
        unpack_body,
        in_specs=[pl.BlockSpec(memory_space=pltpu.VMEM)],
        out_specs=pl.BlockSpec(memory_space=pltpu.HBM),
        out_shape=jax.ShapeDtypeStruct((token_rows, heads * DH), array.dtype),
        scratch_shapes=[pltpu.SemaphoreType.DMA((heads,))],
        compiler_params=pltpu.CompilerParams(vmem_limit_bytes=COPY_VMEM),
        name="unpack_heads",
    )(array)


def decode_body(
    grid_rows,
    width,
    share_rows,
    own_ref,
    other_ref,
    tile_ref,
    in_weight_hbm,
    in_bias_hbm,
    gain_hbm,
    mid_weight_hbm,
    mid_bias_hbm,
    out_ref,
    mid_weight,
    in_weight_ref,
    in_bias_ref,
    gain_ref,
    mid_bias_ref,
    taps,
    rows_held,
    patches,
    raw,
    hidden,
    activated,
    active,
    summed,
    weight_sems,
    small_sems,
):
    pairs = active.shape[1] // 16
    channels, features = in_weight_ref.shape[3:]
    columns = out_ref.shape[2]
    lane_tiles = features // 128
    position = lax.axis_index("seq")
    section = lax.axis_index("sect")
    small = [
        pltpu.make_async_copy(source, target, small_sems.at[place])
        for place, (source, target) in enumerate(
            (
                (in_weight_hbm, in_weight_ref),
                (in_bias_hbm, in_bias_ref),
                (gain_hbm, gain_ref),
                (mid_bias_hbm, mid_bias_ref),
            )
        )
    ]
    for copy in small:
        copy.start()

    def load(col_tap):
        return [
            pltpu.make_async_copy(
                mid_weight_hbm.at[tap, row_tap, col_tap],
                mid_weight.at[
                    col_tap,
                    pl.ds(row_tap * features, features),
                    pl.ds((2 - tap) * features, features),
                ],
                weight_sems.at[col_tap, row_tap, slot],
            )
            for row_tap in range(3)
            for slot, tap in enumerate(TAPS)
        ]

    for col_tap in (0, 2, 1):
        for copy in load(col_tap):
            copy.start()

    filled = tile_ref[position]
    first_row = lax.fori_loop(0, position, lambda d, total: total + tile_ref[d], jnp.int32(0))

    members, message, _ = own_ref.shape
    chunks = rows_held.shape[1] // 128
    extra = -(-share_rows * chunks // 16) * 16
    for side, ref in enumerate((own_ref, other_ref)):
        for member in range(members):
            lines = ref[member, message - extra :].astype(jnp.float32)
            low = (side * members + member) * share_rows
            for chunk in range(chunks):
                rows_held[low : low + share_rows, chunk * 128 : (chunk + 1) * 128] = lines[
                    chunk * share_rows : (chunk + 1) * share_rows
                ]
    latent = rows_held[...]
    aside = pltpu.roll(latent, latent.shape[1] - RIM, 1).astype(jnp.bfloat16)
    latent = latent.astype(jnp.bfloat16)
    held_rows = latent.shape[0]
    unit = lax.broadcasted_iota(jnp.int32, (UNITS, held_rows), 0)
    held = lax.broadcasted_iota(jnp.int32, (UNITS, held_rows), 1)
    side = (held >= members * share_rows).astype(jnp.int32)
    member = held // share_rows - side * members
    held = (2 * member + ((position & 1) ^ side)) * share_rows + held % share_rows
    frame = sum((unit >= (k + 1) * REACH).astype(jnp.int32) for k in range(LF))
    reach = unit - frame * REACH
    selectors = []
    for tap in TAPS:
        for row_parity in range(2):
            for i in range(2):
                token_row = first_row + (reach >> 1) - 1 + i
                source = frame + tap - 2
                wanted = (
                    ((reach & 1) == row_parity)
                    & (token_row >= 0)
                    & (token_row < grid_rows)
                    & (source >= 0)
                    & (source < LF)
                )
                target = jnp.where(wanted, source * grid_rows + token_row, -1)
                selectors.append(jnp.where(held == target, 1.0, 0.0).astype(jnp.bfloat16))
    selector = jnp.concatenate(selectors, axis=0)
    even = jnp.dot(selector, latent, preferred_element_type=jnp.float32)
    odd = jnp.dot(selector, aside, preferred_element_type=jnp.float32)
    for chunk in range(chunks):
        lanes = slice(chunk * 128, (chunk + 1) * 128)
        for group in range(len(selectors)):
            rows = slice(group * UNITS, (group + 1) * UNITS)
            piece = jnp.concatenate([even[rows, lanes], odd[rows, lanes]], axis=0)
            patches[
                chunk * 2 * UNITS : (chunk + 1) * 2 * UNITS, group * 128 : (group + 1) * 128
            ] = piece.astype(jnp.bfloat16)

    for copy in small:
        copy.wait()
    nothing = jnp.zeros((channels, features), jnp.bfloat16)
    base = 0
    for tap in TAPS:
        for row_parity in range(2):
            for i, j, p, q in [
                (i, j, p, q) for i in range(2) for j in range(2) for p in range(2) for q in range(2)
            ]:
                for col_parity in range(2):
                    row_tap, col_tap = 2 * i + p - row_parity, 2 * j + q - col_parity
                    inside = 0 <= row_tap < 3 and 0 <= col_tap < 3
                    taps[base : base + channels, col_parity * features : (col_parity + 1) * features] = (
                        in_weight_ref[tap, row_tap, col_tap] if inside else nothing
                    )
                base += channels

    unit_row = lax.broadcasted_iota(jnp.int32, (UNITS, 1), 0)
    row_frame = sum((unit_row >= (k + 1) * REACH).astype(jnp.int32) for k in range(LF))
    pixel_row = 2 * first_row + unit_row - row_frame * REACH - 1
    row_inside = (pixel_row >= 0) & (pixel_row < 2 * grid_rows)
    in_bias = in_bias_ref[...].reshape(1, features)
    half_gain = gain_ref[...].reshape(1, features) * 0.5

    def first_layer(chunk):
        for corner in range(2):
            start = (chunk * 2 + corner) * UNITS
            for col_parity in range(2):
                value = (
                    raw[pl.ds(start, UNITS), col_parity * features : (col_parity + 1) * features]
                    + in_bias
                )
                value = value.astype(jnp.bfloat16).astype(jnp.float32)
                scale = lax.rsqrt(jnp.mean(value * value, axis=1, keepdims=True) + 1e-06)
                column = chunk * 4 + corner * 2 + col_parity
                pixel = section * columns + column - 1
                keep = row_inside & (pixel >= 0) & (pixel < width)
                half = value * jnp.where(keep, scale, 0.0) * half_gain
                result = half + half * jnp.tanh(half)
                at = pl.ds(column * UNITS, UNITS)
                for lane in range(lane_tiles):
                    lanes = slice(lane * 128, (lane + 1) * 128)
                    hidden[lane, at] = value[:, lanes]
                    activated[lane, at] = result[:, lanes]

    middle = (chunks + 1) // 2
    groups = ((0, middle), (middle, chunks))
    for low, high in groups:
        rows = slice(low * 2 * UNITS, high * 2 * UNITS)
        raw[rows] = jnp.dot(patches[rows], taps[...], preferred_element_type=jnp.float32)
    for low, high in groups:
        for chunk in range(low, high):
            first_layer(chunk)

    def pair_up(phase, pair):
        at = slice(pair * 16, pair * 16 + 16)
        for lane in range(lane_tiles):
            for field in range(LF):
                for row_tap in range(3):
                    start = (2 * pair + phase) * UNITS + field * REACH + row_tap
                    joined = jnp.concatenate(
                        [activated[lane, pl.ds(start + k * UNITS, ROWS)] for k in range(2)], axis=0
                    )
                    to_lane = (field * 3 + row_tap) * features + lane * 128
                    active[phase, at, to_lane : to_lane + 128] = joined.astype(jnp.bfloat16)

    rows = columns * ROWS
    depth = 3 * features

    mid_bias = mid_bias_ref[...].reshape(1, features)

    def finish(field):
        for row in range(ROWS):
            for lane in range(lane_tiles):
                lanes = slice(lane * 128, (lane + 1) * 128)
                skip = hidden[lane, pl.ds(UNITS + field * REACH + 1 + row, columns, stride=UNITS), :]
                value = summed[field, lane, pl.ds(row, columns, stride=ROWS), :]
                value = value + skip + mid_bias[:, lanes]
                value = jnp.where(row < 2 * filled, value, 0.0)
                out_ref[field, row, :, lanes] = value.astype(jnp.bfloat16)

    for place, tap in enumerate((0, 2, 1)):
        if place != 1:
            phase = tap % 2
            for pair in range(pairs - phase):
                pair_up(phase, pair)
        for copy in load(tap):
            copy.wait()
        low = 16 * (tap // 2)
        early = active[tap % 2, low : low + rows, :depth]
        late = active[tap % 2, low : low + rows, depth:]
        for left in range(0, 2 * features, 256):
            block = jnp.dot(
                early, mid_weight[tap, :, left : left + 256], preferred_element_type=jnp.float32
            )
            for lane in range(2):
                field, tile = divmod(left // 128 + lane, lane_tiles)
                value = block[:, lane * 128 : (lane + 1) * 128]
                summed[field, tile] = summed[field, tile] + value if place else value
        for left in range(0, features, 256):
            right = min(left + 256, features)
            block = jnp.dot(
                late, mid_weight[tap, :, left:right], preferred_element_type=jnp.float32
            )
            for lane in range((right - left) // 128):
                tile = left // 128 + lane
                summed[1, tile] = summed[1, tile] + block[:, lane * 128 : (lane + 1) * 128]
    for field in range(LF):
        finish(field)


def decode_tile(
    own,
    other,
    share_rows,
    grid_rows,
    width,
    tile_rows,
    conv_in_weight,
    conv_in_bias,
    norm_gain,
    conv_mid_weight,
    conv_mid_bias,
):
    sections = lax.axis_size("sect")
    channels, features = conv_in_weight.shape[3:]
    token_width = 4 * channels
    columns = width // sections
    span = columns // 2
    pairs = span + 1
    chunks = (span + 2) * token_width // 128
    lane_tiles = features // 128
    vmem = pl.BlockSpec(memory_space=pltpu.VMEM)
    hbm = pl.BlockSpec(memory_space=pltpu.HBM)
    slots = len(TAPS)
    depth = slots * 2 * 4 * token_width
    held = chunks * 4 * UNITS
    return pl.pallas_call(
        functools.partial(decode_body, grid_rows, width, share_rows),
        in_specs=[vmem, vmem, pl.BlockSpec(memory_space=pltpu.SMEM)] + [hbm] * 5,
        out_specs=vmem,
        out_shape=jax.ShapeDtypeStruct((LF, ROWS, columns, features), jnp.bfloat16),
        scratch_shapes=[
            pltpu.VMEM((3, 3 * features, slots * features), jnp.bfloat16),
            pltpu.VMEM(conv_in_weight.shape, jnp.bfloat16),
            pltpu.VMEM(conv_in_bias.shape, jnp.float32),
            pltpu.VMEM(norm_gain.shape, jnp.float32),
            pltpu.VMEM(conv_mid_bias.shape, jnp.float32),
            pltpu.VMEM((depth, 2 * features), jnp.bfloat16),
            pltpu.VMEM((2 * own.shape[0] * share_rows, chunks * 128), jnp.float32),
            pltpu.VMEM((chunks * 2 * UNITS, depth), jnp.bfloat16),
            pltpu.VMEM((chunks * 2 * UNITS, 2 * features), jnp.float32),
            pltpu.VMEM((lane_tiles, held, 128), jnp.float32),
            pltpu.VMEM((lane_tiles, held, 128), jnp.float32),
            pltpu.VMEM((2, pairs * 16, LF * 3 * features), jnp.bfloat16),
            pltpu.VMEM((LF, lane_tiles, columns * ROWS, 128), jnp.float32),
            pltpu.SemaphoreType.DMA((3, 3, slots)),
            pltpu.SemaphoreType.DMA((4,)),
        ],
        compiler_params=pltpu.CompilerParams(vmem_limit_bytes=DECODE_VMEM),
        cost_estimate=pl.CostEstimate(
            flops=2 * 3 * 9 * columns * ROWS * features * features,
            bytes_accessed=slots * 9 * features * features * 2,
            transcendentals=held * features,
        ),
        name="decode_tile",
    )(
        own,
        other,
        *in_hbm(
            tile_rows, conv_in_weight, conv_in_bias, norm_gain, conv_mid_weight, conv_mid_bias
        ),
    )


def on_device(
    queries,
    key_tokens,
    value_tokens,
    latent,
    tile_rows,
    conv_in_weight,
    conv_in_bias,
    norm_gain,
    conv_mid_weight,
    conv_mid_bias,
):
    devices = lax.axis_size("seq")
    groups = parity_groups(devices)
    grid_rows = latent.shape[0] * devices // LF
    token_width = 4 * conv_in_weight.shape[3]
    packed = pack_heads(queries, key_tokens, value_tokens, latent, token_width)
    own = lax.all_to_all(packed, "seq", 0, 0, axis_index_groups=groups, tiled=True)
    other = lax.ppermute(own, "seq", xor_pairs(1))
    mixed = attend(own, other, queries.shape[0])
    returned = lax.all_to_all(mixed, "seq", 0, 0, axis_index_groups=groups, tiled=True)
    frames = decode_tile(
        own,
        other,
        latent.shape[0],
        grid_rows,
        2 * latent.shape[1] // token_width,
        tile_rows,
        conv_in_weight,
        conv_in_bias,
        norm_gain,
        conv_mid_weight,
        conv_mid_bias,
    )
    return (unpack_heads(returned), frames)


def solution(mesh):
    in_specs = (
        P("seq", None),
        P("seq", None),
        P("seq", None),
        P("seq", None),
        P(),
        P(),
        P(),
        P(),
        P(),
        P(),
    )
    out_specs = (P("seq", "sect"), P(None, "seq", "sect", None))
    return jax.shard_map(
        on_device, mesh=mesh, in_specs=in_specs, out_specs=out_specs, check_vma=False
    )
```

```python
import functools
import math

import jax
import jax.numpy as jnp
from jax import lax
from jax.experimental import pallas as pl
from jax.experimental.pallas import tpu as pltpu
from jax.sharding import PartitionSpec as P

DH = 128
LF = 2
MAXT = 4
RIM = 64
TAPS = (1, 2)
ROWS = 2 * MAXT
REACH = ROWS + 2
UNITS = -(-LF * REACH // 8) * 8
DECODE_VMEM = 32 * 1024 * 1024
ATTEND_VMEM = 32 * 1024 * 1024
COPY_VMEM = 16 * 1024 * 1024


def parity_groups(devices):
    return [list(range(parity, devices, 2)) for parity in range(2)]


def in_hbm(*arrays):
    return [pltpu.with_memory_space_constraint(array, pltpu.HBM) for array in arrays]


def pack_body(query_ref, key_ref, value_ref, latent_ref, packed_ref, held, sems):
    heads = packed_ref.shape[0]
    token_rows = query_ref.shape[0]
    section = lax.axis_index("sect")
    wide_columns = pl.ds(pl.multiple_of(section * heads * DH, DH), heads * DH)
    copies = [
        pltpu.make_async_copy(ref.at[:, wide_columns], held.at[place], sems.at[place])
        for place, ref in enumerate((query_ref, key_ref, value_ref))
    ]
    for copy in copies:
        copy.start()
    rows, width = latent_ref.shape
    half, rim = width // 2, RIM
    wide = latent_ref[...].astype(jnp.float32)
    rim_zeros = jnp.zeros((rows, rim), jnp.float32)
    lower = jnp.concatenate([rim_zeros, wide[:, : half + rim]], axis=1)
    upper = jnp.concatenate([wide[:, half - rim :], rim_zeros], axis=1)
    share = jnp.where(section == 0, lower, upper)
    chunks = share.shape[1] // DH
    lines = [share[:, chunk * DH : (chunk + 1) * DH] for chunk in range(chunks)]
    spare = packed_ref.shape[1] - 3 * token_rows - chunks * rows
    lines.append(jnp.zeros((spare, DH), jnp.float32))
    share = jnp.concatenate(lines, axis=0).astype(packed_ref.dtype)
    for head in range(heads):
        packed_ref[head, 3 * token_rows :] = share
    for place, copy in enumerate(copies):
        copy.wait()
        for head in range(heads):
            packed_ref[head, place * token_rows : (place + 1) * token_rows] = held[
                place, :, head * DH : (head + 1) * DH
            ]


def pack_heads(queries, key_tokens, value_tokens, latent, token_width):
    token_rows, width = queries.shape
    sections = lax.axis_size("sect")
    heads = width // DH // sections
    span = latent.shape[1] // sections + 2 * token_width
    extra = -(-latent.shape[0] * (span // DH) // 16) * 16
    hbm = pl.BlockSpec(memory_space=pltpu.HBM)
    vmem = pl.BlockSpec(memory_space=pltpu.VMEM)
    return pl.pallas_call(
        pack_body,
        in_specs=[hbm, hbm, hbm, vmem],
        out_specs=vmem,
        out_shape=jax.ShapeDtypeStruct((heads, 3 * token_rows + extra, DH), queries.dtype),
        scratch_shapes=[
            pltpu.VMEM((3, token_rows, heads * DH), queries.dtype),
            pltpu.SemaphoreType.DMA((3,)),
        ],
        compiler_params=pltpu.CompilerParams(vmem_limit_bytes=COPY_VMEM),
        name="pack_heads",
    )(*in_hbm(queries, key_tokens, value_tokens, latent))


def xor_pairs(distance):
    return [(i, i ^ distance) for i in range(lax.axis_size("seq"))]


def flat(array):
    return array.reshape(-1, array.shape[-1])


def attend_body(block, own_ref, other_ref, out_ref):
    members, token_rows, _ = out_ref.shape
    at_keys = slice(token_rows, 2 * token_rows)
    at_values = slice(2 * token_rows, 3 * token_rows)
    keys = jnp.concatenate([flat(own_ref[:, at_keys]), flat(other_ref[:, at_keys])], axis=0)
    values = jnp.concatenate([flat(own_ref[:, at_values]), flat(other_ref[:, at_values])], axis=0)

    def one_block(step):
        at = pl.ds(step * block, block)
        scores = lax.dot_general(
            flat(own_ref[at, :token_rows]),
            keys,
            (((1,), (1,)), ((), ())),
            preferred_element_type=jnp.float32,
        ) * (1.0 / math.sqrt(DH))
        exponents = jnp.exp(scores - jnp.max(scores, axis=1, keepdims=True))
        totals = jnp.sum(exponents, axis=1, keepdims=True)
        mixed = jnp.dot(
            exponents.astype(jnp.bfloat16), values, preferred_element_type=jnp.float32
        )
        out_ref[at] = (mixed / totals).astype(out_ref.dtype).reshape(block, token_rows, DH)

    if members <= 8:
        for step in range(members // block):
            one_block(step)
    else:
        pl.loop(0, members // block)(one_block)


def attend(own, other, token_rows):
    members = own.shape[0]
    total = members * token_rows
    vmem = pl.BlockSpec(memory_space=pltpu.VMEM)
    return pl.pallas_call(
        functools.partial(attend_body, min(4, members)),
        in_specs=[vmem, vmem],
        out_specs=vmem,
        out_shape=jax.ShapeDtypeStruct((members, token_rows, DH), own.dtype),
        compiler_params=pltpu.CompilerParams(vmem_limit_bytes=ATTEND_VMEM),
        cost_estimate=pl.CostEstimate(
            flops=8 * total * total * DH,
            bytes_accessed=7 * total * DH * 2,
            transcendentals=2 * total * total,
        ),
        name="attend",
    )(own, other)


def unpack_body(in_ref, out_ref, sems):
    copies = [
        pltpu.make_async_copy(
            in_ref.at[head], out_ref.at[:, pl.ds(head * DH, DH)], sems.at[head]
        )
        for head in range(in_ref.shape[0])
    ]
    for copy in copies:
        copy.start()
    for copy in copies:
        copy.wait()


def unpack_heads(array):
    heads, token_rows, _ = array.shape
    return pl.pallas_call(
        unpack_body,
        in_specs=[pl.BlockSpec(memory_space=pltpu.VMEM)],
        out_specs=pl.BlockSpec(memory_space=pltpu.HBM),
        out_shape=jax.ShapeDtypeStruct((token_rows, heads * DH), array.dtype),
        scratch_shapes=[pltpu.SemaphoreType.DMA((heads,))],
        compiler_params=pltpu.CompilerParams(vmem_limit_bytes=COPY_VMEM),
        name="unpack_heads",
    )(array)


def decode_body(
    grid_rows,
    width,
    share_rows,
    own_ref,
    other_ref,
    tile_ref,
    in_weight_hbm,
    in_bias_hbm,
    gain_hbm,
    mid_weight_hbm,
    mid_bias_hbm,
    out_ref,
    mid_weight,
    in_weight_ref,
    in_bias_ref,
    gain_ref,
    mid_bias_ref,
    taps,
    rows_held,
    patches,
    raw,
    hidden,
    activated,
    active,
    summed,
    weight_sems,
    small_sems,
):
    pairs = active.shape[1] // 16
    channels, features = in_weight_ref.shape[3:]
    columns = out_ref.shape[2]
    lane_tiles = features // 128
    position = lax.axis_index("seq")
    section = lax.axis_index("sect")
    small = [
        pltpu.make_async_copy(source, target, small_sems.at[place])
        for place, (source, target) in enumerate(
            (
                (in_weight_hbm, in_weight_ref),
                (in_bias_hbm, in_bias_ref),
                (gain_hbm, gain_ref),
                (mid_bias_hbm, mid_bias_ref),
            )
        )
    ]
    for copy in small:
        copy.start()

    def load(col_tap):
        return [
            pltpu.make_async_copy(
                mid_weight_hbm.at[tap, row_tap, col_tap],
                mid_weight.at[
                    col_tap,
                    pl.ds(row_tap * features, features),
                    pl.ds((2 - tap) * features, features),
                ],
                weight_sems.at[col_tap, row_tap, slot],
            )
            for row_tap in range(3)
            for slot, tap in enumerate(TAPS)
        ]

    for col_tap in range(3):
        for copy in load(col_tap):
            copy.start()

    filled = tile_ref[position]
    first_row = lax.fori_loop(0, position, lambda d, total: total + tile_ref[d], jnp.int32(0))

    members, message, _ = own_ref.shape
    chunks = rows_held.shape[1] // 128
    extra = -(-share_rows * chunks // 16) * 16
    for side, ref in enumerate((own_ref, other_ref)):
        for member in range(members):
            lines = ref[member, message - extra :].astype(jnp.float32)
            low = (side * members + member) * share_rows
            for chunk in range(chunks):
                rows_held[low : low + share_rows, chunk * 128 : (chunk + 1) * 128] = lines[
                    chunk * share_rows : (chunk + 1) * share_rows
                ]
    latent = rows_held[...]
    aside = pltpu.roll(latent, latent.shape[1] - RIM, 1).astype(jnp.bfloat16)
    latent = latent.astype(jnp.bfloat16)
    held_rows = latent.shape[0]
    unit = lax.broadcasted_iota(jnp.int32, (UNITS, held_rows), 0)
    held = lax.broadcasted_iota(jnp.int32, (UNITS, held_rows), 1)
    side = (held >= members * share_rows).astype(jnp.int32)
    member = held // share_rows - side * members
    held = (2 * member + ((position & 1) ^ side)) * share_rows + held % share_rows
    frame = sum((unit >= (k + 1) * REACH).astype(jnp.int32) for k in range(LF))
    reach = unit - frame * REACH
    selectors = []
    for tap in TAPS:
        for row_parity in range(2):
            for i in range(2):
                token_row = first_row + (reach >> 1) - 1 + i
                source = frame + tap - 2
                wanted = (
                    ((reach & 1) == row_parity)
                    & (token_row >= 0)
                    & (token_row < grid_rows)
                    & (source >= 0)
                    & (source < LF)
                )
                target = jnp.where(wanted, source * grid_rows + token_row, -1)
                selectors.append(jnp.where(held == target, 1.0, 0.0).astype(jnp.bfloat16))
    selector = jnp.concatenate(selectors, axis=0)
    even = jnp.dot(selector, latent, preferred_element_type=jnp.float32)
    odd = jnp.dot(selector, aside, preferred_element_type=jnp.float32)
    for chunk in range(chunks):
        lanes = slice(chunk * 128, (chunk + 1) * 128)
        for group in range(len(selectors)):
            rows = slice(group * UNITS, (group + 1) * UNITS)
            piece = jnp.concatenate([even[rows, lanes], odd[rows, lanes]], axis=0)
            patches[
                chunk * 2 * UNITS : (chunk + 1) * 2 * UNITS, group * 128 : (group + 1) * 128
            ] = piece.astype(jnp.bfloat16)

    for copy in small:
        copy.wait()
    nothing = jnp.zeros((channels, features), jnp.bfloat16)
    base = 0
    for tap in TAPS:
        for row_parity in range(2):
            for i, j, p, q in [
                (i, j, p, q) for i in range(2) for j in range(2) for p in range(2) for q in range(2)
            ]:
                for col_parity in range(2):
                    row_tap, col_tap = 2 * i + p - row_parity, 2 * j + q - col_parity
                    inside = 0 <= row_tap < 3 and 0 <= col_tap < 3
                    taps[base : base + channels, col_parity * features : (col_parity + 1) * features] = (
                        in_weight_ref[tap, row_tap, col_tap] if inside else nothing
                    )
                base += channels

    unit_row = lax.broadcasted_iota(jnp.int32, (UNITS, 1), 0)
    row_frame = sum((unit_row >= (k + 1) * REACH).astype(jnp.int32) for k in range(LF))
    pixel_row = 2 * first_row + unit_row - row_frame * REACH - 1
    row_inside = (pixel_row >= 0) & (pixel_row < 2 * grid_rows)
    in_bias = in_bias_ref[...].reshape(1, features)
    half_gain = gain_ref[...].reshape(1, features) * 0.5

    def first_layer(chunk):
        for corner in range(2):
            start = (chunk * 2 + corner) * UNITS
            for col_parity in range(2):
                value = (
                    raw[pl.ds(start, UNITS), col_parity * features : (col_parity + 1) * features]
                    + in_bias
                )
                value = value.astype(jnp.bfloat16).astype(jnp.float32)
                scale = lax.rsqrt(jnp.mean(value * value, axis=1, keepdims=True) + 1e-06)
                column = chunk * 4 + corner * 2 + col_parity
                pixel = section * columns + column - 1
                keep = row_inside & (pixel >= 0) & (pixel < width)
                half = value * jnp.where(keep, scale, 0.0) * half_gain
                result = half + half * jnp.tanh(half)
                at = pl.ds(column * UNITS, UNITS)
                for lane in range(lane_tiles):
                    lanes = slice(lane * 128, (lane + 1) * 128)
                    hidden[lane, at] = value[:, lanes]
                    activated[lane, at] = result[:, lanes]

    middle = (chunks + 1) // 2
    groups = ((0, middle), (middle, chunks))
    for low, high in groups:
        rows = slice(low * 2 * UNITS, high * 2 * UNITS)
        raw[rows] = jnp.dot(patches[rows], taps[...], preferred_element_type=jnp.float32)
    for low, high in groups:
        for chunk in range(low, high):
            first_layer(chunk)

    def pair_up(phase, pair):
        at = slice(pair * 16, pair * 16 + 16)
        for lane in range(lane_tiles):
            for field in range(LF):
                for row_tap in range(3):
                    start = (2 * pair + phase) * UNITS + field * REACH + row_tap
                    joined = jnp.concatenate(
                        [activated[lane, pl.ds(start + k * UNITS, ROWS)] for k in range(2)], axis=0
                    )
                    to_lane = (field * 3 + row_tap) * features + lane * 128
                    active[phase, at, to_lane : to_lane + 128] = joined.astype(jnp.bfloat16)

    rows = columns * ROWS
    depth = 3 * features

    def windows(low, high, lanes):
        return jnp.concatenate(
            [
                active[tap % 2, 16 * (tap // 2) + low : 16 * (tap // 2) + high, lanes]
                for tap in range(3)
            ],
            axis=1,
        )

    def weights(lanes):
        return jnp.concatenate([mid_weight[tap, :, lanes] for tap in range(3)], axis=0)

    mid_bias = mid_bias_ref[...].reshape(1, features)

    def finish(field):
        tile_row = lax.broadcasted_iota(jnp.int32, (columns * ROWS, 128), 0) & (ROWS - 1)
        for lane in range(lane_tiles):
            lanes = slice(lane * 128, (lane + 1) * 128)
            skip = jnp.concatenate(
                [
                    hidden[lane, pl.ds((column + 1) * UNITS + field * REACH + 1, ROWS)]
                    for column in range(columns)
                ],
                axis=0,
            )
            value = summed[field, lane] + skip + mid_bias[:, lanes]
            value = jnp.where(tile_row < 2 * filled, value, 0.0)
            value = jnp.swapaxes(value.reshape(columns, ROWS, 128), 0, 1)
            out_ref[field, :, :, lanes] = value.astype(jnp.bfloat16)

    for phase in range(2):
        for pair in range(pairs - phase):
            pair_up(phase, pair)
    for tap in range(3):
        for copy in load(tap):
            copy.wait()
    early = windows(0, rows, slice(0, depth))
    late = windows(0, rows, slice(depth, 2 * depth))
    for left in range(0, 2 * features, 256):
        block = jnp.dot(
            early, weights(slice(left, left + 256)), preferred_element_type=jnp.float32
        )
        for lane in range(2):
            field, tile = divmod(left // 128 + lane, lane_tiles)
            summed[field, tile] = block[:, lane * 128 : (lane + 1) * 128]
    for left in range(0, features, 256):
        right = min(left + 256, features)
        block = jnp.dot(late, weights(slice(left, right)), preferred_element_type=jnp.float32)
        for lane in range((right - left) // 128):
            tile = left // 128 + lane
            summed[1, tile] = summed[1, tile] + block[:, lane * 128 : (lane + 1) * 128]
    for field in range(LF):
        finish(field)


def decode_tile(
    own,
    other,
    share_rows,
    grid_rows,
    width,
    tile_rows,
    conv_in_weight,
    conv_in_bias,
    norm_gain,
    conv_mid_weight,
    conv_mid_bias,
):
    sections = lax.axis_size("sect")
    channels, features = conv_in_weight.shape[3:]
    token_width = 4 * channels
    columns = width // sections
    span = columns // 2
    pairs = span + 1
    chunks = (span + 2) * token_width // 128
    lane_tiles = features // 128
    vmem = pl.BlockSpec(memory_space=pltpu.VMEM)
    hbm = pl.BlockSpec(memory_space=pltpu.HBM)
    slots = len(TAPS)
    depth = slots * 2 * 4 * token_width
    held = chunks * 4 * UNITS
    return pl.pallas_call(
        functools.partial(decode_body, grid_rows, width, share_rows),
        in_specs=[vmem, vmem, pl.BlockSpec(memory_space=pltpu.SMEM)] + [hbm] * 5,
        out_specs=vmem,
        out_shape=jax.ShapeDtypeStruct((LF, ROWS, columns, features), jnp.bfloat16),
        scratch_shapes=[
            pltpu.VMEM((3, 3 * features, slots * features), jnp.bfloat16),
            pltpu.VMEM(conv_in_weight.shape, jnp.bfloat16),
            pltpu.VMEM(conv_in_bias.shape, jnp.float32),
            pltpu.VMEM(norm_gain.shape, jnp.float32),
            pltpu.VMEM(conv_mid_bias.shape, jnp.float32),
            pltpu.VMEM((depth, 2 * features), jnp.bfloat16),
            pltpu.VMEM((2 * own.shape[0] * share_rows, chunks * 128), jnp.float32),
            pltpu.VMEM((chunks * 2 * UNITS, depth), jnp.bfloat16),
            pltpu.VMEM((chunks * 2 * UNITS, 2 * features), jnp.float32),
            pltpu.VMEM((lane_tiles, held, 128), jnp.float32),
            pltpu.VMEM((lane_tiles, held, 128), jnp.float32),
            pltpu.VMEM((2, pairs * 16, LF * 3 * features), jnp.bfloat16),
            pltpu.VMEM((LF, lane_tiles, columns * ROWS, 128), jnp.float32),
            pltpu.SemaphoreType.DMA((3, 3, slots)),
            pltpu.SemaphoreType.DMA((4,)),
        ],
        compiler_params=pltpu.CompilerParams(vmem_limit_bytes=DECODE_VMEM),
        cost_estimate=pl.CostEstimate(
            flops=2 * 3 * 9 * columns * ROWS * features * features,
            bytes_accessed=slots * 9 * features * features * 2,
            transcendentals=held * features,
        ),
        name="decode_tile",
    )(
        own,
        other,
        *in_hbm(
            tile_rows, conv_in_weight, conv_in_bias, norm_gain, conv_mid_weight, conv_mid_bias
        ),
    )


def on_device(
    queries,
    key_tokens,
    value_tokens,
    latent,
    tile_rows,
    conv_in_weight,
    conv_in_bias,
    norm_gain,
    conv_mid_weight,
    conv_mid_bias,
):
    devices = lax.axis_size("seq")
    groups = parity_groups(devices)
    grid_rows = latent.shape[0] * devices // LF
    token_width = 4 * conv_in_weight.shape[3]
    packed = pack_heads(queries, key_tokens, value_tokens, latent, token_width)
    own = lax.all_to_all(packed, "seq", 0, 0, axis_index_groups=groups, tiled=True)
    other = lax.ppermute(own, "seq", xor_pairs(1))
    mixed = attend(own, other, queries.shape[0])
    returned = lax.all_to_all(mixed, "seq", 0, 0, axis_index_groups=groups, tiled=True)
    frames = decode_tile(
        own,
        other,
        latent.shape[0],
        grid_rows,
        2 * latent.shape[1] // token_width,
        tile_rows,
        conv_in_weight,
        conv_in_bias,
        norm_gain,
        conv_mid_weight,
        conv_mid_bias,
    )
    return (unpack_heads(returned), frames)


def solution(mesh):
    in_specs = (
        P("seq", None),
        P("seq", None),
        P("seq", None),
        P("seq", None),
        P(),
        P(),
        P(),
        P(),
        P(),
        P(),
    )
    out_specs = (P("seq", "sect"), P(None, "seq", "sect", None))
    return jax.shard_map(
        on_device, mesh=mesh, in_specs=in_specs, out_specs=out_specs, check_vma=False
    )
```

```python
import functools
import math

import jax
import jax.numpy as jnp
from jax import lax
from jax.experimental import pallas as pl
from jax.experimental.pallas import tpu as pltpu
from jax.sharding import PartitionSpec as P

DH = 128
LF = 2
MAXT = 4
RIM = 64
TAPS = (1, 2)
ROWS = 2 * MAXT
REACH = ROWS + 2
UNITS = -(-LF * REACH // 8) * 8
DECODE_VMEM = 32 * 1024 * 1024
ATTEND_VMEM = 32 * 1024 * 1024
COPY_VMEM = 16 * 1024 * 1024


def parity_groups(devices):
    return [list(range(parity, devices, 2)) for parity in range(2)]


def in_hbm(*arrays):
    return [pltpu.with_memory_space_constraint(array, pltpu.HBM) for array in arrays]


def pack_body(query_ref, key_ref, value_ref, latent_ref, *refs):
    packed_refs, (held, sems) = refs[:-2], refs[-2:]
    heads = len(packed_refs)
    chip = lax.axis_index("seq") // 2
    token_rows = query_ref.shape[0]
    section = lax.axis_index("sect")
    wide_columns = pl.ds(pl.multiple_of(section * heads * DH, DH), heads * DH)
    copies = [
        pltpu.make_async_copy(ref.at[:, wide_columns], held.at[place], sems.at[place])
        for place, ref in enumerate((query_ref, key_ref, value_ref))
    ]
    for copy in copies:
        copy.start()
    rows, width = latent_ref.shape
    half, rim = width // 2, RIM
    wide = latent_ref[...].astype(jnp.float32)
    rim_zeros = jnp.zeros((rows, rim), jnp.float32)
    lower = jnp.concatenate([rim_zeros, wide[:, : half + rim]], axis=1)
    upper = jnp.concatenate([wide[:, half - rim :], rim_zeros], axis=1)
    share = jnp.where(section == 0, lower, upper)
    chunks = share.shape[1] // DH
    lines = [share[:, chunk * DH : (chunk + 1) * DH] for chunk in range(chunks)]
    spare = packed_refs[0].shape[0] - 3 * token_rows - chunks * rows
    lines.append(jnp.zeros((spare, DH), jnp.float32))
    share = jnp.concatenate(lines, axis=0).astype(jnp.bfloat16)
    for packed_ref in packed_refs:
        packed_ref[3 * token_rows :] = share
    for place, copy in enumerate(copies):
        copy.wait()
        for m, packed_ref in enumerate(packed_refs):
            columns = pl.ds(pl.multiple_of((chip ^ m) * DH, DH), DH)
            packed_ref[place * token_rows : (place + 1) * token_rows] = held[place, :, columns]


def pack_heads(queries, key_tokens, value_tokens, latent, token_width):
    token_rows, width = queries.shape
    sections = lax.axis_size("sect")
    heads = width // DH // sections
    span = latent.shape[1] // sections + 2 * token_width
    extra = -(-latent.shape[0] * (span // DH) // 16) * 16
    hbm = pl.BlockSpec(memory_space=pltpu.HBM)
    vmem = pl.BlockSpec(memory_space=pltpu.VMEM)
    return pl.pallas_call(
        pack_body,
        in_specs=[hbm, hbm, hbm, vmem],
        out_specs=[vmem] * heads,
        out_shape=[jax.ShapeDtypeStruct((3 * token_rows + extra, DH), queries.dtype)] * heads,
        scratch_shapes=[
            pltpu.VMEM((3, token_rows, heads * DH), queries.dtype),
            pltpu.SemaphoreType.DMA((3,)),
        ],
        compiler_params=pltpu.CompilerParams(vmem_limit_bytes=COPY_VMEM),
        name="pack_heads",
    )(*in_hbm(queries, key_tokens, value_tokens, latent))


def xor_pairs(distance):
    return [(i, i ^ distance) for i in range(lax.axis_size("seq"))]


def flat(array):
    return array.reshape(-1, array.shape[-1])


def attend_body(*refs):
    out_ref = refs[-1]
    members, token_rows, _ = out_ref.shape
    block = min(4, members)
    chip = lax.axis_index("seq") // 2
    pieces = refs[:-1]

    def rows(place, chosen):
        at = slice(place * token_rows, (place + 1) * token_rows)
        return jnp.concatenate([ref[at] for ref in chosen], axis=0)

    keys, values = rows(1, pieces), rows(2, pieces)
    for step in range(0, members, block):
        scores = lax.dot_general(
            rows(0, pieces[step : step + block]),
            keys,
            (((1,), (1,)), ((), ())),
            preferred_element_type=jnp.float32,
        ) * (1.0 / math.sqrt(DH))
        exponents = jnp.exp(scores - jnp.max(scores, axis=1, keepdims=True))
        totals = jnp.sum(exponents, axis=1, keepdims=True)
        mixed = jnp.dot(
            exponents.astype(jnp.bfloat16), values, preferred_element_type=jnp.float32
        )
        mixed = (mixed / totals).astype(out_ref.dtype)
        for m in range(block):
            out_ref[chip ^ (step + m)] = mixed[m * token_rows : (m + 1) * token_rows]


def attend(own, other, token_rows):
    members = len(own)
    total = members * token_rows
    vmem = pl.BlockSpec(memory_space=pltpu.VMEM)
    return pl.pallas_call(
        attend_body,
        in_specs=[vmem] * (2 * members),
        out_specs=vmem,
        out_shape=jax.ShapeDtypeStruct((members, token_rows, DH), own[0].dtype),
        compiler_params=pltpu.CompilerParams(vmem_limit_bytes=ATTEND_VMEM),
        cost_estimate=pl.CostEstimate(
            flops=8 * total * total * DH,
            bytes_accessed=7 * total * DH * 2,
            transcendentals=2 * total * total,
        ),
        name="attend",
    )(*own, *other)


def unpack_body(in_ref, out_ref, sems):
    copies = [
        pltpu.make_async_copy(
            in_ref.at[head], out_ref.at[:, pl.ds(head * DH, DH)], sems.at[head]
        )
        for head in range(in_ref.shape[0])
    ]
    for copy in copies:
        copy.start()
    for copy in copies:
        copy.wait()


def unpack_heads(array):
    heads, token_rows, _ = array.shape
    return pl.pallas_call(
        unpack_body,
        in_specs=[pl.BlockSpec(memory_space=pltpu.VMEM)],
        out_specs=pl.BlockSpec(memory_space=pltpu.HBM),
        out_shape=jax.ShapeDtypeStruct((token_rows, heads * DH), array.dtype),
        scratch_shapes=[pltpu.SemaphoreType.DMA((heads,))],
        compiler_params=pltpu.CompilerParams(vmem_limit_bytes=COPY_VMEM),
        name="unpack_heads",
    )(array)


def decode_body(
    grid_rows,
    width,
    share_rows,
    members,
    *refs,
):
    pieces, refs = refs[: 2 * members], refs[2 * members :]
    (
    tile_ref,
    in_weight_hbm,
    in_bias_hbm,
    gain_hbm,
    mid_weight_hbm,
    mid_bias_hbm,
    out_ref,
    mid_weight,
    in_weight_ref,
    in_bias_ref,
    gain_ref,
    mid_bias_ref,
    taps,
    rows_held,
    patches,
    raw,
    hidden,
    activated,
    active,
    summed,
    weight_sems,
    small_sems,
    ) = refs
    pairs = active.shape[1] // 16
    channels, features = in_weight_ref.shape[3:]
    columns = out_ref.shape[2]
    lane_tiles = features // 128
    position = lax.axis_index("seq")
    section = lax.axis_index("sect")
    small = [
        pltpu.make_async_copy(source, target, small_sems.at[place])
        for place, (source, target) in enumerate(
            (
                (in_weight_hbm, in_weight_ref),
                (in_bias_hbm, in_bias_ref),
                (gain_hbm, gain_ref),
                (mid_bias_hbm, mid_bias_ref),
            )
        )
    ]
    for copy in small:
        copy.start()

    def load(col_tap):
        return [
            pltpu.make_async_copy(
                mid_weight_hbm.at[tap, row_tap, col_tap],
                mid_weight.at[
                    col_tap,
                    pl.ds(row_tap * features, features),
                    pl.ds((2 - tap) * features, features),
                ],
                weight_sems.at[col_tap, row_tap, slot],
            )
            for row_tap in range(3)
            for slot, tap in enumerate(TAPS)
        ]

    for col_tap in range(3):
        for copy in load(col_tap):
            copy.start()

    filled = tile_ref[position]
    first_row = lax.fori_loop(0, position, lambda d, total: total + tile_ref[d], jnp.int32(0))

    chunks = rows_held.shape[1] // 128
    extra = -(-share_rows * chunks // 16) * 16
    for place, ref in enumerate(pieces):
        lines = ref[ref.shape[0] - extra :].astype(jnp.float32)
        low = place * share_rows
        for chunk in range(chunks):
            rows_held[low : low + share_rows, chunk * 128 : (chunk + 1) * 128] = lines[
                chunk * share_rows : (chunk + 1) * share_rows
            ]
    latent = rows_held[...]
    aside = pltpu.roll(latent, latent.shape[1] - RIM, 1).astype(jnp.bfloat16)
    latent = latent.astype(jnp.bfloat16)
    held_rows = latent.shape[0]
    unit = lax.broadcasted_iota(jnp.int32, (UNITS, held_rows), 0)
    held = lax.broadcasted_iota(jnp.int32, (UNITS, held_rows), 1)
    side = (held >= members * share_rows).astype(jnp.int32)
    member = (held // share_rows - side * members) ^ (position // 2)
    held = (2 * member + ((position & 1) ^ side)) * share_rows + held % share_rows
    frame = sum((unit >= (k + 1) * REACH).astype(jnp.int32) for k in range(LF))
    reach = unit - frame * REACH
    selectors = []
    for tap in TAPS:
        for row_parity in range(2):
            for i in range(2):
                token_row = first_row + (reach >> 1) - 1 + i
                source = frame + tap - 2
                wanted = (
                    ((reach & 1) == row_parity)
                    & (token_row >= 0)
                    & (token_row < grid_rows)
                    & (source >= 0)
                    & (source < LF)
                )
                target = jnp.where(wanted, source * grid_rows + token_row, -1)
                selectors.append(jnp.where(held == target, 1.0, 0.0).astype(jnp.bfloat16))
    selector = jnp.concatenate(selectors, axis=0)
    even = jnp.dot(selector, latent, preferred_element_type=jnp.float32)
    odd = jnp.dot(selector, aside, preferred_element_type=jnp.float32)
    for chunk in range(chunks):
        lanes = slice(chunk * 128, (chunk + 1) * 128)
        for group in range(len(selectors)):
            rows = slice(group * UNITS, (group + 1) * UNITS)
            piece = jnp.concatenate([even[rows, lanes], odd[rows, lanes]], axis=0)
            patches[
                chunk * 2 * UNITS : (chunk + 1) * 2 * UNITS, group * 128 : (group + 1) * 128
            ] = piece.astype(jnp.bfloat16)

    for copy in small:
        copy.wait()
    nothing = jnp.zeros((channels, features), jnp.bfloat16)
    base = 0
    for tap in TAPS:
        for row_parity in range(2):
            for i, j, p, q in [
                (i, j, p, q) for i in range(2) for j in range(2) for p in range(2) for q in range(2)
            ]:
                for col_parity in range(2):
                    row_tap, col_tap = 2 * i + p - row_parity, 2 * j + q - col_parity
                    inside = 0 <= row_tap < 3 and 0 <= col_tap < 3
                    taps[base : base + channels, col_parity * features : (col_parity + 1) * features] = (
                        in_weight_ref[tap, row_tap, col_tap] if inside else nothing
                    )
                base += channels

    unit_row = lax.broadcasted_iota(jnp.int32, (UNITS, 1), 0)
    row_frame = sum((unit_row >= (k + 1) * REACH).astype(jnp.int32) for k in range(LF))
    pixel_row = 2 * first_row + unit_row - row_frame * REACH - 1
    row_inside = (pixel_row >= 0) & (pixel_row < 2 * grid_rows)
    in_bias = in_bias_ref[...].reshape(1, features)
    half_gain = gain_ref[...].reshape(1, features) * 0.5

    def first_layer(chunk):
        for corner in range(2):
            start = (chunk * 2 + corner) * UNITS
            for col_parity in range(2):
                value = (
                    raw[pl.ds(start, UNITS), col_parity * features : (col_parity + 1) * features]
                    + in_bias
                )
                value = value.astype(jnp.bfloat16).astype(jnp.float32)
                scale = lax.rsqrt(jnp.mean(value * value, axis=1, keepdims=True) + 1e-06)
                column = chunk * 4 + corner * 2 + col_parity
                pixel = section * columns + column - 1
                keep = row_inside & (pixel >= 0) & (pixel < width)
                half = value * jnp.where(keep, scale, 0.0) * half_gain
                result = half + half * jnp.tanh(half)
                at = pl.ds(column * UNITS, UNITS)
                for lane in range(lane_tiles):
                    lanes = slice(lane * 128, (lane + 1) * 128)
                    hidden[lane, at] = value[:, lanes]
                    activated[lane, at] = result[:, lanes]

    middle = (chunks + 1) // 2
    groups = ((0, middle), (middle, chunks))
    for low, high in groups:
        rows = slice(low * 2 * UNITS, high * 2 * UNITS)
        raw[rows] = jnp.dot(patches[rows], taps[...], preferred_element_type=jnp.float32)
    for low, high in groups:
        for chunk in range(low, high):
            first_layer(chunk)

    def pair_up(phase, pair):
        at = slice(pair * 16, pair * 16 + 16)
        for lane in range(lane_tiles):
            for field in range(LF):
                for row_tap in range(3):
                    start = (2 * pair + phase) * UNITS + field * REACH + row_tap
                    joined = jnp.concatenate(
                        [activated[lane, pl.ds(start + k * UNITS, ROWS)] for k in range(2)], axis=0
                    )
                    to_lane = (field * 3 + row_tap) * features + lane * 128
                    active[phase, at, to_lane : to_lane + 128] = joined.astype(jnp.bfloat16)

    rows = columns * ROWS
    depth = 3 * features

    def windows(low, high, lanes):
        return jnp.concatenate(
            [
                active[tap % 2, 16 * (tap // 2) + low : 16 * (tap // 2) + high, lanes]
                for tap in range(3)
            ],
            axis=1,
        )

    def weights(lanes):
        return jnp.concatenate([mid_weight[tap, :, lanes] for tap in range(3)], axis=0)

    mid_bias = mid_bias_ref[...].reshape(1, features)

    def finish(field):
        tile_row = lax.broadcasted_iota(jnp.int32, (columns * ROWS, 128), 0) & (ROWS - 1)
        for lane in range(lane_tiles):
            lanes = slice(lane * 128, (lane + 1) * 128)
            skip = jnp.concatenate(
                [
                    hidden[lane, pl.ds((column + 1) * UNITS + field * REACH + 1, ROWS)]
                    for column in range(columns)
                ],
                axis=0,
            )
            value = summed[field, lane] + skip + mid_bias[:, lanes]
            value = jnp.where(tile_row < 2 * filled, value, 0.0)
            value = jnp.swapaxes(value.reshape(columns, ROWS, 128), 0, 1)
            out_ref[field, :, :, lanes] = value.astype(jnp.bfloat16)

    for phase in range(2):
        for pair in range(pairs - phase):
            pair_up(phase, pair)
    for tap in range(3):
        for copy in load(tap):
            copy.wait()
    early = windows(0, rows, slice(0, depth))
    late = windows(0, rows, slice(depth, 2 * depth))
    for left in range(0, 2 * features, 256):
        block = jnp.dot(
            early, weights(slice(left, left + 256)), preferred_element_type=jnp.float32
        )
        for lane in range(2):
            field, tile = divmod(left // 128 + lane, lane_tiles)
            summed[field, tile] = block[:, lane * 128 : (lane + 1) * 128]
    for left in range(0, features, 256):
        right = min(left + 256, features)
        block = jnp.dot(late, weights(slice(left, right)), preferred_element_type=jnp.float32)
        for lane in range((right - left) // 128):
            tile = left // 128 + lane
            summed[1, tile] = summed[1, tile] + block[:, lane * 128 : (lane + 1) * 128]
    for field in range(LF):
        finish(field)


def decode_tile(
    own,
    other,
    share_rows,
    grid_rows,
    width,
    tile_rows,
    conv_in_weight,
    conv_in_bias,
    norm_gain,
    conv_mid_weight,
    conv_mid_bias,
):
    sections = lax.axis_size("sect")
    channels, features = conv_in_weight.shape[3:]
    token_width = 4 * channels
    columns = width // sections
    span = columns // 2
    pairs = span + 1
    chunks = (span + 2) * token_width // 128
    lane_tiles = features // 128
    vmem = pl.BlockSpec(memory_space=pltpu.VMEM)
    hbm = pl.BlockSpec(memory_space=pltpu.HBM)
    slots = len(TAPS)
    depth = slots * 2 * 4 * token_width
    held = chunks * 4 * UNITS
    return pl.pallas_call(
        functools.partial(decode_body, grid_rows, width, share_rows, len(own)),
        in_specs=[vmem] * (2 * len(own)) + [pl.BlockSpec(memory_space=pltpu.SMEM)] + [hbm] * 5,
        out_specs=vmem,
        out_shape=jax.ShapeDtypeStruct((LF, ROWS, columns, features), jnp.bfloat16),
        scratch_shapes=[
            pltpu.VMEM((3, 3 * features, slots * features), jnp.bfloat16),
            pltpu.VMEM(conv_in_weight.shape, jnp.bfloat16),
            pltpu.VMEM(conv_in_bias.shape, jnp.float32),
            pltpu.VMEM(norm_gain.shape, jnp.float32),
            pltpu.VMEM(conv_mid_bias.shape, jnp.float32),
            pltpu.VMEM((depth, 2 * features), jnp.bfloat16),
            pltpu.VMEM((2 * len(own) * share_rows, chunks * 128), jnp.float32),
            pltpu.VMEM((chunks * 2 * UNITS, depth), jnp.bfloat16),
            pltpu.VMEM((chunks * 2 * UNITS, 2 * features), jnp.float32),
            pltpu.VMEM((lane_tiles, held, 128), jnp.float32),
            pltpu.VMEM((lane_tiles, held, 128), jnp.float32),
            pltpu.VMEM((2, pairs * 16, LF * 3 * features), jnp.bfloat16),
            pltpu.VMEM((LF, lane_tiles, columns * ROWS, 128), jnp.float32),
            pltpu.SemaphoreType.DMA((3, 3, slots)),
            pltpu.SemaphoreType.DMA((4,)),
        ],
        compiler_params=pltpu.CompilerParams(vmem_limit_bytes=DECODE_VMEM),
        cost_estimate=pl.CostEstimate(
            flops=2 * 3 * 9 * columns * ROWS * features * features,
            bytes_accessed=slots * 9 * features * features * 2,
            transcendentals=held * features,
        ),
        name="decode_tile",
    )(
        *own,
        *other,
        *in_hbm(
            tile_rows, conv_in_weight, conv_in_bias, norm_gain, conv_mid_weight, conv_mid_bias
        ),
    )


def on_device(
    queries,
    key_tokens,
    value_tokens,
    latent,
    tile_rows,
    conv_in_weight,
    conv_in_bias,
    norm_gain,
    conv_mid_weight,
    conv_mid_bias,
):
    devices = lax.axis_size("seq")
    groups = parity_groups(devices)
    grid_rows = latent.shape[0] * devices // LF
    token_width = 4 * conv_in_weight.shape[3]
    packed = pack_heads(queries, key_tokens, value_tokens, latent, token_width)
    chips = len(packed)
    own = list(packed)
    for m in [1, 2, *range(chips // 2, chips), *range(3, chips // 2)]:
        own[m] = lax.ppermute(packed[m], "seq", xor_pairs(2 * m))
    other = [lax.ppermute(piece, "seq", xor_pairs(1)) for piece in own]
    mixed = attend(own, other, queries.shape[0])
    returned = lax.all_to_all(mixed, "seq", 0, 0, axis_index_groups=groups, tiled=True)
    frames = decode_tile(
        own,
        other,
        latent.shape[0],
        grid_rows,
        2 * latent.shape[1] // token_width,
        tile_rows,
        conv_in_weight,
        conv_in_bias,
        norm_gain,
        conv_mid_weight,
        conv_mid_bias,
    )
    return (unpack_heads(returned), frames)


def solution(mesh):
    in_specs = (
        P("seq", None),
        P("seq", None),
        P("seq", None),
        P("seq", None),
        P(),
        P(),
        P(),
        P(),
        P(),
        P(),
    )
    out_specs = (P("seq", "sect"), P(None, "seq", "sect", None))
    return jax.shard_map(
        on_device, mesh=mesh, in_specs=in_specs, out_specs=out_specs, check_vma=False
    )
```

```python
import functools
import math

import jax
import jax.numpy as jnp
from jax import lax
from jax.experimental import pallas as pl
from jax.experimental.pallas import tpu as pltpu
from jax.sharding import PartitionSpec as P

DH = 128
LF = 2
MAXT = 4
RIM = 64
TAPS = (1, 2)
ROWS = 2 * MAXT
REACH = ROWS + 2
UNITS = -(-LF * REACH // 8) * 8
DECODE_VMEM = 32 * 1024 * 1024
ATTEND_VMEM = 32 * 1024 * 1024
COPY_VMEM = 16 * 1024 * 1024


def parity_groups(devices):
    return [list(range(parity, devices, 2)) for parity in range(2)]


def in_hbm(*arrays):
    return [pltpu.with_memory_space_constraint(array, pltpu.HBM) for array in arrays]


def pack_body(query_ref, key_ref, value_ref, latent_ref, *refs):
    packed_refs, (held, latent_held, sems) = refs[:-3], refs[-3:]
    heads = len(packed_refs)
    chip = lax.axis_index("seq") // 2
    token_rows = query_ref.shape[0]
    section = lax.axis_index("sect")
    wide_columns = pl.ds(pl.multiple_of(section * heads * DH, DH), heads * DH)
    copies = [
        pltpu.make_async_copy(ref.at[:, wide_columns], held.at[place], sems.at[place])
        for place, ref in enumerate((query_ref, key_ref, value_ref))
    ]
    latent_copy = pltpu.make_async_copy(latent_ref, latent_held, sems.at[3])
    latent_copy.start()
    for copy in copies:
        copy.start()
    rows, width = latent_ref.shape
    latent_copy.wait()
    half, rim = width // 2, RIM
    wide = latent_held[...].astype(jnp.float32)
    rim_zeros = jnp.zeros((rows, rim), jnp.float32)
    lower = jnp.concatenate([rim_zeros, wide[:, : half + rim]], axis=1)
    upper = jnp.concatenate([wide[:, half - rim :], rim_zeros], axis=1)
    share = jnp.where(section == 0, lower, upper)
    chunks = share.shape[1] // DH
    lines = [share[:, chunk * DH : (chunk + 1) * DH] for chunk in range(chunks)]
    spare = packed_refs[0].shape[0] - 3 * token_rows - chunks * rows
    lines.append(jnp.zeros((spare, DH), jnp.float32))
    share = jnp.concatenate(lines, axis=0).astype(jnp.bfloat16)
    for packed_ref in packed_refs:
        packed_ref[3 * token_rows :] = share
    for place, copy in enumerate(copies):
        copy.wait()
        for m, packed_ref in enumerate(packed_refs):
            columns = pl.ds(pl.multiple_of((chip ^ m) * DH, DH), DH)
            packed_ref[place * token_rows : (place + 1) * token_rows] = held[place, :, columns]


def pack_heads(queries, key_tokens, value_tokens, latent, token_width):
    token_rows, width = queries.shape
    sections = lax.axis_size("sect")
    heads = width // DH // sections
    span = latent.shape[1] // sections + 2 * token_width
    extra = -(-latent.shape[0] * (span // DH) // 16) * 16
    hbm = pl.BlockSpec(memory_space=pltpu.HBM)
    vmem = pl.BlockSpec(memory_space=pltpu.VMEM)
    return pl.pallas_call(
        pack_body,
        in_specs=[hbm] * 4,
        out_specs=[vmem] * heads,
        out_shape=[jax.ShapeDtypeStruct((3 * token_rows + extra, DH), queries.dtype)] * heads,
        scratch_shapes=[
            pltpu.VMEM((3, token_rows, heads * DH), queries.dtype),
            pltpu.VMEM(latent.shape, latent.dtype),
            pltpu.SemaphoreType.DMA((4,)),
        ],
        compiler_params=pltpu.CompilerParams(vmem_limit_bytes=COPY_VMEM),
        name="pack_heads",
    )(*in_hbm(queries, key_tokens, value_tokens, latent))


def xor_pairs(distance):
    return [(i, i ^ distance) for i in range(lax.axis_size("seq"))]


def flat(array):
    return array.reshape(-1, array.shape[-1])


def attend_body(*refs):
    out_ref = refs[-1]
    members, token_rows, _ = out_ref.shape
    block = min(4, members)
    chip = lax.axis_index("seq") // 2
    pieces = refs[:-1]

    def rows(place, chosen):
        at = slice(place * token_rows, (place + 1) * token_rows)
        return jnp.concatenate([ref[at] for ref in chosen], axis=0)

    keys, values = rows(1, pieces), rows(2, pieces)
    for step in range(0, members, block):
        scores = lax.dot_general(
            rows(0, pieces[step : step + block]),
            keys,
            (((1,), (1,)), ((), ())),
            preferred_element_type=jnp.float32,
        ) * (1.0 / math.sqrt(DH))
        exponents = jnp.exp(scores - jnp.max(scores, axis=1, keepdims=True))
        totals = jnp.sum(exponents, axis=1, keepdims=True)
        mixed = jnp.dot(
            exponents.astype(jnp.bfloat16), values, preferred_element_type=jnp.float32
        )
        mixed = (mixed / totals).astype(out_ref.dtype)
        for m in range(block):
            out_ref[chip ^ (step + m)] = mixed[m * token_rows : (m + 1) * token_rows]


def attend(own, other, token_rows):
    members = len(own)
    total = members * token_rows
    vmem = pl.BlockSpec(memory_space=pltpu.VMEM)
    return pl.pallas_call(
        attend_body,
        in_specs=[vmem] * (2 * members),
        out_specs=vmem,
        out_shape=jax.ShapeDtypeStruct((members, token_rows, DH), own[0].dtype),
        compiler_params=pltpu.CompilerParams(vmem_limit_bytes=ATTEND_VMEM),
        cost_estimate=pl.CostEstimate(
            flops=8 * total * total * DH,
            bytes_accessed=7 * total * DH * 2,
            transcendentals=2 * total * total,
        ),
        name="attend",
    )(*own, *other)


def unpack_body(in_ref, out_ref, sems):
    copies = [
        pltpu.make_async_copy(
            in_ref.at[head], out_ref.at[:, pl.ds(head * DH, DH)], sems.at[head]
        )
        for head in range(in_ref.shape[0])
    ]
    for copy in copies:
        copy.start()
    for copy in copies:
        copy.wait()


def unpack_heads(array):
    heads, token_rows, _ = array.shape
    return pl.pallas_call(
        unpack_body,
        in_specs=[pl.BlockSpec(memory_space=pltpu.VMEM)],
        out_specs=pl.BlockSpec(memory_space=pltpu.HBM),
        out_shape=jax.ShapeDtypeStruct((token_rows, heads * DH), array.dtype),
        scratch_shapes=[pltpu.SemaphoreType.DMA((heads,))],
        compiler_params=pltpu.CompilerParams(vmem_limit_bytes=COPY_VMEM),
        name="unpack_heads",
    )(array)


def decode_body(
    grid_rows,
    width,
    share_rows,
    members,
    *refs,
):
    pieces, refs = refs[: 2 * members], refs[2 * members :]
    (
    tile_hbm,
    in_weight_hbm,
    in_bias_hbm,
    gain_hbm,
    mid_weight_hbm,
    mid_bias_hbm,
    out_hbm,
    tile_ref,
    out_ref,
    mid_weight,
    in_weight_ref,
    in_bias_ref,
    gain_ref,
    mid_bias_ref,
    taps,
    rows_held,
    patches,
    raw,
    hidden,
    activated,
    active,
    summed,
    weight_sems,
    small_sems,
    out_sems,
    ) = refs
    pairs = active.shape[1] // 16
    channels, features = in_weight_ref.shape[3:]
    columns = out_ref.shape[2]
    lane_tiles = features // 128
    position = lax.axis_index("seq")
    section = lax.axis_index("sect")
    tile_copy = pltpu.make_async_copy(tile_hbm, tile_ref, small_sems.at[4])
    tile_copy.start()
    small = [
        pltpu.make_async_copy(source, target, small_sems.at[place])
        for place, (source, target) in enumerate(
            (
                (in_weight_hbm, in_weight_ref),
                (in_bias_hbm, in_bias_ref),
                (gain_hbm, gain_ref),
                (mid_bias_hbm, mid_bias_ref),
            )
        )
    ]
    for copy in small:
        copy.start()

    def load(col_tap):
        return [
            pltpu.make_async_copy(
                mid_weight_hbm.at[tap, row_tap, col_tap],
                mid_weight.at[
                    col_tap,
                    pl.ds(row_tap * features, features),
                    pl.ds((2 - tap) * features, features),
                ],
                weight_sems.at[col_tap, row_tap, slot],
            )
            for row_tap in range(3)
            for slot, tap in enumerate(TAPS)
        ]

    for col_tap in range(3):
        for copy in load(col_tap):
            copy.start()

    tile_copy.wait()
    filled = tile_ref[position]
    first_row = lax.fori_loop(0, position, lambda d, total: total + tile_ref[d], jnp.int32(0))

    chunks = rows_held.shape[1] // 128
    extra = -(-share_rows * chunks // 16) * 16
    for place, ref in enumerate(pieces):
        lines = ref[ref.shape[0] - extra :].astype(jnp.float32)
        low = place * share_rows
        for chunk in range(chunks):
            rows_held[low : low + share_rows, chunk * 128 : (chunk + 1) * 128] = lines[
                chunk * share_rows : (chunk + 1) * share_rows
            ]
    latent = rows_held[...]
    aside = pltpu.roll(latent, latent.shape[1] - RIM, 1).astype(jnp.bfloat16)
    latent = latent.astype(jnp.bfloat16)
    held_rows = latent.shape[0]
    unit = lax.broadcasted_iota(jnp.int32, (UNITS, held_rows), 0)
    held = lax.broadcasted_iota(jnp.int32, (UNITS, held_rows), 1)
    side = (held >= members * share_rows).astype(jnp.int32)
    member = (held // share_rows - side * members) ^ (position // 2)
    held = (2 * member + ((position & 1) ^ side)) * share_rows + held % share_rows
    frame = sum((unit >= (k + 1) * REACH).astype(jnp.int32) for k in range(LF))
    reach = unit - frame * REACH
    selectors = []
    for tap in TAPS:
        for row_parity in range(2):
            for i in range(2):
                token_row = first_row + (reach >> 1) - 1 + i
                source = frame + tap - 2
                wanted = (
                    ((reach & 1) == row_parity)
                    & (token_row >= 0)
                    & (token_row < grid_rows)
                    & (source >= 0)
                    & (source < LF)
                )
                target = jnp.where(wanted, source * grid_rows + token_row, -1)
                selectors.append(jnp.where(held == target, 1.0, 0.0).astype(jnp.bfloat16))
    selector = jnp.concatenate(selectors, axis=0)
    even = jnp.dot(selector, latent, preferred_element_type=jnp.float32)
    odd = jnp.dot(selector, aside, preferred_element_type=jnp.float32)
    for chunk in range(chunks):
        lanes = slice(chunk * 128, (chunk + 1) * 128)
        for group in range(len(selectors)):
            rows = slice(group * UNITS, (group + 1) * UNITS)
            piece = jnp.concatenate([even[rows, lanes], odd[rows, lanes]], axis=0)
            patches[
                chunk * 2 * UNITS : (chunk + 1) * 2 * UNITS, group * 128 : (group + 1) * 128
            ] = piece.astype(jnp.bfloat16)

    for copy in small:
        copy.wait()
    nothing = jnp.zeros((channels, features), jnp.bfloat16)
    base = 0
    for tap in TAPS:
        for row_parity in range(2):
            for i, j, p, q in [
                (i, j, p, q) for i in range(2) for j in range(2) for p in range(2) for q in range(2)
            ]:
                for col_parity in range(2):
                    row_tap, col_tap = 2 * i + p - row_parity, 2 * j + q - col_parity
                    inside = 0 <= row_tap < 3 and 0 <= col_tap < 3
                    taps[base : base + channels, col_parity * features : (col_parity + 1) * features] = (
                        in_weight_ref[tap, row_tap, col_tap] if inside else nothing
                    )
                base += channels

    unit_row = lax.broadcasted_iota(jnp.int32, (UNITS, 1), 0)
    row_frame = sum((unit_row >= (k + 1) * REACH).astype(jnp.int32) for k in range(LF))
    pixel_row = 2 * first_row + unit_row - row_frame * REACH - 1
    row_inside = (pixel_row >= 0) & (pixel_row < 2 * grid_rows)
    in_bias = in_bias_ref[...].reshape(1, features)
    half_gain = gain_ref[...].reshape(1, features) * 0.5

    def first_layer(chunk):
        for corner in range(2):
            start = (chunk * 2 + corner) * UNITS
            for col_parity in range(2):
                value = (
                    raw[pl.ds(start, UNITS), col_parity * features : (col_parity + 1) * features]
                    + in_bias
                )
                value = value.astype(jnp.bfloat16).astype(jnp.float32)
                scale = lax.rsqrt(jnp.mean(value * value, axis=1, keepdims=True) + 1e-06)
                column = chunk * 4 + corner * 2 + col_parity
                pixel = section * columns + column - 1
                keep = row_inside & (pixel >= 0) & (pixel < width)
                half = value * jnp.where(keep, scale, 0.0) * half_gain
                result = half + half * jnp.tanh(half)
                at = pl.ds(column * UNITS, UNITS)
                for lane in range(lane_tiles):
                    lanes = slice(lane * 128, (lane + 1) * 128)
                    hidden[lane, at] = value[:, lanes]
                    activated[lane, at] = result[:, lanes]

    middle = (chunks + 1) // 2
    groups = ((0, middle), (middle, chunks))
    for low, high in groups:
        rows = slice(low * 2 * UNITS, high * 2 * UNITS)
        raw[rows] = jnp.dot(patches[rows], taps[...], preferred_element_type=jnp.float32)
    for low, high in groups:
        for chunk in range(low, high):
            first_layer(chunk)

    def pair_up(phase, pair):
        at = slice(pair * 16, pair * 16 + 16)
        for lane in range(lane_tiles):
            for field in range(LF):
                for row_tap in range(3):
                    start = (2 * pair + phase) * UNITS + field * REACH + row_tap
                    joined = jnp.concatenate(
                        [activated[lane, pl.ds(start + k * UNITS, ROWS)] for k in range(2)], axis=0
                    )
                    to_lane = (field * 3 + row_tap) * features + lane * 128
                    active[phase, at, to_lane : to_lane + 128] = joined.astype(jnp.bfloat16)

    rows = columns * ROWS
    depth = 3 * features

    def windows(low, high, lanes):
        return jnp.concatenate(
            [
                active[tap % 2, 16 * (tap // 2) + low : 16 * (tap // 2) + high, lanes]
                for tap in range(3)
            ],
            axis=1,
        )

    def weights(lanes):
        return jnp.concatenate([mid_weight[tap, :, lanes] for tap in range(3)], axis=0)

    mid_bias = mid_bias_ref[...].reshape(1, features)

    def finish(field):
        tile_row = lax.broadcasted_iota(jnp.int32, (columns * ROWS, 128), 0) & (ROWS - 1)
        for lane in range(lane_tiles):
            lanes = slice(lane * 128, (lane + 1) * 128)
            skip = jnp.concatenate(
                [
                    hidden[lane, pl.ds((column + 1) * UNITS + field * REACH + 1, ROWS)]
                    for column in range(columns)
                ],
                axis=0,
            )
            value = summed[field, lane] + skip + mid_bias[:, lanes]
            value = jnp.where(tile_row < 2 * filled, value, 0.0)
            value = jnp.swapaxes(value.reshape(columns, ROWS, 128), 0, 1)
            out_ref[field, :, :, lanes] = value.astype(jnp.bfloat16)
        leave(field).start()

    def leave(field):
        return pltpu.make_async_copy(out_ref.at[field], out_hbm.at[field], out_sems.at[field])

    for phase in range(2):
        for pair in range(pairs - phase):
            pair_up(phase, pair)
    for tap in range(3):
        for copy in load(tap):
            copy.wait()
    early = windows(0, rows, slice(0, depth))
    late = windows(0, rows, slice(depth, 2 * depth))
    for left in range(0, 2 * features, 256):
        block = jnp.dot(
            early, weights(slice(left, left + 256)), preferred_element_type=jnp.float32
        )
        for lane in range(2):
            field, tile = divmod(left // 128 + lane, lane_tiles)
            summed[field, tile] = block[:, lane * 128 : (lane + 1) * 128]
    finish(0)
    for left in range(0, features, 256):
        right = min(left + 256, features)
        block = jnp.dot(late, weights(slice(left, right)), preferred_element_type=jnp.float32)
        for lane in range((right - left) // 128):
            tile = left // 128 + lane
            summed[1, tile] = summed[1, tile] + block[:, lane * 128 : (lane + 1) * 128]
    finish(1)
    for field in range(LF):
        leave(field).wait()


def decode_tile(
    own,
    other,
    share_rows,
    grid_rows,
    width,
    tile_rows,
    conv_in_weight,
    conv_in_bias,
    norm_gain,
    conv_mid_weight,
    conv_mid_bias,
):
    sections = lax.axis_size("sect")
    channels, features = conv_in_weight.shape[3:]
    token_width = 4 * channels
    columns = width // sections
    span = columns // 2
    pairs = span + 1
    chunks = (span + 2) * token_width // 128
    lane_tiles = features // 128
    vmem = pl.BlockSpec(memory_space=pltpu.VMEM)
    hbm = pl.BlockSpec(memory_space=pltpu.HBM)
    slots = len(TAPS)
    depth = slots * 2 * 4 * token_width
    held = chunks * 4 * UNITS
    return pl.pallas_call(
        functools.partial(decode_body, grid_rows, width, share_rows, len(own)),
        in_specs=[vmem] * (2 * len(own)) + [hbm] * 6,
        out_specs=hbm,
        out_shape=jax.ShapeDtypeStruct((LF, ROWS, columns, features), jnp.bfloat16),
        scratch_shapes=[
            pltpu.SMEM(tile_rows.shape, tile_rows.dtype),
            pltpu.VMEM((LF, ROWS, columns, features), jnp.bfloat16),
            pltpu.VMEM((3, 3 * features, slots * features), jnp.bfloat16),
            pltpu.VMEM(conv_in_weight.shape, jnp.bfloat16),
            pltpu.VMEM(conv_in_bias.shape, jnp.float32),
            pltpu.VMEM(norm_gain.shape, jnp.float32),
            pltpu.VMEM(conv_mid_bias.shape, jnp.float32),
            pltpu.VMEM((depth, 2 * features), jnp.bfloat16),
            pltpu.VMEM((2 * len(own) * share_rows, chunks * 128), jnp.float32),
            pltpu.VMEM((chunks * 2 * UNITS, depth), jnp.bfloat16),
            pltpu.VMEM((chunks * 2 * UNITS, 2 * features), jnp.float32),
            pltpu.VMEM((lane_tiles, held, 128), jnp.float32),
            pltpu.VMEM((lane_tiles, held, 128), jnp.float32),
            pltpu.VMEM((2, pairs * 16, LF * 3 * features), jnp.bfloat16),
            pltpu.VMEM((LF, lane_tiles, columns * ROWS, 128), jnp.float32),
            pltpu.SemaphoreType.DMA((3, 3, slots)),
            pltpu.SemaphoreType.DMA((5,)),
            pltpu.SemaphoreType.DMA((LF,)),
        ],
        compiler_params=pltpu.CompilerParams(vmem_limit_bytes=DECODE_VMEM),
        cost_estimate=pl.CostEstimate(
            flops=2 * 3 * 9 * columns * ROWS * features * features,
            bytes_accessed=slots * 9 * features * features * 2,
            transcendentals=held * features,
        ),
        name="decode_tile",
    )(
        *own,
        *other,
        *in_hbm(
            tile_rows, conv_in_weight, conv_in_bias, norm_gain, conv_mid_weight, conv_mid_bias
        ),
    )


def on_device(
    queries,
    key_tokens,
    value_tokens,
    latent,
    tile_rows,
    conv_in_weight,
    conv_in_bias,
    norm_gain,
    conv_mid_weight,
    conv_mid_bias,
):
    devices = lax.axis_size("seq")
    groups = parity_groups(devices)
    grid_rows = latent.shape[0] * devices // LF
    token_width = 4 * conv_in_weight.shape[3]
    packed = pack_heads(queries, key_tokens, value_tokens, latent, token_width)
    chips = len(packed)
    own = list(packed)
    far, near = list(range(chips // 2, chips)), list(range(1, chips // 2))
    for m in [*far[:2], *near[1:2], *far[2:], *near[2:], *near[:1]]:
        own[m] = lax.ppermute(packed[m], "seq", xor_pairs(2 * m))
    other = [lax.ppermute(piece, "seq", xor_pairs(1)) for piece in own]
    mixed = attend(own, other, queries.shape[0])
    returned = lax.all_to_all(mixed, "seq", 0, 0, axis_index_groups=groups, tiled=True)
    frames = decode_tile(
        own,
        other,
        latent.shape[0],
        grid_rows,
        2 * latent.shape[1] // token_width,
        tile_rows,
        conv_in_weight,
        conv_in_bias,
        norm_gain,
        conv_mid_weight,
        conv_mid_bias,
    )
    return (unpack_heads(returned), frames)


def solution(mesh):
    in_specs = (
        P("seq", None),
        P("seq", None),
        P("seq", None),
        P("seq", None),
        P(),
        P(),
        P(),
        P(),
        P(),
        P(),
    )
    out_specs = (P("seq", "sect"), P(None, "seq", "sect", None))
    return jax.shard_map(
        on_device, mesh=mesh, in_specs=in_specs, out_specs=out_specs, check_vma=False
    )
```

```python
import functools
import math

import jax
import jax.numpy as jnp
from jax import lax
from jax.experimental import pallas as pl
from jax.experimental.pallas import tpu as pltpu
from jax.sharding import PartitionSpec as P

DH = 128
LF = 2
MAXT = 4
RIM = 64
TAPS = (1, 2)
ROWS = 2 * MAXT
REACH = ROWS + 2
UNITS = -(-LF * REACH // 8) * 8
DECODE_VMEM = 32 * 1024 * 1024
ATTEND_VMEM = 32 * 1024 * 1024
COPY_VMEM = 16 * 1024 * 1024


def parity_groups(devices):
    return [list(range(parity, devices, 2)) for parity in range(2)]


def in_hbm(*arrays):
    return [pltpu.with_memory_space_constraint(array, pltpu.HBM) for array in arrays]


def pack_body(query_ref, key_ref, value_ref, latent_ref, *refs):
    packed_refs, (held, latent_held, sems) = refs[:-3], refs[-3:]
    heads = len(packed_refs)
    chip = lax.axis_index("seq") // 2
    token_rows = query_ref.shape[0]
    section = lax.axis_index("sect")
    wide_columns = pl.ds(pl.multiple_of(section * heads * DH, DH), heads * DH)
    copies = [
        pltpu.make_async_copy(ref.at[:, wide_columns], held.at[place], sems.at[place])
        for place, ref in enumerate((query_ref, key_ref, value_ref))
    ]
    latent_copy = pltpu.make_async_copy(latent_ref, latent_held, sems.at[3])
    latent_copy.start()
    for copy in copies:
        copy.start()
    rows, width = latent_ref.shape
    latent_copy.wait()
    half, rim = width // 2, RIM
    wide = latent_held[...].astype(jnp.float32)
    rim_zeros = jnp.zeros((rows, rim), jnp.float32)
    lower = jnp.concatenate([rim_zeros, wide[:, : half + rim]], axis=1)
    upper = jnp.concatenate([wide[:, half - rim :], rim_zeros], axis=1)
    share = jnp.where(section == 0, lower, upper)
    chunks = share.shape[1] // DH
    lines = [share[:, chunk * DH : (chunk + 1) * DH] for chunk in range(chunks)]
    spare = packed_refs[0].shape[0] - 3 * token_rows - chunks * rows
    lines.append(jnp.zeros((spare, DH), jnp.float32))
    share = jnp.concatenate(lines, axis=0).astype(jnp.bfloat16)
    for packed_ref in packed_refs:
        packed_ref[3 * token_rows :] = share
    for place, copy in enumerate(copies):
        copy.wait()
        for m, packed_ref in zip(sending_order(heads), packed_refs):
            columns = pl.ds(pl.multiple_of((chip ^ m) * DH, DH), DH)
            packed_ref[place * token_rows : (place + 1) * token_rows] = held[place, :, columns]


def pack_heads(queries, key_tokens, value_tokens, latent, token_width):
    token_rows, width = queries.shape
    sections = lax.axis_size("sect")
    heads = width // DH // sections
    span = latent.shape[1] // sections + 2 * token_width
    extra = -(-latent.shape[0] * (span // DH) // 16) * 16
    hbm = pl.BlockSpec(memory_space=pltpu.HBM)
    vmem = pl.BlockSpec(memory_space=pltpu.VMEM)
    return pl.pallas_call(
        pack_body,
        in_specs=[hbm] * 4,
        out_specs=[vmem] * heads,
        out_shape=[jax.ShapeDtypeStruct((3 * token_rows + extra, DH), queries.dtype)] * heads,
        scratch_shapes=[
            pltpu.VMEM((3, token_rows, heads * DH), queries.dtype),
            pltpu.VMEM(latent.shape, latent.dtype),
            pltpu.SemaphoreType.DMA((4,)),
        ],
        compiler_params=pltpu.CompilerParams(vmem_limit_bytes=COPY_VMEM),
        name="pack_heads",
    )(*in_hbm(queries, key_tokens, value_tokens, latent))


def sending_order(chips):
    far, near = list(range(chips // 2, chips)), list(range(1, chips // 2))
    return [0, *far[:2], *near[1:2], *far[2:], *near[2:], *near[:1]]


def xor_pairs(distance):
    return [(i, i ^ distance) for i in range(lax.axis_size("seq"))]


def flat(array):
    return array.reshape(-1, array.shape[-1])


def attend_body(*refs):
    out_ref = refs[-1]
    members, token_rows, _ = out_ref.shape
    block = min(4, members)
    chip = lax.axis_index("seq") // 2
    order = sending_order(members)
    pieces = refs[:-1]

    def rows(place, chosen):
        at = slice(place * token_rows, (place + 1) * token_rows)
        return jnp.concatenate([ref[at] for ref in chosen], axis=0)

    keys, values = rows(1, pieces), rows(2, pieces)
    for step in range(0, members, block):
        scores = lax.dot_general(
            rows(0, pieces[step : step + block]),
            keys,
            (((1,), (1,)), ((), ())),
            preferred_element_type=jnp.float32,
        ) * (1.0 / math.sqrt(DH))
        exponents = jnp.exp(scores - jnp.max(scores, axis=1, keepdims=True))
        totals = jnp.sum(exponents, axis=1, keepdims=True)
        mixed = jnp.dot(
            exponents.astype(jnp.bfloat16), values, preferred_element_type=jnp.float32
        )
        mixed = (mixed / totals).astype(out_ref.dtype)
        for m in range(block):
            out_ref[chip ^ order[step + m]] = mixed[m * token_rows : (m + 1) * token_rows]


def attend(own, other, token_rows):
    members = len(own)
    total = members * token_rows
    vmem = pl.BlockSpec(memory_space=pltpu.VMEM)
    return pl.pallas_call(
        attend_body,
        in_specs=[vmem] * (2 * members),
        out_specs=vmem,
        out_shape=jax.ShapeDtypeStruct((members, token_rows, DH), own[0].dtype),
        compiler_params=pltpu.CompilerParams(vmem_limit_bytes=ATTEND_VMEM),
        cost_estimate=pl.CostEstimate(
            flops=8 * total * total * DH,
            bytes_accessed=7 * total * DH * 2,
            transcendentals=2 * total * total,
        ),
        name="attend",
    )(*own, *other)


def unpack_body(in_ref, out_ref, sems):
    copies = [
        pltpu.make_async_copy(
            in_ref.at[head], out_ref.at[:, pl.ds(head * DH, DH)], sems.at[head]
        )
        for head in range(in_ref.shape[0])
    ]
    for copy in copies:
        copy.start()
    for copy in copies:
        copy.wait()


def unpack_heads(array):
    heads, token_rows, _ = array.shape
    return pl.pallas_call(
        unpack_body,
        in_specs=[pl.BlockSpec(memory_space=pltpu.VMEM)],
        out_specs=pl.BlockSpec(memory_space=pltpu.HBM),
        out_shape=jax.ShapeDtypeStruct((token_rows, heads * DH), array.dtype),
        scratch_shapes=[pltpu.SemaphoreType.DMA((heads,))],
        compiler_params=pltpu.CompilerParams(vmem_limit_bytes=COPY_VMEM),
        name="unpack_heads",
    )(array)


def decode_body(
    grid_rows,
    width,
    share_rows,
    members,
    *refs,
):
    pieces, refs = refs[: 2 * members], refs[2 * members :]
    order = sending_order(members)
    (
    tile_hbm,
    in_weight_hbm,
    in_bias_hbm,
    gain_hbm,
    mid_weight_hbm,
    mid_bias_hbm,
    out_hbm,
    tile_ref,
    out_ref,
    mid_weight,
    in_weight_ref,
    in_bias_ref,
    gain_ref,
    mid_bias_ref,
    taps,
    rows_held,
    patches,
    raw,
    hidden,
    activated,
    active,
    summed,
    weight_sems,
    small_sems,
    out_sems,
    ) = refs
    pairs = active.shape[1] // 16
    channels, features = in_weight_ref.shape[3:]
    columns = out_ref.shape[2]
    lane_tiles = features // 128
    position = lax.axis_index("seq")
    section = lax.axis_index("sect")
    tile_copy = pltpu.make_async_copy(tile_hbm, tile_ref, small_sems.at[4])
    tile_copy.start()
    small = [
        pltpu.make_async_copy(source, target, small_sems.at[place])
        for place, (source, target) in enumerate(
            (
                (in_weight_hbm, in_weight_ref),
                (in_bias_hbm, in_bias_ref),
                (gain_hbm, gain_ref),
                (mid_bias_hbm, mid_bias_ref),
            )
        )
    ]
    for copy in small:
        copy.start()

    def load(col_tap):
        return [
            pltpu.make_async_copy(
                mid_weight_hbm.at[tap, row_tap, col_tap],
                mid_weight.at[
                    col_tap,
                    pl.ds(row_tap * features, features),
                    pl.ds((2 - tap) * features, features),
                ],
                weight_sems.at[col_tap, row_tap, slot],
            )
            for row_tap in range(3)
            for slot, tap in enumerate(TAPS)
        ]

    for col_tap in range(3):
        for copy in load(col_tap):
            copy.start()

    tile_copy.wait()
    filled = tile_ref[position]
    first_row = lax.fori_loop(0, position, lambda d, total: total + tile_ref[d], jnp.int32(0))

    chunks = rows_held.shape[1] // 128
    extra = -(-share_rows * chunks // 16) * 16
    for place, ref in enumerate(pieces):
        lines = ref[ref.shape[0] - extra :].astype(jnp.float32)
        low = (place // members * members + order[place % members]) * share_rows
        for chunk in range(chunks):
            rows_held[low : low + share_rows, chunk * 128 : (chunk + 1) * 128] = lines[
                chunk * share_rows : (chunk + 1) * share_rows
            ]
    latent = rows_held[...]
    aside = pltpu.roll(latent, latent.shape[1] - RIM, 1).astype(jnp.bfloat16)
    latent = latent.astype(jnp.bfloat16)
    held_rows = latent.shape[0]
    unit = lax.broadcasted_iota(jnp.int32, (UNITS, held_rows), 0)
    held = lax.broadcasted_iota(jnp.int32, (UNITS, held_rows), 1)
    side = (held >= members * share_rows).astype(jnp.int32)
    member = (held // share_rows - side * members) ^ (position // 2)
    held = (2 * member + ((position & 1) ^ side)) * share_rows + held % share_rows
    frame = sum((unit >= (k + 1) * REACH).astype(jnp.int32) for k in range(LF))
    reach = unit - frame * REACH
    selectors = []
    for tap in TAPS:
        for row_parity in range(2):
            for i in range(2):
                token_row = first_row + (reach >> 1) - 1 + i
                source = frame + tap - 2
                wanted = (
                    ((reach & 1) == row_parity)
                    & (token_row >= 0)
                    & (token_row < grid_rows)
                    & (source >= 0)
                    & (source < LF)
                )
                target = jnp.where(wanted, source * grid_rows + token_row, -1)
                selectors.append(jnp.where(held == target, 1.0, 0.0).astype(jnp.bfloat16))
    selector = jnp.concatenate(selectors, axis=0)
    even = jnp.dot(selector, latent, preferred_element_type=jnp.float32)
    odd = jnp.dot(selector, aside, preferred_element_type=jnp.float32)
    for chunk in range(chunks):
        lanes = slice(chunk * 128, (chunk + 1) * 128)
        for group in range(len(selectors)):
            rows = slice(group * UNITS, (group + 1) * UNITS)
            piece = jnp.concatenate([even[rows, lanes], odd[rows, lanes]], axis=0)
            patches[
                chunk * 2 * UNITS : (chunk + 1) * 2 * UNITS, group * 128 : (group + 1) * 128
            ] = piece.astype(jnp.bfloat16)

    for copy in small:
        copy.wait()
    nothing = jnp.zeros((channels, features), jnp.bfloat16)
    base = 0
    for tap in TAPS:
        for row_parity in range(2):
            for i, j, p, q in [
                (i, j, p, q) for i in range(2) for j in range(2) for p in range(2) for q in range(2)
            ]:
                for col_parity in range(2):
                    row_tap, col_tap = 2 * i + p - row_parity, 2 * j + q - col_parity
                    inside = 0 <= row_tap < 3 and 0 <= col_tap < 3
                    taps[base : base + channels, col_parity * features : (col_parity + 1) * features] = (
                        in_weight_ref[tap, row_tap, col_tap] if inside else nothing
                    )
                base += channels

    unit_row = lax.broadcasted_iota(jnp.int32, (UNITS, 1), 0)
    row_frame = sum((unit_row >= (k + 1) * REACH).astype(jnp.int32) for k in range(LF))
    pixel_row = 2 * first_row + unit_row - row_frame * REACH - 1
    row_inside = (pixel_row >= 0) & (pixel_row < 2 * grid_rows)
    in_bias = in_bias_ref[...].reshape(1, features)
    half_gain = gain_ref[...].reshape(1, features) * 0.5

    def first_layer(chunk):
        for corner in range(2):
            start = (chunk * 2 + corner) * UNITS
            for col_parity in range(2):
                value = (
                    raw[pl.ds(start, UNITS), col_parity * features : (col_parity + 1) * features]
                    + in_bias
                )
                value = value.astype(jnp.bfloat16).astype(jnp.float32)
                scale = lax.rsqrt(jnp.mean(value * value, axis=1, keepdims=True) + 1e-06)
                column = chunk * 4 + corner * 2 + col_parity
                pixel = section * columns + column - 1
                keep = row_inside & (pixel >= 0) & (pixel < width)
                half = value * jnp.where(keep, scale, 0.0) * half_gain
                result = half + half * jnp.tanh(half)
                at = pl.ds(column * UNITS, UNITS)
                for lane in range(lane_tiles):
                    lanes = slice(lane * 128, (lane + 1) * 128)
                    hidden[lane, at] = value[:, lanes]
                    activated[lane, at] = result[:, lanes]

    middle = (chunks + 1) // 2
    groups = ((0, middle), (middle, chunks))
    for low, high in groups:
        rows = slice(low * 2 * UNITS, high * 2 * UNITS)
        raw[rows] = jnp.dot(patches[rows], taps[...], preferred_element_type=jnp.float32)
    for low, high in groups:
        for chunk in range(low, high):
            first_layer(chunk)

    def pair_up(phase, pair):
        at = slice(pair * 16, pair * 16 + 16)
        for lane in range(lane_tiles):
            for field in range(LF):
                for row_tap in range(3):
                    start = (2 * pair + phase) * UNITS + field * REACH + row_tap
                    joined = jnp.concatenate(
                        [activated[lane, pl.ds(start + k * UNITS, ROWS)] for k in range(2)], axis=0
                    )
                    to_lane = (field * 3 + row_tap) * features + lane * 128
                    active[phase, at, to_lane : to_lane + 128] = joined.astype(jnp.bfloat16)

    rows = columns * ROWS
    depth = 3 * features

    def windows(low, high, lanes):
        return jnp.concatenate(
            [
                active[tap % 2, 16 * (tap // 2) + low : 16 * (tap // 2) + high, lanes]
                for tap in range(3)
            ],
            axis=1,
        )

    def weights(lanes):
        return jnp.concatenate([mid_weight[tap, :, lanes] for tap in range(3)], axis=0)

    mid_bias = mid_bias_ref[...].reshape(1, features)

    def finish(field):
        tile_row = lax.broadcasted_iota(jnp.int32, (columns * ROWS, 128), 0) & (ROWS - 1)
        for lane in range(lane_tiles):
            lanes = slice(lane * 128, (lane + 1) * 128)
            skip = jnp.concatenate(
                [
                    hidden[lane, pl.ds((column + 1) * UNITS + field * REACH + 1, ROWS)]
                    for column in range(columns)
                ],
                axis=0,
            )
            value = summed[field, lane] + skip + mid_bias[:, lanes]
            value = jnp.where(tile_row < 2 * filled, value, 0.0)
            value = jnp.swapaxes(value.reshape(columns, ROWS, 128), 0, 1)
            out_ref[field, :, :, lanes] = value.astype(jnp.bfloat16)
        leave(field).start()

    def leave(field):
        return pltpu.make_async_copy(out_ref.at[field], out_hbm.at[field], out_sems.at[field])

    for phase in range(2):
        for pair in range(pairs - phase):
            pair_up(phase, pair)
    for tap in range(3):
        for copy in load(tap):
            copy.wait()
    early = windows(0, rows, slice(0, depth))
    late = windows(0, rows, slice(depth, 2 * depth))
    for left in range(0, 2 * features, 256):
        block = jnp.dot(
            early, weights(slice(left, left + 256)), preferred_element_type=jnp.float32
        )
        for lane in range(2):
            field, tile = divmod(left // 128 + lane, lane_tiles)
            summed[field, tile] = block[:, lane * 128 : (lane + 1) * 128]
    finish(0)
    for left in range(0, features, 256):
        right = min(left + 256, features)
        block = jnp.dot(late, weights(slice(left, right)), preferred_element_type=jnp.float32)
        for lane in range((right - left) // 128):
            tile = left // 128 + lane
            summed[1, tile] = summed[1, tile] + block[:, lane * 128 : (lane + 1) * 128]
    finish(1)
    for field in range(LF):
        leave(field).wait()


def decode_tile(
    own,
    other,
    share_rows,
    grid_rows,
    width,
    tile_rows,
    conv_in_weight,
    conv_in_bias,
    norm_gain,
    conv_mid_weight,
    conv_mid_bias,
):
    sections = lax.axis_size("sect")
    channels, features = conv_in_weight.shape[3:]
    token_width = 4 * channels
    columns = width // sections
    span = columns // 2
    pairs = span + 1
    chunks = (span + 2) * token_width // 128
    lane_tiles = features // 128
    vmem = pl.BlockSpec(memory_space=pltpu.VMEM)
    hbm = pl.BlockSpec(memory_space=pltpu.HBM)
    slots = len(TAPS)
    depth = slots * 2 * 4 * token_width
    held = chunks * 4 * UNITS
    return pl.pallas_call(
        functools.partial(decode_body, grid_rows, width, share_rows, len(own)),
        in_specs=[vmem] * (2 * len(own)) + [hbm] * 6,
        out_specs=hbm,
        out_shape=jax.ShapeDtypeStruct((LF, ROWS, columns, features), jnp.bfloat16),
        scratch_shapes=[
            pltpu.SMEM(tile_rows.shape, tile_rows.dtype),
            pltpu.VMEM((LF, ROWS, columns, features), jnp.bfloat16),
            pltpu.VMEM((3, 3 * features, slots * features), jnp.bfloat16),
            pltpu.VMEM(conv_in_weight.shape, jnp.bfloat16),
            pltpu.VMEM(conv_in_bias.shape, jnp.float32),
            pltpu.VMEM(norm_gain.shape, jnp.float32),
            pltpu.VMEM(conv_mid_bias.shape, jnp.float32),
            pltpu.VMEM((depth, 2 * features), jnp.bfloat16),
            pltpu.VMEM((2 * len(own) * share_rows, chunks * 128), jnp.float32),
            pltpu.VMEM((chunks * 2 * UNITS, depth), jnp.bfloat16),
            pltpu.VMEM((chunks * 2 * UNITS, 2 * features), jnp.float32),
            pltpu.VMEM((lane_tiles, held, 128), jnp.float32),
            pltpu.VMEM((lane_tiles, held, 128), jnp.float32),
            pltpu.VMEM((2, pairs * 16, LF * 3 * features), jnp.bfloat16),
            pltpu.VMEM((LF, lane_tiles, columns * ROWS, 128), jnp.float32),
            pltpu.SemaphoreType.DMA((3, 3, slots)),
            pltpu.SemaphoreType.DMA((5,)),
            pltpu.SemaphoreType.DMA((LF,)),
        ],
        compiler_params=pltpu.CompilerParams(vmem_limit_bytes=DECODE_VMEM),
        cost_estimate=pl.CostEstimate(
            flops=2 * 3 * 9 * columns * ROWS * features * features,
            bytes_accessed=slots * 9 * features * features * 2,
            transcendentals=held * features,
        ),
        name="decode_tile",
    )(
        *own,
        *other,
        *in_hbm(
            tile_rows, conv_in_weight, conv_in_bias, norm_gain, conv_mid_weight, conv_mid_bias
        ),
    )


def on_device(
    queries,
    key_tokens,
    value_tokens,
    latent,
    tile_rows,
    conv_in_weight,
    conv_in_bias,
    norm_gain,
    conv_mid_weight,
    conv_mid_bias,
):
    devices = lax.axis_size("seq")
    groups = parity_groups(devices)
    grid_rows = latent.shape[0] * devices // LF
    token_width = 4 * conv_in_weight.shape[3]
    packed = pack_heads(queries, key_tokens, value_tokens, latent, token_width)
    own = [
        lax.ppermute(piece, "seq", xor_pairs(2 * m)) if m else piece
        for m, piece in zip(sending_order(len(packed)), packed)
    ]
    other = [lax.ppermute(piece, "seq", xor_pairs(1)) for piece in own]
    mixed = attend(own, other, queries.shape[0])
    returned = lax.all_to_all(mixed, "seq", 0, 0, axis_index_groups=groups, tiled=True)
    frames = decode_tile(
        own,
        other,
        latent.shape[0],
        grid_rows,
        2 * latent.shape[1] // token_width,
        tile_rows,
        conv_in_weight,
        conv_in_bias,
        norm_gain,
        conv_mid_weight,
        conv_mid_bias,
    )
    return (unpack_heads(returned), frames)


def solution(mesh):
    in_specs = (
        P("seq", None),
        P("seq", None),
        P("seq", None),
        P("seq", None),
        P(),
        P(),
        P(),
        P(),
        P(),
        P(),
    )
    out_specs = (P("seq", "sect"), P(None, "seq", "sect", None))
    return jax.shard_map(
        on_device, mesh=mesh, in_specs=in_specs, out_specs=out_specs, check_vma=False
    )
```

```python
import functools
import math

import jax
import jax.numpy as jnp
from jax import lax
from jax.experimental import pallas as pl
from jax.experimental.pallas import tpu as pltpu
from jax.sharding import PartitionSpec as P

DH = 128
LF = 2
MAXT = 4
RIM = 64
TAPS = (1, 2)
ROWS = 2 * MAXT
REACH = ROWS + 2
UNITS = -(-LF * REACH // 8) * 8
DECODE_VMEM = 32 * 1024 * 1024
ATTEND_VMEM = 32 * 1024 * 1024
COPY_VMEM = 16 * 1024 * 1024


def parity_groups(devices):
    return [list(range(parity, devices, 2)) for parity in range(2)]


def in_hbm(*arrays):
    return [pltpu.with_memory_space_constraint(array, pltpu.HBM) for array in arrays]


def pack_body(query_ref, key_ref, value_ref, latent_ref, *refs):
    packed_refs, (held, latent_held, sems) = refs[:-3], refs[-3:]
    heads = len(packed_refs)
    chip = lax.axis_index("seq") // 2
    token_rows = query_ref.shape[0]
    section = lax.axis_index("sect")
    wide_columns = pl.ds(pl.multiple_of(section * heads * DH, DH), heads * DH)
    copies = [
        pltpu.make_async_copy(ref.at[:, wide_columns], held.at[place], sems.at[place])
        for place, ref in enumerate((query_ref, key_ref, value_ref))
    ]
    latent_copy = pltpu.make_async_copy(latent_ref, latent_held, sems.at[3])
    latent_copy.start()
    for copy in copies:
        copy.start()
    rows, width = latent_ref.shape
    latent_copy.wait()
    half, rim = width // 2, RIM
    wide = latent_held[...].astype(jnp.float32)
    rim_zeros = jnp.zeros((rows, rim), jnp.float32)
    lower = jnp.concatenate([rim_zeros, wide[:, : half + rim]], axis=1)
    upper = jnp.concatenate([wide[:, half - rim :], rim_zeros], axis=1)
    share = jnp.where(section == 0, lower, upper)
    chunks = share.shape[1] // DH
    lines = [share[:, chunk * DH : (chunk + 1) * DH] for chunk in range(chunks)]
    spare = packed_refs[0].shape[0] - 3 * token_rows - chunks * rows
    lines.append(jnp.zeros((spare, DH), jnp.float32))
    share = jnp.concatenate(lines, axis=0).astype(jnp.bfloat16)
    for packed_ref in packed_refs:
        packed_ref[3 * token_rows :] = share
    for place, copy in enumerate(copies):
        copy.wait()
        for m, packed_ref in zip(sending_order(heads), packed_refs):
            columns = pl.ds(pl.multiple_of((chip ^ m) * DH, DH), DH)
            packed_ref[place * token_rows : (place + 1) * token_rows] = held[place, :, columns]


def pack_heads(queries, key_tokens, value_tokens, latent, token_width):
    token_rows, width = queries.shape
    sections = lax.axis_size("sect")
    heads = width // DH // sections
    span = latent.shape[1] // sections + 2 * token_width
    extra = -(-latent.shape[0] * (span // DH) // 16) * 16
    hbm = pl.BlockSpec(memory_space=pltpu.HBM)
    vmem = pl.BlockSpec(memory_space=pltpu.VMEM)
    return pl.pallas_call(
        pack_body,
        in_specs=[hbm] * 4,
        out_specs=[vmem] * heads,
        out_shape=[jax.ShapeDtypeStruct((3 * token_rows + extra, DH), queries.dtype)] * heads,
        scratch_shapes=[
            pltpu.VMEM((3, token_rows, heads * DH), queries.dtype),
            pltpu.VMEM(latent.shape, latent.dtype),
            pltpu.SemaphoreType.DMA((4,)),
        ],
        compiler_params=pltpu.CompilerParams(vmem_limit_bytes=COPY_VMEM),
        name="pack_heads",
    )(*in_hbm(queries, key_tokens, value_tokens, latent))


def sending_order(chips):
    far, near = list(range(chips // 2, chips)), list(range(1, chips // 2))
    return [0, *far[:2], *near[1:2], *far[2:], *near[2:], *near[:1]]


def xor_pairs(distance):
    return [(i, i ^ distance) for i in range(lax.axis_size("seq"))]


def join_body(count, *refs):
    out_ref = refs[-1]
    for place, ref in enumerate(refs[:count]):
        out_ref[place] = ref[ref.shape[0] - out_ref.shape[1] :]


def join(pieces, earlier, skipped):
    rows, width = pieces[0].shape
    vmem = pl.BlockSpec(memory_space=pltpu.VMEM)
    return pl.pallas_call(
        functools.partial(join_body, len(pieces)),
        in_specs=[vmem] * len(pieces) + [pl.BlockSpec(memory_space=pl.ANY)] * len(earlier),
        out_specs=vmem,
        out_shape=jax.ShapeDtypeStruct((len(pieces), rows - skipped, width), pieces[0].dtype),
        compiler_params=pltpu.CompilerParams(vmem_limit_bytes=COPY_VMEM),
        name="join",
    )(*pieces, *earlier)


def flat(array):
    return array.reshape(-1, array.shape[-1])


def attend_body(*refs):
    out_hbm, out_ref, sems = refs[-3:]
    members, token_rows, _ = out_ref.shape
    block = min(4, members)
    chip = lax.axis_index("seq") // 2
    order = sending_order(members)
    own, other = refs[:members], refs[members:-3]

    def rows(place, chosen):
        at = slice(place * token_rows, (place + 1) * token_rows)
        return jnp.concatenate([ref[at] for ref in chosen], axis=0)

    def both(place):
        at = slice((place - 1) * token_rows, place * token_rows)
        return jnp.concatenate([rows(place, own)] + [flat(ref[:, at]) for ref in other], axis=0)

    def leave(m):
        target = out_hbm.at[chip ^ order[m]]
        return pltpu.make_async_copy(out_ref.at[m], target, sems.at[m])

    keys, values = both(1), both(2)
    for step in range(0, members, block):
        scores = lax.dot_general(
            rows(0, own[step : step + block]),
            keys,
            (((1,), (1,)), ((), ())),
            preferred_element_type=jnp.float32,
        ) * (1.0 / math.sqrt(DH))
        exponents = jnp.exp(scores - jnp.max(scores, axis=1, keepdims=True))
        totals = jnp.sum(exponents, axis=1, keepdims=True)
        mixed = jnp.dot(
            exponents.astype(jnp.bfloat16), values, preferred_element_type=jnp.float32
        )
        mixed = (mixed / totals).astype(out_ref.dtype)
        for m in range(block):
            out_ref[step + m] = mixed[m * token_rows : (m + 1) * token_rows]
            leave(step + m).start()
    for m in range(members):
        leave(m).wait()


def attend(own, other, token_rows):
    members = len(own)
    total = members * token_rows
    vmem = pl.BlockSpec(memory_space=pltpu.VMEM)
    return pl.pallas_call(
        attend_body,
        in_specs=[vmem] * (members + len(other)),
        out_specs=pl.BlockSpec(memory_space=pltpu.HBM),
        out_shape=jax.ShapeDtypeStruct((members, token_rows, DH), own[0].dtype),
        scratch_shapes=[
            pltpu.VMEM((members, token_rows, DH), own[0].dtype),
            pltpu.SemaphoreType.DMA((members,)),
        ],
        compiler_params=pltpu.CompilerParams(vmem_limit_bytes=ATTEND_VMEM),
        cost_estimate=pl.CostEstimate(
            flops=8 * total * total * DH,
            bytes_accessed=7 * total * DH * 2,
            transcendentals=2 * total * total,
        ),
        name="attend",
    )(*own, *other)


def unpack_body(in_ref, out_ref, sems):
    copies = [
        pltpu.make_async_copy(
            in_ref.at[head], out_ref.at[:, pl.ds(head * DH, DH)], sems.at[head]
        )
        for head in range(in_ref.shape[0])
    ]
    for copy in copies:
        copy.start()
    for copy in copies:
        copy.wait()


def unpack_heads(array):
    heads, token_rows, _ = array.shape
    return pl.pallas_call(
        unpack_body,
        in_specs=[pl.BlockSpec(memory_space=pltpu.VMEM)],
        out_specs=pl.BlockSpec(memory_space=pltpu.HBM),
        out_shape=jax.ShapeDtypeStruct((token_rows, heads * DH), array.dtype),
        scratch_shapes=[pltpu.SemaphoreType.DMA((heads,))],
        compiler_params=pltpu.CompilerParams(vmem_limit_bytes=COPY_VMEM),
        name="unpack_heads",
    )(array)


def decode_body(
    grid_rows,
    width,
    share_rows,
    members,
    halves,
    *refs,
):
    own, other, refs = refs[:members], refs[members : members + halves], refs[members + halves :]
    order = sending_order(members)
    (
    tile_hbm,
    in_weight_hbm,
    in_bias_hbm,
    gain_hbm,
    mid_weight_hbm,
    mid_bias_hbm,
    out_hbm,
    tile_ref,
    out_ref,
    mid_weight,
    in_weight_ref,
    in_bias_ref,
    gain_ref,
    mid_bias_ref,
    taps,
    rows_held,
    patches,
    raw,
    hidden,
    activated,
    active,
    summed,
    weight_sems,
    small_sems,
    out_sems,
    ) = refs
    pairs = active.shape[1] // 16
    channels, features = in_weight_ref.shape[3:]
    columns = out_ref.shape[2]
    lane_tiles = features // 128
    position = lax.axis_index("seq")
    section = lax.axis_index("sect")
    tile_copy = pltpu.make_async_copy(tile_hbm, tile_ref, small_sems.at[4])
    tile_copy.start()
    small = [
        pltpu.make_async_copy(source, target, small_sems.at[place])
        for place, (source, target) in enumerate(
            (
                (in_weight_hbm, in_weight_ref),
                (in_bias_hbm, in_bias_ref),
                (gain_hbm, gain_ref),
                (mid_bias_hbm, mid_bias_ref),
            )
        )
    ]
    for copy in small:
        copy.start()

    def load(col_tap):
        return [
            pltpu.make_async_copy(
                mid_weight_hbm.at[tap, row_tap, col_tap],
                mid_weight.at[
                    col_tap,
                    pl.ds(row_tap * features, features),
                    pl.ds((2 - tap) * features, features),
                ],
                weight_sems.at[col_tap, row_tap, slot],
            )
            for row_tap in range(3)
            for slot, tap in enumerate(TAPS)
        ]

    for col_tap in range(3):
        for copy in load(col_tap):
            copy.start()

    tile_copy.wait()
    filled = tile_ref[position]
    first_row = lax.fori_loop(0, position, lambda d, total: total + tile_ref[d], jnp.int32(0))

    chunks = rows_held.shape[1] // 128
    extra = -(-share_rows * chunks // 16) * 16
    shares = [ref[ref.shape[0] - extra :] for ref in own]
    shares += [ref[m, ref.shape[1] - extra :] for ref in other for m in range(ref.shape[0])]
    for place, share in enumerate(shares):
        lines = share.astype(jnp.float32)
        low = (place // members * members + order[place % members]) * share_rows
        for chunk in range(chunks):
            rows_held[low : low + share_rows, chunk * 128 : (chunk + 1) * 128] = lines[
                chunk * share_rows : (chunk + 1) * share_rows
            ]
    latent = rows_held[...]
    aside = pltpu.roll(latent, latent.shape[1] - RIM, 1).astype(jnp.bfloat16)
    latent = latent.astype(jnp.bfloat16)
    held_rows = latent.shape[0]
    unit = lax.broadcasted_iota(jnp.int32, (UNITS, held_rows), 0)
    held = lax.broadcasted_iota(jnp.int32, (UNITS, held_rows), 1)
    side = (held >= members * share_rows).astype(jnp.int32)
    member = (held // share_rows - side * members) ^ (position // 2)
    held = (2 * member + ((position & 1) ^ side)) * share_rows + held % share_rows
    frame = sum((unit >= (k + 1) * REACH).astype(jnp.int32) for k in range(LF))
    reach = unit - frame * REACH
    selectors = []
    for tap in TAPS:
        for row_parity in range(2):
            for i in range(2):
                token_row = first_row + (reach >> 1) - 1 + i
                source = frame + tap - 2
                wanted = (
                    ((reach & 1) == row_parity)
                    & (token_row >= 0)
                    & (token_row < grid_rows)
                    & (source >= 0)
                    & (source < LF)
                )
                target = jnp.where(wanted, source * grid_rows + token_row, -1)
                selectors.append(jnp.where(held == target, 1.0, 0.0).astype(jnp.bfloat16))
    selector = jnp.concatenate(selectors, axis=0)
    even = jnp.dot(selector, latent, preferred_element_type=jnp.float32)
    odd = jnp.dot(selector, aside, preferred_element_type=jnp.float32)
    for chunk in range(chunks):
        lanes = slice(chunk * 128, (chunk + 1) * 128)
        for group in range(len(selectors)):
            rows = slice(group * UNITS, (group + 1) * UNITS)
            piece = jnp.concatenate([even[rows, lanes], odd[rows, lanes]], axis=0)
            patches[
                chunk * 2 * UNITS : (chunk + 1) * 2 * UNITS, group * 128 : (group + 1) * 128
            ] = piece.astype(jnp.bfloat16)

    for copy in small:
        copy.wait()
    nothing = jnp.zeros((channels, features), jnp.bfloat16)
    base = 0
    for tap in TAPS:
        for row_parity in range(2):
            for i, j, p, q in [
                (i, j, p, q) for i in range(2) for j in range(2) for p in range(2) for q in range(2)
            ]:
                for col_parity in range(2):
                    row_tap, col_tap = 2 * i + p - row_parity, 2 * j + q - col_parity
                    inside = 0 <= row_tap < 3 and 0 <= col_tap < 3
                    taps[base : base + channels, col_parity * features : (col_parity + 1) * features] = (
                        in_weight_ref[tap, row_tap, col_tap] if inside else nothing
                    )
                base += channels

    unit_row = lax.broadcasted_iota(jnp.int32, (UNITS, 1), 0)
    row_frame = sum((unit_row >= (k + 1) * REACH).astype(jnp.int32) for k in range(LF))
    pixel_row = 2 * first_row + unit_row - row_frame * REACH - 1
    row_inside = (pixel_row >= 0) & (pixel_row < 2 * grid_rows)
    in_bias = in_bias_ref[...].reshape(1, features)
    half_gain = gain_ref[...].reshape(1, features) * 0.5

    def first_layer(chunk):
        for corner in range(2):
            start = (chunk * 2 + corner) * UNITS
            for col_parity in range(2):
                value = (
                    raw[pl.ds(start, UNITS), col_parity * features : (col_parity + 1) * features]
                    + in_bias
                )
                value = value.astype(jnp.bfloat16).astype(jnp.float32)
                scale = lax.rsqrt(jnp.mean(value * value, axis=1, keepdims=True) + 1e-06)
                column = chunk * 4 + corner * 2 + col_parity
                pixel = section * columns + column - 1
                keep = row_inside & (pixel >= 0) & (pixel < width)
                half = value * jnp.where(keep, scale, 0.0) * half_gain
                result = half + half * jnp.tanh(half)
                at = pl.ds(column * UNITS, UNITS)
                for lane in range(lane_tiles):
                    lanes = slice(lane * 128, (lane + 1) * 128)
                    hidden[lane, at] = value[:, lanes]
                    activated[lane, at] = result[:, lanes]

    middle = (chunks + 1) // 2
    groups = ((0, middle), (middle, chunks))
    for low, high in groups:
        rows = slice(low * 2 * UNITS, high * 2 * UNITS)
        raw[rows] = jnp.dot(patches[rows], taps[...], preferred_element_type=jnp.float32)
    for low, high in groups:
        for chunk in range(low, high):
            first_layer(chunk)

    def pair_up(phase, pair):
        at = slice(pair * 16, pair * 16 + 16)
        for lane in range(lane_tiles):
            for field in range(LF):
                for row_tap in range(3):
                    start = (2 * pair + phase) * UNITS + field * REACH + row_tap
                    joined = jnp.concatenate(
                        [activated[lane, pl.ds(start + k * UNITS, ROWS)] for k in range(2)], axis=0
                    )
                    to_lane = (field * 3 + row_tap) * features + lane * 128
                    active[phase, at, to_lane : to_lane + 128] = joined.astype(jnp.bfloat16)

    rows = columns * ROWS
    depth = 3 * features

    def windows(low, high, lanes):
        return jnp.concatenate(
            [
                active[tap % 2, 16 * (tap // 2) + low : 16 * (tap // 2) + high, lanes]
                for tap in range(3)
            ],
            axis=1,
        )

    def weights(lanes):
        return jnp.concatenate([mid_weight[tap, :, lanes] for tap in range(3)], axis=0)

    mid_bias = mid_bias_ref[...].reshape(1, features)

    def finish(field):
        tile_row = lax.broadcasted_iota(jnp.int32, (columns * ROWS, 128), 0) & (ROWS - 1)
        for lane in range(lane_tiles):
            lanes = slice(lane * 128, (lane + 1) * 128)
            skip = jnp.concatenate(
                [
                    hidden[lane, pl.ds((column + 1) * UNITS + field * REACH + 1, ROWS)]
                    for column in range(columns)
                ],
                axis=0,
            )
            value = summed[field, lane] + skip + mid_bias[:, lanes]
            value = jnp.where(tile_row < 2 * filled, value, 0.0)
            value = jnp.swapaxes(value.reshape(columns, ROWS, 128), 0, 1)
            out_ref[field, :, :, lanes] = value.astype(jnp.bfloat16)
        leave(field).start()

    def leave(field):
        return pltpu.make_async_copy(out_ref.at[field], out_hbm.at[field], out_sems.at[field])

    for phase in range(2):
        for pair in range(pairs - phase):
            pair_up(phase, pair)
    for tap in range(3):
        for copy in load(tap):
            copy.wait()
    early = windows(0, rows, slice(0, depth))
    late = windows(0, rows, slice(depth, 2 * depth))
    for left in range(0, 2 * features, 256):
        block = jnp.dot(
            early, weights(slice(left, left + 256)), preferred_element_type=jnp.float32
        )
        for lane in range(2):
            field, tile = divmod(left // 128 + lane, lane_tiles)
            summed[field, tile] = block[:, lane * 128 : (lane + 1) * 128]
    finish(0)
    for left in range(0, features, 256):
        right = min(left + 256, features)
        block = jnp.dot(late, weights(slice(left, right)), preferred_element_type=jnp.float32)
        for lane in range((right - left) // 128):
            tile = left // 128 + lane
            summed[1, tile] = summed[1, tile] + block[:, lane * 128 : (lane + 1) * 128]
    finish(1)
    for field in range(LF):
        leave(field).wait()


def decode_tile(
    own,
    other,
    share_rows,
    grid_rows,
    width,
    tile_rows,
    conv_in_weight,
    conv_in_bias,
    norm_gain,
    conv_mid_weight,
    conv_mid_bias,
):
    sections = lax.axis_size("sect")
    channels, features = conv_in_weight.shape[3:]
    token_width = 4 * channels
    columns = width // sections
    span = columns // 2
    pairs = span + 1
    chunks = (span + 2) * token_width // 128
    lane_tiles = features // 128
    vmem = pl.BlockSpec(memory_space=pltpu.VMEM)
    hbm = pl.BlockSpec(memory_space=pltpu.HBM)
    slots = len(TAPS)
    depth = slots * 2 * 4 * token_width
    held = chunks * 4 * UNITS
    return pl.pallas_call(
        functools.partial(decode_body, grid_rows, width, share_rows, len(own), len(other)),
        in_specs=[vmem] * (len(own) + len(other)) + [hbm] * 6,
        out_specs=hbm,
        out_shape=jax.ShapeDtypeStruct((LF, ROWS, columns, features), jnp.bfloat16),
        scratch_shapes=[
            pltpu.SMEM(tile_rows.shape, tile_rows.dtype),
            pltpu.VMEM((LF, ROWS, columns, features), jnp.bfloat16),
            pltpu.VMEM((3, 3 * features, slots * features), jnp.bfloat16),
            pltpu.VMEM(conv_in_weight.shape, jnp.bfloat16),
            pltpu.VMEM(conv_in_bias.shape, jnp.float32),
            pltpu.VMEM(norm_gain.shape, jnp.float32),
            pltpu.VMEM(conv_mid_bias.shape, jnp.float32),
            pltpu.VMEM((depth, 2 * features), jnp.bfloat16),
            pltpu.VMEM((2 * len(own) * share_rows, chunks * 128), jnp.float32),
            pltpu.VMEM((chunks * 2 * UNITS, depth), jnp.bfloat16),
            pltpu.VMEM((chunks * 2 * UNITS, 2 * features), jnp.float32),
            pltpu.VMEM((lane_tiles, held, 128), jnp.float32),
            pltpu.VMEM((lane_tiles, held, 128), jnp.float32),
            pltpu.VMEM((2, pairs * 16, LF * 3 * features), jnp.bfloat16),
            pltpu.VMEM((LF, lane_tiles, columns * ROWS, 128), jnp.float32),
            pltpu.SemaphoreType.DMA((3, 3, slots)),
            pltpu.SemaphoreType.DMA((5,)),
            pltpu.SemaphoreType.DMA((LF,)),
        ],
        compiler_params=pltpu.CompilerParams(vmem_limit_bytes=DECODE_VMEM),
        cost_estimate=pl.CostEstimate(
            flops=2 * 3 * 9 * columns * ROWS * features * features,
            bytes_accessed=slots * 9 * features * features * 2,
            transcendentals=held * features,
        ),
        name="decode_tile",
    )(
        *own,
        *other,
        *in_hbm(
            tile_rows, conv_in_weight, conv_in_bias, norm_gain, conv_mid_weight, conv_mid_bias
        ),
    )


def on_device(
    queries,
    key_tokens,
    value_tokens,
    latent,
    tile_rows,
    conv_in_weight,
    conv_in_bias,
    norm_gain,
    conv_mid_weight,
    conv_mid_bias,
):
    devices = lax.axis_size("seq")
    groups = parity_groups(devices)
    grid_rows = latent.shape[0] * devices // LF
    token_width = 4 * conv_in_weight.shape[3]
    packed = pack_heads(queries, key_tokens, value_tokens, latent, token_width)
    own = [
        lax.ppermute(piece, "seq", xor_pairs(2 * m)) if m else piece
        for m, piece in zip(sending_order(len(packed)), packed)
    ]
    half, other = len(own) // 2, []
    for low in (0, half):
        joined = join(own[low : low + half], other[-1:], queries.shape[0])
        other.append(lax.ppermute(joined, "seq", xor_pairs(1)))
    mixed = attend(own, other, queries.shape[0])
    returned = lax.all_to_all(mixed, "seq", 0, 0, axis_index_groups=groups, tiled=True)
    frames = decode_tile(
        own,
        other,
        latent.shape[0],
        grid_rows,
        2 * latent.shape[1] // token_width,
        tile_rows,
        conv_in_weight,
        conv_in_bias,
        norm_gain,
        conv_mid_weight,
        conv_mid_bias,
    )
    return (unpack_heads(returned), frames)


def solution(mesh):
    in_specs = (
        P("seq", None),
        P("seq", None),
        P("seq", None),
        P("seq", None),
        P(),
        P(),
        P(),
        P(),
        P(),
        P(),
    )
    out_specs = (P("seq", "sect"), P(None, "seq", "sect", None))
    return jax.shard_map(
        on_device, mesh=mesh, in_specs=in_specs, out_specs=out_specs, check_vma=False
    )
```

```python
import functools
import math

import jax
import jax.numpy as jnp
from jax import lax
from jax.experimental import pallas as pl
from jax.experimental.pallas import tpu as pltpu
from jax.sharding import PartitionSpec as P

DH = 128
LF = 2
MAXT = 4
RIM = 64
TAPS = (1, 2)
ROWS = 2 * MAXT
REACH = ROWS + 2
UNITS = -(-LF * REACH // 8) * 8
DECODE_VMEM = 32 * 1024 * 1024
ATTEND_VMEM = 32 * 1024 * 1024
COPY_VMEM = 16 * 1024 * 1024


def parity_groups(devices):
    return [list(range(parity, devices, 2)) for parity in range(2)]


def in_hbm(*arrays):
    return [pltpu.with_memory_space_constraint(array, pltpu.HBM) for array in arrays]


def pack_body(query_ref, key_ref, value_ref, latent_ref, *refs):
    packed_refs, (held, latent_held, sems) = refs[:-3], refs[-3:]
    heads = len(packed_refs)
    chip = lax.axis_index("seq") // 2
    token_rows = query_ref.shape[0]
    section = lax.axis_index("sect")
    wide_columns = pl.ds(pl.multiple_of(section * heads * DH, DH), heads * DH)
    copies = [
        pltpu.make_async_copy(ref.at[:, wide_columns], held.at[place], sems.at[place])
        for place, ref in enumerate((query_ref, key_ref, value_ref))
    ]
    latent_copy = pltpu.make_async_copy(latent_ref, latent_held, sems.at[3])
    latent_copy.start()
    for copy in copies:
        copy.start()
    rows, width = latent_ref.shape
    latent_copy.wait()
    half, rim = width // 2, RIM
    wide = latent_held[...].astype(jnp.float32)
    rim_zeros = jnp.zeros((rows, rim), jnp.float32)
    lower = jnp.concatenate([rim_zeros, wide[:, : half + rim]], axis=1)
    upper = jnp.concatenate([wide[:, half - rim :], rim_zeros], axis=1)
    share = jnp.where(section == 0, lower, upper)
    chunks = share.shape[1] // DH
    lines = [share[:, chunk * DH : (chunk + 1) * DH] for chunk in range(chunks)]
    spare = packed_refs[0].shape[0] - 3 * token_rows - chunks * rows
    lines.append(jnp.zeros((spare, DH), jnp.float32))
    share = jnp.concatenate(lines, axis=0).astype(jnp.bfloat16)
    for packed_ref in packed_refs:
        packed_ref[3 * token_rows :] = share
    for place, copy in enumerate(copies):
        copy.wait()
        for m, packed_ref in zip(sending_order(heads), packed_refs):
            columns = pl.ds(pl.multiple_of((chip ^ m) * DH, DH), DH)
            packed_ref[place * token_rows : (place + 1) * token_rows] = held[place, :, columns]


def pack_heads(queries, key_tokens, value_tokens, latent, token_width):
    token_rows, width = queries.shape
    sections = lax.axis_size("sect")
    heads = width // DH // sections
    span = latent.shape[1] // sections + 2 * token_width
    extra = -(-latent.shape[0] * (span // DH) // 16) * 16
    hbm = pl.BlockSpec(memory_space=pltpu.HBM)
    vmem = pl.BlockSpec(memory_space=pltpu.VMEM)
    return pl.pallas_call(
        pack_body,
        in_specs=[hbm] * 4,
        out_specs=[vmem] * heads,
        out_shape=[jax.ShapeDtypeStruct((3 * token_rows + extra, DH), queries.dtype)] * heads,
        scratch_shapes=[
            pltpu.VMEM((3, token_rows, heads * DH), queries.dtype),
            pltpu.VMEM(latent.shape, latent.dtype),
            pltpu.SemaphoreType.DMA((4,)),
        ],
        compiler_params=pltpu.CompilerParams(vmem_limit_bytes=COPY_VMEM),
        name="pack_heads",
    )(*in_hbm(queries, key_tokens, value_tokens, latent))


def sending_order(chips):
    far, near = list(range(chips // 2, chips)), list(range(1, chips // 2))
    return [0, *far[:2], *near[1:2], *far[2:], *near[2:], *near[:1]]


def xor_pairs(distance):
    return [(i, i ^ distance) for i in range(lax.axis_size("seq"))]


def join_body(*refs):
    out_ref = refs[-1]
    for place, ref in enumerate(refs[:-1]):
        out_ref[place] = ref[ref.shape[0] - out_ref.shape[1] :]


def join(pieces, skipped):
    rows, width = pieces[0].shape
    vmem = pl.BlockSpec(memory_space=pltpu.VMEM)
    return pl.pallas_call(
        join_body,
        in_specs=[vmem] * len(pieces),
        out_specs=vmem,
        out_shape=jax.ShapeDtypeStruct((len(pieces), rows - skipped, width), pieces[0].dtype),
        compiler_params=pltpu.CompilerParams(vmem_limit_bytes=COPY_VMEM),
        name="join",
    )(*pieces)


def flat(array):
    return array.reshape(-1, array.shape[-1])


def attend_body(*refs):
    out_hbm, out_ref, sems = refs[-3:]
    members, token_rows, _ = out_ref.shape
    block = min(4, members)
    chip = lax.axis_index("seq") // 2
    order = sending_order(members)
    own, other = refs[:members], refs[members:-3]

    def rows(place, chosen):
        at = slice(place * token_rows, (place + 1) * token_rows)
        return jnp.concatenate([ref[at] for ref in chosen], axis=0)

    def both(place):
        at = slice((place - 1) * token_rows, place * token_rows)
        return jnp.concatenate([rows(place, own)] + [flat(ref[:, at]) for ref in other], axis=0)

    def leave(m):
        target = out_hbm.at[chip ^ order[m]]
        return pltpu.make_async_copy(out_ref.at[m], target, sems.at[m])

    keys, values = both(1), both(2)
    for step in range(0, members, block):
        scores = lax.dot_general(
            rows(0, own[step : step + block]),
            keys,
            (((1,), (1,)), ((), ())),
            preferred_element_type=jnp.float32,
        ) * (1.0 / math.sqrt(DH))
        exponents = jnp.exp(scores - jnp.max(scores, axis=1, keepdims=True))
        totals = jnp.sum(exponents, axis=1, keepdims=True)
        mixed = jnp.dot(
            exponents.astype(jnp.bfloat16), values, preferred_element_type=jnp.float32
        )
        mixed = (mixed / totals).astype(out_ref.dtype)
        for m in range(block):
            out_ref[step + m] = mixed[m * token_rows : (m + 1) * token_rows]
            leave(step + m).start()
    for m in range(members):
        leave(m).wait()


def attend(own, other, token_rows):
    members = len(own)
    total = members * token_rows
    vmem = pl.BlockSpec(memory_space=pltpu.VMEM)
    return pl.pallas_call(
        attend_body,
        in_specs=[vmem] * (members + len(other)),
        out_specs=pl.BlockSpec(memory_space=pltpu.HBM),
        out_shape=jax.ShapeDtypeStruct((members, token_rows, DH), own[0].dtype),
        scratch_shapes=[
            pltpu.VMEM((members, token_rows, DH), own[0].dtype),
            pltpu.SemaphoreType.DMA((members,)),
        ],
        compiler_params=pltpu.CompilerParams(vmem_limit_bytes=ATTEND_VMEM),
        cost_estimate=pl.CostEstimate(
            flops=8 * total * total * DH,
            bytes_accessed=7 * total * DH * 2,
            transcendentals=2 * total * total,
        ),
        name="attend",
    )(*own, *other)


def unpack_body(in_ref, out_ref, sems):
    copies = [
        pltpu.make_async_copy(
            in_ref.at[head], out_ref.at[:, pl.ds(head * DH, DH)], sems.at[head]
        )
        for head in range(in_ref.shape[0])
    ]
    for copy in copies:
        copy.start()
    for copy in copies:
        copy.wait()


def unpack_heads(array):
    heads, token_rows, _ = array.shape
    return pl.pallas_call(
        unpack_body,
        in_specs=[pl.BlockSpec(memory_space=pltpu.VMEM)],
        out_specs=pl.BlockSpec(memory_space=pltpu.HBM),
        out_shape=jax.ShapeDtypeStruct((token_rows, heads * DH), array.dtype),
        scratch_shapes=[pltpu.SemaphoreType.DMA((heads,))],
        compiler_params=pltpu.CompilerParams(vmem_limit_bytes=COPY_VMEM),
        name="unpack_heads",
    )(array)


def decode_body(
    grid_rows,
    width,
    share_rows,
    members,
    halves,
    *refs,
):
    own, other, refs = refs[:members], refs[members : members + halves], refs[members + halves :]
    order = sending_order(members)
    (
    tile_hbm,
    in_weight_hbm,
    in_bias_hbm,
    gain_hbm,
    mid_weight_hbm,
    mid_bias_hbm,
    out_hbm,
    tile_ref,
    out_ref,
    mid_weight,
    in_weight_ref,
    in_bias_ref,
    gain_ref,
    mid_bias_ref,
    taps,
    rows_held,
    patches,
    raw,
    hidden,
    activated,
    active,
    summed,
    weight_sems,
    small_sems,
    out_sems,
    ) = refs
    pairs = active.shape[1] // 16
    channels, features = in_weight_ref.shape[3:]
    columns = out_ref.shape[2]
    lane_tiles = features // 128
    position = lax.axis_index("seq")
    section = lax.axis_index("sect")
    tile_copy = pltpu.make_async_copy(tile_hbm, tile_ref, small_sems.at[4])
    tile_copy.start()
    small = [
        pltpu.make_async_copy(source, target, small_sems.at[place])
        for place, (source, target) in enumerate(
            (
                (in_weight_hbm, in_weight_ref),
                (in_bias_hbm, in_bias_ref),
                (gain_hbm, gain_ref),
                (mid_bias_hbm, mid_bias_ref),
            )
        )
    ]
    for copy in small:
        copy.start()

    def load(col_tap):
        return [
            pltpu.make_async_copy(
                mid_weight_hbm.at[tap, row_tap, col_tap],
                mid_weight.at[
                    col_tap,
                    pl.ds(row_tap * features, features),
                    pl.ds((2 - tap) * features, features),
                ],
                weight_sems.at[col_tap, row_tap, slot],
            )
            for row_tap in range(3)
            for slot, tap in enumerate(TAPS)
        ]

    for col_tap in range(3):
        for copy in load(col_tap):
            copy.start()

    tile_copy.wait()
    filled = tile_ref[position]
    first_row = lax.fori_loop(0, position, lambda d, total: total + tile_ref[d], jnp.int32(0))

    chunks = rows_held.shape[1] // 128
    extra = -(-share_rows * chunks // 16) * 16
    shares = [ref[ref.shape[0] - extra :] for ref in own]
    shares += [ref[m, ref.shape[1] - extra :] for ref in other for m in range(ref.shape[0])]
    for place, share in enumerate(shares):
        lines = share.astype(jnp.float32)
        low = (place // members * members + order[place % members]) * share_rows
        for chunk in range(chunks):
            rows_held[low : low + share_rows, chunk * 128 : (chunk + 1) * 128] = lines[
                chunk * share_rows : (chunk + 1) * share_rows
            ]
    latent = rows_held[...]
    aside = pltpu.roll(latent, latent.shape[1] - RIM, 1).astype(jnp.bfloat16)
    latent = latent.astype(jnp.bfloat16)
    held_rows = latent.shape[0]
    unit = lax.broadcasted_iota(jnp.int32, (UNITS, held_rows), 0)
    held = lax.broadcasted_iota(jnp.int32, (UNITS, held_rows), 1)
    side = (held >= members * share_rows).astype(jnp.int32)
    member = (held // share_rows - side * members) ^ (position // 2)
    held = (2 * member + ((position & 1) ^ side)) * share_rows + held % share_rows
    frame = sum((unit >= (k + 1) * REACH).astype(jnp.int32) for k in range(LF))
    reach = unit - frame * REACH
    selectors = []
    for tap in TAPS:
        for row_parity in range(2):
            for i in range(2):
                token_row = first_row + (reach >> 1) - 1 + i
                source = frame + tap - 2
                wanted = (
                    ((reach & 1) == row_parity)
                    & (token_row >= 0)
                    & (token_row < grid_rows)
                    & (source >= 0)
                    & (source < LF)
                )
                target = jnp.where(wanted, source * grid_rows + token_row, -1)
                selectors.append(jnp.where(held == target, 1.0, 0.0).astype(jnp.bfloat16))
    selector = jnp.concatenate(selectors, axis=0)
    even = jnp.dot(selector, latent, preferred_element_type=jnp.float32)
    odd = jnp.dot(selector, aside, preferred_element_type=jnp.float32)
    for chunk in range(chunks):
        lanes = slice(chunk * 128, (chunk + 1) * 128)
        for group in range(len(selectors)):
            rows = slice(group * UNITS, (group + 1) * UNITS)
            piece = jnp.concatenate([even[rows, lanes], odd[rows, lanes]], axis=0)
            patches[
                chunk * 2 * UNITS : (chunk + 1) * 2 * UNITS, group * 128 : (group + 1) * 128
            ] = piece.astype(jnp.bfloat16)

    for copy in small:
        copy.wait()
    nothing = jnp.zeros((channels, features), jnp.bfloat16)
    base = 0
    for tap in TAPS:
        for row_parity in range(2):
            for i, j, p, q in [
                (i, j, p, q) for i in range(2) for j in range(2) for p in range(2) for q in range(2)
            ]:
                for col_parity in range(2):
                    row_tap, col_tap = 2 * i + p - row_parity, 2 * j + q - col_parity
                    inside = 0 <= row_tap < 3 and 0 <= col_tap < 3
                    taps[base : base + channels, col_parity * features : (col_parity + 1) * features] = (
                        in_weight_ref[tap, row_tap, col_tap] if inside else nothing
                    )
                base += channels

    unit_row = lax.broadcasted_iota(jnp.int32, (UNITS, 1), 0)
    row_frame = sum((unit_row >= (k + 1) * REACH).astype(jnp.int32) for k in range(LF))
    pixel_row = 2 * first_row + unit_row - row_frame * REACH - 1
    row_inside = (pixel_row >= 0) & (pixel_row < 2 * grid_rows)
    in_bias = in_bias_ref[...].reshape(1, features)
    half_gain = gain_ref[...].reshape(1, features) * 0.5

    def first_layer(chunk):
        for corner in range(2):
            start = (chunk * 2 + corner) * UNITS
            for col_parity in range(2):
                value = (
                    raw[pl.ds(start, UNITS), col_parity * features : (col_parity + 1) * features]
                    + in_bias
                )
                value = value.astype(jnp.bfloat16).astype(jnp.float32)
                scale = lax.rsqrt(jnp.mean(value * value, axis=1, keepdims=True) + 1e-06)
                column = chunk * 4 + corner * 2 + col_parity
                pixel = section * columns + column - 1
                keep = row_inside & (pixel >= 0) & (pixel < width)
                half = value * jnp.where(keep, scale, 0.0) * half_gain
                result = half + half * jnp.tanh(half)
                at = pl.ds(column * UNITS, UNITS)
                for lane in range(lane_tiles):
                    lanes = slice(lane * 128, (lane + 1) * 128)
                    hidden[lane, at] = value[:, lanes]
                    activated[lane, at] = result[:, lanes]

    middle = (chunks + 1) // 2
    groups = ((0, middle), (middle, chunks))
    for low, high in groups:
        rows = slice(low * 2 * UNITS, high * 2 * UNITS)
        raw[rows] = jnp.dot(patches[rows], taps[...], preferred_element_type=jnp.float32)
    for low, high in groups:
        for chunk in range(low, high):
            first_layer(chunk)

    def pair_up(phase, pair):
        at = slice(pair * 16, pair * 16 + 16)
        for lane in range(lane_tiles):
            for field in range(LF):
                for row_tap in range(3):
                    start = (2 * pair + phase) * UNITS + field * REACH + row_tap
                    joined = jnp.concatenate(
                        [activated[lane, pl.ds(start + k * UNITS, ROWS)] for k in range(2)], axis=0
                    )
                    to_lane = (field * 3 + row_tap) * features + lane * 128
                    active[phase, at, to_lane : to_lane + 128] = joined.astype(jnp.bfloat16)

    rows = columns * ROWS
    depth = 3 * features

    def windows(low, high, lanes):
        return jnp.concatenate(
            [
                active[tap % 2, 16 * (tap // 2) + low : 16 * (tap // 2) + high, lanes]
                for tap in range(3)
            ],
            axis=1,
        )

    def weights(lanes):
        return jnp.concatenate([mid_weight[tap, :, lanes] for tap in range(3)], axis=0)

    mid_bias = mid_bias_ref[...].reshape(1, features)

    def finish(field):
        tile_row = lax.broadcasted_iota(jnp.int32, (columns * ROWS, 128), 0) & (ROWS - 1)
        for lane in range(lane_tiles):
            lanes = slice(lane * 128, (lane + 1) * 128)
            skip = jnp.concatenate(
                [
                    hidden[lane, pl.ds((column + 1) * UNITS + field * REACH + 1, ROWS)]
                    for column in range(columns)
                ],
                axis=0,
            )
            value = summed[field, lane] + skip + mid_bias[:, lanes]
            value = jnp.where(tile_row < 2 * filled, value, 0.0)
            value = jnp.swapaxes(value.reshape(columns, ROWS, 128), 0, 1)
            out_ref[field, :, :, lanes] = value.astype(jnp.bfloat16)
        leave(field).start()

    def leave(field):
        return pltpu.make_async_copy(out_ref.at[field], out_hbm.at[field], out_sems.at[field])

    for phase in range(2):
        for pair in range(pairs - phase):
            pair_up(phase, pair)
    for tap in range(3):
        for copy in load(tap):
            copy.wait()
    early = windows(0, rows, slice(0, depth))
    late = windows(0, rows, slice(depth, 2 * depth))
    for left in range(0, 2 * features, 256):
        block = jnp.dot(
            early, weights(slice(left, left + 256)), preferred_element_type=jnp.float32
        )
        for lane in range(2):
            field, tile = divmod(left // 128 + lane, lane_tiles)
            summed[field, tile] = block[:, lane * 128 : (lane + 1) * 128]
    finish(0)
    for left in range(0, features, 256):
        right = min(left + 256, features)
        block = jnp.dot(late, weights(slice(left, right)), preferred_element_type=jnp.float32)
        for lane in range((right - left) // 128):
            tile = left // 128 + lane
            summed[1, tile] = summed[1, tile] + block[:, lane * 128 : (lane + 1) * 128]
    finish(1)
    for field in range(LF):
        leave(field).wait()


def decode_tile(
    own,
    other,
    share_rows,
    grid_rows,
    width,
    tile_rows,
    conv_in_weight,
    conv_in_bias,
    norm_gain,
    conv_mid_weight,
    conv_mid_bias,
):
    sections = lax.axis_size("sect")
    channels, features = conv_in_weight.shape[3:]
    token_width = 4 * channels
    columns = width // sections
    span = columns // 2
    pairs = span + 1
    chunks = (span + 2) * token_width // 128
    lane_tiles = features // 128
    vmem = pl.BlockSpec(memory_space=pltpu.VMEM)
    hbm = pl.BlockSpec(memory_space=pltpu.HBM)
    slots = len(TAPS)
    depth = slots * 2 * 4 * token_width
    held = chunks * 4 * UNITS
    return pl.pallas_call(
        functools.partial(decode_body, grid_rows, width, share_rows, len(own), len(other)),
        in_specs=[vmem] * (len(own) + len(other)) + [hbm] * 6,
        out_specs=hbm,
        out_shape=jax.ShapeDtypeStruct((LF, ROWS, columns, features), jnp.bfloat16),
        scratch_shapes=[
            pltpu.SMEM(tile_rows.shape, tile_rows.dtype),
            pltpu.VMEM((LF, ROWS, columns, features), jnp.bfloat16),
            pltpu.VMEM((3, 3 * features, slots * features), jnp.bfloat16),
            pltpu.VMEM(conv_in_weight.shape, jnp.bfloat16),
            pltpu.VMEM(conv_in_bias.shape, jnp.float32),
            pltpu.VMEM(norm_gain.shape, jnp.float32),
            pltpu.VMEM(conv_mid_bias.shape, jnp.float32),
            pltpu.VMEM((depth, 2 * features), jnp.bfloat16),
            pltpu.VMEM((2 * len(own) * share_rows, chunks * 128), jnp.float32),
            pltpu.VMEM((chunks * 2 * UNITS, depth), jnp.bfloat16),
            pltpu.VMEM((chunks * 2 * UNITS, 2 * features), jnp.float32),
            pltpu.VMEM((lane_tiles, held, 128), jnp.float32),
            pltpu.VMEM((lane_tiles, held, 128), jnp.float32),
            pltpu.VMEM((2, pairs * 16, LF * 3 * features), jnp.bfloat16),
            pltpu.VMEM((LF, lane_tiles, columns * ROWS, 128), jnp.float32),
            pltpu.SemaphoreType.DMA((3, 3, slots)),
            pltpu.SemaphoreType.DMA((5,)),
            pltpu.SemaphoreType.DMA((LF,)),
        ],
        compiler_params=pltpu.CompilerParams(vmem_limit_bytes=DECODE_VMEM),
        cost_estimate=pl.CostEstimate(
            flops=2 * 3 * 9 * columns * ROWS * features * features,
            bytes_accessed=slots * 9 * features * features * 2,
            transcendentals=held * features,
        ),
        name="decode_tile",
    )(
        *own,
        *other,
        *in_hbm(
            tile_rows, conv_in_weight, conv_in_bias, norm_gain, conv_mid_weight, conv_mid_bias
        ),
    )


def on_device(
    queries,
    key_tokens,
    value_tokens,
    latent,
    tile_rows,
    conv_in_weight,
    conv_in_bias,
    norm_gain,
    conv_mid_weight,
    conv_mid_bias,
):
    devices = lax.axis_size("seq")
    groups = parity_groups(devices)
    grid_rows = latent.shape[0] * devices // LF
    token_width = 4 * conv_in_weight.shape[3]
    packed = pack_heads(queries, key_tokens, value_tokens, latent, token_width)
    own = [
        lax.ppermute(piece, "seq", xor_pairs(2 * m)) if m else piece
        for m, piece in zip(sending_order(len(packed)), packed)
    ]
    joined = join(own, queries.shape[0])
    other = [lax.ppermute(joined, "seq", xor_pairs(1))]
    mixed = attend(own, other, queries.shape[0])
    returned = lax.all_to_all(mixed, "seq", 0, 0, axis_index_groups=groups, tiled=True)
    frames = decode_tile(
        own,
        other,
        latent.shape[0],
        grid_rows,
        2 * latent.shape[1] // token_width,
        tile_rows,
        conv_in_weight,
        conv_in_bias,
        norm_gain,
        conv_mid_weight,
        conv_mid_bias,
    )
    return (unpack_heads(returned), frames)


def solution(mesh):
    in_specs = (
        P("seq", None),
        P("seq", None),
        P("seq", None),
        P("seq", None),
        P(),
        P(),
        P(),
        P(),
        P(),
        P(),
    )
    out_specs = (P("seq", "sect"), P(None, "seq", "sect", None))
    return jax.shard_map(
        on_device, mesh=mesh, in_specs=in_specs, out_specs=out_specs, check_vma=False
    )
```

```python
import functools
import math

import jax
import jax.numpy as jnp
from jax import lax
from jax.experimental import pallas as pl
from jax.experimental.pallas import tpu as pltpu
from jax.sharding import PartitionSpec as P

DH = 128
LF = 2
MAXT = 4
RIM = 64
TAPS = (1, 2)
ROWS = 2 * MAXT
REACH = ROWS + 2
UNITS = -(-LF * REACH // 8) * 8
DECODE_VMEM = 32 * 1024 * 1024
ATTEND_VMEM = 32 * 1024 * 1024
COPY_VMEM = 16 * 1024 * 1024


def parity_groups(devices):
    return [list(range(parity, devices, 2)) for parity in range(2)]


def in_hbm(*arrays):
    return [pltpu.with_memory_space_constraint(array, pltpu.HBM) for array in arrays]


def pack_body(query_ref, key_ref, value_ref, latent_ref, *refs):
    packed_refs, (held, latent_held, sems) = refs[:-3], refs[-3:]
    heads = len(packed_refs)
    chip = lax.axis_index("seq") // 2
    token_rows = query_ref.shape[0]
    section = lax.axis_index("sect")
    wide_columns = pl.ds(pl.multiple_of(section * heads * DH, DH), heads * DH)
    copies = [
        pltpu.make_async_copy(ref.at[:, wide_columns], held.at[place], sems.at[place])
        for place, ref in enumerate((query_ref, key_ref, value_ref))
    ]
    latent_copy = pltpu.make_async_copy(latent_ref, latent_held, sems.at[3])
    latent_copy.start()
    for copy in copies:
        copy.start()
    rows, width = latent_ref.shape
    latent_copy.wait()
    half, rim = width // 2, RIM
    wide = latent_held[...].astype(jnp.float32)
    rim_zeros = jnp.zeros((rows, rim), jnp.float32)
    lower = jnp.concatenate([rim_zeros, wide[:, : half + rim]], axis=1)
    upper = jnp.concatenate([wide[:, half - rim :], rim_zeros], axis=1)
    share = jnp.where(section == 0, lower, upper)
    chunks = share.shape[1] // DH
    lines = [share[:, chunk * DH : (chunk + 1) * DH] for chunk in range(chunks)]
    spare = packed_refs[0].shape[0] - 3 * token_rows - chunks * rows
    lines.append(jnp.zeros((spare, DH), jnp.float32))
    share = jnp.concatenate(lines, axis=0).astype(jnp.bfloat16)
    for packed_ref in packed_refs:
        packed_ref[3 * token_rows :] = share
    for place, copy in enumerate(copies):
        copy.wait()
        for m, packed_ref in zip(sending_order(heads), packed_refs):
            columns = pl.ds(pl.multiple_of((chip ^ m) * DH, DH), DH)
            packed_ref[place * token_rows : (place + 1) * token_rows] = held[place, :, columns]


def pack_heads(queries, key_tokens, value_tokens, latent, token_width):
    token_rows, width = queries.shape
    sections = lax.axis_size("sect")
    heads = width // DH // sections
    span = latent.shape[1] // sections + 2 * token_width
    extra = -(-latent.shape[0] * (span // DH) // 16) * 16
    hbm = pl.BlockSpec(memory_space=pltpu.HBM)
    vmem = pl.BlockSpec(memory_space=pltpu.VMEM)
    return pl.pallas_call(
        pack_body,
        in_specs=[hbm] * 4,
        out_specs=[vmem] * heads,
        out_shape=[jax.ShapeDtypeStruct((3 * token_rows + extra, DH), queries.dtype)] * heads,
        scratch_shapes=[
            pltpu.VMEM((3, token_rows, heads * DH), queries.dtype),
            pltpu.VMEM(latent.shape, latent.dtype),
            pltpu.SemaphoreType.DMA((4,)),
        ],
        compiler_params=pltpu.CompilerParams(vmem_limit_bytes=COPY_VMEM),
        name="pack_heads",
    )(*in_hbm(queries, key_tokens, value_tokens, latent))


def sending_order(chips):
    far, near = list(range(chips // 2, chips)), list(range(1, chips // 2))
    return [0, *far[:2], *near[1:2], *far[2:], *near[2:], *near[:1]]


def xor_pairs(distance):
    return [(i, i ^ distance) for i in range(lax.axis_size("seq"))]


def join_body(*refs):
    out_ref = refs[-1]
    for place, ref in enumerate(refs[:-1]):
        out_ref[place] = ref[ref.shape[0] - out_ref.shape[1] :]


def join(pieces, skipped):
    rows, width = pieces[0].shape
    vmem = pl.BlockSpec(memory_space=pltpu.VMEM)
    return pl.pallas_call(
        join_body,
        in_specs=[vmem] * len(pieces),
        out_specs=vmem,
        out_shape=jax.ShapeDtypeStruct((len(pieces), rows - skipped, width), pieces[0].dtype),
        compiler_params=pltpu.CompilerParams(vmem_limit_bytes=COPY_VMEM),
        name="join",
    )(*pieces)


def flat(array):
    return array.reshape(-1, array.shape[-1])


def softmax_part(query, keys, values):
    scores = lax.dot_general(
        query, keys, (((1,), (1,)), ((), ())), preferred_element_type=jnp.float32
    ) * (1.0 / math.sqrt(DH))
    largest = jnp.max(scores, axis=1, keepdims=True)
    exponents = jnp.exp(scores - largest)
    totals = jnp.sum(exponents, axis=1, keepdims=True)
    mixed = jnp.dot(exponents.astype(jnp.bfloat16), values, preferred_element_type=jnp.float32)
    return largest, totals, mixed


def piece_rows(place, token_rows, pieces):
    at = slice(place * token_rows, (place + 1) * token_rows)
    return jnp.concatenate([ref[at] for ref in pieces], axis=0)


def attend_own_body(token_rows, *refs):
    pieces, (mixed_ref, stats_ref) = refs[:-2], refs[-2:]
    block = min(4, len(pieces))
    keys = piece_rows(1, token_rows, pieces)
    values = piece_rows(2, token_rows, pieces)
    for step in range(0, len(pieces), block):
        query = piece_rows(0, token_rows, pieces[step : step + block])
        largest, totals, mixed = softmax_part(query, keys, values)
        at = slice(step * token_rows, (step + block) * token_rows)
        mixed_ref[at] = mixed
        stats_ref[0, at] = jnp.broadcast_to(largest, mixed.shape)
        stats_ref[1, at] = jnp.broadcast_to(totals, mixed.shape)


def attend_body(*refs):
    other_ref, mixed_ref, stats_ref, out_hbm, out_ref, sems = refs[-6:]
    pieces = refs[:-6]
    members, token_rows, _ = out_ref.shape
    block = min(4, members)
    chip = lax.axis_index("seq") // 2
    order = sending_order(members)

    def leave(m):
        target = out_hbm.at[chip ^ order[m]]
        return pltpu.make_async_copy(out_ref.at[m], target, sems.at[m])

    keys = flat(other_ref[:, :token_rows])
    values = flat(other_ref[:, token_rows : 2 * token_rows])
    for step in range(0, members, block):
        query = piece_rows(0, token_rows, pieces[step : step + block])
        largest, totals, mixed = softmax_part(query, keys, values)
        at = slice(step * token_rows, (step + block) * token_rows)
        earlier = stats_ref[0, at]
        top = jnp.maximum(earlier, largest)
        before, now = jnp.exp(earlier - top), jnp.exp(largest - top)
        totals = stats_ref[1, at] * before + totals * now
        mixed = (mixed_ref[at] * before + mixed * now) / totals
        mixed = mixed.astype(out_ref.dtype)
        for m in range(block):
            out_ref[step + m] = mixed[m * token_rows : (m + 1) * token_rows]
            leave(step + m).start()
    for m in range(members):
        leave(m).wait()


def attend(own, other, token_rows):
    members = len(own)
    total = members * token_rows
    vmem = pl.BlockSpec(memory_space=pltpu.VMEM)
    params = pltpu.CompilerParams(vmem_limit_bytes=ATTEND_VMEM)
    cost = pl.CostEstimate(
        flops=4 * total * total * DH,
        bytes_accessed=7 * total * DH * 2,
        transcendentals=total * total,
    )
    mixed, stats = pl.pallas_call(
        functools.partial(attend_own_body, token_rows),
        in_specs=[vmem] * members,
        out_specs=[vmem] * 2,
        out_shape=[
            jax.ShapeDtypeStruct((total, DH), jnp.float32),
            jax.ShapeDtypeStruct((2, total, DH), jnp.float32),
        ],
        compiler_params=params,
        cost_estimate=cost,
        name="attend_own",
    )(*own)
    return pl.pallas_call(
        attend_body,
        in_specs=[vmem] * (members + 3),
        out_specs=pl.BlockSpec(memory_space=pltpu.HBM),
        out_shape=jax.ShapeDtypeStruct((members, token_rows, DH), own[0].dtype),
        scratch_shapes=[
            pltpu.VMEM((members, token_rows, DH), own[0].dtype),
            pltpu.SemaphoreType.DMA((members,)),
        ],
        compiler_params=params,
        cost_estimate=cost,
        name="attend",
    )(*own, other, mixed, stats)


def unpack_body(in_ref, out_ref, sems):
    copies = [
        pltpu.make_async_copy(
            in_ref.at[head], out_ref.at[:, pl.ds(head * DH, DH)], sems.at[head]
        )
        for head in range(in_ref.shape[0])
    ]
    for copy in copies:
        copy.start()
    for copy in copies:
        copy.wait()


def unpack_heads(array):
    heads, token_rows, _ = array.shape
    return pl.pallas_call(
        unpack_body,
        in_specs=[pl.BlockSpec(memory_space=pltpu.VMEM)],
        out_specs=pl.BlockSpec(memory_space=pltpu.HBM),
        out_shape=jax.ShapeDtypeStruct((token_rows, heads * DH), array.dtype),
        scratch_shapes=[pltpu.SemaphoreType.DMA((heads,))],
        compiler_params=pltpu.CompilerParams(vmem_limit_bytes=COPY_VMEM),
        name="unpack_heads",
    )(array)


def decode_body(
    grid_rows,
    width,
    share_rows,
    members,
    halves,
    *refs,
):
    own, other, refs = refs[:members], refs[members : members + halves], refs[members + halves :]
    order = sending_order(members)
    (
    tile_hbm,
    in_weight_hbm,
    in_bias_hbm,
    gain_hbm,
    mid_weight_hbm,
    mid_bias_hbm,
    out_hbm,
    tile_ref,
    out_ref,
    mid_weight,
    in_weight_ref,
    in_bias_ref,
    gain_ref,
    mid_bias_ref,
    taps,
    rows_held,
    patches,
    raw,
    hidden,
    activated,
    active,
    summed,
    weight_sems,
    small_sems,
    out_sems,
    ) = refs
    pairs = active.shape[1] // 16
    channels, features = in_weight_ref.shape[3:]
    columns = out_ref.shape[2]
    lane_tiles = features // 128
    position = lax.axis_index("seq")
    section = lax.axis_index("sect")
    tile_copy = pltpu.make_async_copy(tile_hbm, tile_ref, small_sems.at[4])
    tile_copy.start()
    small = [
        pltpu.make_async_copy(source, target, small_sems.at[place])
        for place, (source, target) in enumerate(
            (
                (in_weight_hbm, in_weight_ref),
                (in_bias_hbm, in_bias_ref),
                (gain_hbm, gain_ref),
                (mid_bias_hbm, mid_bias_ref),
            )
        )
    ]
    for copy in small:
        copy.start()

    def load(col_tap):
        return [
            pltpu.make_async_copy(
                mid_weight_hbm.at[tap, row_tap, col_tap],
                mid_weight.at[
                    col_tap,
                    pl.ds(row_tap * features, features),
                    pl.ds((2 - tap) * features, features),
                ],
                weight_sems.at[col_tap, row_tap, slot],
            )
            for row_tap in range(3)
            for slot, tap in enumerate(TAPS)
        ]

    for col_tap in range(3):
        for copy in load(col_tap):
            copy.start()

    tile_copy.wait()
    filled = tile_ref[position]
    first_row = lax.fori_loop(0, position, lambda d, total: total + tile_ref[d], jnp.int32(0))

    chunks = rows_held.shape[1] // 128
    extra = -(-share_rows * chunks // 16) * 16
    shares = [ref[ref.shape[0] - extra :] for ref in own]
    shares += [ref[m, ref.shape[1] - extra :] for ref in other for m in range(ref.shape[0])]
    for place, share in enumerate(shares):
        lines = share.astype(jnp.float32)
        low = (place // members * members + order[place % members]) * share_rows
        for chunk in range(chunks):
            rows_held[low : low + share_rows, chunk * 128 : (chunk + 1) * 128] = lines[
                chunk * share_rows : (chunk + 1) * share_rows
            ]
    latent = rows_held[...]
    aside = pltpu.roll(latent, latent.shape[1] - RIM, 1).astype(jnp.bfloat16)
    latent = latent.astype(jnp.bfloat16)
    held_rows = latent.shape[0]
    unit = lax.broadcasted_iota(jnp.int32, (UNITS, held_rows), 0)
    held = lax.broadcasted_iota(jnp.int32, (UNITS, held_rows), 1)
    side = (held >= members * share_rows).astype(jnp.int32)
    member = (held // share_rows - side * members) ^ (position // 2)
    held = (2 * member + ((position & 1) ^ side)) * share_rows + held % share_rows
    frame = sum((unit >= (k + 1) * REACH).astype(jnp.int32) for k in range(LF))
    reach = unit - frame * REACH
    selectors = []
    for tap in TAPS:
        for row_parity in range(2):
            for i in range(2):
                token_row = first_row + (reach >> 1) - 1 + i
                source = frame + tap - 2
                wanted = (
                    ((reach & 1) == row_parity)
                    & (token_row >= 0)
                    & (token_row < grid_rows)
                    & (source >= 0)
                    & (source < LF)
                )
                target = jnp.where(wanted, source * grid_rows + token_row, -1)
                selectors.append(jnp.where(held == target, 1.0, 0.0).astype(jnp.bfloat16))
    selector = jnp.concatenate(selectors, axis=0)
    even = jnp.dot(selector, latent, preferred_element_type=jnp.float32)
    odd = jnp.dot(selector, aside, preferred_element_type=jnp.float32)
    for chunk in range(chunks):
        lanes = slice(chunk * 128, (chunk + 1) * 128)
        for group in range(len(selectors)):
            rows = slice(group * UNITS, (group + 1) * UNITS)
            piece = jnp.concatenate([even[rows, lanes], odd[rows, lanes]], axis=0)
            patches[
                chunk * 2 * UNITS : (chunk + 1) * 2 * UNITS, group * 128 : (group + 1) * 128
            ] = piece.astype(jnp.bfloat16)

    for copy in small:
        copy.wait()
    nothing = jnp.zeros((channels, features), jnp.bfloat16)
    base = 0
    for tap in TAPS:
        for row_parity in range(2):
            for i, j, p, q in [
                (i, j, p, q) for i in range(2) for j in range(2) for p in range(2) for q in range(2)
            ]:
                for col_parity in range(2):
                    row_tap, col_tap = 2 * i + p - row_parity, 2 * j + q - col_parity
                    inside = 0 <= row_tap < 3 and 0 <= col_tap < 3
                    taps[base : base + channels, col_parity * features : (col_parity + 1) * features] = (
                        in_weight_ref[tap, row_tap, col_tap] if inside else nothing
                    )
                base += channels

    unit_row = lax.broadcasted_iota(jnp.int32, (UNITS, 1), 0)
    row_frame = sum((unit_row >= (k + 1) * REACH).astype(jnp.int32) for k in range(LF))
    pixel_row = 2 * first_row + unit_row - row_frame * REACH - 1
    row_inside = (pixel_row >= 0) & (pixel_row < 2 * grid_rows)
    in_bias = in_bias_ref[...].reshape(1, features)
    half_gain = gain_ref[...].reshape(1, features) * 0.5

    def first_layer(chunk):
        for corner in range(2):
            start = (chunk * 2 + corner) * UNITS
            for col_parity in range(2):
                value = (
                    raw[pl.ds(start, UNITS), col_parity * features : (col_parity + 1) * features]
                    + in_bias
                )
                value = value.astype(jnp.bfloat16).astype(jnp.float32)
                scale = lax.rsqrt(jnp.mean(value * value, axis=1, keepdims=True) + 1e-06)
                column = chunk * 4 + corner * 2 + col_parity
                pixel = section * columns + column - 1
                keep = row_inside & (pixel >= 0) & (pixel < width)
                half = value * jnp.where(keep, scale, 0.0) * half_gain
                result = half + half * jnp.tanh(half)
                at = pl.ds(column * UNITS, UNITS)
                for lane in range(lane_tiles):
                    lanes = slice(lane * 128, (lane + 1) * 128)
                    hidden[lane, at] = value[:, lanes]
                    activated[lane, at] = result[:, lanes]

    middle = (chunks + 1) // 2
    groups = ((0, middle), (middle, chunks))
    for low, high in groups:
        rows = slice(low * 2 * UNITS, high * 2 * UNITS)
        raw[rows] = jnp.dot(patches[rows], taps[...], preferred_element_type=jnp.float32)
    for low, high in groups:
        for chunk in range(low, high):
            first_layer(chunk)

    def pair_up(phase, pair):
        at = slice(pair * 16, pair * 16 + 16)
        for lane in range(lane_tiles):
            for field in range(LF):
                for row_tap in range(3):
                    start = (2 * pair + phase) * UNITS + field * REACH + row_tap
                    joined = jnp.concatenate(
                        [activated[lane, pl.ds(start + k * UNITS, ROWS)] for k in range(2)], axis=0
                    )
                    to_lane = (field * 3 + row_tap) * features + lane * 128
                    active[phase, at, to_lane : to_lane + 128] = joined.astype(jnp.bfloat16)

    rows = columns * ROWS
    depth = 3 * features

    def windows(low, high, lanes):
        return jnp.concatenate(
            [
                active[tap % 2, 16 * (tap // 2) + low : 16 * (tap // 2) + high, lanes]
                for tap in range(3)
            ],
            axis=1,
        )

    def weights(lanes):
        return jnp.concatenate([mid_weight[tap, :, lanes] for tap in range(3)], axis=0)

    mid_bias = mid_bias_ref[...].reshape(1, features)

    def finish(field):
        tile_row = lax.broadcasted_iota(jnp.int32, (columns * ROWS, 128), 0) & (ROWS - 1)
        for lane in range(lane_tiles):
            lanes = slice(lane * 128, (lane + 1) * 128)
            skip = jnp.concatenate(
                [
                    hidden[lane, pl.ds((column + 1) * UNITS + field * REACH + 1, ROWS)]
                    for column in range(columns)
                ],
                axis=0,
            )
            value = summed[field, lane] + skip + mid_bias[:, lanes]
            value = jnp.where(tile_row < 2 * filled, value, 0.0)
            value = jnp.swapaxes(value.reshape(columns, ROWS, 128), 0, 1)
            out_ref[field, :, :, lanes] = value.astype(jnp.bfloat16)
        leave(field).start()

    def leave(field):
        return pltpu.make_async_copy(out_ref.at[field], out_hbm.at[field], out_sems.at[field])

    for phase in range(2):
        for pair in range(pairs - phase):
            pair_up(phase, pair)
    for tap in range(3):
        for copy in load(tap):
            copy.wait()
    early = windows(0, rows, slice(0, depth))
    late = windows(0, rows, slice(depth, 2 * depth))
    for left in range(0, 2 * features, 256):
        block = jnp.dot(
            early, weights(slice(left, left + 256)), preferred_element_type=jnp.float32
        )
        for lane in range(2):
            field, tile = divmod(left // 128 + lane, lane_tiles)
            summed[field, tile] = block[:, lane * 128 : (lane + 1) * 128]
    finish(0)
    for left in range(0, features, 256):
        right = min(left + 256, features)
        block = jnp.dot(late, weights(slice(left, right)), preferred_element_type=jnp.float32)
        for lane in range((right - left) // 128):
            tile = left // 128 + lane
            summed[1, tile] = summed[1, tile] + block[:, lane * 128 : (lane + 1) * 128]
    finish(1)
    for field in range(LF):
        leave(field).wait()


def decode_tile(
    own,
    other,
    share_rows,
    grid_rows,
    width,
    tile_rows,
    conv_in_weight,
    conv_in_bias,
    norm_gain,
    conv_mid_weight,
    conv_mid_bias,
):
    sections = lax.axis_size("sect")
    channels, features = conv_in_weight.shape[3:]
    token_width = 4 * channels
    columns = width // sections
    span = columns // 2
    pairs = span + 1
    chunks = (span + 2) * token_width // 128
    lane_tiles = features // 128
    vmem = pl.BlockSpec(memory_space=pltpu.VMEM)
    hbm = pl.BlockSpec(memory_space=pltpu.HBM)
    slots = len(TAPS)
    depth = slots * 2 * 4 * token_width
    held = chunks * 4 * UNITS
    return pl.pallas_call(
        functools.partial(decode_body, grid_rows, width, share_rows, len(own), len(other)),
        in_specs=[vmem] * (len(own) + len(other)) + [hbm] * 6,
        out_specs=hbm,
        out_shape=jax.ShapeDtypeStruct((LF, ROWS, columns, features), jnp.bfloat16),
        scratch_shapes=[
            pltpu.SMEM(tile_rows.shape, tile_rows.dtype),
            pltpu.VMEM((LF, ROWS, columns, features), jnp.bfloat16),
            pltpu.VMEM((3, 3 * features, slots * features), jnp.bfloat16),
            pltpu.VMEM(conv_in_weight.shape, jnp.bfloat16),
            pltpu.VMEM(conv_in_bias.shape, jnp.float32),
            pltpu.VMEM(norm_gain.shape, jnp.float32),
            pltpu.VMEM(conv_mid_bias.shape, jnp.float32),
            pltpu.VMEM((depth, 2 * features), jnp.bfloat16),
            pltpu.VMEM((2 * len(own) * share_rows, chunks * 128), jnp.float32),
            pltpu.VMEM((chunks * 2 * UNITS, depth), jnp.bfloat16),
            pltpu.VMEM((chunks * 2 * UNITS, 2 * features), jnp.float32),
            pltpu.VMEM((lane_tiles, held, 128), jnp.float32),
            pltpu.VMEM((lane_tiles, held, 128), jnp.float32),
            pltpu.VMEM((2, pairs * 16, LF * 3 * features), jnp.bfloat16),
            pltpu.VMEM((LF, lane_tiles, columns * ROWS, 128), jnp.float32),
            pltpu.SemaphoreType.DMA((3, 3, slots)),
            pltpu.SemaphoreType.DMA((5,)),
            pltpu.SemaphoreType.DMA((LF,)),
        ],
        compiler_params=pltpu.CompilerParams(vmem_limit_bytes=DECODE_VMEM),
        cost_estimate=pl.CostEstimate(
            flops=2 * 3 * 9 * columns * ROWS * features * features,
            bytes_accessed=slots * 9 * features * features * 2,
            transcendentals=held * features,
        ),
        name="decode_tile",
    )(
        *own,
        *other,
        *in_hbm(
            tile_rows, conv_in_weight, conv_in_bias, norm_gain, conv_mid_weight, conv_mid_bias
        ),
    )


def on_device(
    queries,
    key_tokens,
    value_tokens,
    latent,
    tile_rows,
    conv_in_weight,
    conv_in_bias,
    norm_gain,
    conv_mid_weight,
    conv_mid_bias,
):
    devices = lax.axis_size("seq")
    groups = parity_groups(devices)
    grid_rows = latent.shape[0] * devices // LF
    token_width = 4 * conv_in_weight.shape[3]
    packed = pack_heads(queries, key_tokens, value_tokens, latent, token_width)
    own = [
        lax.ppermute(piece, "seq", xor_pairs(2 * m)) if m else piece
        for m, piece in zip(sending_order(len(packed)), packed)
    ]
    joined = join(own, queries.shape[0])
    other = [lax.ppermute(joined, "seq", xor_pairs(1))]
    mixed = attend(own, other[0], queries.shape[0])
    returned = lax.all_to_all(mixed, "seq", 0, 0, axis_index_groups=groups, tiled=True)
    frames = decode_tile(
        own,
        other,
        latent.shape[0],
        grid_rows,
        2 * latent.shape[1] // token_width,
        tile_rows,
        conv_in_weight,
        conv_in_bias,
        norm_gain,
        conv_mid_weight,
        conv_mid_bias,
    )
    return (unpack_heads(returned), frames)


def solution(mesh):
    in_specs = (
        P("seq", None),
        P("seq", None),
        P("seq", None),
        P("seq", None),
        P(),
        P(),
        P(),
        P(),
        P(),
        P(),
    )
    out_specs = (P("seq", "sect"), P(None, "seq", "sect", None))
    return jax.shard_map(
        on_device, mesh=mesh, in_specs=in_specs, out_specs=out_specs, check_vma=False
    )
```

```python
import functools
import math

import jax
import jax.numpy as jnp
from jax import lax
from jax.experimental import pallas as pl
from jax.experimental.pallas import tpu as pltpu
from jax.sharding import PartitionSpec as P

DH = 128
LF = 2
MAXT = 4
RIM = 64
TAPS = (1, 2)
ROWS = 2 * MAXT
REACH = ROWS + 2
UNITS = -(-LF * REACH // 8) * 8
DECODE_VMEM = 32 * 1024 * 1024
ATTEND_VMEM = 32 * 1024 * 1024
COPY_VMEM = 16 * 1024 * 1024


def parity_groups(devices):
    return [list(range(parity, devices, 2)) for parity in range(2)]


def in_hbm(*arrays):
    return [pltpu.with_memory_space_constraint(array, pltpu.HBM) for array in arrays]


def pack_body(query_ref, key_ref, value_ref, latent_ref, *refs):
    packed_refs, (held, latent_held, sems) = refs[:-3], refs[-3:]
    heads = len(packed_refs)
    chip = lax.axis_index("seq") // 2
    token_rows = query_ref.shape[0]
    section = lax.axis_index("sect")
    wide_columns = pl.ds(pl.multiple_of(section * heads * DH, DH), heads * DH)
    copies = [
        pltpu.make_async_copy(ref.at[:, wide_columns], held.at[place], sems.at[place])
        for place, ref in enumerate((query_ref, key_ref, value_ref))
    ]
    latent_copy = pltpu.make_async_copy(latent_ref, latent_held, sems.at[3])
    latent_copy.start()
    for copy in copies:
        copy.start()
    rows, width = latent_ref.shape
    latent_copy.wait()
    half, rim = width // 2, RIM
    wide = latent_held[...].astype(jnp.float32)
    rim_zeros = jnp.zeros((rows, rim), jnp.float32)
    lower = jnp.concatenate([rim_zeros, wide[:, : half + rim]], axis=1)
    upper = jnp.concatenate([wide[:, half - rim :], rim_zeros], axis=1)
    share = jnp.where(section == 0, lower, upper)
    chunks = share.shape[1] // DH
    lines = [share[:, chunk * DH : (chunk + 1) * DH] for chunk in range(chunks)]
    spare = packed_refs[0].shape[0] - 3 * token_rows - chunks * rows
    lines.append(jnp.zeros((spare, DH), jnp.float32))
    share = jnp.concatenate(lines, axis=0).astype(jnp.bfloat16)
    for packed_ref in packed_refs:
        packed_ref[3 * token_rows :] = share
    for place, copy in enumerate(copies):
        copy.wait()
        for m, packed_ref in zip(sending_order(heads), packed_refs):
            columns = pl.ds(pl.multiple_of((chip ^ m) * DH, DH), DH)
            packed_ref[place * token_rows : (place + 1) * token_rows] = held[place, :, columns]


def pack_heads(queries, key_tokens, value_tokens, latent, token_width):
    token_rows, width = queries.shape
    sections = lax.axis_size("sect")
    heads = width // DH // sections
    span = latent.shape[1] // sections + 2 * token_width
    extra = -(-latent.shape[0] * (span // DH) // 16) * 16
    hbm = pl.BlockSpec(memory_space=pltpu.HBM)
    vmem = pl.BlockSpec(memory_space=pltpu.VMEM)
    return pl.pallas_call(
        pack_body,
        in_specs=[hbm] * 4,
        out_specs=[vmem] * heads,
        out_shape=[jax.ShapeDtypeStruct((3 * token_rows + extra, DH), queries.dtype)] * heads,
        scratch_shapes=[
            pltpu.VMEM((3, token_rows, heads * DH), queries.dtype),
            pltpu.VMEM(latent.shape, latent.dtype),
            pltpu.SemaphoreType.DMA((4,)),
        ],
        compiler_params=pltpu.CompilerParams(vmem_limit_bytes=COPY_VMEM),
        name="pack_heads",
    )(*in_hbm(queries, key_tokens, value_tokens, latent))


def sending_order(chips):
    far, near = list(range(chips // 2, chips)), list(range(1, chips // 2))
    return [0, *far[:1], *near[1:2], *far[1:], *near[2:], *near[:1]]


def xor_pairs(distance):
    return [(i, i ^ distance) for i in range(lax.axis_size("seq"))]


def join_body(*refs):
    out_ref = refs[-1]
    for place, ref in enumerate(refs[:-1]):
        out_ref[place] = ref[ref.shape[0] - out_ref.shape[1] :]


def join(pieces, skipped):
    rows, width = pieces[0].shape
    vmem = pl.BlockSpec(memory_space=pltpu.VMEM)
    return pl.pallas_call(
        join_body,
        in_specs=[vmem] * len(pieces),
        out_specs=vmem,
        out_shape=jax.ShapeDtypeStruct((len(pieces), rows - skipped, width), pieces[0].dtype),
        compiler_params=pltpu.CompilerParams(vmem_limit_bytes=COPY_VMEM),
        name="join",
    )(*pieces)


def flat(array):
    return array.reshape(-1, array.shape[-1])


def softmax_part(query, keys, values):
    scores = lax.dot_general(
        query, keys, (((1,), (1,)), ((), ())), preferred_element_type=jnp.float32
    ) * (1.0 / math.sqrt(DH))
    largest = jnp.max(scores, axis=1, keepdims=True)
    exponents = jnp.exp(scores - largest)
    totals = jnp.sum(exponents, axis=1, keepdims=True)
    mixed = jnp.dot(exponents.astype(jnp.bfloat16), values, preferred_element_type=jnp.float32)
    return largest, totals, mixed


def piece_rows(place, token_rows, pieces):
    at = slice(place * token_rows, (place + 1) * token_rows)
    return jnp.concatenate([ref[at] for ref in pieces], axis=0)


def attend_own_body(token_rows, *refs):
    pieces, (mixed_ref, stats_ref) = refs[:-2], refs[-2:]
    block = min(4, len(pieces))
    keys = piece_rows(1, token_rows, pieces)
    values = piece_rows(2, token_rows, pieces)
    for step in range(0, len(pieces), block):
        query = piece_rows(0, token_rows, pieces[step : step + block])
        largest, totals, mixed = softmax_part(query, keys, values)
        at = slice(step * token_rows, (step + block) * token_rows)
        mixed_ref[at] = mixed
        stats_ref[0, at] = jnp.broadcast_to(largest, mixed.shape)
        stats_ref[1, at] = jnp.broadcast_to(totals, mixed.shape)


def attend_body(*refs):
    other_ref, mixed_ref, stats_ref, out_hbm, out_ref, sems = refs[-6:]
    pieces = refs[:-6]
    members, token_rows, _ = out_ref.shape
    block = min(4, members)
    chip = lax.axis_index("seq") // 2
    order = sending_order(members)

    def leave(m):
        target = out_hbm.at[chip ^ order[m]]
        return pltpu.make_async_copy(out_ref.at[m], target, sems.at[m])

    keys = flat(other_ref[:, :token_rows])
    values = flat(other_ref[:, token_rows : 2 * token_rows])
    for step in range(0, members, block):
        query = piece_rows(0, token_rows, pieces[step : step + block])
        largest, totals, mixed = softmax_part(query, keys, values)
        at = slice(step * token_rows, (step + block) * token_rows)
        earlier = stats_ref[0, at]
        top = jnp.maximum(earlier, largest)
        before, now = jnp.exp(earlier - top), jnp.exp(largest - top)
        totals = stats_ref[1, at] * before + totals * now
        mixed = (mixed_ref[at] * before + mixed * now) / totals
        mixed = mixed.astype(out_ref.dtype)
        for m in range(block):
            out_ref[step + m] = mixed[m * token_rows : (m + 1) * token_rows]
            leave(step + m).start()
    for m in range(members):
        leave(m).wait()


def attend(own, other, token_rows):
    members = len(own)
    total = members * token_rows
    vmem = pl.BlockSpec(memory_space=pltpu.VMEM)
    params = pltpu.CompilerParams(vmem_limit_bytes=ATTEND_VMEM)
    cost = pl.CostEstimate(
        flops=4 * total * total * DH,
        bytes_accessed=7 * total * DH * 2,
        transcendentals=total * total,
    )
    mixed, stats = pl.pallas_call(
        functools.partial(attend_own_body, token_rows),
        in_specs=[vmem] * members,
        out_specs=[vmem] * 2,
        out_shape=[
            jax.ShapeDtypeStruct((total, DH), jnp.float32),
            jax.ShapeDtypeStruct((2, total, DH), jnp.float32),
        ],
        compiler_params=params,
        cost_estimate=cost,
        name="attend_own",
    )(*own)
    return pl.pallas_call(
        attend_body,
        in_specs=[vmem] * (members + 3),
        out_specs=pl.BlockSpec(memory_space=pltpu.HBM),
        out_shape=jax.ShapeDtypeStruct((members, token_rows, DH), own[0].dtype),
        scratch_shapes=[
            pltpu.VMEM((members, token_rows, DH), own[0].dtype),
            pltpu.SemaphoreType.DMA((members,)),
        ],
        compiler_params=params,
        cost_estimate=cost,
        name="attend",
    )(*own, other, mixed, stats)


def unpack_body(in_ref, out_ref, sems):
    copies = [
        pltpu.make_async_copy(
            in_ref.at[head], out_ref.at[:, pl.ds(head * DH, DH)], sems.at[head]
        )
        for head in range(in_ref.shape[0])
    ]
    for copy in copies:
        copy.start()
    for copy in copies:
        copy.wait()


def unpack_heads(array):
    heads, token_rows, _ = array.shape
    return pl.pallas_call(
        unpack_body,
        in_specs=[pl.BlockSpec(memory_space=pltpu.VMEM)],
        out_specs=pl.BlockSpec(memory_space=pltpu.HBM),
        out_shape=jax.ShapeDtypeStruct((token_rows, heads * DH), array.dtype),
        scratch_shapes=[pltpu.SemaphoreType.DMA((heads,))],
        compiler_params=pltpu.CompilerParams(vmem_limit_bytes=COPY_VMEM),
        name="unpack_heads",
    )(array)


def decode_body(
    grid_rows,
    width,
    share_rows,
    members,
    halves,
    *refs,
):
    own, other, refs = refs[:members], refs[members : members + halves], refs[members + halves :]
    order = sending_order(members)
    (
    tile_hbm,
    in_weight_hbm,
    in_bias_hbm,
    gain_hbm,
    mid_weight_hbm,
    mid_bias_hbm,
    out_hbm,
    tile_ref,
    out_ref,
    mid_weight,
    in_weight_ref,
    in_bias_ref,
    gain_ref,
    mid_bias_ref,
    taps,
    rows_held,
    patches,
    raw,
    hidden,
    activated,
    active,
    summed,
    weight_sems,
    small_sems,
    out_sems,
    ) = refs
    pairs = active.shape[1] // 16
    channels, features = in_weight_ref.shape[3:]
    columns = out_ref.shape[2]
    lane_tiles = features // 128
    position = lax.axis_index("seq")
    section = lax.axis_index("sect")
    tile_copy = pltpu.make_async_copy(tile_hbm, tile_ref, small_sems.at[4])
    tile_copy.start()
    small = [
        pltpu.make_async_copy(source, target, small_sems.at[place])
        for place, (source, target) in enumerate(
            (
                (in_weight_hbm, in_weight_ref),
                (in_bias_hbm, in_bias_ref),
                (gain_hbm, gain_ref),
                (mid_bias_hbm, mid_bias_ref),
            )
        )
    ]
    for copy in small:
        copy.start()

    def load(col_tap):
        return [
            pltpu.make_async_copy(
                mid_weight_hbm.at[tap, row_tap, col_tap],
                mid_weight.at[
                    col_tap,
                    pl.ds(row_tap * features, features),
                    pl.ds((2 - tap) * features, features),
                ],
                weight_sems.at[col_tap, row_tap, slot],
            )
            for row_tap in range(3)
            for slot, tap in enumerate(TAPS)
        ]

    for col_tap in range(3):
        for copy in load(col_tap):
            copy.start()

    tile_copy.wait()
    filled = tile_ref[position]
    first_row = lax.fori_loop(0, position, lambda d, total: total + tile_ref[d], jnp.int32(0))

    chunks = rows_held.shape[1] // 128
    extra = -(-share_rows * chunks // 16) * 16
    shares = [ref[ref.shape[0] - extra :] for ref in own]
    shares += [ref[m, ref.shape[1] - extra :] for ref in other for m in range(ref.shape[0])]
    for place, share in enumerate(shares):
        lines = share.astype(jnp.float32)
        low = (place // members * members + order[place % members]) * share_rows
        for chunk in range(chunks):
            rows_held[low : low + share_rows, chunk * 128 : (chunk + 1) * 128] = lines[
                chunk * share_rows : (chunk + 1) * share_rows
            ]
    latent = rows_held[...]
    aside = pltpu.roll(latent, latent.shape[1] - RIM, 1).astype(jnp.bfloat16)
    latent = latent.astype(jnp.bfloat16)
    held_rows = latent.shape[0]
    unit = lax.broadcasted_iota(jnp.int32, (UNITS, held_rows), 0)
    held = lax.broadcasted_iota(jnp.int32, (UNITS, held_rows), 1)
    side = (held >= members * share_rows).astype(jnp.int32)
    member = (held // share_rows - side * members) ^ (position // 2)
    held = (2 * member + ((position & 1) ^ side)) * share_rows + held % share_rows
    frame = sum((unit >= (k + 1) * REACH).astype(jnp.int32) for k in range(LF))
    reach = unit - frame * REACH
    selectors = []
    for tap in TAPS:
        for row_parity in range(2):
            for i in range(2):
                token_row = first_row + (reach >> 1) - 1 + i
                source = frame + tap - 2
                wanted = (
                    ((reach & 1) == row_parity)
                    & (token_row >= 0)
                    & (token_row < grid_rows)
                    & (source >= 0)
                    & (source < LF)
                )
                target = jnp.where(wanted, source * grid_rows + token_row, -1)
                selectors.append(jnp.where(held == target, 1.0, 0.0).astype(jnp.bfloat16))
    selector = jnp.concatenate(selectors, axis=0)
    even = jnp.dot(selector, latent, preferred_element_type=jnp.float32)
    odd = jnp.dot(selector, aside, preferred_element_type=jnp.float32)
    for chunk in range(chunks):
        lanes = slice(chunk * 128, (chunk + 1) * 128)
        for group in range(len(selectors)):
            rows = slice(group * UNITS, (group + 1) * UNITS)
            piece = jnp.concatenate([even[rows, lanes], odd[rows, lanes]], axis=0)
            patches[
                chunk * 2 * UNITS : (chunk + 1) * 2 * UNITS, group * 128 : (group + 1) * 128
            ] = piece.astype(jnp.bfloat16)

    for copy in small:
        copy.wait()
    nothing = jnp.zeros((channels, features), jnp.bfloat16)
    base = 0
    for tap in TAPS:
        for row_parity in range(2):
            for i, j, p, q in [
                (i, j, p, q) for i in range(2) for j in range(2) for p in range(2) for q in range(2)
            ]:
                for col_parity in range(2):
                    row_tap, col_tap = 2 * i + p - row_parity, 2 * j + q - col_parity
                    inside = 0 <= row_tap < 3 and 0 <= col_tap < 3
                    taps[base : base + channels, col_parity * features : (col_parity + 1) * features] = (
                        in_weight_ref[tap, row_tap, col_tap] if inside else nothing
                    )
                base += channels

    unit_row = lax.broadcasted_iota(jnp.int32, (UNITS, 1), 0)
    row_frame = sum((unit_row >= (k + 1) * REACH).astype(jnp.int32) for k in range(LF))
    pixel_row = 2 * first_row + unit_row - row_frame * REACH - 1
    row_inside = (pixel_row >= 0) & (pixel_row < 2 * grid_rows)
    in_bias = in_bias_ref[...].reshape(1, features)
    half_gain = gain_ref[...].reshape(1, features) * 0.5

    def first_layer(chunk):
        for corner in range(2):
            start = (chunk * 2 + corner) * UNITS
            for col_parity in range(2):
                value = (
                    raw[pl.ds(start, UNITS), col_parity * features : (col_parity + 1) * features]
                    + in_bias
                )
                value = value.astype(jnp.bfloat16).astype(jnp.float32)
                scale = lax.rsqrt(jnp.mean(value * value, axis=1, keepdims=True) + 1e-06)
                column = chunk * 4 + corner * 2 + col_parity
                pixel = section * columns + column - 1
                keep = row_inside & (pixel >= 0) & (pixel < width)
                half = value * jnp.where(keep, scale, 0.0) * half_gain
                result = half + half * jnp.tanh(half)
                at = pl.ds(column * UNITS, UNITS)
                for lane in range(lane_tiles):
                    lanes = slice(lane * 128, (lane + 1) * 128)
                    hidden[lane, at] = value[:, lanes]
                    activated[lane, at] = result[:, lanes]

    middle = (chunks + 1) // 2
    groups = ((0, middle), (middle, chunks))
    for low, high in groups:
        rows = slice(low * 2 * UNITS, high * 2 * UNITS)
        raw[rows] = jnp.dot(patches[rows], taps[...], preferred_element_type=jnp.float32)
    for low, high in groups:
        for chunk in range(low, high):
            first_layer(chunk)

    def pair_up(phase, pair):
        at = slice(pair * 16, pair * 16 + 16)
        for lane in range(lane_tiles):
            for field in range(LF):
                for row_tap in range(3):
                    start = (2 * pair + phase) * UNITS + field * REACH + row_tap
                    joined = jnp.concatenate(
                        [activated[lane, pl.ds(start + k * UNITS, ROWS)] for k in range(2)], axis=0
                    )
                    to_lane = (field * 3 + row_tap) * features + lane * 128
                    active[phase, at, to_lane : to_lane + 128] = joined.astype(jnp.bfloat16)

    rows = columns * ROWS
    depth = 3 * features

    def windows(low, high, lanes):
        return jnp.concatenate(
            [
                active[tap % 2, 16 * (tap // 2) + low : 16 * (tap // 2) + high, lanes]
                for tap in range(3)
            ],
            axis=1,
        )

    def weights(lanes):
        return jnp.concatenate([mid_weight[tap, :, lanes] for tap in range(3)], axis=0)

    mid_bias = mid_bias_ref[...].reshape(1, features)

    def finish(field):
        tile_row = lax.broadcasted_iota(jnp.int32, (columns * ROWS, 128), 0) & (ROWS - 1)
        for lane in range(lane_tiles):
            lanes = slice(lane * 128, (lane + 1) * 128)
            skip = jnp.concatenate(
                [
                    hidden[lane, pl.ds((column + 1) * UNITS + field * REACH + 1, ROWS)]
                    for column in range(columns)
                ],
                axis=0,
            )
            value = summed[field, lane] + skip + mid_bias[:, lanes]
            value = jnp.where(tile_row < 2 * filled, value, 0.0)
            value = jnp.swapaxes(value.reshape(columns, ROWS, 128), 0, 1)
            out_ref[field, :, :, lanes] = value.astype(jnp.bfloat16)
        leave(field).start()

    def leave(field):
        return pltpu.make_async_copy(out_ref.at[field], out_hbm.at[field], out_sems.at[field])

    for phase in range(2):
        for pair in range(pairs - phase):
            pair_up(phase, pair)
    for tap in range(3):
        for copy in load(tap):
            copy.wait()
    early = windows(0, rows, slice(0, depth))
    late = windows(0, rows, slice(depth, 2 * depth))
    for left in range(0, 2 * features, 256):
        block = jnp.dot(
            early, weights(slice(left, left + 256)), preferred_element_type=jnp.float32
        )
        for lane in range(2):
            field, tile = divmod(left // 128 + lane, lane_tiles)
            summed[field, tile] = block[:, lane * 128 : (lane + 1) * 128]
    finish(0)
    for left in range(0, features, 256):
        right = min(left + 256, features)
        block = jnp.dot(late, weights(slice(left, right)), preferred_element_type=jnp.float32)
        for lane in range((right - left) // 128):
            tile = left // 128 + lane
            summed[1, tile] = summed[1, tile] + block[:, lane * 128 : (lane + 1) * 128]
    finish(1)
    for field in range(LF):
        leave(field).wait()


def decode_tile(
    own,
    other,
    share_rows,
    grid_rows,
    width,
    tile_rows,
    conv_in_weight,
    conv_in_bias,
    norm_gain,
    conv_mid_weight,
    conv_mid_bias,
):
    sections = lax.axis_size("sect")
    channels, features = conv_in_weight.shape[3:]
    token_width = 4 * channels
    columns = width // sections
    span = columns // 2
    pairs = span + 1
    chunks = (span + 2) * token_width // 128
    lane_tiles = features // 128
    vmem = pl.BlockSpec(memory_space=pltpu.VMEM)
    hbm = pl.BlockSpec(memory_space=pltpu.HBM)
    slots = len(TAPS)
    depth = slots * 2 * 4 * token_width
    held = chunks * 4 * UNITS
    return pl.pallas_call(
        functools.partial(decode_body, grid_rows, width, share_rows, len(own), len(other)),
        in_specs=[vmem] * (len(own) + len(other)) + [hbm] * 6,
        out_specs=hbm,
        out_shape=jax.ShapeDtypeStruct((LF, ROWS, columns, features), jnp.bfloat16),
        scratch_shapes=[
            pltpu.SMEM(tile_rows.shape, tile_rows.dtype),
            pltpu.VMEM((LF, ROWS, columns, features), jnp.bfloat16),
            pltpu.VMEM((3, 3 * features, slots * features), jnp.bfloat16),
            pltpu.VMEM(conv_in_weight.shape, jnp.bfloat16),
            pltpu.VMEM(conv_in_bias.shape, jnp.float32),
            pltpu.VMEM(norm_gain.shape, jnp.float32),
            pltpu.VMEM(conv_mid_bias.shape, jnp.float32),
            pltpu.VMEM((depth, 2 * features), jnp.bfloat16),
            pltpu.VMEM((2 * len(own) * share_rows, chunks * 128), jnp.float32),
            pltpu.VMEM((chunks * 2 * UNITS, depth), jnp.bfloat16),
            pltpu.VMEM((chunks * 2 * UNITS, 2 * features), jnp.float32),
            pltpu.VMEM((lane_tiles, held, 128), jnp.float32),
            pltpu.VMEM((lane_tiles, held, 128), jnp.float32),
            pltpu.VMEM((2, pairs * 16, LF * 3 * features), jnp.bfloat16),
            pltpu.VMEM((LF, lane_tiles, columns * ROWS, 128), jnp.float32),
            pltpu.SemaphoreType.DMA((3, 3, slots)),
            pltpu.SemaphoreType.DMA((5,)),
            pltpu.SemaphoreType.DMA((LF,)),
        ],
        compiler_params=pltpu.CompilerParams(vmem_limit_bytes=DECODE_VMEM),
        cost_estimate=pl.CostEstimate(
            flops=2 * 3 * 9 * columns * ROWS * features * features,
            bytes_accessed=slots * 9 * features * features * 2,
            transcendentals=held * features,
        ),
        name="decode_tile",
    )(
        *own,
        *other,
        *in_hbm(
            tile_rows, conv_in_weight, conv_in_bias, norm_gain, conv_mid_weight, conv_mid_bias
        ),
    )


def on_device(
    queries,
    key_tokens,
    value_tokens,
    latent,
    tile_rows,
    conv_in_weight,
    conv_in_bias,
    norm_gain,
    conv_mid_weight,
    conv_mid_bias,
):
    devices = lax.axis_size("seq")
    groups = parity_groups(devices)
    grid_rows = latent.shape[0] * devices // LF
    token_width = 4 * conv_in_weight.shape[3]
    packed = pack_heads(queries, key_tokens, value_tokens, latent, token_width)
    own = [
        lax.ppermute(piece, "seq", xor_pairs(2 * m)) if m else piece
        for m, piece in zip(sending_order(len(packed)), packed)
    ]
    joined = join(own, queries.shape[0])
    other = [lax.ppermute(joined, "seq", xor_pairs(1))]
    mixed = attend(own, other[0], queries.shape[0])
    returned = lax.all_to_all(mixed, "seq", 0, 0, axis_index_groups=groups, tiled=True)
    frames = decode_tile(
        own,
        other,
        latent.shape[0],
        grid_rows,
        2 * latent.shape[1] // token_width,
        tile_rows,
        conv_in_weight,
        conv_in_bias,
        norm_gain,
        conv_mid_weight,
        conv_mid_bias,
    )
    return (unpack_heads(returned), frames)


def solution(mesh):
    in_specs = (
        P("seq", None),
        P("seq", None),
        P("seq", None),
        P("seq", None),
        P(),
        P(),
        P(),
        P(),
        P(),
        P(),
    )
    out_specs = (P("seq", "sect"), P(None, "seq", "sect", None))
    return jax.shard_map(
        on_device, mesh=mesh, in_specs=in_specs, out_specs=out_specs, check_vma=False
    )
```

```python
import functools
import math

import jax
import jax.numpy as jnp
from jax import lax
from jax.experimental import pallas as pl
from jax.experimental.pallas import tpu as pltpu
from jax.sharding import PartitionSpec as P

DH = 128
LF = 2
MAXT = 4
RIM = 64
TAPS = (1, 2)
ROWS = 2 * MAXT
REACH = ROWS + 2
UNITS = -(-LF * REACH // 8) * 8
DECODE_VMEM = 32 * 1024 * 1024
ATTEND_VMEM = 32 * 1024 * 1024
COPY_VMEM = 16 * 1024 * 1024


def parity_groups(devices):
    return [list(range(parity, devices, 2)) for parity in range(2)]


def in_hbm(*arrays):
    return [pltpu.with_memory_space_constraint(array, pltpu.HBM) for array in arrays]


def pack_body(query_ref, key_ref, value_ref, latent_ref, *refs):
    packed_refs, (held, latent_held, sems) = refs[:-3], refs[-3:]
    heads = len(packed_refs)
    chip = lax.axis_index("seq") // 2
    token_rows = query_ref.shape[0]
    section = lax.axis_index("sect")
    wide_columns = pl.ds(pl.multiple_of(section * heads * DH, DH), heads * DH)
    copies = [
        pltpu.make_async_copy(ref.at[:, wide_columns], held.at[place], sems.at[place])
        for place, ref in enumerate((query_ref, key_ref, value_ref))
    ]
    latent_copy = pltpu.make_async_copy(latent_ref, latent_held, sems.at[3])
    latent_copy.start()
    for copy in copies:
        copy.start()
    rows, width = latent_ref.shape
    latent_copy.wait()
    half, rim = width // 2, RIM
    wide = latent_held[...].astype(jnp.float32)
    rim_zeros = jnp.zeros((rows, rim), jnp.float32)
    lower = jnp.concatenate([rim_zeros, wide[:, : half + rim]], axis=1)
    upper = jnp.concatenate([wide[:, half - rim :], rim_zeros], axis=1)
    share = jnp.where(section == 0, lower, upper)
    chunks = share.shape[1] // DH
    lines = [share[:, chunk * DH : (chunk + 1) * DH] for chunk in range(chunks)]
    spare = packed_refs[0].shape[0] - 3 * token_rows - chunks * rows
    lines.append(jnp.zeros((spare, DH), jnp.float32))
    share = jnp.concatenate(lines, axis=0).astype(jnp.bfloat16)
    for packed_ref in packed_refs:
        packed_ref[3 * token_rows :] = share
    for place, copy in enumerate(copies):
        copy.wait()
        for m, packed_ref in zip(sending_order(heads), packed_refs):
            columns = pl.ds(pl.multiple_of((chip ^ m) * DH, DH), DH)
            packed_ref[place * token_rows : (place + 1) * token_rows] = held[place, :, columns]


def pack_heads(queries, key_tokens, value_tokens, latent, token_width):
    token_rows, width = queries.shape
    sections = lax.axis_size("sect")
    heads = width // DH // sections
    span = latent.shape[1] // sections + 2 * token_width
    extra = -(-latent.shape[0] * (span // DH) // 16) * 16
    hbm = pl.BlockSpec(memory_space=pltpu.HBM)
    vmem = pl.BlockSpec(memory_space=pltpu.VMEM)
    return pl.pallas_call(
        pack_body,
        in_specs=[hbm] * 4,
        out_specs=[vmem] * heads,
        out_shape=[jax.ShapeDtypeStruct((3 * token_rows + extra, DH), queries.dtype)] * heads,
        scratch_shapes=[
            pltpu.VMEM((3, token_rows, heads * DH), queries.dtype),
            pltpu.VMEM(latent.shape, latent.dtype),
            pltpu.SemaphoreType.DMA((4,)),
        ],
        compiler_params=pltpu.CompilerParams(vmem_limit_bytes=COPY_VMEM),
        name="pack_heads",
    )(*in_hbm(queries, key_tokens, value_tokens, latent))


def sending_order(chips):
    far, near = list(range(chips // 2, chips)), list(range(1, chips // 2))
    return [0, *far[:1], *near[1:2], *far[1:], *near[2:], *near[:1]]


def xor_pairs(distance):
    return [(i, i ^ distance) for i in range(lax.axis_size("seq"))]


def join_body(*refs):
    out_ref = refs[-1]
    for place, ref in enumerate(refs[:-1]):
        out_ref[place] = ref[ref.shape[0] - out_ref.shape[1] :]


def join(pieces, skipped):
    rows, width = pieces[0].shape
    vmem = pl.BlockSpec(memory_space=pltpu.VMEM)
    return pl.pallas_call(
        join_body,
        in_specs=[vmem] * len(pieces),
        out_specs=vmem,
        out_shape=jax.ShapeDtypeStruct((len(pieces), rows - skipped, width), pieces[0].dtype),
        compiler_params=pltpu.CompilerParams(vmem_limit_bytes=COPY_VMEM),
        name="join",
    )(*pieces)


def flat(array):
    return array.reshape(-1, array.shape[-1])


def softmax_part(query, keys, values):
    scores = lax.dot_general(
        query, keys, (((1,), (1,)), ((), ())), preferred_element_type=jnp.float32
    ) * (1.0 / math.sqrt(DH))
    largest = jnp.max(scores, axis=1, keepdims=True)
    exponents = jnp.exp(scores - largest)
    totals = jnp.sum(exponents, axis=1, keepdims=True)
    mixed = jnp.dot(exponents.astype(jnp.bfloat16), values, preferred_element_type=jnp.float32)
    return largest, totals, mixed


def piece_rows(place, token_rows, pieces):
    at = slice(place * token_rows, (place + 1) * token_rows)
    return jnp.concatenate([ref[at] for ref in pieces], axis=0)


def attend_own_body(token_rows, *refs):
    pieces, (other_ref, mixed_ref, stats_ref) = refs[:-3], refs[-3:]
    block = min(4, len(pieces))
    keys = jnp.concatenate(
        [piece_rows(1, token_rows, pieces), flat(other_ref[:, :token_rows])], axis=0
    )
    values = jnp.concatenate(
        [piece_rows(2, token_rows, pieces), flat(other_ref[:, token_rows : 2 * token_rows])], axis=0
    )
    for step in range(0, len(pieces), block):
        query = piece_rows(0, token_rows, pieces[step : step + block])
        largest, totals, mixed = softmax_part(query, keys, values)
        at = slice(step * token_rows, (step + block) * token_rows)
        mixed_ref[at] = mixed
        stats_ref[0, at] = jnp.broadcast_to(largest, mixed.shape)
        stats_ref[1, at] = jnp.broadcast_to(totals, mixed.shape)


def attend_body(*refs):
    other_ref, mixed_ref, stats_ref, out_hbm, out_ref, sems = refs[-6:]
    pieces = refs[:-6]
    members, token_rows, _ = out_ref.shape
    block = min(4, members)
    chip = lax.axis_index("seq") // 2
    order = sending_order(members)

    def leave(m):
        target = out_hbm.at[chip ^ order[m]]
        return pltpu.make_async_copy(out_ref.at[m], target, sems.at[m])

    keys = flat(other_ref[:, :token_rows])
    values = flat(other_ref[:, token_rows : 2 * token_rows])
    for step in range(0, members, block):
        query = piece_rows(0, token_rows, pieces[step : step + block])
        largest, totals, mixed = softmax_part(query, keys, values)
        at = slice(step * token_rows, (step + block) * token_rows)
        earlier = stats_ref[0, at]
        top = jnp.maximum(earlier, largest)
        before, now = jnp.exp(earlier - top), jnp.exp(largest - top)
        totals = stats_ref[1, at] * before + totals * now
        mixed = (mixed_ref[at] * before + mixed * now) / totals
        mixed = mixed.astype(out_ref.dtype)
        for m in range(block):
            out_ref[step + m] = mixed[m * token_rows : (m + 1) * token_rows]
            leave(step + m).start()
    for m in range(members):
        leave(m).wait()


def attend(own, other, token_rows):
    members = len(own)
    total = members * token_rows
    vmem = pl.BlockSpec(memory_space=pltpu.VMEM)
    params = pltpu.CompilerParams(vmem_limit_bytes=ATTEND_VMEM)
    cost = pl.CostEstimate(
        flops=4 * total * total * DH,
        bytes_accessed=7 * total * DH * 2,
        transcendentals=total * total,
    )
    mixed, stats = pl.pallas_call(
        functools.partial(attend_own_body, token_rows),
        in_specs=[vmem] * (members + 1),
        out_specs=[vmem] * 2,
        out_shape=[
            jax.ShapeDtypeStruct((total, DH), jnp.float32),
            jax.ShapeDtypeStruct((2, total, DH), jnp.float32),
        ],
        compiler_params=params,
        cost_estimate=cost,
        name="attend_own",
    )(*own, other[0])
    return pl.pallas_call(
        attend_body,
        in_specs=[vmem] * (members + 3),
        out_specs=pl.BlockSpec(memory_space=pltpu.HBM),
        out_shape=jax.ShapeDtypeStruct((members, token_rows, DH), own[0].dtype),
        scratch_shapes=[
            pltpu.VMEM((members, token_rows, DH), own[0].dtype),
            pltpu.SemaphoreType.DMA((members,)),
        ],
        compiler_params=params,
        cost_estimate=cost,
        name="attend",
    )(*own, other[1], mixed, stats)


def unpack_body(in_ref, out_ref, sems):
    copies = [
        pltpu.make_async_copy(
            in_ref.at[head], out_ref.at[:, pl.ds(head * DH, DH)], sems.at[head]
        )
        for head in range(in_ref.shape[0])
    ]
    for copy in copies:
        copy.start()
    for copy in copies:
        copy.wait()


def unpack_heads(array):
    heads, token_rows, _ = array.shape
    return pl.pallas_call(
        unpack_body,
        in_specs=[pl.BlockSpec(memory_space=pltpu.VMEM)],
        out_specs=pl.BlockSpec(memory_space=pltpu.HBM),
        out_shape=jax.ShapeDtypeStruct((token_rows, heads * DH), array.dtype),
        scratch_shapes=[pltpu.SemaphoreType.DMA((heads,))],
        compiler_params=pltpu.CompilerParams(vmem_limit_bytes=COPY_VMEM),
        name="unpack_heads",
    )(array)


def decode_body(
    grid_rows,
    width,
    share_rows,
    members,
    halves,
    *refs,
):
    own, other, refs = refs[:members], refs[members : members + halves], refs[members + halves :]
    order = sending_order(members)
    (
    tile_hbm,
    in_weight_hbm,
    in_bias_hbm,
    gain_hbm,
    mid_weight_hbm,
    mid_bias_hbm,
    out_hbm,
    tile_ref,
    out_ref,
    mid_weight,
    in_weight_ref,
    in_bias_ref,
    gain_ref,
    mid_bias_ref,
    taps,
    rows_held,
    patches,
    raw,
    hidden,
    activated,
    active,
    summed,
    weight_sems,
    small_sems,
    out_sems,
    ) = refs
    pairs = active.shape[1] // 16
    channels, features = in_weight_ref.shape[3:]
    columns = out_ref.shape[2]
    lane_tiles = features // 128
    position = lax.axis_index("seq")
    section = lax.axis_index("sect")
    tile_copy = pltpu.make_async_copy(tile_hbm, tile_ref, small_sems.at[4])
    tile_copy.start()
    small = [
        pltpu.make_async_copy(source, target, small_sems.at[place])
        for place, (source, target) in enumerate(
            (
                (in_weight_hbm, in_weight_ref),
                (in_bias_hbm, in_bias_ref),
                (gain_hbm, gain_ref),
                (mid_bias_hbm, mid_bias_ref),
            )
        )
    ]
    for copy in small:
        copy.start()

    def load(col_tap):
        return [
            pltpu.make_async_copy(
                mid_weight_hbm.at[tap, row_tap, col_tap],
                mid_weight.at[
                    col_tap,
                    pl.ds(row_tap * features, features),
                    pl.ds((2 - tap) * features, features),
                ],
                weight_sems.at[col_tap, row_tap, slot],
            )
            for row_tap in range(3)
            for slot, tap in enumerate(TAPS)
        ]

    for col_tap in range(3):
        for copy in load(col_tap):
            copy.start()

    tile_copy.wait()
    filled = tile_ref[position]
    first_row = lax.fori_loop(0, position, lambda d, total: total + tile_ref[d], jnp.int32(0))

    chunks = rows_held.shape[1] // 128
    extra = -(-share_rows * chunks // 16) * 16
    shares = [ref[ref.shape[0] - extra :] for ref in own]
    shares += [ref[m, ref.shape[1] - extra :] for ref in other for m in range(ref.shape[0])]
    for place, share in enumerate(shares):
        lines = share.astype(jnp.float32)
        low = (place // members * members + order[place % members]) * share_rows
        for chunk in range(chunks):
            rows_held[low : low + share_rows, chunk * 128 : (chunk + 1) * 128] = lines[
                chunk * share_rows : (chunk + 1) * share_rows
            ]
    latent = rows_held[...]
    aside = pltpu.roll(latent, latent.shape[1] - RIM, 1).astype(jnp.bfloat16)
    latent = latent.astype(jnp.bfloat16)
    held_rows = latent.shape[0]
    unit = lax.broadcasted_iota(jnp.int32, (UNITS, held_rows), 0)
    held = lax.broadcasted_iota(jnp.int32, (UNITS, held_rows), 1)
    side = (held >= members * share_rows).astype(jnp.int32)
    member = (held // share_rows - side * members) ^ (position // 2)
    held = (2 * member + ((position & 1) ^ side)) * share_rows + held % share_rows
    frame = sum((unit >= (k + 1) * REACH).astype(jnp.int32) for k in range(LF))
    reach = unit - frame * REACH
    selectors = []
    for tap in TAPS:
        for row_parity in range(2):
            for i in range(2):
                token_row = first_row + (reach >> 1) - 1 + i
                source = frame + tap - 2
                wanted = (
                    ((reach & 1) == row_parity)
                    & (token_row >= 0)
                    & (token_row < grid_rows)
                    & (source >= 0)
                    & (source < LF)
                )
                target = jnp.where(wanted, source * grid_rows + token_row, -1)
                selectors.append(jnp.where(held == target, 1.0, 0.0).astype(jnp.bfloat16))
    selector = jnp.concatenate(selectors, axis=0)
    even = jnp.dot(selector, latent, preferred_element_type=jnp.float32)
    odd = jnp.dot(selector, aside, preferred_element_type=jnp.float32)
    for chunk in range(chunks):
        lanes = slice(chunk * 128, (chunk + 1) * 128)
        for group in range(len(selectors)):
            rows = slice(group * UNITS, (group + 1) * UNITS)
            piece = jnp.concatenate([even[rows, lanes], odd[rows, lanes]], axis=0)
            patches[
                chunk * 2 * UNITS : (chunk + 1) * 2 * UNITS, group * 128 : (group + 1) * 128
            ] = piece.astype(jnp.bfloat16)

    for copy in small:
        copy.wait()
    nothing = jnp.zeros((channels, features), jnp.bfloat16)
    base = 0
    for tap in TAPS:
        for row_parity in range(2):
            for i, j, p, q in [
                (i, j, p, q) for i in range(2) for j in range(2) for p in range(2) for q in range(2)
            ]:
                for col_parity in range(2):
                    row_tap, col_tap = 2 * i + p - row_parity, 2 * j + q - col_parity
                    inside = 0 <= row_tap < 3 and 0 <= col_tap < 3
                    taps[base : base + channels, col_parity * features : (col_parity + 1) * features] = (
                        in_weight_ref[tap, row_tap, col_tap] if inside else nothing
                    )
                base += channels

    unit_row = lax.broadcasted_iota(jnp.int32, (UNITS, 1), 0)
    row_frame = sum((unit_row >= (k + 1) * REACH).astype(jnp.int32) for k in range(LF))
    pixel_row = 2 * first_row + unit_row - row_frame * REACH - 1
    row_inside = (pixel_row >= 0) & (pixel_row < 2 * grid_rows)
    in_bias = in_bias_ref[...].reshape(1, features)
    half_gain = gain_ref[...].reshape(1, features) * 0.5

    def first_layer(chunk):
        for corner in range(2):
            start = (chunk * 2 + corner) * UNITS
            for col_parity in range(2):
                value = (
                    raw[pl.ds(start, UNITS), col_parity * features : (col_parity + 1) * features]
                    + in_bias
                )
                value = value.astype(jnp.bfloat16).astype(jnp.float32)
                scale = lax.rsqrt(jnp.mean(value * value, axis=1, keepdims=True) + 1e-06)
                column = chunk * 4 + corner * 2 + col_parity
                pixel = section * columns + column - 1
                keep = row_inside & (pixel >= 0) & (pixel < width)
                half = value * jnp.where(keep, scale, 0.0) * half_gain
                result = half + half * jnp.tanh(half)
                at = pl.ds(column * UNITS, UNITS)
                for lane in range(lane_tiles):
                    lanes = slice(lane * 128, (lane + 1) * 128)
                    hidden[lane, at] = value[:, lanes]
                    activated[lane, at] = result[:, lanes]

    middle = (chunks + 1) // 2
    groups = ((0, middle), (middle, chunks))
    for low, high in groups:
        rows = slice(low * 2 * UNITS, high * 2 * UNITS)
        raw[rows] = jnp.dot(patches[rows], taps[...], preferred_element_type=jnp.float32)
    for low, high in groups:
        for chunk in range(low, high):
            first_layer(chunk)

    def pair_up(phase, pair):
        at = slice(pair * 16, pair * 16 + 16)
        for lane in range(lane_tiles):
            for field in range(LF):
                for row_tap in range(3):
                    start = (2 * pair + phase) * UNITS + field * REACH + row_tap
                    joined = jnp.concatenate(
                        [activated[lane, pl.ds(start + k * UNITS, ROWS)] for k in range(2)], axis=0
                    )
                    to_lane = (field * 3 + row_tap) * features + lane * 128
                    active[phase, at, to_lane : to_lane + 128] = joined.astype(jnp.bfloat16)

    rows = columns * ROWS
    depth = 3 * features

    def windows(low, high, lanes):
        return jnp.concatenate(
            [
                active[tap % 2, 16 * (tap // 2) + low : 16 * (tap // 2) + high, lanes]
                for tap in range(3)
            ],
            axis=1,
        )

    def weights(lanes):
        return jnp.concatenate([mid_weight[tap, :, lanes] for tap in range(3)], axis=0)

    mid_bias = mid_bias_ref[...].reshape(1, features)

    def finish(field):
        tile_row = lax.broadcasted_iota(jnp.int32, (columns * ROWS, 128), 0) & (ROWS - 1)
        for lane in range(lane_tiles):
            lanes = slice(lane * 128, (lane + 1) * 128)
            skip = jnp.concatenate(
                [
                    hidden[lane, pl.ds((column + 1) * UNITS + field * REACH + 1, ROWS)]
                    for column in range(columns)
                ],
                axis=0,
            )
            value = summed[field, lane] + skip + mid_bias[:, lanes]
            value = jnp.where(tile_row < 2 * filled, value, 0.0)
            value = jnp.swapaxes(value.reshape(columns, ROWS, 128), 0, 1)
            out_ref[field, :, :, lanes] = value.astype(jnp.bfloat16)
        leave(field).start()

    def leave(field):
        return pltpu.make_async_copy(out_ref.at[field], out_hbm.at[field], out_sems.at[field])

    for phase in range(2):
        for pair in range(pairs - phase):
            pair_up(phase, pair)
    for tap in range(3):
        for copy in load(tap):
            copy.wait()
    early = windows(0, rows, slice(0, depth))
    late = windows(0, rows, slice(depth, 2 * depth))
    for left in range(0, 2 * features, 256):
        block = jnp.dot(
            early, weights(slice(left, left + 256)), preferred_element_type=jnp.float32
        )
        for lane in range(2):
            field, tile = divmod(left // 128 + lane, lane_tiles)
            summed[field, tile] = block[:, lane * 128 : (lane + 1) * 128]
    finish(0)
    for left in range(0, features, 256):
        right = min(left + 256, features)
        block = jnp.dot(late, weights(slice(left, right)), preferred_element_type=jnp.float32)
        for lane in range((right - left) // 128):
            tile = left // 128 + lane
            summed[1, tile] = summed[1, tile] + block[:, lane * 128 : (lane + 1) * 128]
    finish(1)
    for field in range(LF):
        leave(field).wait()


def decode_tile(
    own,
    other,
    share_rows,
    grid_rows,
    width,
    tile_rows,
    conv_in_weight,
    conv_in_bias,
    norm_gain,
    conv_mid_weight,
    conv_mid_bias,
):
    sections = lax.axis_size("sect")
    channels, features = conv_in_weight.shape[3:]
    token_width = 4 * channels
    columns = width // sections
    span = columns // 2
    pairs = span + 1
    chunks = (span + 2) * token_width // 128
    lane_tiles = features // 128
    vmem = pl.BlockSpec(memory_space=pltpu.VMEM)
    hbm = pl.BlockSpec(memory_space=pltpu.HBM)
    slots = len(TAPS)
    depth = slots * 2 * 4 * token_width
    held = chunks * 4 * UNITS
    return pl.pallas_call(
        functools.partial(decode_body, grid_rows, width, share_rows, len(own), len(other)),
        in_specs=[vmem] * (len(own) + len(other)) + [hbm] * 6,
        out_specs=hbm,
        out_shape=jax.ShapeDtypeStruct((LF, ROWS, columns, features), jnp.bfloat16),
        scratch_shapes=[
            pltpu.SMEM(tile_rows.shape, tile_rows.dtype),
            pltpu.VMEM((LF, ROWS, columns, features), jnp.bfloat16),
            pltpu.VMEM((3, 3 * features, slots * features), jnp.bfloat16),
            pltpu.VMEM(conv_in_weight.shape, jnp.bfloat16),
            pltpu.VMEM(conv_in_bias.shape, jnp.float32),
            pltpu.VMEM(norm_gain.shape, jnp.float32),
            pltpu.VMEM(conv_mid_bias.shape, jnp.float32),
            pltpu.VMEM((depth, 2 * features), jnp.bfloat16),
            pltpu.VMEM((2 * len(own) * share_rows, chunks * 128), jnp.float32),
            pltpu.VMEM((chunks * 2 * UNITS, depth), jnp.bfloat16),
            pltpu.VMEM((chunks * 2 * UNITS, 2 * features), jnp.float32),
            pltpu.VMEM((lane_tiles, held, 128), jnp.float32),
            pltpu.VMEM((lane_tiles, held, 128), jnp.float32),
            pltpu.VMEM((2, pairs * 16, LF * 3 * features), jnp.bfloat16),
            pltpu.VMEM((LF, lane_tiles, columns * ROWS, 128), jnp.float32),
            pltpu.SemaphoreType.DMA((3, 3, slots)),
            pltpu.SemaphoreType.DMA((5,)),
            pltpu.SemaphoreType.DMA((LF,)),
        ],
        compiler_params=pltpu.CompilerParams(vmem_limit_bytes=DECODE_VMEM),
        cost_estimate=pl.CostEstimate(
            flops=2 * 3 * 9 * columns * ROWS * features * features,
            bytes_accessed=slots * 9 * features * features * 2,
            transcendentals=held * features,
        ),
        name="decode_tile",
    )(
        *own,
        *other,
        *in_hbm(
            tile_rows, conv_in_weight, conv_in_bias, norm_gain, conv_mid_weight, conv_mid_bias
        ),
    )


def on_device(
    queries,
    key_tokens,
    value_tokens,
    latent,
    tile_rows,
    conv_in_weight,
    conv_in_bias,
    norm_gain,
    conv_mid_weight,
    conv_mid_bias,
):
    devices = lax.axis_size("seq")
    groups = parity_groups(devices)
    grid_rows = latent.shape[0] * devices // LF
    token_width = 4 * conv_in_weight.shape[3]
    packed = pack_heads(queries, key_tokens, value_tokens, latent, token_width)
    own = [
        lax.ppermute(piece, "seq", xor_pairs(2 * m)) if m else piece
        for m, piece in zip(sending_order(len(packed)), packed)
    ]
    token_rows, half = queries.shape[0], len(own) // 2
    other = [
        lax.ppermute(join(part, token_rows), "seq", xor_pairs(1))
        for part in (own[:half], own[half:])
    ]
    mixed = attend(own, other, token_rows)
    returned = lax.all_to_all(mixed, "seq", 0, 0, axis_index_groups=groups, tiled=True)
    frames = decode_tile(
        own,
        other,
        latent.shape[0],
        grid_rows,
        2 * latent.shape[1] // token_width,
        tile_rows,
        conv_in_weight,
        conv_in_bias,
        norm_gain,
        conv_mid_weight,
        conv_mid_bias,
    )
    return (unpack_heads(returned), frames)


def solution(mesh):
    in_specs = (
        P("seq", None),
        P("seq", None),
        P("seq", None),
        P("seq", None),
        P(),
        P(),
        P(),
        P(),
        P(),
        P(),
    )
    out_specs = (P("seq", "sect"), P(None, "seq", "sect", None))
    return jax.shard_map(
        on_device, mesh=mesh, in_specs=in_specs, out_specs=out_specs, check_vma=False
    )
```

```python
import functools
import math

import jax
import jax.numpy as jnp
from jax import lax
from jax.experimental import pallas as pl
from jax.experimental.pallas import tpu as pltpu
from jax.sharding import PartitionSpec as P

DH = 128
LF = 2
MAXT = 4
RIM = 64
TAPS = (1, 2)
ROWS = 2 * MAXT
REACH = ROWS + 2
UNITS = -(-LF * REACH // 8) * 8
DECODE_VMEM = 32 * 1024 * 1024
ATTEND_VMEM = 32 * 1024 * 1024
COPY_VMEM = 16 * 1024 * 1024


def parity_groups(devices):
    return [list(range(parity, devices, 2)) for parity in range(2)]


def in_hbm(*arrays):
    return [pltpu.with_memory_space_constraint(array, pltpu.HBM) for array in arrays]


def pack_body(query_ref, key_ref, value_ref, latent_ref, *refs):
    packed_refs, (held, latent_held, sems) = refs[:-3], refs[-3:]
    heads = len(packed_refs)
    chip = lax.axis_index("seq") // 2
    token_rows = query_ref.shape[0]
    section = lax.axis_index("sect")
    wide_columns = pl.ds(pl.multiple_of(section * heads * DH, DH), heads * DH)
    copies = [
        pltpu.make_async_copy(ref.at[:, wide_columns], held.at[place], sems.at[place])
        for place, ref in enumerate((query_ref, key_ref, value_ref))
    ]
    latent_copy = pltpu.make_async_copy(latent_ref, latent_held, sems.at[3])
    latent_copy.start()
    for copy in copies:
        copy.start()
    rows, width = latent_ref.shape
    latent_copy.wait()
    half, rim = width // 2, RIM
    wide = latent_held[...].astype(jnp.float32)
    rim_zeros = jnp.zeros((rows, rim), jnp.float32)
    lower = jnp.concatenate([rim_zeros, wide[:, : half + rim]], axis=1)
    upper = jnp.concatenate([wide[:, half - rim :], rim_zeros], axis=1)
    share = jnp.where(section == 0, lower, upper)
    chunks = share.shape[1] // DH
    lines = [share[:, chunk * DH : (chunk + 1) * DH] for chunk in range(chunks)]
    spare = packed_refs[0].shape[0] - 3 * token_rows - chunks * rows
    lines.append(jnp.zeros((spare, DH), jnp.float32))
    share = jnp.concatenate(lines, axis=0).astype(jnp.bfloat16)
    for packed_ref in packed_refs:
        packed_ref[3 * token_rows :] = share
    for place, copy in enumerate(copies):
        copy.wait()
        for m, packed_ref in zip(sending_order(heads), packed_refs):
            columns = pl.ds(pl.multiple_of((chip ^ m) * DH, DH), DH)
            packed_ref[place * token_rows : (place + 1) * token_rows] = held[place, :, columns]


def pack_heads(queries, key_tokens, value_tokens, latent, token_width):
    token_rows, width = queries.shape
    sections = lax.axis_size("sect")
    heads = width // DH // sections
    span = latent.shape[1] // sections + 2 * token_width
    extra = -(-latent.shape[0] * (span // DH) // 16) * 16
    hbm = pl.BlockSpec(memory_space=pltpu.HBM)
    vmem = pl.BlockSpec(memory_space=pltpu.VMEM)
    return pl.pallas_call(
        pack_body,
        in_specs=[hbm] * 4,
        out_specs=[vmem] * heads,
        out_shape=[jax.ShapeDtypeStruct((3 * token_rows + extra, DH), queries.dtype)] * heads,
        scratch_shapes=[
            pltpu.VMEM((3, token_rows, heads * DH), queries.dtype),
            pltpu.VMEM(latent.shape, latent.dtype),
            pltpu.SemaphoreType.DMA((4,)),
        ],
        compiler_params=pltpu.CompilerParams(vmem_limit_bytes=COPY_VMEM),
        name="pack_heads",
    )(*in_hbm(queries, key_tokens, value_tokens, latent))


def sending_order(chips):
    far, near = list(range(chips // 2, chips)), list(range(1, chips // 2))
    return [0, *far[:1], *near[1:2], *far[1:], *near[2:], *near[:1]]


def xor_pairs(distance):
    return [(i, i ^ distance) for i in range(lax.axis_size("seq"))]


def join_body(*refs):
    out_ref = refs[-1]
    for place, ref in enumerate(refs[:-1]):
        out_ref[place] = ref[ref.shape[0] - out_ref.shape[1] :]


def join(pieces, skipped):
    rows, width = pieces[0].shape
    vmem = pl.BlockSpec(memory_space=pltpu.VMEM)
    return pl.pallas_call(
        join_body,
        in_specs=[vmem] * len(pieces),
        out_specs=vmem,
        out_shape=jax.ShapeDtypeStruct((len(pieces), rows - skipped, width), pieces[0].dtype),
        compiler_params=pltpu.CompilerParams(vmem_limit_bytes=COPY_VMEM),
        name="join",
    )(*pieces)


def flat(array):
    return array.reshape(-1, array.shape[-1])


def softmax_part(query, keys, values):
    scores = lax.dot_general(
        query, keys, (((1,), (1,)), ((), ())), preferred_element_type=jnp.float32
    ) * (1.0 / math.sqrt(DH))
    largest = jnp.max(scores, axis=1, keepdims=True)
    exponents = jnp.exp(scores - largest)
    totals = jnp.sum(exponents, axis=1, keepdims=True)
    mixed = jnp.dot(exponents.astype(jnp.bfloat16), values, preferred_element_type=jnp.float32)
    return largest, totals, mixed


def piece_rows(place, token_rows, pieces):
    at = slice(place * token_rows, (place + 1) * token_rows)
    return jnp.concatenate([ref[at] for ref in pieces], axis=0)


def attend_own_body(token_rows, *refs):
    pieces, (other_ref, mixed_ref, stats_ref) = refs[:-3], refs[-3:]
    block = len(pieces) if len(pieces) <= 8 else 4
    keys = jnp.concatenate(
        [piece_rows(1, token_rows, pieces), flat(other_ref[:, :token_rows])], axis=0
    )
    values = jnp.concatenate(
        [piece_rows(2, token_rows, pieces), flat(other_ref[:, token_rows : 2 * token_rows])], axis=0
    )
    for step in range(0, len(pieces), block):
        query = piece_rows(0, token_rows, pieces[step : step + block])
        largest, totals, mixed = softmax_part(query, keys, values)
        at = slice(step * token_rows, (step + block) * token_rows)
        mixed_ref[at] = mixed
        stats_ref[0, at] = jnp.broadcast_to(largest, mixed.shape)
        stats_ref[1, at] = jnp.broadcast_to(totals, mixed.shape)


def attend_body(*refs):
    other_ref, mixed_ref, stats_ref, out_hbm, out_ref, sems = refs[-6:]
    pieces = refs[:-6]
    members, token_rows, _ = out_ref.shape
    block = members if members <= 8 else 4
    chip = lax.axis_index("seq") // 2
    order = sending_order(members)

    def leave(m):
        target = out_hbm.at[chip ^ order[m]]
        return pltpu.make_async_copy(out_ref.at[m], target, sems.at[m])

    keys = flat(other_ref[:, :token_rows])
    values = flat(other_ref[:, token_rows : 2 * token_rows])
    for step in range(0, members, block):
        query = piece_rows(0, token_rows, pieces[step : step + block])
        largest, totals, mixed = softmax_part(query, keys, values)
        at = slice(step * token_rows, (step + block) * token_rows)
        earlier = stats_ref[0, at]
        top = jnp.maximum(earlier, largest)
        before, now = jnp.exp(earlier - top), jnp.exp(largest - top)
        totals = stats_ref[1, at] * before + totals * now
        mixed = (mixed_ref[at] * before + mixed * now) / totals
        mixed = mixed.astype(out_ref.dtype)
        for m in range(block):
            out_ref[step + m] = mixed[m * token_rows : (m + 1) * token_rows]
            leave(step + m).start()
    for m in range(members):
        leave(m).wait()


def attend(own, other, token_rows):
    members = len(own)
    total = members * token_rows
    vmem = pl.BlockSpec(memory_space=pltpu.VMEM)
    params = pltpu.CompilerParams(vmem_limit_bytes=ATTEND_VMEM)
    cost = pl.CostEstimate(
        flops=4 * total * total * DH,
        bytes_accessed=7 * total * DH * 2,
        transcendentals=total * total,
    )
    mixed, stats = pl.pallas_call(
        functools.partial(attend_own_body, token_rows),
        in_specs=[vmem] * (members + 1),
        out_specs=[vmem] * 2,
        out_shape=[
            jax.ShapeDtypeStruct((total, DH), jnp.float32),
            jax.ShapeDtypeStruct((2, total, DH), jnp.float32),
        ],
        compiler_params=params,
        cost_estimate=cost,
        name="attend_own",
    )(*own, other[0])
    return pl.pallas_call(
        attend_body,
        in_specs=[vmem] * (members + 3),
        out_specs=pl.BlockSpec(memory_space=pltpu.HBM),
        out_shape=jax.ShapeDtypeStruct((members, token_rows, DH), own[0].dtype),
        scratch_shapes=[
            pltpu.VMEM((members, token_rows, DH), own[0].dtype),
            pltpu.SemaphoreType.DMA((members,)),
        ],
        compiler_params=params,
        cost_estimate=cost,
        name="attend",
    )(*own, other[1], mixed, stats)


def unpack_body(in_ref, out_ref, sems):
    copies = [
        pltpu.make_async_copy(
            in_ref.at[head], out_ref.at[:, pl.ds(head * DH, DH)], sems.at[head]
        )
        for head in range(in_ref.shape[0])
    ]
    for copy in copies:
        copy.start()
    for copy in copies:
        copy.wait()


def unpack_heads(array):
    heads, token_rows, _ = array.shape
    return pl.pallas_call(
        unpack_body,
        in_specs=[pl.BlockSpec(memory_space=pltpu.VMEM)],
        out_specs=pl.BlockSpec(memory_space=pltpu.HBM),
        out_shape=jax.ShapeDtypeStruct((token_rows, heads * DH), array.dtype),
        scratch_shapes=[pltpu.SemaphoreType.DMA((heads,))],
        compiler_params=pltpu.CompilerParams(vmem_limit_bytes=COPY_VMEM),
        name="unpack_heads",
    )(array)


def decode_body(
    grid_rows,
    width,
    share_rows,
    members,
    halves,
    *refs,
):
    own, other, refs = refs[:members], refs[members : members + halves], refs[members + halves :]
    order = sending_order(members)
    (
    tile_hbm,
    in_weight_hbm,
    in_bias_hbm,
    gain_hbm,
    mid_weight_hbm,
    mid_bias_hbm,
    out_hbm,
    tile_ref,
    out_ref,
    mid_weight,
    in_weight_ref,
    in_bias_ref,
    gain_ref,
    mid_bias_ref,
    taps,
    rows_held,
    patches,
    raw,
    hidden,
    activated,
    active,
    summed,
    weight_sems,
    small_sems,
    out_sems,
    ) = refs
    pairs = active.shape[1] // 16
    channels, features = in_weight_ref.shape[3:]
    columns = out_ref.shape[2]
    lane_tiles = features // 128
    position = lax.axis_index("seq")
    section = lax.axis_index("sect")
    tile_copy = pltpu.make_async_copy(tile_hbm, tile_ref, small_sems.at[4])
    tile_copy.start()
    small = [
        pltpu.make_async_copy(source, target, small_sems.at[place])
        for place, (source, target) in enumerate(
            (
                (in_weight_hbm, in_weight_ref),
                (in_bias_hbm, in_bias_ref),
                (gain_hbm, gain_ref),
                (mid_bias_hbm, mid_bias_ref),
            )
        )
    ]
    for copy in small:
        copy.start()

    def load(col_tap):
        return [
            pltpu.make_async_copy(
                mid_weight_hbm.at[tap, row_tap, col_tap],
                mid_weight.at[
                    col_tap,
                    pl.ds(row_tap * features, features),
                    pl.ds((2 - tap) * features, features),
                ],
                weight_sems.at[col_tap, row_tap, slot],
            )
            for row_tap in range(3)
            for slot, tap in enumerate(TAPS)
        ]

    for col_tap in range(3):
        for copy in load(col_tap):
            copy.start()

    tile_copy.wait()
    filled = tile_ref[position]
    first_row = lax.fori_loop(0, position, lambda d, total: total + tile_ref[d], jnp.int32(0))

    chunks = rows_held.shape[1] // 128
    extra = -(-share_rows * chunks // 16) * 16
    shares = [ref[ref.shape[0] - extra :] for ref in own]
    shares += [ref[m, ref.shape[1] - extra :] for ref in other for m in range(ref.shape[0])]
    for place, share in enumerate(shares):
        lines = share.astype(jnp.float32)
        low = (place // members * members + order[place % members]) * share_rows
        for chunk in range(chunks):
            rows_held[low : low + share_rows, chunk * 128 : (chunk + 1) * 128] = lines[
                chunk * share_rows : (chunk + 1) * share_rows
            ]
    latent = rows_held[...]
    aside = pltpu.roll(latent, latent.shape[1] - RIM, 1).astype(jnp.bfloat16)
    latent = latent.astype(jnp.bfloat16)
    held_rows = latent.shape[0]
    unit = lax.broadcasted_iota(jnp.int32, (UNITS, held_rows), 0)
    held = lax.broadcasted_iota(jnp.int32, (UNITS, held_rows), 1)
    side = (held >= members * share_rows).astype(jnp.int32)
    member = (held // share_rows - side * members) ^ (position // 2)
    held = (2 * member + ((position & 1) ^ side)) * share_rows + held % share_rows
    frame = sum((unit >= (k + 1) * REACH).astype(jnp.int32) for k in range(LF))
    reach = unit - frame * REACH
    selectors = []
    for tap in TAPS:
        for row_parity in range(2):
            for i in range(2):
                token_row = first_row + (reach >> 1) - 1 + i
                source = frame + tap - 2
                wanted = (
                    ((reach & 1) == row_parity)
                    & (token_row >= 0)
                    & (token_row < grid_rows)
                    & (source >= 0)
                    & (source < LF)
                )
                target = jnp.where(wanted, source * grid_rows + token_row, -1)
                selectors.append(jnp.where(held == target, 1.0, 0.0).astype(jnp.bfloat16))
    selector = jnp.concatenate(selectors, axis=0)
    even = jnp.dot(selector, latent, preferred_element_type=jnp.float32)
    odd = jnp.dot(selector, aside, preferred_element_type=jnp.float32)
    for chunk in range(chunks):
        lanes = slice(chunk * 128, (chunk + 1) * 128)
        for group in range(len(selectors)):
            rows = slice(group * UNITS, (group + 1) * UNITS)
            piece = jnp.concatenate([even[rows, lanes], odd[rows, lanes]], axis=0)
            patches[
                chunk * 2 * UNITS : (chunk + 1) * 2 * UNITS, group * 128 : (group + 1) * 128
            ] = piece.astype(jnp.bfloat16)

    for copy in small:
        copy.wait()
    nothing = jnp.zeros((channels, features), jnp.bfloat16)
    base = 0
    for tap in TAPS:
        for row_parity in range(2):
            for i, j, p, q in [
                (i, j, p, q) for i in range(2) for j in range(2) for p in range(2) for q in range(2)
            ]:
                for col_parity in range(2):
                    row_tap, col_tap = 2 * i + p - row_parity, 2 * j + q - col_parity
                    inside = 0 <= row_tap < 3 and 0 <= col_tap < 3
                    taps[base : base + channels, col_parity * features : (col_parity + 1) * features] = (
                        in_weight_ref[tap, row_tap, col_tap] if inside else nothing
                    )
                base += channels

    unit_row = lax.broadcasted_iota(jnp.int32, (UNITS, 1), 0)
    row_frame = sum((unit_row >= (k + 1) * REACH).astype(jnp.int32) for k in range(LF))
    pixel_row = 2 * first_row + unit_row - row_frame * REACH - 1
    row_inside = (pixel_row >= 0) & (pixel_row < 2 * grid_rows)
    in_bias = in_bias_ref[...].reshape(1, features)
    half_gain = gain_ref[...].reshape(1, features) * 0.5

    def first_layer(chunk):
        for corner in range(2):
            start = (chunk * 2 + corner) * UNITS
            for col_parity in range(2):
                value = (
                    raw[pl.ds(start, UNITS), col_parity * features : (col_parity + 1) * features]
                    + in_bias
                )
                value = value.astype(jnp.bfloat16).astype(jnp.float32)
                scale = lax.rsqrt(jnp.mean(value * value, axis=1, keepdims=True) + 1e-06)
                column = chunk * 4 + corner * 2 + col_parity
                pixel = section * columns + column - 1
                keep = row_inside & (pixel >= 0) & (pixel < width)
                half = value * jnp.where(keep, scale, 0.0) * half_gain
                result = half + half * jnp.tanh(half)
                at = pl.ds(column * UNITS, UNITS)
                for lane in range(lane_tiles):
                    lanes = slice(lane * 128, (lane + 1) * 128)
                    hidden[lane, at] = value[:, lanes]
                    activated[lane, at] = result[:, lanes]

    middle = (chunks + 1) // 2
    groups = ((0, middle), (middle, chunks))
    for low, high in groups:
        rows = slice(low * 2 * UNITS, high * 2 * UNITS)
        raw[rows] = jnp.dot(patches[rows], taps[...], preferred_element_type=jnp.float32)
    for low, high in groups:
        for chunk in range(low, high):
            first_layer(chunk)

    def pair_up(phase, pair):
        at = slice(pair * 16, pair * 16 + 16)
        for lane in range(lane_tiles):
            for field in range(LF):
                for row_tap in range(3):
                    start = (2 * pair + phase) * UNITS + field * REACH + row_tap
                    joined = jnp.concatenate(
                        [activated[lane, pl.ds(start + k * UNITS, ROWS)] for k in range(2)], axis=0
                    )
                    to_lane = (field * 3 + row_tap) * features + lane * 128
                    active[phase, at, to_lane : to_lane + 128] = joined.astype(jnp.bfloat16)

    rows = columns * ROWS
    depth = 3 * features

    def windows(low, high, lanes):
        return jnp.concatenate(
            [
                active[tap % 2, 16 * (tap // 2) + low : 16 * (tap // 2) + high, lanes]
                for tap in range(3)
            ],
            axis=1,
        )

    def weights(lanes):
        return jnp.concatenate([mid_weight[tap, :, lanes] for tap in range(3)], axis=0)

    mid_bias = mid_bias_ref[...].reshape(1, features)

    def finish(field):
        tile_row = lax.broadcasted_iota(jnp.int32, (columns * ROWS, 128), 0) & (ROWS - 1)
        for lane in range(lane_tiles):
            lanes = slice(lane * 128, (lane + 1) * 128)
            skip = jnp.concatenate(
                [
                    hidden[lane, pl.ds((column + 1) * UNITS + field * REACH + 1, ROWS)]
                    for column in range(columns)
                ],
                axis=0,
            )
            value = summed[field, lane] + skip + mid_bias[:, lanes]
            value = jnp.where(tile_row < 2 * filled, value, 0.0)
            value = jnp.swapaxes(value.reshape(columns, ROWS, 128), 0, 1)
            out_ref[field, :, :, lanes] = value.astype(jnp.bfloat16)
        leave(field).start()

    def leave(field):
        return pltpu.make_async_copy(out_ref.at[field], out_hbm.at[field], out_sems.at[field])

    for phase in range(2):
        for pair in range(pairs - phase):
            pair_up(phase, pair)
    for tap in range(3):
        for copy in load(tap):
            copy.wait()
    early = windows(0, rows, slice(0, depth))
    late = windows(0, rows, slice(depth, 2 * depth))
    for left in range(0, 2 * features, 256):
        block = jnp.dot(
            early, weights(slice(left, left + 256)), preferred_element_type=jnp.float32
        )
        for lane in range(2):
            field, tile = divmod(left // 128 + lane, lane_tiles)
            summed[field, tile] = block[:, lane * 128 : (lane + 1) * 128]
    finish(0)
    for left in range(0, features, 256):
        right = min(left + 256, features)
        block = jnp.dot(late, weights(slice(left, right)), preferred_element_type=jnp.float32)
        for lane in range((right - left) // 128):
            tile = left // 128 + lane
            summed[1, tile] = summed[1, tile] + block[:, lane * 128 : (lane + 1) * 128]
    finish(1)
    for field in range(LF):
        leave(field).wait()


def decode_tile(
    own,
    other,
    share_rows,
    grid_rows,
    width,
    tile_rows,
    conv_in_weight,
    conv_in_bias,
    norm_gain,
    conv_mid_weight,
    conv_mid_bias,
):
    sections = lax.axis_size("sect")
    channels, features = conv_in_weight.shape[3:]
    token_width = 4 * channels
    columns = width // sections
    span = columns // 2
    pairs = span + 1
    chunks = (span + 2) * token_width // 128
    lane_tiles = features // 128
    vmem = pl.BlockSpec(memory_space=pltpu.VMEM)
    hbm = pl.BlockSpec(memory_space=pltpu.HBM)
    slots = len(TAPS)
    depth = slots * 2 * 4 * token_width
    held = chunks * 4 * UNITS
    return pl.pallas_call(
        functools.partial(decode_body, grid_rows, width, share_rows, len(own), len(other)),
        in_specs=[vmem] * (len(own) + len(other)) + [hbm] * 6,
        out_specs=hbm,
        out_shape=jax.ShapeDtypeStruct((LF, ROWS, columns, features), jnp.bfloat16),
        scratch_shapes=[
            pltpu.SMEM(tile_rows.shape, tile_rows.dtype),
            pltpu.VMEM((LF, ROWS, columns, features), jnp.bfloat16),
            pltpu.VMEM((3, 3 * features, slots * features), jnp.bfloat16),
            pltpu.VMEM(conv_in_weight.shape, jnp.bfloat16),
            pltpu.VMEM(conv_in_bias.shape, jnp.float32),
            pltpu.VMEM(norm_gain.shape, jnp.float32),
            pltpu.VMEM(conv_mid_bias.shape, jnp.float32),
            pltpu.VMEM((depth, 2 * features), jnp.bfloat16),
            pltpu.VMEM((2 * len(own) * share_rows, chunks * 128), jnp.float32),
            pltpu.VMEM((chunks * 2 * UNITS, depth), jnp.bfloat16),
            pltpu.VMEM((chunks * 2 * UNITS, 2 * features), jnp.float32),
            pltpu.VMEM((lane_tiles, held, 128), jnp.float32),
            pltpu.VMEM((lane_tiles, held, 128), jnp.float32),
            pltpu.VMEM((2, pairs * 16, LF * 3 * features), jnp.bfloat16),
            pltpu.VMEM((LF, lane_tiles, columns * ROWS, 128), jnp.float32),
            pltpu.SemaphoreType.DMA((3, 3, slots)),
            pltpu.SemaphoreType.DMA((5,)),
            pltpu.SemaphoreType.DMA((LF,)),
        ],
        compiler_params=pltpu.CompilerParams(vmem_limit_bytes=DECODE_VMEM),
        cost_estimate=pl.CostEstimate(
            flops=2 * 3 * 9 * columns * ROWS * features * features,
            bytes_accessed=slots * 9 * features * features * 2,
            transcendentals=held * features,
        ),
        name="decode_tile",
    )(
        *own,
        *other,
        *in_hbm(
            tile_rows, conv_in_weight, conv_in_bias, norm_gain, conv_mid_weight, conv_mid_bias
        ),
    )


def on_device(
    queries,
    key_tokens,
    value_tokens,
    latent,
    tile_rows,
    conv_in_weight,
    conv_in_bias,
    norm_gain,
    conv_mid_weight,
    conv_mid_bias,
):
    devices = lax.axis_size("seq")
    groups = parity_groups(devices)
    grid_rows = latent.shape[0] * devices // LF
    token_width = 4 * conv_in_weight.shape[3]
    packed = pack_heads(queries, key_tokens, value_tokens, latent, token_width)
    own = [
        lax.ppermute(piece, "seq", xor_pairs(2 * m)) if m else piece
        for m, piece in zip(sending_order(len(packed)), packed)
    ]
    token_rows, half = queries.shape[0], len(own) // 2
    other = [
        lax.ppermute(join(part, token_rows), "seq", xor_pairs(1))
        for part in (own[:half], own[half:])
    ]
    mixed = attend(own, other, token_rows)
    returned = lax.all_to_all(mixed, "seq", 0, 0, axis_index_groups=groups, tiled=True)
    frames = decode_tile(
        own,
        other,
        latent.shape[0],
        grid_rows,
        2 * latent.shape[1] // token_width,
        tile_rows,
        conv_in_weight,
        conv_in_bias,
        norm_gain,
        conv_mid_weight,
        conv_mid_bias,
    )
    return (unpack_heads(returned), frames)


def solution(mesh):
    in_specs = (
        P("seq", None),
        P("seq", None),
        P("seq", None),
        P("seq", None),
        P(),
        P(),
        P(),
        P(),
        P(),
        P(),
    )
    out_specs = (P("seq", "sect"), P(None, "seq", "sect", None))
    return jax.shard_map(
        on_device, mesh=mesh, in_specs=in_specs, out_specs=out_specs, check_vma=False
    )
```

```python
import functools
import math

import jax
import jax.numpy as jnp
from jax import lax
from jax.experimental import pallas as pl
from jax.experimental.pallas import tpu as pltpu
from jax.sharding import PartitionSpec as P

DH = 128
LF = 2
MAXT = 4
RIM = 64
TAPS = (1, 2)
ROWS = 2 * MAXT
REACH = ROWS + 2
UNITS = -(-LF * REACH // 8) * 8
DECODE_VMEM = 32 * 1024 * 1024
ATTEND_VMEM = 32 * 1024 * 1024
COPY_VMEM = 16 * 1024 * 1024


def parity_groups(devices):
    return [list(range(parity, devices, 2)) for parity in range(2)]


def in_hbm(*arrays):
    return [pltpu.with_memory_space_constraint(array, pltpu.HBM) for array in arrays]


def pack_body(query_ref, key_ref, value_ref, latent_ref, *refs):
    packed_refs, (held, latent_held, sems) = refs[:-3], refs[-3:]
    heads = len(packed_refs)
    chip = lax.axis_index("seq") // 2
    token_rows = query_ref.shape[0]
    section = lax.axis_index("sect")
    wide_columns = pl.ds(pl.multiple_of(section * heads * DH, DH), heads * DH)
    copies = [
        pltpu.make_async_copy(ref.at[:, wide_columns], held.at[place], sems.at[place])
        for place, ref in enumerate((query_ref, key_ref, value_ref))
    ]
    latent_copy = pltpu.make_async_copy(latent_ref, latent_held, sems.at[3])
    latent_copy.start()
    for copy in copies:
        copy.start()
    rows, width = latent_ref.shape
    latent_copy.wait()
    half, rim = width // 2, RIM
    wide = latent_held[...].astype(jnp.float32)
    rim_zeros = jnp.zeros((rows, rim), jnp.float32)
    lower = jnp.concatenate([rim_zeros, wide[:, : half + rim]], axis=1)
    upper = jnp.concatenate([wide[:, half - rim :], rim_zeros], axis=1)
    share = jnp.where(section == 0, lower, upper)
    chunks = share.shape[1] // DH
    lines = [share[:, chunk * DH : (chunk + 1) * DH] for chunk in range(chunks)]
    spare = packed_refs[0].shape[0] - 3 * token_rows - chunks * rows
    lines.append(jnp.zeros((spare, DH), jnp.float32))
    share = jnp.concatenate(lines, axis=0).astype(jnp.bfloat16)
    for packed_ref in packed_refs:
        packed_ref[3 * token_rows :] = share
    for place, copy in enumerate(copies):
        copy.wait()
        for m, packed_ref in zip(sending_order(heads), packed_refs):
            columns = pl.ds(pl.multiple_of((chip ^ m) * DH, DH), DH)
            packed_ref[place * token_rows : (place + 1) * token_rows] = held[place, :, columns]


def pack_heads(queries, key_tokens, value_tokens, latent, token_width):
    token_rows, width = queries.shape
    sections = lax.axis_size("sect")
    heads = width // DH // sections
    span = latent.shape[1] // sections + 2 * token_width
    extra = -(-latent.shape[0] * (span // DH) // 16) * 16
    hbm = pl.BlockSpec(memory_space=pltpu.HBM)
    vmem = pl.BlockSpec(memory_space=pltpu.VMEM)
    return pl.pallas_call(
        pack_body,
        in_specs=[hbm] * 4,
        out_specs=[vmem] * heads,
        out_shape=[jax.ShapeDtypeStruct((3 * token_rows + extra, DH), queries.dtype)] * heads,
        scratch_shapes=[
            pltpu.VMEM((3, token_rows, heads * DH), queries.dtype),
            pltpu.VMEM(latent.shape, latent.dtype),
            pltpu.SemaphoreType.DMA((4,)),
        ],
        compiler_params=pltpu.CompilerParams(vmem_limit_bytes=COPY_VMEM),
        name="pack_heads",
    )(*in_hbm(queries, key_tokens, value_tokens, latent))


def sending_order(chips):
    far, near = list(range(chips // 2, chips)), list(range(1, chips // 2))
    return [0, *far[:1], *near[1:2], *far[1:], *near[2:], *near[:1]]


def xor_pairs(distance):
    return [(i, i ^ distance) for i in range(lax.axis_size("seq"))]


def join_body(*refs):
    out_ref = refs[-1]
    for place, ref in enumerate(refs[:-1]):
        out_ref[place] = ref[ref.shape[0] - out_ref.shape[1] :]


def join(pieces, skipped):
    rows, width = pieces[0].shape
    vmem = pl.BlockSpec(memory_space=pltpu.VMEM)
    return pl.pallas_call(
        join_body,
        in_specs=[vmem] * len(pieces),
        out_specs=vmem,
        out_shape=jax.ShapeDtypeStruct((len(pieces), rows - skipped, width), pieces[0].dtype),
        compiler_params=pltpu.CompilerParams(vmem_limit_bytes=COPY_VMEM),
        name="join",
    )(*pieces)


def flat(array):
    return array.reshape(-1, array.shape[-1])


def softmax_part(query, keys, values):
    scores = lax.dot_general(
        query, keys, (((1,), (1,)), ((), ())), preferred_element_type=jnp.float32
    ) * (1.0 / math.sqrt(DH))
    largest = jnp.max(scores, axis=1, keepdims=True)
    exponents = jnp.exp(scores - largest)
    totals = jnp.sum(exponents, axis=1, keepdims=True)
    mixed = jnp.dot(exponents.astype(jnp.bfloat16), values, preferred_element_type=jnp.float32)
    return largest, totals, mixed


def piece_rows(place, token_rows, pieces):
    at = slice(place * token_rows, (place + 1) * token_rows)
    return jnp.concatenate([ref[at] for ref in pieces], axis=0)


def attend_own_body(token_rows, *refs):
    pieces, (other_ref, mixed_ref, stats_ref) = refs[:-3], refs[-3:]
    block = min(4, len(pieces))
    keys = jnp.concatenate(
        [piece_rows(1, token_rows, pieces), flat(other_ref[:, :token_rows])], axis=0
    )
    values = jnp.concatenate(
        [piece_rows(2, token_rows, pieces), flat(other_ref[:, token_rows : 2 * token_rows])], axis=0
    )
    for step in range(0, len(pieces), block):
        query = piece_rows(0, token_rows, pieces[step : step + block])
        largest, totals, mixed = softmax_part(query, keys, values)
        at = slice(step * token_rows, (step + block) * token_rows)
        mixed_ref[at] = mixed
        stats_ref[0, at] = jnp.broadcast_to(largest, mixed.shape)
        stats_ref[1, at] = jnp.broadcast_to(totals, mixed.shape)


def attend_body(*refs):
    other_ref, mixed_ref, stats_ref, out_hbm, out_ref, sems = refs[-6:]
    pieces = refs[:-6]
    members, token_rows, _ = out_ref.shape
    block = members if members <= 8 else 4
    chip = lax.axis_index("seq") // 2
    order = sending_order(members)

    def leave(m):
        target = out_hbm.at[chip ^ order[m]]
        return pltpu.make_async_copy(out_ref.at[m], target, sems.at[m])

    keys = flat(other_ref[:, :token_rows])
    values = flat(other_ref[:, token_rows : 2 * token_rows])
    for step in range(0, members, block):
        query = piece_rows(0, token_rows, pieces[step : step + block])
        largest, totals, mixed = softmax_part(query, keys, values)
        at = slice(step * token_rows, (step + block) * token_rows)
        earlier = stats_ref[0, at]
        top = jnp.maximum(earlier, largest)
        before, now = jnp.exp(earlier - top), jnp.exp(largest - top)
        totals = stats_ref[1, at] * before + totals * now
        mixed = (mixed_ref[at] * before + mixed * now) / totals
        mixed = mixed.astype(out_ref.dtype)
        for m in range(block):
            out_ref[step + m] = mixed[m * token_rows : (m + 1) * token_rows]
            leave(step + m).start()
    for m in range(members):
        leave(m).wait()


def attend(own, other, token_rows):
    members = len(own)
    total = members * token_rows
    vmem = pl.BlockSpec(memory_space=pltpu.VMEM)
    params = pltpu.CompilerParams(vmem_limit_bytes=ATTEND_VMEM)
    cost = pl.CostEstimate(
        flops=4 * total * total * DH,
        bytes_accessed=7 * total * DH * 2,
        transcendentals=total * total,
    )
    mixed, stats = pl.pallas_call(
        functools.partial(attend_own_body, token_rows),
        in_specs=[vmem] * (members + 1),
        out_specs=[vmem] * 2,
        out_shape=[
            jax.ShapeDtypeStruct((total, DH), jnp.float32),
            jax.ShapeDtypeStruct((2, total, DH), jnp.float32),
        ],
        compiler_params=params,
        cost_estimate=cost,
        name="attend_own",
    )(*own, other[0])
    return pl.pallas_call(
        attend_body,
        in_specs=[vmem] * (members + 3),
        out_specs=pl.BlockSpec(memory_space=pltpu.HBM),
        out_shape=jax.ShapeDtypeStruct((members, token_rows, DH), own[0].dtype),
        scratch_shapes=[
            pltpu.VMEM((members, token_rows, DH), own[0].dtype),
            pltpu.SemaphoreType.DMA((members,)),
        ],
        compiler_params=params,
        cost_estimate=cost,
        name="attend",
    )(*own, other[1], mixed, stats)


def unpack_body(in_ref, out_ref, sems):
    copies = [
        pltpu.make_async_copy(
            in_ref.at[head], out_ref.at[:, pl.ds(head * DH, DH)], sems.at[head]
        )
        for head in range(in_ref.shape[0])
    ]
    for copy in copies:
        copy.start()
    for copy in copies:
        copy.wait()


def unpack_heads(array):
    heads, token_rows, _ = array.shape
    return pl.pallas_call(
        unpack_body,
        in_specs=[pl.BlockSpec(memory_space=pltpu.VMEM)],
        out_specs=pl.BlockSpec(memory_space=pltpu.HBM),
        out_shape=jax.ShapeDtypeStruct((token_rows, heads * DH), array.dtype),
        scratch_shapes=[pltpu.SemaphoreType.DMA((heads,))],
        compiler_params=pltpu.CompilerParams(vmem_limit_bytes=COPY_VMEM),
        name="unpack_heads",
    )(array)


def decode_body(
    grid_rows,
    width,
    share_rows,
    members,
    halves,
    *refs,
):
    own, other, refs = refs[:members], refs[members : members + halves], refs[members + halves :]
    order = sending_order(members)
    (
    tile_hbm,
    in_weight_hbm,
    in_bias_hbm,
    gain_hbm,
    mid_weight_hbm,
    mid_bias_hbm,
    out_hbm,
    tile_ref,
    out_ref,
    mid_weight,
    in_weight_ref,
    in_bias_ref,
    gain_ref,
    mid_bias_ref,
    taps,
    rows_held,
    patches,
    raw,
    hidden,
    activated,
    active,
    summed,
    weight_sems,
    small_sems,
    out_sems,
    ) = refs
    pairs = active.shape[1] // 16
    channels, features = in_weight_ref.shape[3:]
    columns = out_ref.shape[2]
    lane_tiles = features // 128
    position = lax.axis_index("seq")
    section = lax.axis_index("sect")
    tile_copy = pltpu.make_async_copy(tile_hbm, tile_ref, small_sems.at[4])
    tile_copy.start()
    small = [
        pltpu.make_async_copy(source, target, small_sems.at[place])
        for place, (source, target) in enumerate(
            (
                (in_weight_hbm, in_weight_ref),
                (in_bias_hbm, in_bias_ref),
                (gain_hbm, gain_ref),
                (mid_bias_hbm, mid_bias_ref),
            )
        )
    ]
    for copy in small:
        copy.start()

    def load(col_tap):
        return [
            pltpu.make_async_copy(
                mid_weight_hbm.at[tap, row_tap, col_tap],
                mid_weight.at[
                    col_tap,
                    pl.ds(row_tap * features, features),
                    pl.ds((2 - tap) * features, features),
                ],
                weight_sems.at[col_tap, row_tap, slot],
            )
            for row_tap in range(3)
            for slot, tap in enumerate(TAPS)
        ]

    for col_tap in range(3):
        for copy in load(col_tap):
            copy.start()

    tile_copy.wait()
    filled = tile_ref[position]
    first_row = lax.fori_loop(0, position, lambda d, total: total + tile_ref[d], jnp.int32(0))

    chunks = rows_held.shape[1] // 128
    extra = -(-share_rows * chunks // 16) * 16
    shares = [ref[ref.shape[0] - extra :] for ref in own]
    shares += [ref[m, ref.shape[1] - extra :] for ref in other for m in range(ref.shape[0])]
    for place, share in enumerate(shares):
        lines = share.astype(jnp.float32)
        low = (place // members * members + order[place % members]) * share_rows
        for chunk in range(chunks):
            rows_held[low : low + share_rows, chunk * 128 : (chunk + 1) * 128] = lines[
                chunk * share_rows : (chunk + 1) * share_rows
            ]
    latent = rows_held[...]
    aside = pltpu.roll(latent, latent.shape[1] - RIM, 1).astype(jnp.bfloat16)
    latent = latent.astype(jnp.bfloat16)
    held_rows = latent.shape[0]
    unit = lax.broadcasted_iota(jnp.int32, (UNITS, held_rows), 0)
    held = lax.broadcasted_iota(jnp.int32, (UNITS, held_rows), 1)
    side = (held >= members * share_rows).astype(jnp.int32)
    member = (held // share_rows - side * members) ^ (position // 2)
    held = (2 * member + ((position & 1) ^ side)) * share_rows + held % share_rows
    frame = sum((unit >= (k + 1) * REACH).astype(jnp.int32) for k in range(LF))
    reach = unit - frame * REACH
    selectors = []
    for tap in TAPS:
        for row_parity in range(2):
            for i in range(2):
                token_row = first_row + (reach >> 1) - 1 + i
                source = frame + tap - 2
                wanted = (
                    ((reach & 1) == row_parity)
                    & (token_row >= 0)
                    & (token_row < grid_rows)
                    & (source >= 0)
                    & (source < LF)
                )
                target = jnp.where(wanted, source * grid_rows + token_row, -1)
                selectors.append(jnp.where(held == target, 1.0, 0.0).astype(jnp.bfloat16))
    selector = jnp.concatenate(selectors, axis=0)
    even = jnp.dot(selector, latent, preferred_element_type=jnp.float32)
    odd = jnp.dot(selector, aside, preferred_element_type=jnp.float32)
    for chunk in range(chunks):
        lanes = slice(chunk * 128, (chunk + 1) * 128)
        for group in range(len(selectors)):
            rows = slice(group * UNITS, (group + 1) * UNITS)
            piece = jnp.concatenate([even[rows, lanes], odd[rows, lanes]], axis=0)
            patches[
                chunk * 2 * UNITS : (chunk + 1) * 2 * UNITS, group * 128 : (group + 1) * 128
            ] = piece.astype(jnp.bfloat16)

    for copy in small:
        copy.wait()
    nothing = jnp.zeros((channels, features), jnp.bfloat16)
    base = 0
    for tap in TAPS:
        for row_parity in range(2):
            for i, j, p, q in [
                (i, j, p, q) for i in range(2) for j in range(2) for p in range(2) for q in range(2)
            ]:
                for col_parity in range(2):
                    row_tap, col_tap = 2 * i + p - row_parity, 2 * j + q - col_parity
                    inside = 0 <= row_tap < 3 and 0 <= col_tap < 3
                    taps[base : base + channels, col_parity * features : (col_parity + 1) * features] = (
                        in_weight_ref[tap, row_tap, col_tap] if inside else nothing
                    )
                base += channels

    unit_row = lax.broadcasted_iota(jnp.int32, (UNITS, 1), 0)
    row_frame = sum((unit_row >= (k + 1) * REACH).astype(jnp.int32) for k in range(LF))
    pixel_row = 2 * first_row + unit_row - row_frame * REACH - 1
    row_inside = (pixel_row >= 0) & (pixel_row < 2 * grid_rows)
    in_bias = in_bias_ref[...].reshape(1, features)
    half_gain = gain_ref[...].reshape(1, features) * 0.5

    def first_layer(chunk):
        for corner in range(2):
            start = (chunk * 2 + corner) * UNITS
            for col_parity in range(2):
                value = (
                    raw[pl.ds(start, UNITS), col_parity * features : (col_parity + 1) * features]
                    + in_bias
                )
                value = value.astype(jnp.bfloat16).astype(jnp.float32)
                scale = lax.rsqrt(jnp.mean(value * value, axis=1, keepdims=True) + 1e-06)
                column = chunk * 4 + corner * 2 + col_parity
                pixel = section * columns + column - 1
                keep = row_inside & (pixel >= 0) & (pixel < width)
                half = value * jnp.where(keep, scale, 0.0) * half_gain
                result = half + half * jnp.tanh(half)
                at = pl.ds(column * UNITS, UNITS)
                for lane in range(lane_tiles):
                    lanes = slice(lane * 128, (lane + 1) * 128)
                    hidden[lane, at] = value[:, lanes]
                    activated[lane, at] = result[:, lanes]

    middle = (chunks + 1) // 2
    groups = ((0, middle), (middle, chunks))
    for low, high in groups:
        rows = slice(low * 2 * UNITS, high * 2 * UNITS)
        raw[rows] = jnp.dot(patches[rows], taps[...], preferred_element_type=jnp.float32)
    for low, high in groups:
        for chunk in range(low, high):
            first_layer(chunk)

    def pair_up(phase, pair):
        at = slice(pair * 16, pair * 16 + 16)
        for lane in range(lane_tiles):
            for field in range(LF):
                for row_tap in range(3):
                    start = (2 * pair + phase) * UNITS + field * REACH + row_tap
                    joined = jnp.concatenate(
                        [activated[lane, pl.ds(start + k * UNITS, ROWS)] for k in range(2)], axis=0
                    )
                    to_lane = (field * 3 + row_tap) * features + lane * 128
                    active[phase, at, to_lane : to_lane + 128] = joined.astype(jnp.bfloat16)

    rows = columns * ROWS
    depth = 3 * features

    def windows(low, high, lanes):
        return jnp.concatenate(
            [
                active[tap % 2, 16 * (tap // 2) + low : 16 * (tap // 2) + high, lanes]
                for tap in range(3)
            ],
            axis=1,
        )

    def weights(lanes):
        return jnp.concatenate([mid_weight[tap, :, lanes] for tap in range(3)], axis=0)

    mid_bias = mid_bias_ref[...].reshape(1, features)

    def finish(field):
        tile_row = lax.broadcasted_iota(jnp.int32, (columns * ROWS, 128), 0) & (ROWS - 1)
        for lane in range(lane_tiles):
            lanes = slice(lane * 128, (lane + 1) * 128)
            skip = jnp.concatenate(
                [
                    hidden[lane, pl.ds((column + 1) * UNITS + field * REACH + 1, ROWS)]
                    for column in range(columns)
                ],
                axis=0,
            )
            value = summed[field, lane] + skip + mid_bias[:, lanes]
            value = jnp.where(tile_row < 2 * filled, value, 0.0)
            value = jnp.swapaxes(value.reshape(columns, ROWS, 128), 0, 1)
            out_ref[field, :, :, lanes] = value.astype(jnp.bfloat16)
        leave(field).start()

    def leave(field):
        return pltpu.make_async_copy(out_ref.at[field], out_hbm.at[field], out_sems.at[field])

    for phase in range(2):
        for pair in range(pairs - phase):
            pair_up(phase, pair)
    for tap in range(3):
        for copy in load(tap):
            copy.wait()
    early = windows(0, rows, slice(0, depth))
    late = windows(0, rows, slice(depth, 2 * depth))
    for left in range(0, 2 * features, 256):
        block = jnp.dot(
            early, weights(slice(left, left + 256)), preferred_element_type=jnp.float32
        )
        for lane in range(2):
            field, tile = divmod(left // 128 + lane, lane_tiles)
            summed[field, tile] = block[:, lane * 128 : (lane + 1) * 128]
    finish(0)
    for left in range(0, features, 256):
        right = min(left + 256, features)
        block = jnp.dot(late, weights(slice(left, right)), preferred_element_type=jnp.float32)
        for lane in range((right - left) // 128):
            tile = left // 128 + lane
            summed[1, tile] = summed[1, tile] + block[:, lane * 128 : (lane + 1) * 128]
    finish(1)
    for field in range(LF):
        leave(field).wait()


def decode_tile(
    own,
    other,
    share_rows,
    grid_rows,
    width,
    tile_rows,
    conv_in_weight,
    conv_in_bias,
    norm_gain,
    conv_mid_weight,
    conv_mid_bias,
):
    sections = lax.axis_size("sect")
    channels, features = conv_in_weight.shape[3:]
    token_width = 4 * channels
    columns = width // sections
    span = columns // 2
    pairs = span + 1
    chunks = (span + 2) * token_width // 128
    lane_tiles = features // 128
    vmem = pl.BlockSpec(memory_space=pltpu.VMEM)
    hbm = pl.BlockSpec(memory_space=pltpu.HBM)
    slots = len(TAPS)
    depth = slots * 2 * 4 * token_width
    held = chunks * 4 * UNITS
    return pl.pallas_call(
        functools.partial(decode_body, grid_rows, width, share_rows, len(own), len(other)),
        in_specs=[vmem] * (len(own) + len(other)) + [hbm] * 6,
        out_specs=hbm,
        out_shape=jax.ShapeDtypeStruct((LF, ROWS, columns, features), jnp.bfloat16),
        scratch_shapes=[
            pltpu.SMEM(tile_rows.shape, tile_rows.dtype),
            pltpu.VMEM((LF, ROWS, columns, features), jnp.bfloat16),
            pltpu.VMEM((3, 3 * features, slots * features), jnp.bfloat16),
            pltpu.VMEM(conv_in_weight.shape, jnp.bfloat16),
            pltpu.VMEM(conv_in_bias.shape, jnp.float32),
            pltpu.VMEM(norm_gain.shape, jnp.float32),
            pltpu.VMEM(conv_mid_bias.shape, jnp.float32),
            pltpu.VMEM((depth, 2 * features), jnp.bfloat16),
            pltpu.VMEM((2 * len(own) * share_rows, chunks * 128), jnp.float32),
            pltpu.VMEM((chunks * 2 * UNITS, depth), jnp.bfloat16),
            pltpu.VMEM((chunks * 2 * UNITS, 2 * features), jnp.float32),
            pltpu.VMEM((lane_tiles, held, 128), jnp.float32),
            pltpu.VMEM((lane_tiles, held, 128), jnp.float32),
            pltpu.VMEM((2, pairs * 16, LF * 3 * features), jnp.bfloat16),
            pltpu.VMEM((LF, lane_tiles, columns * ROWS, 128), jnp.float32),
            pltpu.SemaphoreType.DMA((3, 3, slots)),
            pltpu.SemaphoreType.DMA((5,)),
            pltpu.SemaphoreType.DMA((LF,)),
        ],
        compiler_params=pltpu.CompilerParams(vmem_limit_bytes=DECODE_VMEM),
        cost_estimate=pl.CostEstimate(
            flops=2 * 3 * 9 * columns * ROWS * features * features,
            bytes_accessed=slots * 9 * features * features * 2,
            transcendentals=held * features,
        ),
        name="decode_tile",
    )(
        *own,
        *other,
        *in_hbm(
            tile_rows, conv_in_weight, conv_in_bias, norm_gain, conv_mid_weight, conv_mid_bias
        ),
    )


def on_device(
    queries,
    key_tokens,
    value_tokens,
    latent,
    tile_rows,
    conv_in_weight,
    conv_in_bias,
    norm_gain,
    conv_mid_weight,
    conv_mid_bias,
):
    devices = lax.axis_size("seq")
    groups = parity_groups(devices)
    grid_rows = latent.shape[0] * devices // LF
    token_width = 4 * conv_in_weight.shape[3]
    packed = pack_heads(queries, key_tokens, value_tokens, latent, token_width)
    own = [
        lax.ppermute(piece, "seq", xor_pairs(2 * m)) if m else piece
        for m, piece in zip(sending_order(len(packed)), packed)
    ]
    token_rows, half = queries.shape[0], len(own) // 2
    other = [
        lax.ppermute(join(part, token_rows), "seq", xor_pairs(1))
        for part in (own[:half], own[half:])
    ]
    mixed = attend(own, other, token_rows)
    returned = lax.all_to_all(mixed, "seq", 0, 0, axis_index_groups=groups, tiled=True)
    frames = decode_tile(
        own,
        other,
        latent.shape[0],
        grid_rows,
        2 * latent.shape[1] // token_width,
        tile_rows,
        conv_in_weight,
        conv_in_bias,
        norm_gain,
        conv_mid_weight,
        conv_mid_bias,
    )
    return (unpack_heads(returned), frames)


def solution(mesh):
    in_specs = (
        P("seq", None),
        P("seq", None),
        P("seq", None),
        P("seq", None),
        P(),
        P(),
        P(),
        P(),
        P(),
        P(),
    )
    out_specs = (P("seq", "sect"), P(None, "seq", "sect", None))
    return jax.shard_map(
        on_device, mesh=mesh, in_specs=in_specs, out_specs=out_specs, check_vma=False
    )
```

```python
import functools
import math

import jax
import jax.numpy as jnp
from jax import lax
from jax.experimental import pallas as pl
from jax.experimental.pallas import tpu as pltpu
from jax.sharding import PartitionSpec as P

DH = 128
LF = 2
MAXT = 4
RIM = 64
TAPS = (1, 2)
ROWS = 2 * MAXT
REACH = ROWS + 2
UNITS = -(-LF * REACH // 8) * 8
DECODE_VMEM = 32 * 1024 * 1024
ATTEND_VMEM = 32 * 1024 * 1024
COPY_VMEM = 16 * 1024 * 1024


def parity_groups(devices):
    return [list(range(parity, devices, 2)) for parity in range(2)]


def in_hbm(*arrays):
    return [pltpu.with_memory_space_constraint(array, pltpu.HBM) for array in arrays]


def pack_body(query_ref, key_ref, value_ref, latent_ref, *refs):
    packed_refs, (held, latent_held, sems) = refs[:-3], refs[-3:]
    heads = len(packed_refs)
    chip = lax.axis_index("seq") // 2
    token_rows = query_ref.shape[0]
    section = lax.axis_index("sect")
    wide_columns = pl.ds(pl.multiple_of(section * heads * DH, DH), heads * DH)
    copies = [
        pltpu.make_async_copy(ref.at[:, wide_columns], held.at[place], sems.at[place])
        for place, ref in enumerate((query_ref, key_ref, value_ref))
    ]
    latent_copy = pltpu.make_async_copy(latent_ref, latent_held, sems.at[3])
    latent_copy.start()
    for copy in copies:
        copy.start()
    rows, width = latent_ref.shape
    latent_copy.wait()
    half, rim = width // 2, RIM
    wide = latent_held[...].astype(jnp.float32)
    rim_zeros = jnp.zeros((rows, rim), jnp.float32)
    lower = jnp.concatenate([rim_zeros, wide[:, : half + rim]], axis=1)
    upper = jnp.concatenate([wide[:, half - rim :], rim_zeros], axis=1)
    share = jnp.where(section == 0, lower, upper)
    chunks = share.shape[1] // DH
    lines = [share[:, chunk * DH : (chunk + 1) * DH] for chunk in range(chunks)]
    spare = packed_refs[0].shape[0] - 3 * token_rows - chunks * rows
    lines.append(jnp.zeros((spare, DH), jnp.float32))
    share = jnp.concatenate(lines, axis=0).astype(jnp.bfloat16)
    for packed_ref in packed_refs:
        packed_ref[3 * token_rows :] = share
    for place, copy in enumerate(copies):
        copy.wait()
        for m, packed_ref in zip(sending_order(heads), packed_refs):
            columns = pl.ds(pl.multiple_of((chip ^ m) * DH, DH), DH)
            packed_ref[place * token_rows : (place + 1) * token_rows] = held[place, :, columns]


def pack_heads(queries, key_tokens, value_tokens, latent, token_width):
    token_rows, width = queries.shape
    sections = lax.axis_size("sect")
    heads = width // DH // sections
    span = latent.shape[1] // sections + 2 * token_width
    extra = -(-latent.shape[0] * (span // DH) // 16) * 16
    hbm = pl.BlockSpec(memory_space=pltpu.HBM)
    vmem = pl.BlockSpec(memory_space=pltpu.VMEM)
    return pl.pallas_call(
        pack_body,
        in_specs=[hbm] * 4,
        out_specs=[vmem] * heads,
        out_shape=[jax.ShapeDtypeStruct((3 * token_rows + extra, DH), queries.dtype)] * heads,
        scratch_shapes=[
            pltpu.VMEM((3, token_rows, heads * DH), queries.dtype),
            pltpu.VMEM(latent.shape, latent.dtype),
            pltpu.SemaphoreType.DMA((4,)),
        ],
        compiler_params=pltpu.CompilerParams(vmem_limit_bytes=COPY_VMEM),
        name="pack_heads",
    )(*in_hbm(queries, key_tokens, value_tokens, latent))


def sending_order(chips):
    far, near = list(range(chips // 2, chips)), list(range(1, chips // 2))
    return [0, *far[:1], *near[1:2], *far[2:3], *far[1:2], *far[3:], *near[2:], *near[:1]]


def xor_pairs(distance):
    return [(i, i ^ distance) for i in range(lax.axis_size("seq"))]


def join_body(*refs):
    out_ref = refs[-1]
    for place, ref in enumerate(refs[:-1]):
        out_ref[place] = ref[ref.shape[0] - out_ref.shape[1] :]


def join(pieces, skipped):
    rows, width = pieces[0].shape
    vmem = pl.BlockSpec(memory_space=pltpu.VMEM)
    return pl.pallas_call(
        join_body,
        in_specs=[vmem] * len(pieces),
        out_specs=vmem,
        out_shape=jax.ShapeDtypeStruct((len(pieces), rows - skipped, width), pieces[0].dtype),
        compiler_params=pltpu.CompilerParams(vmem_limit_bytes=COPY_VMEM),
        name="join",
    )(*pieces)


def flat(array):
    return array.reshape(-1, array.shape[-1])


def softmax_part(query, keys, values):
    scores = lax.dot_general(
        query, keys, (((1,), (1,)), ((), ())), preferred_element_type=jnp.float32
    ) * (1.0 / math.sqrt(DH))
    largest = jnp.max(scores, axis=1, keepdims=True)
    exponents = jnp.exp(scores - largest)
    totals = jnp.sum(exponents, axis=1, keepdims=True)
    mixed = jnp.dot(exponents.astype(jnp.bfloat16), values, preferred_element_type=jnp.float32)
    return largest, totals, mixed


def piece_rows(place, token_rows, pieces):
    at = slice(place * token_rows, (place + 1) * token_rows)
    return jnp.concatenate([ref[at] for ref in pieces], axis=0)


def attend_own_body(token_rows, *refs):
    pieces, (other_ref, mixed_ref, stats_ref) = refs[:-3], refs[-3:]
    block = len(pieces) if len(pieces) <= 8 else 4
    keys = jnp.concatenate(
        [piece_rows(1, token_rows, pieces), flat(other_ref[:, :token_rows])], axis=0
    )
    values = jnp.concatenate(
        [piece_rows(2, token_rows, pieces), flat(other_ref[:, token_rows : 2 * token_rows])], axis=0
    )
    for step in range(0, len(pieces), block):
        query = piece_rows(0, token_rows, pieces[step : step + block])
        largest, totals, mixed = softmax_part(query, keys, values)
        at = slice(step * token_rows, (step + block) * token_rows)
        mixed_ref[at] = mixed
        stats_ref[0, at] = jnp.broadcast_to(largest, mixed.shape)
        stats_ref[1, at] = jnp.broadcast_to(totals, mixed.shape)


def attend_body(*refs):
    other_ref, mixed_ref, stats_ref, out_hbm, out_ref, sems = refs[-6:]
    pieces = refs[:-6]
    members, token_rows, _ = out_ref.shape
    block = members if members <= 8 else 4
    chip = lax.axis_index("seq") // 2
    order = sending_order(members)

    def leave(m):
        target = out_hbm.at[chip ^ order[m]]
        return pltpu.make_async_copy(out_ref.at[m], target, sems.at[m])

    keys = flat(other_ref[:, :token_rows])
    values = flat(other_ref[:, token_rows : 2 * token_rows])
    for step in range(0, members, block):
        query = piece_rows(0, token_rows, pieces[step : step + block])
        largest, totals, mixed = softmax_part(query, keys, values)
        at = slice(step * token_rows, (step + block) * token_rows)
        earlier = stats_ref[0, at]
        top = jnp.maximum(earlier, largest)
        before, now = jnp.exp(earlier - top), jnp.exp(largest - top)
        totals = stats_ref[1, at] * before + totals * now
        mixed = (mixed_ref[at] * before + mixed * now) / totals
        mixed = mixed.astype(out_ref.dtype)
        for m in range(block):
            out_ref[step + m] = mixed[m * token_rows : (m + 1) * token_rows]
            leave(step + m).start()
    for m in range(members):
        leave(m).wait()


def attend(own, other, token_rows):
    members = len(own)
    total = members * token_rows
    vmem = pl.BlockSpec(memory_space=pltpu.VMEM)
    params = pltpu.CompilerParams(vmem_limit_bytes=ATTEND_VMEM)
    cost = pl.CostEstimate(
        flops=4 * total * total * DH,
        bytes_accessed=7 * total * DH * 2,
        transcendentals=total * total,
    )
    mixed, stats = pl.pallas_call(
        functools.partial(attend_own_body, token_rows),
        in_specs=[vmem] * (members + 1),
        out_specs=[vmem] * 2,
        out_shape=[
            jax.ShapeDtypeStruct((total, DH), jnp.float32),
            jax.ShapeDtypeStruct((2, total, DH), jnp.float32),
        ],
        compiler_params=params,
        cost_estimate=cost,
        name="attend_own",
    )(*own, other[0])
    return pl.pallas_call(
        attend_body,
        in_specs=[vmem] * (members + 3),
        out_specs=pl.BlockSpec(memory_space=pltpu.HBM),
        out_shape=jax.ShapeDtypeStruct((members, token_rows, DH), own[0].dtype),
        scratch_shapes=[
            pltpu.VMEM((members, token_rows, DH), own[0].dtype),
            pltpu.SemaphoreType.DMA((members,)),
        ],
        compiler_params=params,
        cost_estimate=cost,
        name="attend",
    )(*own, other[1], mixed, stats)


def unpack_body(in_ref, out_ref, sems):
    copies = [
        pltpu.make_async_copy(
            in_ref.at[head], out_ref.at[:, pl.ds(head * DH, DH)], sems.at[head]
        )
        for head in range(in_ref.shape[0])
    ]
    for copy in copies:
        copy.start()
    for copy in copies:
        copy.wait()


def unpack_heads(array):
    heads, token_rows, _ = array.shape
    return pl.pallas_call(
        unpack_body,
        in_specs=[pl.BlockSpec(memory_space=pltpu.VMEM)],
        out_specs=pl.BlockSpec(memory_space=pltpu.HBM),
        out_shape=jax.ShapeDtypeStruct((token_rows, heads * DH), array.dtype),
        scratch_shapes=[pltpu.SemaphoreType.DMA((heads,))],
        compiler_params=pltpu.CompilerParams(vmem_limit_bytes=COPY_VMEM),
        name="unpack_heads",
    )(array)


def decode_body(
    grid_rows,
    width,
    share_rows,
    members,
    halves,
    *refs,
):
    own, other, refs = refs[:members], refs[members : members + halves], refs[members + halves :]
    order = sending_order(members)
    (
    tile_hbm,
    in_weight_hbm,
    in_bias_hbm,
    gain_hbm,
    mid_weight_hbm,
    mid_bias_hbm,
    out_hbm,
    tile_ref,
    out_ref,
    mid_weight,
    in_weight_ref,
    in_bias_ref,
    gain_ref,
    mid_bias_ref,
    taps,
    rows_held,
    patches,
    raw,
    hidden,
    activated,
    active,
    summed,
    weight_sems,
    small_sems,
    out_sems,
    ) = refs
    pairs = active.shape[1] // 16
    channels, features = in_weight_ref.shape[3:]
    columns = out_ref.shape[2]
    lane_tiles = features // 128
    position = lax.axis_index("seq")
    section = lax.axis_index("sect")
    tile_copy = pltpu.make_async_copy(tile_hbm, tile_ref, small_sems.at[4])
    tile_copy.start()
    small = [
        pltpu.make_async_copy(source, target, small_sems.at[place])
        for place, (source, target) in enumerate(
            (
                (in_weight_hbm, in_weight_ref),
                (in_bias_hbm, in_bias_ref),
                (gain_hbm, gain_ref),
                (mid_bias_hbm, mid_bias_ref),
            )
        )
    ]
    for copy in small:
        copy.start()

    def load(col_tap):
        return [
            pltpu.make_async_copy(
                mid_weight_hbm.at[tap, row_tap, col_tap],
                mid_weight.at[
                    col_tap,
                    pl.ds(row_tap * features, features),
                    pl.ds((2 - tap) * features, features),
                ],
                weight_sems.at[col_tap, row_tap, slot],
            )
            for row_tap in range(3)
            for slot, tap in enumerate(TAPS)
        ]

    for col_tap in range(3):
        for copy in load(col_tap):
            copy.start()

    tile_copy.wait()
    filled = tile_ref[position]
    first_row = lax.fori_loop(0, position, lambda d, total: total + tile_ref[d], jnp.int32(0))

    chunks = rows_held.shape[1] // 128
    extra = -(-share_rows * chunks // 16) * 16
    shares = [ref[ref.shape[0] - extra :] for ref in own]
    shares += [ref[m, ref.shape[1] - extra :] for ref in other for m in range(ref.shape[0])]
    for place, share in enumerate(shares):
        lines = share.astype(jnp.float32)
        low = (place // members * members + order[place % members]) * share_rows
        for chunk in range(chunks):
            rows_held[low : low + share_rows, chunk * 128 : (chunk + 1) * 128] = lines[
                chunk * share_rows : (chunk + 1) * share_rows
            ]
    latent = rows_held[...]
    aside = pltpu.roll(latent, latent.shape[1] - RIM, 1).astype(jnp.bfloat16)
    latent = latent.astype(jnp.bfloat16)
    held_rows = latent.shape[0]
    unit = lax.broadcasted_iota(jnp.int32, (UNITS, held_rows), 0)
    held = lax.broadcasted_iota(jnp.int32, (UNITS, held_rows), 1)
    side = (held >= members * share_rows).astype(jnp.int32)
    member = (held // share_rows - side * members) ^ (position // 2)
    held = (2 * member + ((position & 1) ^ side)) * share_rows + held % share_rows
    frame = sum((unit >= (k + 1) * REACH).astype(jnp.int32) for k in range(LF))
    reach = unit - frame * REACH
    selectors = []
    for tap in TAPS:
        for row_parity in range(2):
            for i in range(2):
                token_row = first_row + (reach >> 1) - 1 + i
                source = frame + tap - 2
                wanted = (
                    ((reach & 1) == row_parity)
                    & (token_row >= 0)
                    & (token_row < grid_rows)
                    & (source >= 0)
                    & (source < LF)
                )
                target = jnp.where(wanted, source * grid_rows + token_row, -1)
                selectors.append(jnp.where(held == target, 1.0, 0.0).astype(jnp.bfloat16))
    selector = jnp.concatenate(selectors, axis=0)
    even = jnp.dot(selector, latent, preferred_element_type=jnp.float32)
    odd = jnp.dot(selector, aside, preferred_element_type=jnp.float32)
    for chunk in range(chunks):
        lanes = slice(chunk * 128, (chunk + 1) * 128)
        for group in range(len(selectors)):
            rows = slice(group * UNITS, (group + 1) * UNITS)
            piece = jnp.concatenate([even[rows, lanes], odd[rows, lanes]], axis=0)
            patches[
                chunk * 2 * UNITS : (chunk + 1) * 2 * UNITS, group * 128 : (group + 1) * 128
            ] = piece.astype(jnp.bfloat16)

    for copy in small:
        copy.wait()
    nothing = jnp.zeros((channels, features), jnp.bfloat16)
    base = 0
    for tap in TAPS:
        for row_parity in range(2):
            for i, j, p, q in [
                (i, j, p, q) for i in range(2) for j in range(2) for p in range(2) for q in range(2)
            ]:
                for col_parity in range(2):
                    row_tap, col_tap = 2 * i + p - row_parity, 2 * j + q - col_parity
                    inside = 0 <= row_tap < 3 and 0 <= col_tap < 3
                    taps[base : base + channels, col_parity * features : (col_parity + 1) * features] = (
                        in_weight_ref[tap, row_tap, col_tap] if inside else nothing
                    )
                base += channels

    unit_row = lax.broadcasted_iota(jnp.int32, (UNITS, 1), 0)
    row_frame = sum((unit_row >= (k + 1) * REACH).astype(jnp.int32) for k in range(LF))
    pixel_row = 2 * first_row + unit_row - row_frame * REACH - 1
    row_inside = (pixel_row >= 0) & (pixel_row < 2 * grid_rows)
    in_bias = in_bias_ref[...].reshape(1, features)
    half_gain = gain_ref[...].reshape(1, features) * 0.5

    def first_layer(chunk):
        for corner in range(2):
            start = (chunk * 2 + corner) * UNITS
            for col_parity in range(2):
                value = (
                    raw[pl.ds(start, UNITS), col_parity * features : (col_parity + 1) * features]
                    + in_bias
                )
                value = value.astype(jnp.bfloat16).astype(jnp.float32)
                scale = lax.rsqrt(jnp.mean(value * value, axis=1, keepdims=True) + 1e-06)
                column = chunk * 4 + corner * 2 + col_parity
                pixel = section * columns + column - 1
                keep = row_inside & (pixel >= 0) & (pixel < width)
                half = value * jnp.where(keep, scale, 0.0) * half_gain
                result = half + half * jnp.tanh(half)
                at = pl.ds(column * UNITS, UNITS)
                for lane in range(lane_tiles):
                    lanes = slice(lane * 128, (lane + 1) * 128)
                    hidden[lane, at] = value[:, lanes]
                    activated[lane, at] = result[:, lanes]

    middle = (chunks + 1) // 2
    groups = ((0, middle), (middle, chunks))
    for low, high in groups:
        rows = slice(low * 2 * UNITS, high * 2 * UNITS)
        raw[rows] = jnp.dot(patches[rows], taps[...], preferred_element_type=jnp.float32)
    for low, high in groups:
        for chunk in range(low, high):
            first_layer(chunk)

    def pair_up(phase, pair):
        at = slice(pair * 16, pair * 16 + 16)
        for lane in range(lane_tiles):
            for field in range(LF):
                for row_tap in range(3):
                    start = (2 * pair + phase) * UNITS + field * REACH + row_tap
                    joined = jnp.concatenate(
                        [activated[lane, pl.ds(start + k * UNITS, ROWS)] for k in range(2)], axis=0
                    )
                    to_lane = (field * 3 + row_tap) * features + lane * 128
                    active[phase, at, to_lane : to_lane + 128] = joined.astype(jnp.bfloat16)

    rows = columns * ROWS
    depth = 3 * features

    def windows(low, high, lanes):
        return jnp.concatenate(
            [
                active[tap % 2, 16 * (tap // 2) + low : 16 * (tap // 2) + high, lanes]
                for tap in range(3)
            ],
            axis=1,
        )

    def weights(lanes):
        return jnp.concatenate([mid_weight[tap, :, lanes] for tap in range(3)], axis=0)

    mid_bias = mid_bias_ref[...].reshape(1, features)

    def finish(field):
        tile_row = lax.broadcasted_iota(jnp.int32, (columns * ROWS, 128), 0) & (ROWS - 1)
        for lane in range(lane_tiles):
            lanes = slice(lane * 128, (lane + 1) * 128)
            skip = jnp.concatenate(
                [
                    hidden[lane, pl.ds((column + 1) * UNITS + field * REACH + 1, ROWS)]
                    for column in range(columns)
                ],
                axis=0,
            )
            value = summed[field, lane] + skip + mid_bias[:, lanes]
            value = jnp.where(tile_row < 2 * filled, value, 0.0)
            value = jnp.swapaxes(value.reshape(columns, ROWS, 128), 0, 1)
            out_ref[field, :, :, lanes] = value.astype(jnp.bfloat16)
        leave(field).start()

    def leave(field):
        return pltpu.make_async_copy(out_ref.at[field], out_hbm.at[field], out_sems.at[field])

    for phase in range(2):
        for pair in range(pairs - phase):
            pair_up(phase, pair)
    for tap in range(3):
        for copy in load(tap):
            copy.wait()
    early = windows(0, rows, slice(0, depth))
    late = windows(0, rows, slice(depth, 2 * depth))
    for left in range(0, 2 * features, 256):
        block = jnp.dot(
            early, weights(slice(left, left + 256)), preferred_element_type=jnp.float32
        )
        for lane in range(2):
            field, tile = divmod(left // 128 + lane, lane_tiles)
            summed[field, tile] = block[:, lane * 128 : (lane + 1) * 128]
    finish(0)
    for left in range(0, features, 256):
        right = min(left + 256, features)
        block = jnp.dot(late, weights(slice(left, right)), preferred_element_type=jnp.float32)
        for lane in range((right - left) // 128):
            tile = left // 128 + lane
            summed[1, tile] = summed[1, tile] + block[:, lane * 128 : (lane + 1) * 128]
    finish(1)
    for field in range(LF):
        leave(field).wait()


def decode_tile(
    own,
    other,
    share_rows,
    grid_rows,
    width,
    tile_rows,
    conv_in_weight,
    conv_in_bias,
    norm_gain,
    conv_mid_weight,
    conv_mid_bias,
):
    sections = lax.axis_size("sect")
    channels, features = conv_in_weight.shape[3:]
    token_width = 4 * channels
    columns = width // sections
    span = columns // 2
    pairs = span + 1
    chunks = (span + 2) * token_width // 128
    lane_tiles = features // 128
    vmem = pl.BlockSpec(memory_space=pltpu.VMEM)
    hbm = pl.BlockSpec(memory_space=pltpu.HBM)
    slots = len(TAPS)
    depth = slots * 2 * 4 * token_width
    held = chunks * 4 * UNITS
    return pl.pallas_call(
        functools.partial(decode_body, grid_rows, width, share_rows, len(own), len(other)),
        in_specs=[vmem] * (len(own) + len(other)) + [hbm] * 6,
        out_specs=hbm,
        out_shape=jax.ShapeDtypeStruct((LF, ROWS, columns, features), jnp.bfloat16),
        scratch_shapes=[
            pltpu.SMEM(tile_rows.shape, tile_rows.dtype),
            pltpu.VMEM((LF, ROWS, columns, features), jnp.bfloat16),
            pltpu.VMEM((3, 3 * features, slots * features), jnp.bfloat16),
            pltpu.VMEM(conv_in_weight.shape, jnp.bfloat16),
            pltpu.VMEM(conv_in_bias.shape, jnp.float32),
            pltpu.VMEM(norm_gain.shape, jnp.float32),
            pltpu.VMEM(conv_mid_bias.shape, jnp.float32),
            pltpu.VMEM((depth, 2 * features), jnp.bfloat16),
            pltpu.VMEM((2 * len(own) * share_rows, chunks * 128), jnp.float32),
            pltpu.VMEM((chunks * 2 * UNITS, depth), jnp.bfloat16),
            pltpu.VMEM((chunks * 2 * UNITS, 2 * features), jnp.float32),
            pltpu.VMEM((lane_tiles, held, 128), jnp.float32),
            pltpu.VMEM((lane_tiles, held, 128), jnp.float32),
            pltpu.VMEM((2, pairs * 16, LF * 3 * features), jnp.bfloat16),
            pltpu.VMEM((LF, lane_tiles, columns * ROWS, 128), jnp.float32),
            pltpu.SemaphoreType.DMA((3, 3, slots)),
            pltpu.SemaphoreType.DMA((5,)),
            pltpu.SemaphoreType.DMA((LF,)),
        ],
        compiler_params=pltpu.CompilerParams(vmem_limit_bytes=DECODE_VMEM),
        cost_estimate=pl.CostEstimate(
            flops=2 * 3 * 9 * columns * ROWS * features * features,
            bytes_accessed=slots * 9 * features * features * 2,
            transcendentals=held * features,
        ),
        name="decode_tile",
    )(
        *own,
        *other,
        *in_hbm(
            tile_rows, conv_in_weight, conv_in_bias, norm_gain, conv_mid_weight, conv_mid_bias
        ),
    )


def on_device(
    queries,
    key_tokens,
    value_tokens,
    latent,
    tile_rows,
    conv_in_weight,
    conv_in_bias,
    norm_gain,
    conv_mid_weight,
    conv_mid_bias,
):
    devices = lax.axis_size("seq")
    groups = parity_groups(devices)
    grid_rows = latent.shape[0] * devices // LF
    token_width = 4 * conv_in_weight.shape[3]
    packed = pack_heads(queries, key_tokens, value_tokens, latent, token_width)
    own = [
        lax.ppermute(piece, "seq", xor_pairs(2 * m)) if m else piece
        for m, piece in zip(sending_order(len(packed)), packed)
    ]
    token_rows, half = queries.shape[0], len(own) // 2
    other = [
        lax.ppermute(join(part, token_rows), "seq", xor_pairs(1))
        for part in (own[:half], own[half:])
    ]
    mixed = attend(own, other, token_rows)
    returned = lax.all_to_all(mixed, "seq", 0, 0, axis_index_groups=groups, tiled=True)
    frames = decode_tile(
        own,
        other,
        latent.shape[0],
        grid_rows,
        2 * latent.shape[1] // token_width,
        tile_rows,
        conv_in_weight,
        conv_in_bias,
        norm_gain,
        conv_mid_weight,
        conv_mid_bias,
    )
    return (unpack_heads(returned), frames)


def solution(mesh):
    in_specs = (
        P("seq", None),
        P("seq", None),
        P("seq", None),
        P("seq", None),
        P(),
        P(),
        P(),
        P(),
        P(),
        P(),
    )
    out_specs = (P("seq", "sect"), P(None, "seq", "sect", None))
    return jax.shard_map(
        on_device, mesh=mesh, in_specs=in_specs, out_specs=out_specs, check_vma=False
    )
```
